32 devices in a mesh: hst: 8 (over y, x, core), tp: 4 (over z).
Axes of the slice: x: 2, y: 2, z: 4, core: 2. Of those that a mesh axis runs over, the one named last changes fastest.
Arguments:
- ctx_q: bfloat16 [6144, 8192], P('hst', 'tp'), may hold values from -11.2 to 11.2
- ctx_kv: bfloat16 [2, 6144, 1024], P(None, 'hst'), may hold values from -4.5 to 4.5
- lengths: int32 [8], replicated, may hold values from 192 to 768, as said below
- query_q: bfloat16 [64, 8192], P('hst', 'tp'), may hold values from -11.2 to 11.2
- query_kv: bfloat16 [2, 64, 1024], P(None, 'hst'), may hold values from -4.5 to 4.5
- out_weight: bfloat16 [8192, 8192], P('tp', 'hst'), may hold values from -0.0625 to 0.0625
Outputs:
- context_out: bfloat16 [6144, 8192], P('hst', 'tp')
- query_out: bfloat16 [64, 8192], P(None, 'hst')
The draws below stay inside these ranges and needn't reach their ends.
Inputs may be any that keep to these rules, and one draw needn't show every extreme that they name: lengths[0] is 768; blocks with index below three quarters of 8 are full, the last block holds 192 live positions.
All inputs are finite; a program needn't handle non-finite values.
Results may differ from the reference program's by a relative error of at most 0.012.
Values may be sent and summed in bfloat16 or wider, within the bound.
No kernel may reach another device: no remote copies, remote signals or barrier semaphores. Data moves between devices by JAX's collectives and lax.ppermute only.
A program may use at most 64 MiB of HBM per device.

```python
import jax
import jax.numpy as jnp
from jax import lax

D = 8192
H = 64
KVH = 8
HD = 128
SLAB = 768
QN = 64
TOKENS = 6144
N_HST = 8


def draw_ctx_q(key, part):
    key = jax.random.fold_in(key, 1)
    full_shape = (TOKENS, H, HD)
    result = jnp.clip(2.8 * jax.random.normal(key, full_shape, jnp.float32), -11.2, 11.2)
    return result.reshape(TOKENS, H * HD).astype(jnp.bfloat16)


def draw_ctx_kv(key, part):
    key = jax.random.fold_in(key, 2)
    key_draw, value_draw = jax.random.split(key)
    full_shape = (TOKENS, KVH, HD)
    key_rows = jnp.clip(jax.random.normal(key_draw, full_shape, jnp.float32), -4.5, 4.5)
    value_rows = jnp.clip(jax.random.normal(value_draw, full_shape, jnp.float32), -4.5, 4.5)
    stacked = jnp.stack([key_rows, value_rows], 0)
    return stacked.reshape(2, TOKENS, KVH * HD).astype(jnp.bfloat16)


def draw_lengths(key, part):
    key = jax.random.fold_in(key, 5)
    host_count = TOKENS // SLAB
    host_ids = jnp.arange(host_count)
    random_len = jax.random.randint(key, (host_count,), SLAB // 4, SLAB + 1)
    result = jnp.where(host_ids * 4 < host_count * 3, SLAB, random_len)
    return jnp.where(host_ids == host_count - 1, SLAB // 4, result).astype(jnp.int32)


def draw_query_q(key, part):
    key = jax.random.fold_in(key, 3)
    full_shape = (QN, H, HD)
    result = jnp.clip(2.8 * jax.random.normal(key, full_shape, jnp.float32), -11.2, 11.2)
    return result.reshape(QN, H * HD).astype(jnp.bfloat16)


def draw_query_kv(key, part):
    key = jax.random.fold_in(key, 4)
    full_shape = (2, QN, KVH * HD)
    result = jnp.clip(jax.random.normal(key, full_shape, jnp.float32), -4.5, 4.5)
    return result.astype(jnp.bfloat16)


def levels(key, extent, pieces, low, largest):
    factor_of = 1.0
    for axis_at, parts in pieces:
        draws = jax.random.uniform(jax.random.fold_in(jax.random.fold_in(key, 6), axis_at), (parts,), jnp.float32, low / len(pieces), largest / len(pieces))
        factor_of = factor_of * jnp.repeat(jnp.exp(draws), extent[axis_at] // parts).reshape((-1,) + (1,) * (len(extent) - 1 - axis_at))
    return factor_of


def noise(rng, shape, spread, bound, cuts=(), held_as=jnp.bfloat16):
    loudness = levels(rng, shape, cuts, -0.22, 0.18) if cuts else 1.0
    entries = jax.random.normal(rng, shape, jnp.float32) * spread * loudness
    return jnp.minimum(jnp.maximum(entries, -bound), bound).astype(held_as)


def setup_inputs(seed: int = 0) -> dict:
    key_list = jax.random.split(jax.random.key(seed), 7)
    return {
        "ctx_q": draw_ctx_q(jax.random.fold_in(key_list[6], 71), 0),
        "ctx_kv": draw_ctx_kv(jax.random.fold_in(key_list[6], 71), 0),
        "lengths": draw_lengths(jax.random.fold_in(key_list[6], 71), 0),
        "query_q": draw_query_q(jax.random.fold_in(key_list[6], 71), 0),
        "query_kv": draw_query_kv(jax.random.fold_in(key_list[6], 71), 0),
        "out_weight": noise(key_list[5], (H * HD, D), (H * HD) ** -0.5, 0.0625, ((0, 4), (1, 8))),
    }


MASKED = -1.0e30


def reference(ctx_q, ctx_kv, lengths, query_q, query_kv, out_weight):
    group_size = H // KVH
    score_scale = HD ** -0.5
    q_rows = QN // N_HST
    row_ids = jnp.arange(SLAB)
    query_ids = jnp.arange(QN)
    block_q = ctx_q.reshape(N_HST, SLAB, H, HD)
    block_k = ctx_kv[0].reshape(N_HST, SLAB, KVH, HD)
    block_v = ctx_kv[1].reshape(N_HST, SLAB, KVH, HD)
    anchor_k = block_k[0]
    anchor_v = block_v[0]
    first_len = lengths[0]

    def encode_block(operands):
        host_id, q_block, k_block, v_block, own_len = operands
        own_ok = (row_ids[None, :] <= row_ids[:, None]) & (row_ids[None, :] < own_len)
        anchor_ok = (row_ids[None, :] < first_len) & (host_id > 0)
        allowed = jnp.concatenate([jnp.broadcast_to(anchor_ok, (SLAB, SLAB)), own_ok], 1)
        key_rows = jnp.concatenate([anchor_k, k_block], 0).transpose(1, 0, 2)
        value_rows = jnp.concatenate([anchor_v, v_block], 0).transpose(1, 0, 2)

        def per_group(inner):
            query_group, key_group, value_group = inner
            scores = jnp.einsum("igd,jd->gij", query_group.astype(jnp.float32), key_group.astype(jnp.float32)) * score_scale
            scores = jnp.where(allowed[None], scores, MASKED)
            peak = jnp.max(scores, axis=2, keepdims=True)
            expo = jnp.exp(scores - peak)
            probs = (expo / jnp.sum(expo, axis=2, keepdims=True)).astype(jnp.bfloat16)
            encoded = jnp.einsum("gij,jd->igd", probs.astype(jnp.float32), value_group.astype(jnp.float32))
            return encoded.astype(jnp.bfloat16)

        grouped = q_block.reshape(SLAB, KVH, group_size, HD).transpose(1, 0, 2, 3)
        encoded = lax.map(per_group, (grouped, key_rows, value_rows))
        encoded = encoded.transpose(1, 0, 2, 3).reshape(SLAB, H * HD)
        return jnp.where((row_ids < own_len)[:, None], encoded, jnp.zeros_like(encoded))

    context_out = lax.map(encode_block, (jnp.arange(N_HST), block_q, block_k, block_v, lengths))
    context_out = context_out.reshape(TOKENS, H * HD)

    query_groups = query_q.reshape(QN, KVH, group_size, HD).transpose(1, 0, 2, 3)
    self_k = query_kv[0].reshape(N_HST, q_rows, KVH, HD)
    self_v = query_kv[1].reshape(N_HST, q_rows, KVH, HD)

    def score_source(operands):
        host_id, k_block, v_block, own_len, self_keys, self_values = operands
        key_rows = jnp.concatenate([k_block, self_keys], 0).transpose(1, 0, 2)
        value_rows = jnp.concatenate([v_block, self_values], 0).transpose(1, 0, 2)
        context_ok = jnp.broadcast_to(row_ids[None, :] < own_len, (QN, SLAB))
        self_ok = (host_id * q_rows + jnp.arange(q_rows))[None, :] <= query_ids[:, None]
        allowed = jnp.concatenate([context_ok, self_ok], 1)

        def per_group(inner):
            query_group, key_group, value_group = inner
            scores = jnp.einsum("igd,jd->gij", query_group.astype(jnp.float32), key_group.astype(jnp.float32)) * score_scale
            scores = jnp.where(allowed[None], scores, MASKED)
            peak = jnp.max(scores, axis=2)
            expo = jnp.exp(scores - peak[:, :, None])
            denominator = jnp.sum(expo, axis=2)
            weighted = jnp.einsum("gij,jd->gid", expo.astype(jnp.bfloat16).astype(jnp.float32), value_group.astype(jnp.float32))
            return peak, denominator, weighted

        peak, denominator, weighted = lax.map(per_group, (query_groups, key_rows, value_rows))
        return peak.reshape(H, QN), denominator.reshape(H, QN), weighted.reshape(H, QN, HD)

    maxima, totals, outputs = lax.map(score_source, (jnp.arange(N_HST), block_k, block_v, lengths, self_k, self_v))
    global_max = jnp.max(maxima, axis=0)
    factor = jnp.exp(maxima - global_max[None])
    denominator = jnp.sum(totals * factor, axis=0)
    summed = jnp.sum(outputs * factor[..., None], axis=0)
    attended = (summed / denominator[..., None]).astype(jnp.bfloat16)
    attended = attended.transpose(1, 0, 2).reshape(QN, H * HD)
    query_out = jnp.dot(attended, out_weight, preferred_element_type=jnp.float32).astype(jnp.bfloat16)
    return context_out, query_out
```

```python
import functools

import jax
import jax.numpy as jnp
from jax import lax
from jax.experimental import pallas as pl
from jax.experimental.pallas import tpu as pltpu
from jax.sharding import PartitionSpec as P

H = 64
KVH = 8
HD = 128
MASKED = -1e30
LOG2E = 1.4426950408889634
SCALE2 = HD ** (-0.5) * LOG2E
TINY = 2.0 ** -90
BF = jnp.bfloat16
F32 = jnp.float32
VMEM = pl.BlockSpec(memory_space=pltpu.VMEM)
SMEM = pl.BlockSpec(memory_space=pltpu.SMEM)
ANY = pl.BlockSpec(memory_space=pl.ANY)


def params(mib=40):
    return pltpu.CompilerParams(vmem_limit_bytes=mib * 2**20)


def dot_t(a, b):
    return lax.dot_general(a, b, (((1,), (1,)), ((), ())), preferred_element_type=F32)


def dot(a, b):
    return lax.dot_general(a, b, (((1,), (0,)), ((), ())), preferred_element_type=F32)


def spread(value, axis, source):
    kept = jnp.where(lax.axis_index(axis) == source, value, 0).astype(value.dtype)
    return lax.psum(kept, axis)


def xor_pairs(size, bits, skip=()):
    return [(i, i ^ bits) for i in range(size) if (i ^ bits) not in skip]


def exchange(slots, axis, size, skip=()):
    return [slots[0]] + [
        lax.ppermute(slots[k], axis, xor_pairs(size, k, skip)) for k in range(1, size)
    ]


def pick_kernel(parts, group_size, local_heads, kv_ref, own_ref, *rest):
    piece_refs, sems = rest[: parts - 1], rest[parts - 1]
    width = own_ref.shape[2]
    rows = own_ref.shape[1]
    first = lax.axis_index("tp") * local_heads // group_size * HD
    cols = pl.ds(pl.multiple_of(first, HD), width)
    copies = [pltpu.make_async_copy(kv_ref.at[:, :, cols], own_ref, sems.at[0])]
    step = rows // parts
    for k in range(1, parts):
        copies.append(
            pltpu.make_async_copy(
                kv_ref.at[:, pl.ds(k * step, step), cols], piece_refs[k - 1], sems.at[k]
            )
        )
    for copy in copies:
        copy.start()
    for copy in copies:
        copy.wait()


def pick_kv(ctx_kv, kv_local, local_heads, parts):
    rows = ctx_kv.shape[1]
    width = kv_local * HD
    shapes = [jax.ShapeDtypeStruct((2, rows, width), BF)]
    shapes += [jax.ShapeDtypeStruct((2, rows // parts, width), BF)] * (parts - 1)
    return pl.pallas_call(
        functools.partial(pick_kernel, parts, H // KVH, local_heads),
        out_shape=shapes,
        in_specs=[ANY],
        out_specs=[ANY] * len(shapes),
        scratch_shapes=[pltpu.SemaphoreType.DMA((parts,))],
        compiler_params=params(),
        name="pick_kv",
    )(ctx_kv)


def fill_values(vaug, values):
    vaug[:, :HD] = values
    vaug[:, HD:] = jnp.ones_like(values)


def row_tile(slab):
    return 256 if slab % 256 == 0 else slab


def own_kernel(heads, q_ref, kv_ref, *rest):
    state_ref, vaug = rest[-2], rest[-1]
    slab = q_ref.shape[0]
    tile = row_tile(slab)

    @pl.when(pl.program_id(0) == 0)
    def _():
        fill_values(vaug, kv_ref[1])

    rows = lax.broadcasted_iota(jnp.int32, (tile, tile), 0)
    cols = lax.broadcasted_iota(jnp.int32, (tile, tile), 1)
    causal = cols <= rows
    tiles = [(h, r) for h in range(heads) for r in range(slab // tile)]

    def scores(at):
        h, r = tiles[at]
        query = q_ref[r * tile : (r + 1) * tile, h * HD : (h + 1) * HD]
        return dot_t(query, kv_ref[0, : (r + 1) * tile, :])

    current = scores(0)
    for at, (h, r) in enumerate(tiles):
        following = scores(at + 1) if at + 1 < len(tiles) else None
        expo = jnp.exp2(current * SCALE2)
        last = jnp.where(causal, expo[:, r * tile :], 0.0)
        expo = last if r == 0 else jnp.concatenate([expo[:, : r * tile], last], 1)
        total = dot(expo.astype(BF), vaug[: (r + 1) * tile, :])
        state_ref[r * tile : (r + 1) * tile, h * 2 * HD : (h + 1) * 2 * HD] = total.astype(BF)
        current = following


def own_part(ctx_q, own_kv, first, count, per_kv, after=()):
    slab = ctx_q.shape[0]
    heads = min(2, count)
    steps = count // heads
    kv = first // per_kv
    work = count * slab * (slab + row_tile(slab)) // 2
    return pl.pallas_call(
        functools.partial(own_kernel, heads),
        grid=(steps,),
        out_shape=jax.ShapeDtypeStruct((slab, count * 2 * HD), BF),
        in_specs=[
            pl.BlockSpec((slab, heads * HD), lambda i: (0, first // heads + i)),
            pl.BlockSpec((2, slab, HD), lambda i: (0, 0, kv)),
        ]
        + [ANY] * len(after),
        out_specs=pl.BlockSpec((slab, heads * 2 * HD), lambda i: (0, i)),
        scratch_shapes=[pltpu.VMEM((slab, 2 * HD), BF)],
        compiler_params=params(),
        cost_estimate=pl.CostEstimate(
            flops=work * HD * 8, bytes_accessed=count * slab * HD * 6, transcendentals=work
        ),
        name="context_own",
    )(ctx_q, own_kv, *after)


def anchor_kernel(heads, pieces, count_after, lengths_ref, q_ref, state_ref, kv_ref, *rest):
    piece_refs = rest[:pieces]
    out_ref, keys, vaug = rest[-3], rest[-2], rest[-1]
    slab = q_ref.shape[0]
    tile = row_tile(slab)
    host = lax.axis_index("hst")
    own_len = lengths_ref[host]
    step = slab // pieces

    @pl.when(pl.program_id(0) == 0)
    def _():
        for k in range(pieces):
            keys[k * step : (k + 1) * step, :] = piece_refs[k][0]
            vaug[k * step : (k + 1) * step, :HD] = piece_refs[k][1]
            vaug[k * step : (k + 1) * step, HD:] = jnp.ones((step, HD), BF)

    tiles = [(h, r) for h in range(heads) for r in range(slab // tile)]
    row_ids = lax.broadcasted_iota(jnp.int32, (tile, HD), 0)

    def query_of(at):
        h, r = tiles[at]
        return q_ref[r * tile : (r + 1) * tile, h * HD : (h + 1) * HD]

    def finish(at, total, worst):
        h, r = tiles[at]
        sums = total[:, HD:]
        inverse = 1.0 / sums
        live = row_ids < own_len - r * tile
        result = jnp.where(live, total[:, :HD] * inverse, 0.0)
        out_ref[r * tile : (r + 1) * tile, h * HD : (h + 1) * HD] = result.astype(BF)
        return jnp.minimum(worst, jnp.minimum(sums, inverse))

    def state_of(at):
        h, r = tiles[at]
        return state_ref[r * tile : (r + 1) * tile, h * 2 * HD : (h + 1) * 2 * HD].astype(F32)

    def check(worst):
        @pl.when(jnp.logical_not(jnp.min(worst) > TINY))
        def _():
            exact_block(heads, host, own_len, q_ref, kv_ref, keys, vaug, out_ref)

    @pl.when(host == 0)
    def _():
        worst = jnp.ones((tile, HD), F32)
        for at in range(len(tiles)):
            worst = finish(at, state_of(at), worst)
        check(worst)

    @pl.when(host > 0)
    def _():
        worst = jnp.ones((tile, HD), F32)
        current = dot_t(query_of(0), keys[...])
        for at in range(len(tiles)):
            following = dot_t(query_of(at + 1), keys[...]) if at + 1 < len(tiles) else None
            expo = jnp.exp2(current * SCALE2).astype(BF)
            total = dot(expo, vaug[...]) + state_of(at)
            worst = finish(at, total, worst)
            current = following
        check(worst)


def exact_block(heads, host, own_len, q_ref, kv_ref, keys, vaug, out_ref):
    slab = q_ref.shape[0]
    tile = 128

    def body(i, carry):
        h = i // (slab // tile)
        r = i % (slab // tile)
        at = pl.ds(pl.multiple_of(r * tile, tile), tile)
        lanes = pl.ds(pl.multiple_of(h * HD, HD), HD)
        query = q_ref[at, lanes]
        row_ids = lax.broadcasted_iota(jnp.int32, (tile, slab), 0) + r * tile
        key_ids = lax.broadcasted_iota(jnp.int32, (tile, slab), 1)
        own = dot_t(query, kv_ref[0]) * SCALE2
        own = jnp.where((key_ids <= row_ids) & (key_ids < own_len), own, MASKED)
        far = dot_t(query, keys[...]) * SCALE2
        far = jnp.where(host > 0, far, MASKED)
        peak = jnp.maximum(jnp.max(own, 1, keepdims=True), jnp.max(far, 1, keepdims=True))
        own = jnp.exp2(own - peak)
        far = jnp.where(host > 0, jnp.exp2(far - peak), 0.0)
        sums = jnp.sum(own, 1, keepdims=True) + jnp.sum(far, 1, keepdims=True)
        values = jnp.where(host > 0, vaug[:, :HD].astype(F32), 0.0).astype(BF)
        total = dot(own.astype(BF), kv_ref[1]) + dot(far.astype(BF), values)
        live = row_ids[:, :1] < own_len
        out_ref[at, lanes] = jnp.where(live, total / sums, 0.0).astype(BF)
        return carry

    lax.fori_loop(0, heads * (slab // tile), body, 0)


def anchor_part(lengths, ctx_q, state, state_first, own_kv, anchor, first, count, per_kv, out, after=()):
    slab, width = ctx_q.shape
    heads = min(2, count)
    kv = first // per_kv
    pieces = len(anchor)
    work = count * slab * slab
    extra = ([] if out is None else [out]) + list(after)
    aliases = {} if out is None else {4 + pieces: 0}
    return pl.pallas_call(
        functools.partial(anchor_kernel, heads, pieces, len(extra)),
        grid=(count // heads,),
        out_shape=jax.ShapeDtypeStruct((slab, width), BF),
        in_specs=[
            SMEM,
            pl.BlockSpec((slab, heads * HD), lambda i: (0, first // heads + i)),
            pl.BlockSpec((slab, heads * 2 * HD), lambda i: (0, (first - state_first) // heads + i)),
            pl.BlockSpec((2, slab, HD), lambda i: (0, 0, kv)),
        ]
        + [pl.BlockSpec((2, slab // pieces, HD), lambda i: (0, 0, kv))] * pieces
        + [ANY] * len(extra),
        out_specs=pl.BlockSpec((slab, heads * HD), lambda i: (0, first // heads + i)),
        scratch_shapes=[pltpu.VMEM((slab, HD), BF), pltpu.VMEM((slab, 2 * HD), BF)],
        input_output_aliases=aliases,
        compiler_params=params(),
        cost_estimate=pl.CostEstimate(
            flops=work * HD * 8, bytes_accessed=count * slab * HD * 8, transcendentals=work
        ),
        name="context_anchor",
    )(lengths, ctx_q, state, own_kv, *anchor, *extra)


def source_kernel(slots, per_kv, lengths_ref, kv_ref, self_ref, *rest):
    q_refs, out_refs = rest[:slots], rest[slots : 2 * slots]
    q_rows, width = q_refs[0].shape
    slab = kv_ref.shape[1]
    host = lax.axis_index("hst")
    own_len = lengths_ref[host]
    query_count = slots * q_rows
    rows = per_kv * query_count
    lane = lax.broadcasted_iota(jnp.int32, (query_count, HD), 1)
    place = lax.broadcasted_iota(jnp.int32, (query_count, HD), 0)
    query_ids = jnp.bitwise_xor(place // q_rows, host) * q_rows + place % q_rows
    self_ok = (host * q_rows + lane <= query_ids) & (lane < q_rows)
    self_ok = jnp.concatenate([self_ok] * per_kv, 0)
    stats = jnp.zeros((query_count, HD), F32)
    key_ids = lax.broadcasted_iota(jnp.int32, (rows, slab), 1)
    pad = jnp.zeros((HD - q_rows, HD), F32)
    for j in range(width // HD // per_kv):
        cols = slice(j * HD, (j + 1) * HD)
        parts = []
        for h in range(per_kv):
            at = (j * per_kv + h) * HD
            parts += [q_refs[k][:, at : at + HD].astype(F32) for k in range(slots)]
        queries = jnp.concatenate(parts, 0).astype(BF)
        self_keys = jnp.concatenate([self_ref[0, :, cols].astype(F32), pad], 0).astype(BF)
        self_values = jnp.concatenate([self_ref[1, :, cols].astype(F32), pad], 0).astype(BF)
        near = dot_t(queries, kv_ref[0, :, cols]) * SCALE2
        near = jnp.where(key_ids < own_len, near, MASKED)
        selves = dot_t(queries, self_keys) * SCALE2
        selves = jnp.where(self_ok, selves, MASKED)
        peak = jnp.maximum(jnp.max(near, 1, keepdims=True), jnp.max(selves, 1, keepdims=True))
        near = jnp.exp2(near - peak)
        selves = jnp.exp2(selves - peak)
        sums = jnp.sum(near, 1, keepdims=True) + jnp.sum(selves, 1, keepdims=True)
        total = dot(near.astype(BF), kv_ref[1, :, cols]) + dot(selves.astype(BF), self_values)
        total = total / sums
        level = peak + jnp.log2(sums)
        for h in range(per_kv):
            head = j * per_kv + h
            at = h * query_count
            stats = jnp.where(lane == head, level[at : at + query_count, :], stats)
            for k in range(slots):
                out_refs[k][:, head * HD : (head + 1) * HD] = total[
                    at + k * q_rows : at + (k + 1) * q_rows, :
                ].astype(BF)
    high = stats.astype(BF)
    left = stats - high.astype(F32)
    middle = left.astype(BF)
    low = (left - middle.astype(F32)).astype(BF)
    for k in range(slots):
        take = slice(k * q_rows, (k + 1) * q_rows)
        for at, part in enumerate((high, middle, low)):
            out_refs[k][:, width + at * HD : width + (at + 1) * HD] = part.astype(F32)[take].astype(BF)


def source_part(lengths, own_kv, self_kv, query_slots, per_kv, after=()):
    slots = len(query_slots)
    q_rows, width = query_slots[0].shape
    slab = own_kv.shape[1]
    work = slots * q_rows * (width // HD) * slab

    def body(*refs):
        count = 3 + slots
        return source_kernel(slots, per_kv, *refs[:count], *refs[count + len(after) :])

    return pl.pallas_call(
        body,
        out_shape=[jax.ShapeDtypeStruct((q_rows, width + 3 * HD), BF)] * slots,
        in_specs=[SMEM, VMEM, VMEM] + [VMEM] * slots + [ANY] * len(after),
        out_specs=[VMEM] * slots,
        compiler_params=params(),
        cost_estimate=pl.CostEstimate(flops=work * HD * 8, bytes_accessed=2**21, transcendentals=work),
        name="query_source",
    )(lengths, own_kv, self_kv, *query_slots, *after)


def merge_kernel(slots, *refs):
    in_refs, out_ref = refs[:slots], refs[-1]
    width = out_ref.shape[1]

    def level(ref):
        parts = [ref[:, width + i * HD : width + (i + 1) * HD].astype(F32) for i in range(3)]
        return parts[0] + parts[1] + parts[2]

    levels = [level(ref) for ref in in_refs]
    peak = functools.reduce(jnp.maximum, levels)
    weights = [jnp.exp2(x - peak) for x in levels]
    whole = functools.reduce(jnp.add, weights)
    weights = [w / whole for w in weights]
    for h in range(width // HD):
        cols = slice(h * HD, (h + 1) * HD)
        total = sum(weights[k][:, h : h + 1] * in_refs[k][:, cols].astype(F32) for k in range(slots))
        out_ref[:, cols] = total.astype(BF)


def merge_part(slots, after=()):
    q_rows, wide = slots[0].shape
    width = wide - 3 * HD
    return pl.pallas_call(
        functools.partial(merge_kernel, len(slots)),
        out_shape=jax.ShapeDtypeStruct((q_rows, width), BF),
        in_specs=[VMEM] * len(slots) + [ANY] * len(after),
        out_specs=VMEM,
        compiler_params=params(),
        name="query_merge",
    )(*slots, *after)


def project_kernel(slots, targets, w_ref, *rest):
    in_refs = rest[:slots]
    out_refs, attended, partial = rest[-2 - targets : -2], rest[-2], rest[-1]
    q_rows = in_refs[0].shape[0]

    @pl.when(pl.program_id(0) == 0)
    def _():
        rows = jnp.concatenate([ref[...].astype(F32) for ref in in_refs], 0)
        attended[...] = rows.astype(BF)

    partial[...] = dot(attended[...], w_ref[...])
    part = slots * q_rows // targets
    me = lax.axis_index("tp")
    for k in range(targets):
        start = pl.multiple_of(jnp.bitwise_xor(me, k) * part, part)
        out_refs[k][...] = partial[pl.ds(start, part), :].astype(BF)


def project_part(attended_slots, out_weight, targets, after=()):
    slots = len(attended_slots)
    q_rows, depth = attended_slots[0].shape
    columns = out_weight.shape[1]
    rows = slots * q_rows
    part = rows // targets
    tile = min(256, columns)
    return pl.pallas_call(
        functools.partial(project_kernel, slots, targets),
        grid=(columns // tile,),
        out_shape=[jax.ShapeDtypeStruct((part, columns), BF)] * targets,
        in_specs=[pl.BlockSpec((depth, tile), lambda i: (0, i))]
        + [pl.BlockSpec((q_rows, depth), lambda i: (0, 0))] * slots
        + [ANY] * len(after),
        out_specs=[pl.BlockSpec((part, tile), lambda i: (0, i))] * targets,
        scratch_shapes=[pltpu.VMEM((rows, depth), BF), pltpu.VMEM((rows, tile), F32)],
        compiler_params=params(),
        cost_estimate=pl.CostEstimate(
            flops=2 * rows * depth * columns, bytes_accessed=2 * depth * columns, transcendentals=0
        ),
        name="query_project",
    )(out_weight, *attended_slots, *after)


def arrange_kernel(slots, targets, *refs):
    in_refs, out_ref, rows_ref = refs[:targets], refs[-2], refs[-1]
    part = in_refs[0].shape[0]
    q_rows = part * targets // slots
    me = lax.axis_index("tp")
    host = lax.axis_index("hst")
    for k in range(targets):
        piece = in_refs[k][...].astype(F32)
        for i in range(part // q_rows):
            slot = jnp.bitwise_xor(me, k) * (part // q_rows) + i
            start = pl.multiple_of(jnp.bitwise_xor(slot, host) * q_rows, q_rows)
            rows_ref[pl.ds(start, q_rows), :] = piece[i * q_rows : (i + 1) * q_rows]
    out_ref[...] = rows_ref[...].astype(BF)


def arrange(parts, slots):
    targets = len(parts)
    part, columns = parts[0].shape
    return pl.pallas_call(
        functools.partial(arrange_kernel, slots, targets),
        out_shape=jax.ShapeDtypeStruct((part * targets, columns), BF),
        in_specs=[VMEM] * targets,
        out_specs=VMEM,
        scratch_shapes=[pltpu.VMEM((part * targets, columns), F32)],
        compiler_params=params(),
        name="query_arrange",
    )(*parts)


def general_queries(lengths, own_kv, self_kv, query_q, out_weight, per_kv):
    host_id = lax.axis_index("hst")
    local_heads = query_q.shape[1] // HD
    kv_local = own_kv.shape[2] // HD
    slab_rows = own_kv.shape[1]
    own_len = lengths[host_id]
    row_ids = jnp.arange(slab_rows)
    all_queries = lax.all_gather(query_q, "hst", axis=0, tiled=True)
    query_count = all_queries.shape[0]
    q_rows = query_q.shape[0]
    source = jnp.concatenate([own_kv, self_kv], 1)
    source = source.reshape(2, slab_rows + q_rows, kv_local, HD).transpose(0, 2, 1, 3)
    query_ids = jnp.arange(query_count)
    context_ok = jnp.broadcast_to(row_ids[None, :] < own_len, (query_count, slab_rows))
    self_ok = (host_id * q_rows + jnp.arange(q_rows))[None, :] <= query_ids[:, None]
    seen_ok = jnp.concatenate([context_ok, self_ok], 1)
    query_heads = all_queries.reshape(query_count, local_heads, HD).transpose(1, 0, 2)

    def score_head(operands):
        query_rows, head_index = operands
        kv_index = head_index // per_kv
        scores = dot_t(query_rows, source[0, kv_index]) * HD ** (-0.5)
        scores = jnp.where(seen_ok, scores, MASKED)
        peak = jnp.max(scores, axis=1)
        expo = jnp.exp(scores - peak[:, None])
        return peak, jnp.sum(expo, axis=1), dot(expo.astype(BF), source[1, kv_index])

    maxima, totals, outputs = lax.map(score_head, (query_heads, jnp.arange(local_heads)))
    factor = jnp.exp(maxima - lax.pmax(maxima, "hst"))
    denominator, summed = lax.psum((totals * factor, outputs * factor[..., None]), "hst")
    attended = (summed / denominator[..., None]).astype(BF)
    attended = attended.transpose(1, 0, 2).reshape(query_count, local_heads * HD)
    return lax.psum(dot(attended, out_weight), "tp").astype(BF)


def per_device(hosts, groups, ctx_q, ctx_kv, lengths, query_q, query_kv, out_weight):
    slab = ctx_q.shape[0]
    local_heads = ctx_q.shape[1] // HD
    group_size = H // KVH
    kv_local = max(1, local_heads // group_size)
    per_kv = min(local_heads, group_size)
    q_rows = query_q.shape[0]
    host = lax.axis_index("hst")
    kv_first = lax.axis_index("tp") * local_heads // group_size
    self_kv = lax.dynamic_slice_in_dim(query_kv, kv_first * HD, kv_local * HD, 2)

    tiled = slab % (16 * hosts) == 0 and hosts & (hosts - 1) == 0
    fast = tiled and q_rows % 8 == 0 and groups & (groups - 1) == 0
    fast = fast and (hosts * q_rows) % (16 * groups) == 0
    own_count = per_kv
    anchor_count = min(4, per_kv)

    if not fast:
        own_kv = pick_kv(ctx_kv, kv_local, local_heads, 1)[0]
        query_out = general_queries(lengths, own_kv, self_kv, query_q, out_weight, per_kv)
        anchor = [spread(own_kv, "hst", 0)]
        context_out = None
        for first in range(0, local_heads, own_count):
            state = own_part(ctx_q, own_kv, first, own_count, per_kv)
            context_out = anchor_part(
                lengths, ctx_q, state, first, own_kv, anchor, first, own_count, per_kv, context_out
            )
        return context_out, query_out

    query_slots = exchange([query_q] * hosts, "hst", hosts)
    own_kv, *pieces = pick_kv(ctx_kv, kv_local, local_heads, hosts)
    dealt = [lax.ppermute(pieces[k - 1], "hst", [(0, k)]) for k in range(1, hosts)]
    states = [own_part(ctx_q, own_kv, 0, own_count, per_kv)]
    mine = jnp.where(host == 0, own_kv[:, : slab // hosts], functools.reduce(jnp.add, dealt))
    anchor = exchange([mine] * hosts, "hst", hosts, skip=(0,))
    sources = source_part(lengths, own_kv, self_kv, query_slots, per_kv, after=(states[0],))
    landed = exchange(sources, "hst", hosts)
    for first in range(own_count, local_heads, own_count):
        states.append(own_part(ctx_q, own_kv, first, own_count, per_kv, after=(sources[0],)))
    merged = merge_part(landed, after=(states[-1],))
    attended = exchange([merged] * hosts, "hst", hosts)

    context_out = None
    shared = None
    firsts = list(range(0, local_heads, anchor_count))
    for at, first in enumerate(firsts):
        if at == 1:
            shared = project_part(attended, out_weight, groups, after=(context_out,))
            arrived = exchange(shared, "tp", groups)
        if at == len(firsts) - 1:
            total = functools.reduce(jnp.add, [x.astype(F32) for x in arrived]).astype(BF)
            pieces_out = exchange([total] * groups, "tp", groups)
        after = {0: (merged,), 1: (shared[0],) if shared else ()}.get(at, ())
        if at == len(firsts) - 1:
            after = (total,)
        context_out = anchor_part(
            lengths,
            ctx_q,
            states[first // own_count],
            first // own_count * own_count,
            own_kv,
            anchor,
            first,
            anchor_count,
            per_kv,
            context_out,
            after,
        )
    query_out = arrange(pieces_out, hosts)
    return context_out, query_out


def solution(mesh):
    hosts, groups = mesh.shape["hst"], mesh.shape["tp"]
    return jax.shard_map(
        functools.partial(per_device, hosts, groups),
        mesh=mesh,
        in_specs=(
            P("hst", "tp"),
            P(None, "hst", None),
            P(),
            P("hst", "tp"),
            P(None, "hst", None),
            P("tp", "hst"),
        ),
        out_specs=(P("hst", "tp"), P(None, "hst")),
        check_vma=False,
    )
```

```python
import functools

import jax
import jax.numpy as jnp
from jax import lax
from jax.experimental import pallas as pl
from jax.experimental.pallas import tpu as pltpu
from jax.sharding import PartitionSpec as P

H = 64
KVH = 8
HD = 128
MASKED = -1e30
LOG2E = 1.4426950408889634
SCALE2 = HD ** (-0.5) * LOG2E
TINY = 2.0 ** -90
BF = jnp.bfloat16
F32 = jnp.float32
VMEM = pl.BlockSpec(memory_space=pltpu.VMEM)
SMEM = pl.BlockSpec(memory_space=pltpu.SMEM)
ANY = pl.BlockSpec(memory_space=pl.ANY)
HBM = pl.BlockSpec(memory_space=pltpu.HBM)


def params(mib=20):
    return pltpu.CompilerParams(vmem_limit_bytes=mib * 2**20)


def dot_t(a, b):
    return lax.dot_general(a, b, (((1,), (1,)), ((), ())), preferred_element_type=F32)


def dot(a, b):
    return lax.dot_general(a, b, (((1,), (0,)), ((), ())), preferred_element_type=F32)


def spread(value, axis, source):
    kept = jnp.where(lax.axis_index(axis) == source, value, 0).astype(value.dtype)
    return lax.psum(kept, axis)


def swap(value, axis, size, even, odd):
    return lax.ppermute(value, axis, [(i, i ^ (odd if i & 1 else even)) for i in range(size)])


def pick_kernel(group_size, local_heads, kv_ref, query_ref, k_ref, v_ref, pay_ref, sems):
    slab, width = k_ref.shape
    first = lax.axis_index("tp") * local_heads // group_size * HD
    cols = pl.ds(pl.multiple_of(first, HD), width)
    moves = [
        pltpu.make_async_copy(kv_ref.at[1, :, cols], v_ref, sems.at[1]),
        pltpu.make_async_copy(kv_ref.at[0, :, cols], k_ref, sems.at[0]),
    ]
    for move in moves:
        move.start()
    if pay_ref is not None:
        blocks = [
            query_ref[:, i * width : (i + 1) * width].astype(F32)
            for i in range(query_ref.shape[1] // width)
        ]
        pay_ref[slab:, :] = jnp.concatenate(blocks, 0).astype(BF)
    moves[0].wait()
    if pay_ref is not None:
        pay_ref[:slab, :] = v_ref[...]
    moves[1].wait()


def pick(ctx_kv, query_q, kv_local, local_heads, share):
    rows = ctx_kv.shape[1]
    width = kv_local * HD
    shapes = [jax.ShapeDtypeStruct((rows, width), BF)] * 2
    kernel = functools.partial(pick_kernel, H // KVH, local_heads)
    if share:
        shapes.append(jax.ShapeDtypeStruct((rows + query_q.size // width, width), BF))
        body = kernel
    else:
        body = lambda kv, q, k, v, sems: kernel(kv, q, k, v, None, sems)
    return pl.pallas_call(
        body,
        out_shape=shapes,
        in_specs=[HBM, VMEM],
        out_specs=[VMEM] * len(shapes),
        scratch_shapes=[pltpu.SemaphoreType.DMA((2,))],
        compiler_params=params(52),
        name="pick_columns",
    )(ctx_kv, query_q)


def relay_call(kernel, name, shapes, inputs, after):
    return pl.pallas_call(
        kernel,
        out_shape=[jax.ShapeDtypeStruct(x, BF) for x in shapes],
        in_specs=[VMEM] * len(inputs) + [ANY] * len(after),
        out_specs=[VMEM] * len(shapes),
        compiler_params=params(),
        name=name,
    )(*inputs, *after)


def choose(condition, one, two):
    pl.when(condition)(one)
    pl.when(jnp.logical_not(condition))(two)


def copy_rows(target, at, source, start, rows):
    def run():
        target[at : at + rows, :] = source[start : start + rows, :]

    return run


def join_rows(low, target, at, known, landed, start, rows):
    def run(first, second):
        def body():
            target[at : at + rows, :] = first[start : start + rows, :]
            target[at + rows : at + 2 * rows, :] = second[start : start + rows, :]

        return body

    choose(low, run(known, landed), run(landed, known))


def first_relay(slab, cut, pay, own_k, landed, after):
    rows = pay.shape[0] - slab
    width = pay.shape[1]

    def kernel(pay_ref, k_ref, landed_ref, *rest):
        one_ref, two_ref = rest[-2:]
        even = bit(lax.axis_index("hst"), 0) == 0
        choose(even, copy_rows(one_ref, 0, k_ref, 0, cut), copy_rows(one_ref, 0, landed_ref, 0, cut))
        choose(
            even,
            copy_rows(two_ref, 0, k_ref, cut, slab - cut),
            copy_rows(two_ref, 0, landed_ref, cut, slab - cut),
        )
        join_rows(even, one_ref, cut, pay_ref, landed_ref, slab, rows)

    shapes = [(cut + 2 * rows, width), (slab - cut, width)]
    return relay_call(kernel, "relay_first", shapes, (pay, own_k, landed), after)


def second_relay(slab, cut, one, two, one_landed, two_landed, after):
    rows = one.shape[0] - cut
    width = one.shape[1]

    def kernel(one_ref, two_ref, one_landed_ref, two_landed_ref, *rest):
        back_ref, front_ref = rest[-2:]
        host = lax.axis_index("hst")
        source = host < 2
        choose(source, copy_rows(front_ref, 0, one_ref, 0, cut), copy_rows(front_ref, 0, one_landed_ref, 0, cut))
        left = slab - cut
        choose(source, copy_rows(back_ref, 0, two_ref, 0, left), copy_rows(back_ref, 0, two_landed_ref, 0, left))
        low = jnp.where(bit(host, 0) == 1, bit(host, 2), bit(host, 1)) == 0
        join_rows(low, front_ref, cut, one_ref, one_landed_ref, cut, rows)

    shapes = [(slab - cut, width), (cut + 2 * rows, width)]
    return relay_call(kernel, "relay_second", shapes, (one, two, one_landed, two_landed), after)


def third_relay(slab, cut, back, front, back_landed, front_landed, after):
    width = back.shape[1]

    def kernel(back_ref, front_ref, back_landed_ref, front_landed_ref, *rest):
        held_ref = rest[-1]
        host = lax.axis_index("hst")
        kept = (host <= 2) | (host == 5)
        choose(kept, copy_rows(held_ref, 0, front_ref, 0, cut), copy_rows(held_ref, 0, front_landed_ref, 0, cut))
        kept = (host < 2) | (host == 3) | (host == 4)
        left = slab - cut
        choose(kept, copy_rows(held_ref, cut, back_ref, 0, left), copy_rows(held_ref, cut, back_landed_ref, 0, left))

    return relay_call(kernel, "relay_third", [(slab, width)], (back, front, back_landed, front_landed), after)[0]


def bit(value, at):
    return (value >> at) & 1


def fill_values(vaug, values):
    for j in range(values.shape[1] // HD):
        vaug[:, 2 * j * HD : (2 * j + 1) * HD] = values[:, j * HD : (j + 1) * HD]
        vaug[:, (2 * j + 1) * HD : (2 * j + 2) * HD] = jnp.ones((values.shape[0], HD), BF)


def lanes(index, width):
    return pl.ds(pl.multiple_of(index * width, width), width)


def row_tile(slab):
    return 256 if slab % 256 == 0 else slab


def own_kernel(first, count, per_kv, q_ref, k_ref, v_ref, *rest):
    state_ref, vaug = rest[-2], rest[-1]
    slab = q_ref.shape[0]
    tile = row_tile(slab)
    heads = min(2, count)
    fill_values(vaug, v_ref)
    rows = lax.broadcasted_iota(jnp.int32, (tile, tile), 0)
    cols = lax.broadcasted_iota(jnp.int32, (tile, tile), 1)
    causal = cols <= rows
    chunks = slab // tile
    units = [(h, j) for h in range(heads) for j in range(chunks)]

    def body(i, carry):
        kv = lax.div(first + i * heads, per_kv)

        def scores(at):
            h, j = units[at]
            query = q_ref[j * tile :, lanes(first + i * heads + h, HD)]
            return dot_t(query, k_ref[j * tile : (j + 1) * tile, lanes(kv, HD)])

        current = scores(0)
        totals = [None] * chunks
        for at, (h, j) in enumerate(units):
            following = scores(at + 1) if at + 1 < len(units) else None
            expo = jnp.exp2(current * SCALE2)
            corner = jnp.where(causal, expo[:tile], 0.0)
            expo = corner if j == chunks - 1 else jnp.concatenate([corner, expo[tile:]], 0)
            part = dot(expo.astype(BF), vaug[j * tile : (j + 1) * tile, lanes(kv, 2 * HD)])
            for r in range(j, chunks):
                piece = part[(r - j) * tile : (r - j + 1) * tile]
                totals[r] = piece if j == 0 else totals[r] + piece
            state_ref[j * tile : (j + 1) * tile, lanes(i * heads + h, 2 * HD)] = totals[j].astype(BF)
            current = following
        return carry

    lax.fori_loop(0, count // heads, body, 0)


def own_part(ctx_q, own_k, own_v, first, count, per_kv, after=()):
    slab = ctx_q.shape[0]
    work = count * slab * (slab + row_tile(slab)) // 2
    return pl.pallas_call(
        functools.partial(own_kernel, first, count, per_kv),
        out_shape=jax.ShapeDtypeStruct((slab, count * 2 * HD), BF),
        in_specs=[VMEM] * 3 + [ANY] * len(after),
        out_specs=VMEM,
        scratch_shapes=[pltpu.VMEM((slab, 2 * own_v.shape[1]), BF)],
        compiler_params=params(),
        cost_estimate=pl.CostEstimate(
            flops=work * HD * 8, bytes_accessed=count * slab * HD * 6, transcendentals=work
        ),
        name="context_own",
    )(ctx_q, own_k, own_v, *after)


def anchor_kernel(first, count, base, per_kv, last, befores, *refs):
    lengths_ref, q_ref, state_ref, k_ref, v_ref, even_ref, odd_ref = refs[:7]
    earlier = refs[7 : 7 + len(befores)]
    if last:
        full_ref, out_ref, keys, vaug, sems = refs[-5:]
    else:
        out_ref, keys, vaug = refs[-3:]
    slab = q_ref.shape[0]
    heads = min(2, count)
    host = lax.axis_index("hst")
    own_len = lengths_ref[host]

    def hand_over(source, at, width, sem):
        return pltpu.make_async_copy(source, full_ref.at[:, at], sems.at[sem])

    moves = []
    for n, (start, width) in enumerate(befores):
        at = pl.ds(start * HD, width * HD)
        moves.append(hand_over(earlier[n], at, width, n))
    for move in moves:
        move.start()

    @pl.when(host % 2 == 0)
    def _():
        keys[...] = even_ref[...]
        fill_values(vaug, odd_ref)

    @pl.when(host % 2 == 1)
    def _():
        keys[...] = odd_ref[...]
        fill_values(vaug, even_ref)

    row_ids = lax.broadcasted_iota(jnp.int32, (slab, HD), 0)
    live = row_ids < own_len

    def result_move(i):
        cols = pl.ds(pl.multiple_of(i * heads * HD, heads * HD), heads * HD)
        target = pl.ds(pl.multiple_of((first + i * heads) * HD, heads * HD), heads * HD)
        return hand_over(out_ref.at[:, cols], target, heads, len(befores) + i)

    def body(i, carry):
        kv = lax.div(first + i * heads, per_kv)

        def scores(h):
            return dot_t(q_ref[:, lanes(first + i * heads + h, HD)], keys[:, lanes(kv, HD)])

        def state_of(h):
            return state_ref[:, lanes(first - base + i * heads + h, 2 * HD)].astype(F32)

        def finish(h, total, worst):
            sums = total[:, HD:]
            inverse = 1.0 / sums
            result = jnp.where(live, total[:, :HD] * inverse, 0.0)
            out_ref[:, lanes(i * heads + h, HD)] = result.astype(BF)
            return jnp.minimum(worst, jnp.minimum(sums, inverse))

        def check(worst):
            @pl.when(jnp.logical_not(jnp.min(worst) > TINY))
            def _():
                exact_block(first + i * heads, i * heads, heads, host, own_len, kv, q_ref, k_ref, v_ref, keys, vaug, out_ref)

        @pl.when(host == 0)
        def _():
            worst = jnp.ones((slab, HD), F32)
            for h in range(heads):
                worst = finish(h, state_of(h), worst)
            check(worst)

        @pl.when(host > 0)
        def _():
            worst = jnp.ones((slab, HD), F32)
            current = scores(0)
            for h in range(heads):
                following = scores(h + 1) if h + 1 < heads else None
                expo = jnp.exp2(current * SCALE2).astype(BF)
                total = dot(expo, vaug[:, lanes(kv, 2 * HD)]) + state_of(h)
                worst = finish(h, total, worst)
                current = following
            check(worst)

        if last:
            result_move(i).start()
        return carry

    lax.fori_loop(0, count // heads, body, 0)
    for move in moves:
        move.wait()
    if last:
        for i in range(count // heads):
            result_move(i).wait()


def exact_block(q_head, out_head, heads, host, own_len, kv, q_ref, k_ref, v_ref, keys, vaug, out_ref):
    slab = q_ref.shape[0]
    tile = 128

    def body(i, carry):
        h = lax.div(i, slab // tile)
        r = lax.rem(i, slab // tile)
        at = pl.ds(pl.multiple_of(r * tile, tile), tile)
        query = q_ref[at, lanes(q_head + h, HD)]
        row_ids = lax.broadcasted_iota(jnp.int32, (tile, slab), 0) + r * tile
        key_ids = lax.broadcasted_iota(jnp.int32, (tile, slab), 1)
        own = dot_t(query, k_ref[:, lanes(kv, HD)]) * SCALE2
        own = jnp.where((key_ids <= row_ids) & (key_ids < own_len), own, MASKED)
        far = dot_t(query, keys[:, lanes(kv, HD)]) * SCALE2
        far = jnp.where(host > 0, far, MASKED)
        peak = jnp.maximum(jnp.max(own, 1, keepdims=True), jnp.max(far, 1, keepdims=True))
        own = jnp.exp2(own - peak)
        far = jnp.where(host > 0, jnp.exp2(far - peak), 0.0)
        sums = jnp.sum(own, 1, keepdims=True) + jnp.sum(far, 1, keepdims=True)
        values = jnp.where(host > 0, vaug[:, lanes(2 * kv, HD)].astype(F32), 0.0).astype(BF)
        total = dot(own.astype(BF), v_ref[:, lanes(kv, HD)]) + dot(far.astype(BF), values)
        live = row_ids[:, :1] < own_len
        out_ref[at, lanes(out_head + h, HD)] = jnp.where(live, total / sums, 0.0).astype(BF)
        return carry

    lax.fori_loop(0, heads * (slab // tile), body, 0)


def anchor_part(lengths, ctx_q, state, base, own_k, own_v, anchor, first, count, per_kv, befores=None, after=()):
    slab, width = ctx_q.shape
    work = count * slab * slab
    last = befores is not None
    heads = min(2, count)
    earlier = list(befores.values()) if last else []
    places = tuple((at, x.shape[1] // HD) for at, x in befores.items()) if last else ()
    results = jax.ShapeDtypeStruct((slab, count * HD), BF)
    scratch = [pltpu.VMEM((slab, own_k.shape[1]), BF), pltpu.VMEM((slab, 2 * own_k.shape[1]), BF)]
    if last:
        scratch = [pltpu.VMEM(results.shape, BF)] + scratch
        scratch += [pltpu.SemaphoreType.DMA((len(earlier) + count // heads,))]
        results = jax.ShapeDtypeStruct((slab, width), BF)
    return pl.pallas_call(
        functools.partial(anchor_kernel, first, count, base, per_kv, last, places),
        out_shape=results,
        in_specs=[SMEM] + [VMEM] * (6 + len(earlier)) + [ANY] * len(after),
        out_specs=ANY if last else VMEM,
        scratch_shapes=scratch,
        compiler_params=params(),
        cost_estimate=pl.CostEstimate(
            flops=work * HD * 8, bytes_accessed=count * slab * HD * 8, transcendentals=work
        ),
        name="context_anchor",
    )(lengths, ctx_q, state, own_k, own_v, *anchor, *earlier, *after)


def write_level(ref, width, level):
    for at in range(3):
        part = level.astype(BF)
        ref[:, width + at * HD : width + (at + 1) * HD] = part
        level = level - part.astype(F32)


def read_level(ref, width):
    parts = [ref[:, width + i * HD : width + (i + 1) * HD].astype(F32) for i in range(3)]
    return parts[0] + parts[1] + parts[2]


def source_kernel(cut, per_kv, q_rows, group_size, lengths_ref, k_ref, v_ref, self_ref, known_ref, landed_ref, *rest):
    out_ref, q_all = rest[-2], rest[-1]
    slab, columns = k_ref.shape
    width = per_kv * columns
    half = known_ref.shape[0] - cut
    quarter = half // 2
    query_count = out_ref.shape[1]
    slots = query_count // q_rows
    host = lax.axis_index("hst")
    own_len = lengths_ref[host]
    rows = per_kv * query_count
    odd = bit(host, 0) == 1
    low = jnp.where(odd, bit(host, 1), bit(host, 2)) == 0

    def place(lower, upper, spread_out):
        middle = (2, 1) if spread_out else (1, 2)
        for ref, (one, two) in ((lower, (0, middle[0])), (upper, (middle[1], 3))):
            q_all[one * quarter : (one + 1) * quarter, :] = ref[cut : cut + quarter, :]
            q_all[two * quarter : (two + 1) * quarter, :] = ref[cut + quarter :, :]

    for is_low, is_odd in ((False, False), (False, True), (True, False), (True, True)):
        @pl.when((low == is_low) & (odd == is_odd))
        def _():
            pair = (known_ref, landed_ref) if is_low else (landed_ref, known_ref)
            place(*pair, is_odd)

    first = lax.axis_index("tp") * (width // HD) // group_size * HD
    own_cols = pl.ds(pl.multiple_of(first, HD), columns)
    selves_kv = [self_ref[i, :, own_cols].astype(F32) for i in range(2)]
    lane = lax.broadcasted_iota(jnp.int32, (query_count, HD), 1)
    query_ids = lax.broadcasted_iota(jnp.int32, (query_count, HD), 0)
    self_ok = (host * q_rows + lane <= query_ids) & (lane < q_rows)
    self_ok = jnp.concatenate([self_ok] * per_kv, 0)
    key_ids = lax.broadcasted_iota(jnp.int32, (rows, slab), 1)
    pad = jnp.zeros((HD - q_rows, HD), F32)
    heads_wide = columns // HD
    q_lanes = [q_all[:, i * HD : (i + 1) * HD].astype(F32) for i in range(heads_wide)]
    stride = width // columns * q_rows
    for j in range(columns // HD):
        cols = slice(j * HD, (j + 1) * HD)
        parts = []
        for h in range(per_kv):
            block, lanes = divmod(j * per_kv + h, heads_wide)
            starts = [k * stride + block * q_rows for k in range(slots)]
            parts += [q_lanes[lanes][at : at + q_rows] for at in starts]
        queries = jnp.concatenate(parts, 0).astype(BF)
        self_keys = jnp.concatenate([selves_kv[0][:, cols], pad], 0).astype(BF)
        self_values = jnp.concatenate([selves_kv[1][:, cols], pad], 0).astype(BF)
        near = dot_t(queries, k_ref[:, cols]) * SCALE2
        near = jnp.where(key_ids < own_len, near, MASKED)
        selves = dot_t(queries, self_keys) * SCALE2
        selves = jnp.where(self_ok, selves, MASKED)
        peak = jnp.maximum(jnp.max(near, 1, keepdims=True), jnp.max(selves, 1, keepdims=True))
        near = jnp.exp2(near - peak)
        selves = jnp.exp2(selves - peak)
        sums = jnp.sum(near, 1, keepdims=True) + jnp.sum(selves, 1, keepdims=True)
        total = dot(near.astype(BF), v_ref[:, cols]) + dot(selves.astype(BF), self_values)
        total = total / sums
        level = peak + jnp.log2(sums)
        stats = jnp.zeros((query_count, HD), F32)
        for h in range(per_kv):
            at = h * query_count
            stats = jnp.where(lane == h, level[at : at + query_count, :], stats)
            out_ref[j, :, h * HD : (h + 1) * HD] = total[at : at + query_count, :].astype(BF)
        write_level(out_ref.at[j], per_kv * HD, stats)


def source_part(lengths, own_k, own_v, query_kv, known, landed, cut, q_rows, count, per_kv, after=()):
    slab, columns = own_k.shape
    width = per_kv * columns
    work = count * (width // HD) * slab
    return pl.pallas_call(
        functools.partial(source_kernel, cut, per_kv, q_rows, H // KVH),
        out_shape=jax.ShapeDtypeStruct((columns // HD, count, (per_kv + 3) * HD), BF),
        in_specs=[SMEM] + [VMEM] * 5 + [ANY] * len(after),
        out_specs=VMEM,
        scratch_shapes=[pltpu.VMEM((count * width // columns, columns), BF)],
        compiler_params=params(),
        cost_estimate=pl.CostEstimate(flops=work * HD * 8, bytes_accessed=2**21, transcendentals=work),
        name="query_source",
    )(lengths, own_k, own_v, query_kv, known, landed, *after)


def merged(refs, width):
    levels = [read_level(ref, width) for ref in refs]
    peak = jnp.maximum(*levels)
    weights = [jnp.exp2(x - peak) for x in levels]
    whole = weights[0] + weights[1]
    return [w / whole for w in weights], peak + jnp.log2(whole)


def blend(shares, refs, h):
    cols = slice(h * HD, (h + 1) * HD)
    return sum(w[:, h : h + 1] * ref[:, cols].astype(F32) for w, ref in zip(shares, refs))


def merge_kernel(groups, *refs):
    ones, twos, outs = refs[:groups], refs[groups : 2 * groups], refs[-groups:]
    for pair in zip(ones, twos, outs):
        out_ref = pair[2]
        width = out_ref.shape[1] - 3 * HD
        shares, level = merged(pair[:2], width)
        write_level(out_ref, width, level)
        for h in range(width // HD):
            out_ref[:, h * HD : (h + 1) * HD] = blend(shares, pair[:2], h).astype(BF)


def merge_part(ones, twos, after=()):
    stacked = len(ones) == 1
    groups = ones[0].shape[0] if stacked else len(ones)
    shape = ones[0].shape[-2:]

    def body(*refs):
        if stacked:
            refs = [refs[n].at[j] for n in range(2) for j in range(groups)] + list(refs[2:])
        merge_kernel(groups, *refs)

    return pl.pallas_call(
        body,
        out_shape=[jax.ShapeDtypeStruct(shape, BF)] * groups,
        in_specs=[VMEM] * (2 * len(ones)) + [ANY] * len(after),
        out_specs=[VMEM] * groups,
        compiler_params=params(),
        name="query_merge",
    )(*ones, *twos, *after)


def project_kernel(groups, w_ref, *rest):
    ones, twos = rest[:groups], rest[groups : 2 * groups]
    out_ref, attended = rest[-2], rest[-1]
    width = ones[0].shape[1] - 3 * HD

    @pl.when(pl.program_id(0) == 0)
    def _():
        for j, pair in enumerate(zip(ones, twos)):
            shares, _ = merged(pair, width)
            for h in range(width // HD):
                at = j * width + h * HD
                attended[:, at : at + HD] = blend(shares, pair, h).astype(BF)

    out_ref[...] = dot(attended[...], w_ref[...]).astype(BF)


def project_part(ones, twos, out_weight, after=()):
    rows, wide = ones[0].shape
    depth, columns = out_weight.shape
    tile = min(256, columns)
    return pl.pallas_call(
        functools.partial(project_kernel, len(ones)),
        grid=(columns // tile,),
        out_shape=jax.ShapeDtypeStruct((rows, columns), BF),
        in_specs=[pl.BlockSpec((depth, tile), lambda i: (0, i))]
        + [pl.BlockSpec((rows, wide), lambda i: (0, 0))] * (2 * len(ones))
        + [ANY] * len(after),
        out_specs=pl.BlockSpec((rows, tile), lambda i: (0, i)),
        scratch_shapes=[pltpu.VMEM((rows, depth), BF)],
        compiler_params=params(),
        cost_estimate=pl.CostEstimate(
            flops=2 * rows * depth * columns, bytes_accessed=2 * depth * columns, transcendentals=0
        ),
        name="query_project",
    )(out_weight, *ones, *twos, *after)


def general_queries(lengths, own_k, own_v, self_kv, query_q, out_weight, per_kv):
    own_kv = jnp.stack([own_k, own_v], 0)
    host_id = lax.axis_index("hst")
    local_heads = query_q.shape[1] // HD
    kv_local = own_kv.shape[2] // HD
    slab_rows = own_kv.shape[1]
    own_len = lengths[host_id]
    row_ids = jnp.arange(slab_rows)
    all_queries = lax.all_gather(query_q, "hst", axis=0, tiled=True)
    query_count = all_queries.shape[0]
    q_rows = query_q.shape[0]
    source = jnp.concatenate([own_kv, self_kv], 1)
    source = source.reshape(2, slab_rows + q_rows, kv_local, HD).transpose(0, 2, 1, 3)
    query_ids = jnp.arange(query_count)
    context_ok = jnp.broadcast_to(row_ids[None, :] < own_len, (query_count, slab_rows))
    self_ok = (host_id * q_rows + jnp.arange(q_rows))[None, :] <= query_ids[:, None]
    seen_ok = jnp.concatenate([context_ok, self_ok], 1)
    query_heads = all_queries.reshape(query_count, local_heads, HD).transpose(1, 0, 2)

    def score_head(operands):
        query_rows, head_index = operands
        kv_index = head_index // per_kv
        scores = dot_t(query_rows, source[0, kv_index]) * HD ** (-0.5)
        scores = jnp.where(seen_ok, scores, MASKED)
        peak = jnp.max(scores, axis=1)
        expo = jnp.exp(scores - peak[:, None])
        return peak, jnp.sum(expo, axis=1), dot(expo.astype(BF), source[1, kv_index])

    maxima, totals, outputs = lax.map(score_head, (query_heads, jnp.arange(local_heads)))
    factor = jnp.exp(maxima - lax.pmax(maxima, "hst"))
    denominator, summed = lax.psum((totals * factor, outputs * factor[..., None]), "hst")
    attended = (summed / denominator[..., None]).astype(BF)
    attended = attended.transpose(1, 0, 2).reshape(query_count, local_heads * HD)
    return lax.psum(dot(attended, out_weight), "tp").astype(BF)


def per_device(hosts, groups, ctx_q, ctx_kv, lengths, query_q, query_kv, out_weight):
    slab = ctx_q.shape[0]
    local_heads = ctx_q.shape[1] // HD
    group_size = H // KVH
    kv_local = max(1, local_heads // group_size)
    per_kv = min(local_heads, group_size)
    q_rows = query_q.shape[0]
    host = lax.axis_index("hst")
    fast = hosts == 8 and groups & (groups - 1) == 0
    fast = fast and q_rows == 8 and local_heads == 16 and per_kv == 8

    if not fast:
        kv_first = lax.axis_index("tp") * local_heads // group_size
        self_kv = lax.dynamic_slice_in_dim(query_kv, kv_first * HD, kv_local * HD, 2)
        own_k, own_v = pick(ctx_kv, query_q, kv_local, local_heads, False)
        query_out = general_queries(lengths, own_k, own_v, self_kv, query_q, out_weight, per_kv)
        k, v = spread(jnp.stack([own_k, own_v]), "hst", 0)
        anchor = jnp.where(host % 2 == 0, k, v), jnp.where(host % 2 == 0, v, k)
        state = own_part(ctx_q, own_k, own_v, 0, local_heads, per_kv)
        context_out = anchor_part(
            lengths, ctx_q, state, 0, own_k, own_v, anchor, 0, local_heads, per_kv, {}
        )
        return context_out, query_out

    states = {}

    def own(first, count, after=()):
        states[first] = own_part(ctx_q, own_k, own_v, first, count, per_kv, after)
        return states[first]

    cut = slab * 3 // 8
    own_k, own_v, pay = pick(ctx_kv, query_q, kv_local, local_heads, True)
    landed = swap(pay, "hst", hosts, 1, 1)
    done = own(0, 2)
    one, two = first_relay(slab, cut, pay, own_k, landed, (done,))
    one_landed = swap(one, "hst", hosts, 2, 4)
    two_landed = swap(two, "hst", hosts, 4, 2)
    done = own(2, 8, (one,))
    back, front = second_relay(slab, cut, one, two, one_landed, two_landed, (done,))
    back_landed = swap(back, "hst", hosts, 2, 4)
    front_landed = swap(front, "hst", hosts, 4, 2)
    done = own(10, 6, (front,))
    held = third_relay(slab, cut, back, front, back_landed, front_landed, (done,))
    other = swap(held, "hst", hosts, 1, 1)
    source = source_part(
        lengths, own_k, own_v, query_kv, front, front_landed, cut, q_rows, hosts * q_rows, per_kv, (held,)
    )
    results = {}

    def anchors(first, count, after, last=False):
        base = max(x for x in states if x <= first)
        results[first] = anchor_part(
            lengths, ctx_q, states[base], base, own_k, own_v, (held, other),
            first, count, per_kv, dict(results) if last else None, after,
        )
        return results[first]

    landed = swap(source, "hst", hosts, 1, 1)
    done = anchors(0, 2, (source,))
    sources = merge_part([source], [landed], (done,))
    landed = [swap(sources[0], "hst", hosts, 2, 4), swap(sources[1], "hst", hosts, 4, 2)]
    done = anchors(2, 4, (sources[0],))
    sources = merge_part(sources, landed, (done,))
    landed = [swap(sources[0], "hst", hosts, 4, 2), swap(sources[1], "hst", hosts, 2, 4)]
    done = anchors(6, 4, (sources[0],))
    terms = project_part(sources, landed, out_weight, (done,))
    shares = [(12, 4, True), (10, 2, False)]
    step = 1
    while step < groups:
        landed = swap(terms, "tp", groups, step, step)
        if shares:
            first, count, last = shares.pop()
            done = anchors(first, count, (terms,), last)
            if not last:
                landed, _ = lax.optimization_barrier((landed, done))
        terms = (terms.astype(F32) + landed.astype(F32)).astype(BF)
        step *= 2
    for first, count, last in reversed(shares):
        done = anchors(first, count, (), last)
    return done, terms


def solution(mesh):
    hosts, groups = mesh.shape["hst"], mesh.shape["tp"]
    return jax.shard_map(
        functools.partial(per_device, hosts, groups),
        mesh=mesh,
        in_specs=(
            P("hst", "tp"),
            P(None, "hst", None),
            P(),
            P("hst", "tp"),
            P(None, "hst", None),
            P("tp", "hst"),
        ),
        out_specs=(P("hst", "tp"), P(None, "hst")),
        check_vma=False,
    )
```

```python
import functools

import jax
import jax.numpy as jnp
from jax import lax
from jax.experimental import pallas as pl
from jax.experimental.pallas import tpu as pltpu
from jax.sharding import PartitionSpec as P

H = 64
KVH = 8
HD = 128
MASKED = -1e30
LOG2E = 1.4426950408889634
SCALE2 = HD ** (-0.5) * LOG2E
TINY = 2.0 ** -90
BF = jnp.bfloat16
F32 = jnp.float32
VMEM = pl.BlockSpec(memory_space=pltpu.VMEM)
SMEM = pl.BlockSpec(memory_space=pltpu.SMEM)
ANY = pl.BlockSpec(memory_space=pl.ANY)
HBM = pl.BlockSpec(memory_space=pltpu.HBM)


def params(mib=20):
    return pltpu.CompilerParams(vmem_limit_bytes=mib * 2**20)


def dot_t(a, b):
    return lax.dot_general(a, b, (((1,), (1,)), ((), ())), preferred_element_type=F32)


def dot(a, b):
    return lax.dot_general(a, b, (((1,), (0,)), ((), ())), preferred_element_type=F32)


def spread(value, axis, source):
    kept = jnp.where(lax.axis_index(axis) == source, value, 0).astype(value.dtype)
    return lax.psum(kept, axis)


def swap(value, axis, size, even, odd):
    return lax.ppermute(value, axis, [(i, i ^ (odd if i & 1 else even)) for i in range(size)])


def pick_kernel(group_size, local_heads, kv_ref, k_ref, v_ref, sems):
    first = lax.axis_index("tp") * local_heads // group_size * HD
    cols = pl.ds(pl.multiple_of(first, HD), k_ref.shape[1])
    moves = [
        pltpu.make_async_copy(kv_ref.at[1, :, cols], v_ref, sems.at[1]),
        pltpu.make_async_copy(kv_ref.at[0, :, cols], k_ref, sems.at[0]),
    ]
    for move in moves:
        move.start()
    for move in moves:
        move.wait()


def pick(ctx_kv, kv_local, local_heads):
    return pl.pallas_call(
        functools.partial(pick_kernel, H // KVH, local_heads),
        out_shape=[jax.ShapeDtypeStruct((ctx_kv.shape[1], kv_local * HD), BF)] * 2,
        in_specs=[HBM],
        out_specs=[VMEM] * 2,
        scratch_shapes=[pltpu.SemaphoreType.DMA((2,))],
        compiler_params=params(52),
        name="pick_columns",
    )(ctx_kv)


def bit(value, at):
    return (value >> at) & 1


def small_call(kernel, name, shapes, inputs, after=()):
    return pl.pallas_call(
        kernel,
        out_shape=[jax.ShapeDtypeStruct(x, BF) for x in shapes],
        in_specs=[VMEM] * len(inputs) + [ANY] * len(after),
        out_specs=[VMEM] * len(shapes),
        compiler_params=params(),
        name=name,
    )(*inputs, *after)


def choose(condition, one, two):
    pl.when(condition)(one)
    pl.when(jnp.logical_not(condition))(two)


def relay(keep_of, one, two, after):
    def kernel(one_ref, two_ref, *rest):
        out_ref = rest[-1]

        def take(ref):
            def run():
                out_ref[...] = ref[...]

            return run

        choose(keep_of(lax.axis_index("hst")), take(one_ref), take(two_ref))

    return small_call(kernel, "anchor_relay", [one.shape], (one, two), after)[0]


def join(low_of, known, landed, after):
    rows, width = known.shape

    def kernel(known_ref, landed_ref, *rest):
        out_ref = rest[-1]

        def put(first, second):
            def run():
                both = jnp.concatenate([first[...].astype(F32), second[...].astype(F32)], 0)
                out_ref[...] = both.astype(BF)

            return run

        choose(low_of(lax.axis_index("hst")), put(known_ref, landed_ref), put(landed_ref, known_ref))

    return small_call(kernel, "query_join", [(2 * rows, width)], (known, landed), after)[0]


def add_part(one, two, after=()):
    def kernel(one_ref, two_ref, *rest):
        rest[-1][...] = (one_ref[...].astype(F32) + two_ref[...].astype(F32)).astype(BF)

    return small_call(kernel, "query_sum", [one.shape], (one, two), after)[0]


def fill_values(vaug, values):
    for j in range(values.shape[1] // HD):
        vaug[:, 2 * j * HD : (2 * j + 1) * HD] = values[:, j * HD : (j + 1) * HD]
        vaug[:, (2 * j + 1) * HD : (2 * j + 2) * HD] = jnp.ones((values.shape[0], HD), BF)


def lanes(index, width):
    return pl.ds(pl.multiple_of(index * width, width), width)


def row_tile(slab):
    return 256 if slab % 256 == 0 else slab


def own_kernel(first, count, per_kv, q_ref, k_ref, v_ref, *rest):
    state_ref, vaug = rest[-2], rest[-1]
    slab = q_ref.shape[0]
    tile = row_tile(slab)
    heads = min(2, count)
    fill_values(vaug, v_ref)
    rows = lax.broadcasted_iota(jnp.int32, (tile, tile), 0)
    cols = lax.broadcasted_iota(jnp.int32, (tile, tile), 1)
    causal = cols <= rows
    chunks = slab // tile
    units = [(h, j) for h in range(heads) for j in range(chunks)]

    def body(i, carry):
        kv = lax.div(first + i * heads, per_kv)

        def scores(at):
            h, j = units[at]
            query = q_ref[j * tile :, lanes(first + i * heads + h, HD)]
            return dot_t(query, k_ref[j * tile : (j + 1) * tile, lanes(kv, HD)])

        current = scores(0)
        totals = [None] * chunks
        for at, (h, j) in enumerate(units):
            following = scores(at + 1) if at + 1 < len(units) else None
            corner = jnp.where(causal, current[:tile], MASKED)
            masked = corner if j == chunks - 1 else jnp.concatenate([corner, current[tile:]], 0)
            if j == 0:
                peak = jnp.max(masked, axis=1, keepdims=True) * SCALE2
                shift = jnp.broadcast_to(peak, (slab, HD)).astype(BF)
                state_ref[:, pl.ds(pl.multiple_of((i * heads + h) * 3 * HD + 2 * HD, HD), HD)] = shift
                shift = shift.astype(F32)
            shifts = jnp.concatenate([shift[j * tile :]] * (tile // HD), 1)
            expo = jnp.exp2((masked * SCALE2 - shifts).astype(BF))
            part = dot(expo, vaug[j * tile : (j + 1) * tile, lanes(kv, 2 * HD)])
            for r in range(j, chunks):
                piece = part[(r - j) * tile : (r - j + 1) * tile]
                totals[r] = piece if j == 0 else totals[r] + piece
            cols = pl.ds(pl.multiple_of((i * heads + h) * 3 * HD, HD), 2 * HD)
            state_ref[j * tile : (j + 1) * tile, cols] = totals[j].astype(BF)
            current = following
        return carry

    lax.fori_loop(0, count // heads, body, 0)


def own_part(ctx_q, own_k, own_v, first, count, per_kv, after=()):
    slab = ctx_q.shape[0]
    work = count * slab * (slab + row_tile(slab)) // 2
    return pl.pallas_call(
        functools.partial(own_kernel, first, count, per_kv),
        out_shape=jax.ShapeDtypeStruct((slab, count * 3 * HD), BF),
        in_specs=[VMEM] * 3 + [ANY] * len(after),
        out_specs=VMEM,
        scratch_shapes=[pltpu.VMEM((slab, 2 * own_v.shape[1]), BF)],
        compiler_params=params(),
        cost_estimate=pl.CostEstimate(
            flops=work * HD * 8, bytes_accessed=count * slab * HD * 6, transcendentals=work
        ),
        name="context_own",
    )(ctx_q, own_k, own_v, *after)


def anchor_kernel(first, count, base, per_kv, last, befores, *refs):
    lengths_ref, q_ref, state_ref, k_ref, v_ref, even_ref, odd_ref = refs[:7]
    earlier = refs[7 : 7 + len(befores)]
    if last:
        full_ref, out_ref, keys, vaug, sems = refs[-5:]
    else:
        out_ref, keys, vaug = refs[-3:]
    slab = q_ref.shape[0]
    heads = min(2, count)
    host = lax.axis_index("hst")
    own_len = lengths_ref[host]

    def hand_over(source, at, width, sem):
        return pltpu.make_async_copy(source, full_ref.at[:, at], sems.at[sem])

    moves = []
    for n, (start, width) in enumerate(befores):
        at = pl.ds(start * HD, width * HD)
        moves.append(hand_over(earlier[n], at, width, n))
    for move in moves:
        move.start()

    @pl.when(host % 2 == 0)
    def _():
        keys[...] = even_ref[...]
        fill_values(vaug, odd_ref)

    @pl.when(host % 2 == 1)
    def _():
        keys[...] = odd_ref[...]
        fill_values(vaug, even_ref)

    row_ids = lax.broadcasted_iota(jnp.int32, (slab, HD), 0)
    live = row_ids < own_len

    def result_move(i):
        cols = pl.ds(pl.multiple_of(i * heads * HD, heads * HD), heads * HD)
        target = pl.ds(pl.multiple_of((first + i * heads) * HD, heads * HD), heads * HD)
        return hand_over(out_ref.at[:, cols], target, heads, len(befores) + i)

    def body(i, carry):
        kv = lax.div(first + i * heads, per_kv)

        def scores(h):
            return dot_t(q_ref[:, lanes(first + i * heads + h, HD)], keys[:, lanes(kv, HD)])

        def state_of(h, at, width):
            start = (first - base + i * heads + h) * 3 * HD + at
            return state_ref[:, pl.ds(pl.multiple_of(start, HD), width)].astype(F32)

        def finish(h, total, worst):
            sums = total[:, HD:]
            inverse = 1.0 / sums
            result = jnp.where(live, total[:, :HD] * inverse, 0.0)
            out_ref[:, lanes(i * heads + h, HD)] = result.astype(BF)
            return jnp.minimum(worst, jnp.minimum(sums, inverse))

        def check(worst):
            @pl.when(jnp.logical_not(jnp.min(worst) > TINY))
            def _():
                exact_block(first + i * heads, i * heads, heads, host, own_len, kv, q_ref, k_ref, v_ref, keys, vaug, out_ref)

        @pl.when(host == 0)
        def _():
            worst = jnp.ones((slab, HD), F32)
            for h in range(heads):
                worst = finish(h, state_of(h, 0, 2 * HD), worst)
            check(worst)

        @pl.when(host > 0)
        def _():
            worst = jnp.ones((slab, HD), F32)
            current = scores(0)
            for h in range(heads):
                following = scores(h + 1) if h + 1 < heads else None
                shifts = jnp.concatenate([state_of(h, 2 * HD, HD)] * (slab // HD), 1)
                expo = jnp.exp2((current * SCALE2 - shifts).astype(BF))
                total = dot(expo, vaug[:, lanes(kv, 2 * HD)]) + state_of(h, 0, 2 * HD)
                worst = finish(h, total, worst)
                current = following
            check(worst)

        if last:
            result_move(i).start()
        return carry

    lax.fori_loop(0, count // heads, body, 0)
    for move in moves:
        move.wait()
    if last:
        for i in range(count // heads):
            result_move(i).wait()


def exact_block(q_head, out_head, heads, host, own_len, kv, q_ref, k_ref, v_ref, keys, vaug, out_ref):
    slab = q_ref.shape[0]
    tile = 128

    def body(i, carry):
        h = lax.div(i, slab // tile)
        r = lax.rem(i, slab // tile)
        at = pl.ds(pl.multiple_of(r * tile, tile), tile)
        query = q_ref[at, lanes(q_head + h, HD)]
        row_ids = lax.broadcasted_iota(jnp.int32, (tile, slab), 0) + r * tile
        key_ids = lax.broadcasted_iota(jnp.int32, (tile, slab), 1)
        own = dot_t(query, k_ref[:, lanes(kv, HD)]) * SCALE2
        own = jnp.where((key_ids <= row_ids) & (key_ids < own_len), own, MASKED)
        far = dot_t(query, keys[:, lanes(kv, HD)]) * SCALE2
        far = jnp.where(host > 0, far, MASKED)
        peak = jnp.maximum(jnp.max(own, 1, keepdims=True), jnp.max(far, 1, keepdims=True))
        own = jnp.exp2(own - peak)
        far = jnp.where(host > 0, jnp.exp2(far - peak), 0.0)
        sums = jnp.sum(own, 1, keepdims=True) + jnp.sum(far, 1, keepdims=True)
        values = jnp.where(host > 0, vaug[:, lanes(2 * kv, HD)].astype(F32), 0.0).astype(BF)
        total = dot(own.astype(BF), v_ref[:, lanes(kv, HD)]) + dot(far.astype(BF), values)
        live = row_ids[:, :1] < own_len
        out_ref[at, lanes(out_head + h, HD)] = jnp.where(live, total / sums, 0.0).astype(BF)
        return carry

    lax.fori_loop(0, heads * (slab // tile), body, 0)


def anchor_part(lengths, ctx_q, state, base, own_k, own_v, anchor, first, count, per_kv, befores=None, after=()):
    slab, width = ctx_q.shape
    work = count * slab * slab
    last = befores is not None
    heads = min(2, count)
    earlier = list(befores.values()) if last else []
    places = tuple((at, x.shape[1] // HD) for at, x in befores.items()) if last else ()
    results = jax.ShapeDtypeStruct((slab, count * HD), BF)
    scratch = [pltpu.VMEM((slab, own_k.shape[1]), BF), pltpu.VMEM((slab, 2 * own_k.shape[1]), BF)]
    if last:
        scratch = [pltpu.VMEM(results.shape, BF)] + scratch
        scratch += [pltpu.SemaphoreType.DMA((len(earlier) + count // heads,))]
        results = jax.ShapeDtypeStruct((slab, width), BF)
    return pl.pallas_call(
        functools.partial(anchor_kernel, first, count, base, per_kv, last, places),
        out_shape=results,
        in_specs=[SMEM] + [VMEM] * (6 + len(earlier)) + [ANY] * len(after),
        out_specs=ANY if last else VMEM,
        scratch_shapes=scratch,
        compiler_params=params(),
        cost_estimate=pl.CostEstimate(
            flops=work * HD * 8, bytes_accessed=count * slab * HD * 8, transcendentals=work
        ),
        name="context_anchor",
    )(lengths, ctx_q, state, own_k, own_v, *anchor, *earlier, *after)


def write_level(ref, width, level):
    for at in range(3):
        part = level.astype(BF)
        ref[:, width + at * HD : width + (at + 1) * HD] = part
        level = level - part.astype(F32)


def read_level(ref, width):
    parts = [ref[:, width + i * HD : width + (i + 1) * HD].astype(F32) for i in range(3)]
    return parts[0] + parts[1] + parts[2]


def source_kernel(per_kv, q_rows, group_size, lengths_ref, k_ref, v_ref, self_ref, known_ref, landed_ref, *rest):
    keep_ref, send_ref, q_all = rest[-3:]
    slab, columns = k_ref.shape
    width = per_kv * columns
    quarter = known_ref.shape[0] // 2
    query_count = 4 * quarter
    host = lax.axis_index("hst")
    own_len = lengths_ref[host]
    rows = per_kv * query_count
    odd = bit(host, 0) == 1
    low = jnp.where(odd, bit(host, 1), bit(host, 2)) == 0

    def place(lower, upper, spread_out):
        middle = (2, 1) if spread_out else (1, 2)
        for ref, (one, two) in ((lower, (0, middle[0])), (upper, (middle[1], 3))):
            q_all[one * quarter : (one + 1) * quarter, :] = ref[:quarter, :]
            q_all[two * quarter : (two + 1) * quarter, :] = ref[quarter:, :]

    for is_low, is_odd in ((False, False), (False, True), (True, False), (True, True)):
        @pl.when((low == is_low) & (odd == is_odd))
        def _():
            pair = (known_ref, landed_ref) if is_low else (landed_ref, known_ref)
            place(*pair, is_odd)

    first = lax.axis_index("tp") * (width // HD) // group_size * HD
    own_cols = pl.ds(pl.multiple_of(first, HD), columns)
    selves_kv = [self_ref[i, :, own_cols].astype(F32) for i in range(2)]
    lane = lax.broadcasted_iota(jnp.int32, (query_count, HD), 1)
    query_ids = lax.broadcasted_iota(jnp.int32, (query_count, HD), 0)
    self_ok = (host * q_rows + lane <= query_ids) & (lane < q_rows)
    self_ok = jnp.concatenate([self_ok] * per_kv, 0)
    key_ids = lax.broadcasted_iota(jnp.int32, (rows, slab), 1)
    pad = jnp.zeros((HD - q_rows, HD), F32)
    for j in range(columns // HD):
        cols = slice(j * HD, (j + 1) * HD)
        parts = [q_all[:, (j * per_kv + h) * HD : (j * per_kv + h + 1) * HD] for h in range(per_kv)]
        queries = jnp.concatenate(parts, 0)
        self_keys = jnp.concatenate([selves_kv[0][:, cols], pad], 0).astype(BF)
        self_values = jnp.concatenate([selves_kv[1][:, cols], pad], 0).astype(BF)
        near = dot_t(queries, k_ref[:, cols]) * SCALE2
        near = jnp.where(key_ids < own_len, near, MASKED)
        selves = dot_t(queries, self_keys) * SCALE2
        selves = jnp.where(self_ok, selves, MASKED)
        peak = jnp.maximum(jnp.max(near, 1, keepdims=True), jnp.max(selves, 1, keepdims=True))
        near = jnp.exp2(near - peak)
        selves = jnp.exp2(selves - peak)
        sums = jnp.sum(near, 1, keepdims=True) + jnp.sum(selves, 1, keepdims=True)
        total = dot(near.astype(BF), v_ref[:, cols]) + dot(selves.astype(BF), self_values)
        total = total / sums
        level = peak + jnp.log2(sums)
        stats = jnp.zeros((query_count, HD), F32)
        for h in range(per_kv):
            stats = jnp.where(lane == h, level[h * query_count : (h + 1) * query_count, :], stats)

        def put(out_ref):
            def run():
                for h in range(per_kv):
                    part = total[h * query_count : (h + 1) * query_count, :]
                    out_ref[:, h * HD : (h + 1) * HD] = part.astype(BF)
                write_level(out_ref, per_kv * HD, stats)

            return run

        choose(odd if j else jnp.logical_not(odd), put(keep_ref), put(send_ref))


def source_part(lengths, own_k, own_v, query_kv, known, landed, q_rows, per_kv, after=()):
    slab, columns = own_k.shape
    width = per_kv * columns
    count = 2 * known.shape[0]
    work = count * (width // HD) * slab
    return pl.pallas_call(
        functools.partial(source_kernel, per_kv, q_rows, H // KVH),
        out_shape=[jax.ShapeDtypeStruct((count, (per_kv + 3) * HD), BF)] * 2,
        in_specs=[SMEM] + [VMEM] * 5 + [ANY] * len(after),
        out_specs=[VMEM] * 2,
        scratch_shapes=[pltpu.VMEM((count, width), BF)],
        compiler_params=params(),
        cost_estimate=pl.CostEstimate(flops=work * HD * 8, bytes_accessed=2**21, transcendentals=work),
        name="query_source",
    )(lengths, own_k, own_v, query_kv, known, landed, *after)


def merged(refs, width):
    levels = [read_level(ref, width) for ref in refs]
    peak = jnp.maximum(*levels)
    weights = [jnp.exp2(x - peak) for x in levels]
    whole = weights[0] + weights[1]
    return [w / whole for w in weights], peak + jnp.log2(whole)


def blend(shares, refs, h):
    cols = slice(h * HD, (h + 1) * HD)
    return sum(w[:, h : h + 1] * ref[:, cols].astype(F32) for w, ref in zip(shares, refs))


def merge_part(one, two, last, after=()):
    rows, wide = one.shape
    width = wide - 3 * HD

    def kernel(one_ref, two_ref, *rest):
        out_ref = rest[-1]
        shares, level = merged((one_ref, two_ref), width)
        if not last:
            write_level(out_ref, width, level)
        for h in range(width // HD):
            out_ref[:, h * HD : (h + 1) * HD] = blend(shares, (one_ref, two_ref), h).astype(BF)

    return small_call(kernel, "query_merge", [(rows, width if last else wide)], (one, two), after)[0]


def project_part(own, other, out_weight, after=()):
    rows, half = own.shape
    depth, columns = out_weight.shape

    def kernel(w_ref, own_ref, other_ref, *rest):
        out_ref, attended = rest[-2:]

        def put(first, second):
            def run():
                attended[:, :half] = first[...]
                attended[:, half:] = second[...]

            return run

        even = bit(lax.axis_index("hst"), 0) == 0
        choose(even, put(own_ref, other_ref), put(other_ref, own_ref))
        out_ref[...] = dot(attended[...], w_ref[...]).astype(BF)

    return pl.pallas_call(
        kernel,
        out_shape=jax.ShapeDtypeStruct((rows, columns), BF),
        in_specs=[VMEM] * 3 + [ANY] * len(after),
        out_specs=VMEM,
        scratch_shapes=[pltpu.VMEM((rows, depth), BF)],
        compiler_params=params(),
        cost_estimate=pl.CostEstimate(
            flops=2 * rows * depth * columns, bytes_accessed=2 * depth * columns, transcendentals=0
        ),
        name="query_project",
    )(out_weight, own, other, *after)


def general_queries(lengths, own_k, own_v, self_kv, query_q, out_weight, per_kv):
    own_kv = jnp.stack([own_k, own_v], 0)
    host_id = lax.axis_index("hst")
    local_heads = query_q.shape[1] // HD
    kv_local = own_kv.shape[2] // HD
    slab_rows = own_kv.shape[1]
    own_len = lengths[host_id]
    row_ids = jnp.arange(slab_rows)
    all_queries = lax.all_gather(query_q, "hst", axis=0, tiled=True)
    query_count = all_queries.shape[0]
    q_rows = query_q.shape[0]
    source = jnp.concatenate([own_kv, self_kv], 1)
    source = source.reshape(2, slab_rows + q_rows, kv_local, HD).transpose(0, 2, 1, 3)
    query_ids = jnp.arange(query_count)
    context_ok = jnp.broadcast_to(row_ids[None, :] < own_len, (query_count, slab_rows))
    self_ok = (host_id * q_rows + jnp.arange(q_rows))[None, :] <= query_ids[:, None]
    seen_ok = jnp.concatenate([context_ok, self_ok], 1)
    query_heads = all_queries.reshape(query_count, local_heads, HD).transpose(1, 0, 2)

    def score_head(operands):
        query_rows, head_index = operands
        kv_index = head_index // per_kv
        scores = dot_t(query_rows, source[0, kv_index]) * HD ** (-0.5)
        scores = jnp.where(seen_ok, scores, MASKED)
        peak = jnp.max(scores, axis=1)
        expo = jnp.exp(scores - peak[:, None])
        return peak, jnp.sum(expo, axis=1), dot(expo.astype(BF), source[1, kv_index])

    maxima, totals, outputs = lax.map(score_head, (query_heads, jnp.arange(local_heads)))
    factor = jnp.exp(maxima - lax.pmax(maxima, "hst"))
    denominator, summed = lax.psum((totals * factor, outputs * factor[..., None]), "hst")
    attended = (summed / denominator[..., None]).astype(BF)
    attended = attended.transpose(1, 0, 2).reshape(query_count, local_heads * HD)
    return lax.psum(dot(attended, out_weight), "tp").astype(BF)


def per_device(hosts, groups, ctx_q, ctx_kv, lengths, query_q, query_kv, out_weight):
    slab = ctx_q.shape[0]
    local_heads = ctx_q.shape[1] // HD
    group_size = H // KVH
    kv_local = max(1, local_heads // group_size)
    per_kv = min(local_heads, group_size)
    q_rows = query_q.shape[0]
    host = lax.axis_index("hst")
    fast = hosts == 8 and groups & (groups - 1) == 0
    fast = fast and q_rows == 8 and local_heads == 16 and per_kv == 8

    if not fast:
        kv_first = lax.axis_index("tp") * local_heads // group_size
        self_kv = lax.dynamic_slice_in_dim(query_kv, kv_first * HD, kv_local * HD, 2)
        own_k, own_v = pick(ctx_kv, kv_local, local_heads)
        query_out = general_queries(lengths, own_k, own_v, self_kv, query_q, out_weight, per_kv)
        k, v = spread(jnp.stack([own_k, own_v]), "hst", 0)
        anchor = jnp.where(host % 2 == 0, k, v), jnp.where(host % 2 == 0, v, k)
        state = own_part(ctx_q, own_k, own_v, 0, local_heads, per_kv)
        context_out = anchor_part(
            lengths, ctx_q, state, 0, own_k, own_v, anchor, 0, local_heads, per_kv, {}
        )
        return context_out, query_out

    states = {}

    def own(first, count, after=()):
        states[first] = own_part(ctx_q, own_k, own_v, first, count, per_kv, after)
        return states[first]

    along = ((2, 4), (4, 2))

    def near_low(h):
        return jnp.where(bit(h, 0) == 1, bit(h, 2), bit(h, 1)) == 0

    landed = swap(query_q, "hst", hosts, 1, 1)
    own_k, own_v = pick(ctx_kv, kv_local, local_heads)
    value_landed = swap(own_v, "hst", hosts, 1, 1)
    queries = join(lambda h: bit(h, 0) == 0, query_q, landed, (own_v,))
    landed = swap(queries, "hst", hosts, *along[0])
    done = own(0, 2, (queries,))
    held = relay(lambda h: bit(h, 0) == 0, own_k, value_landed, (done,))
    held_landed = swap(held, "hst", hosts, *along[0])
    done = own(2, 2, (held,))
    queries = join(near_low, queries, landed, (done,))
    landed = swap(queries, "hst", hosts, *along[1])
    done = own(4, 4, (queries,))
    keep, send = source_part(lengths, own_k, own_v, query_kv, queries, landed, q_rows, per_kv, (done,))
    landed = swap(send, "hst", hosts, 1, 1)
    done = own(8, 2, (keep,))
    held = relay(lambda h: h < 2, held, held_landed, (done,))
    held_landed = swap(held, "hst", hosts, *along[1])
    source = merge_part(keep, landed, False, (held,))
    landed = swap(source, "hst", hosts, *along[0])
    done = own(10, 6, (source,))
    source = merge_part(source, landed, False, (done,))
    landed = swap(source, "hst", hosts, *along[1])
    held = relay(lambda h: (h <= 2) | (h == 5), held, held_landed, (source,))
    other = swap(held, "hst", hosts, 1, 1)
    results = {}

    def anchors(first, count, after, last=False):
        base = max(x for x in states if x <= first)
        results[first] = anchor_part(
            lengths, ctx_q, states[base], base, own_k, own_v, (held, other),
            first, count, per_kv, dict(results) if last else None, after,
        )
        return results[first]

    done = anchors(0, 2, (held,))
    done = anchors(2, 2, (done,))
    source = merge_part(source, landed, True, (done,))
    landed = swap(source, "hst", hosts, 1, 1)
    done = anchors(4, 2, (source,))
    terms = project_part(source, landed, out_weight, (done,))
    shares = [(10, 6, True), (8, 2, False), (6, 2, False)]
    step = 1
    while step < groups:
        landed = swap(terms, "tp", groups, step, step)
        while shares:
            first, count, last = shares.pop()
            done = anchors(first, count, (terms, done), last)
            if last or (first == 8 and step == 1):
                break
        terms = add_part(terms, landed, () if last else (done,))
        step *= 2
    for first, count, last in reversed(shares):
        done = anchors(first, count, (), last)
    return done, terms


def solution(mesh):
    hosts, groups = mesh.shape["hst"], mesh.shape["tp"]
    return jax.shard_map(
        functools.partial(per_device, hosts, groups),
        mesh=mesh,
        in_specs=(
            P("hst", "tp"),
            P(None, "hst", None),
            P(),
            P("hst", "tp"),
            P(None, "hst", None),
            P("tp", "hst"),
        ),
        out_specs=(P("hst", "tp"), P(None, "hst")),
        check_vma=False,
    )
```

```python
import functools

import jax
import jax.numpy as jnp
from jax import lax
from jax.experimental import pallas as pl
from jax.experimental.pallas import tpu as pltpu
from jax.sharding import PartitionSpec as P

H = 64
KVH = 8
HD = 128
MASKED = -1e30
LOG2E = 1.4426950408889634
SCALE2 = HD ** (-0.5) * LOG2E
TINY = 2.0 ** -90
BF = jnp.bfloat16
F32 = jnp.float32
VMEM = pl.BlockSpec(memory_space=pltpu.VMEM)
SMEM = pl.BlockSpec(memory_space=pltpu.SMEM)
ANY = pl.BlockSpec(memory_space=pl.ANY)
HBM = pl.BlockSpec(memory_space=pltpu.HBM)


def params(mib=20):
    return pltpu.CompilerParams(vmem_limit_bytes=mib * 2**20)


def dot_t(a, b):
    return lax.dot_general(a, b, (((1,), (1,)), ((), ())), preferred_element_type=F32)


def dot(a, b):
    return lax.dot_general(a, b, (((1,), (0,)), ((), ())), preferred_element_type=F32)


def spread(value, axis, source):
    kept = jnp.where(lax.axis_index(axis) == source, value, 0).astype(value.dtype)
    return lax.psum(kept, axis)


def swap(value, axis, size, even, odd):
    return lax.ppermute(value, axis, [(i, i ^ (odd if i & 1 else even)) for i in range(size)])


def pick_kernel(group_size, local_heads, kv_ref, k_ref, v_ref, sems):
    first = lax.axis_index("tp") * local_heads // group_size * HD
    cols = pl.ds(pl.multiple_of(first, HD), k_ref.shape[1])
    moves = [
        pltpu.make_async_copy(kv_ref.at[1, :, cols], v_ref, sems.at[1]),
        pltpu.make_async_copy(kv_ref.at[0, :, cols], k_ref, sems.at[0]),
    ]
    for move in moves:
        move.start()
    for move in moves:
        move.wait()


def pick(ctx_kv, kv_local, local_heads):
    return pl.pallas_call(
        functools.partial(pick_kernel, H // KVH, local_heads),
        out_shape=[jax.ShapeDtypeStruct((ctx_kv.shape[1], kv_local * HD), BF)] * 2,
        in_specs=[HBM],
        out_specs=[VMEM] * 2,
        scratch_shapes=[pltpu.SemaphoreType.DMA((2,))],
        compiler_params=params(52),
        name="pick_columns",
    )(ctx_kv)


def bit(value, at):
    return (value >> at) & 1


def small_call(kernel, name, shapes, inputs, after=()):
    return pl.pallas_call(
        kernel,
        out_shape=[jax.ShapeDtypeStruct(x, BF) for x in shapes],
        in_specs=[VMEM] * len(inputs) + [ANY] * len(after),
        out_specs=[VMEM] * len(shapes),
        compiler_params=params(),
        name=name,
    )(*inputs, *after)


def choose(condition, one, two):
    pl.when(condition)(one)
    pl.when(jnp.logical_not(condition))(two)


def take_rows(target, source, rows, cols=slice(None)):
    def run():
        target[:rows, :] = source[:rows, cols]

    return run


def first_payloads(own_k, value_landed, query_q, query_landed, after):
    slab, columns = own_k.shape
    q_rows, width = query_q.shape

    def kernel(k_ref, v_ref, own_ref, landed_ref, *rest):
        out_refs = rest[-(columns // HD) :]
        even = bit(lax.axis_index("hst"), 0) == 0
        for j, out_ref in enumerate(out_refs):
            cols = slice(j * HD, (j + 1) * HD)
            choose(even, take_rows(out_ref, k_ref, slab, cols), take_rows(out_ref, v_ref, slab, cols))

        def put(first, second):
            def run():
                both = jnp.concatenate([first[...].astype(F32), second[...].astype(F32)], 0).astype(BF)
                for h in range(width // HD):
                    at = slab + 2 * q_rows * h
                    out_refs[0][at : at + 2 * q_rows, :] = both[:, h * HD : (h + 1) * HD]

            return run

        choose(even, put(own_ref, landed_ref), put(landed_ref, own_ref))

    shapes = [(slab, HD)] * (columns // HD)
    shapes[0] = (slab + 2 * q_rows * width // HD, HD)
    return small_call(kernel, "payload_first", shapes, (own_k, value_landed, query_q, query_landed), after)


def relay(keep_of, one, two, slab, low_of=None, after=()):
    rows = one.shape[0] - slab if low_of is not None else 0

    def kernel(one_ref, two_ref, *rest):
        out_ref = rest[-1]
        host = lax.axis_index("hst")
        choose(keep_of(host), take_rows(out_ref, one_ref, slab), take_rows(out_ref, two_ref, slab))

        def put(first, second):
            def run():
                out_ref[slab : slab + rows, :] = first[slab:, :]
                out_ref[slab + rows :, :] = second[slab:, :]

            return run

        if rows:
            choose(low_of(host), put(one_ref, two_ref), put(two_ref, one_ref))

    return small_call(kernel, "payload_relay", [(slab + 2 * rows, HD)], (one, two), after)[0]


def add_part(one, two, after=()):
    def kernel(one_ref, two_ref, *rest):
        rest[-1][...] = (one_ref[...].astype(F32) + two_ref[...].astype(F32)).astype(BF)

    return small_call(kernel, "query_sum", [one.shape], (one, two), after)[0]


def fill_values(vaug, values):
    for j in range(values.shape[1] // HD):
        vaug[:, 2 * j * HD : (2 * j + 1) * HD] = values[:, j * HD : (j + 1) * HD]
        vaug[:, (2 * j + 1) * HD : (2 * j + 2) * HD] = jnp.ones((values.shape[0], HD), BF)


def lanes(index, width):
    return pl.ds(pl.multiple_of(index * width, width), width)


def row_tile(slab):
    return 256 if slab % 256 == 0 else slab


def body_size(count, most):
    return max(x for x in range(1, most + 1) if count % x == 0)


def own_kernel(first, count, per_kv, q_ref, k_ref, v_ref, *rest):
    state_ref, vaug = rest[-2], rest[-1]
    slab = q_ref.shape[0]
    tile = row_tile(slab)
    half = tile // 2
    heads = body_size(count, 4)
    fill_values(vaug, v_ref)
    rows = lax.broadcasted_iota(jnp.int32, (half, half), 0)
    cols = lax.broadcasted_iota(jnp.int32, (half, half), 1)
    causal = cols <= rows
    chunks = slab // tile
    units = [(h, j) for h in range(heads) for j in range(chunks)]

    def body(i, carry):
        kv = lax.div(first + i * heads, per_kv)

        def scores(at):
            h, j = units[at]
            query = q_ref[j * tile :, lanes(first + i * heads + h, HD)]
            return dot_t(query, k_ref[j * tile : (j + 1) * tile, lanes(kv, HD)])

        def power(x):
            return jnp.exp2(x * SCALE2).astype(BF)

        def corner(x):
            return jnp.where(causal, jnp.exp2(x * SCALE2), 0.0).astype(BF)

        current = scores(0)
        totals = [None] * chunks
        for at, (h, j) in enumerate(units):
            following = scores(at + 1) if at + 1 < len(units) else None
            top = jnp.concatenate([corner(current[:half, :half]), jnp.zeros((half, half), BF)], 1)
            low = jnp.concatenate([power(current[half:tile, :half]), corner(current[half:tile, half:])], 1)
            expo = [top, low] if j == chunks - 1 else [top, low, power(current[tile:])]
            part = dot(jnp.concatenate(expo, 0), vaug[j * tile : (j + 1) * tile, lanes(kv, 2 * HD)])
            for r in range(j, chunks):
                piece = part[(r - j) * tile : (r - j + 1) * tile]
                totals[r] = piece if j == 0 else totals[r] + piece
            state_ref[j * tile : (j + 1) * tile, lanes(i * heads + h, 2 * HD)] = totals[j]
            current = following
        return carry

    lax.fori_loop(0, count // heads, body, 0)


def own_part(ctx_q, own_k, own_v, first, count, per_kv, after=()):
    slab = ctx_q.shape[0]
    work = count * slab * (slab + row_tile(slab)) // 2
    return pl.pallas_call(
        functools.partial(own_kernel, first, count, per_kv),
        out_shape=jax.ShapeDtypeStruct((slab, count * 2 * HD), F32),
        in_specs=[VMEM] * 3 + [ANY] * len(after),
        out_specs=VMEM,
        scratch_shapes=[pltpu.VMEM((slab, 2 * own_v.shape[1]), BF)],
        compiler_params=params(),
        cost_estimate=pl.CostEstimate(
            flops=work * HD * 8, bytes_accessed=count * slab * HD * 6, transcendentals=work
        ),
        name="context_own",
    )(ctx_q, own_k, own_v, *after)


def anchor_kernel(first, count, base, per_kv, last, befores, *refs):
    lengths_ref, q_ref, state_ref, k_ref, v_ref, even_ref, odd_ref = refs[:7]
    earlier = refs[7 : 7 + len(befores)]
    if last:
        full_ref, out_ref, keys, vaug, sems = refs[-5:]
    else:
        out_ref, keys, vaug = refs[-3:]
    slab = q_ref.shape[0]
    heads = body_size(count, 2 if last else 4)
    kv = first // per_kv
    host = lax.axis_index("hst")
    own_len = lengths_ref[host]

    def hand_over(source, start, width, sem):
        target = full_ref.at[:, pl.ds(start * HD, width * HD)]
        return pltpu.make_async_copy(source, target, sems.at[sem])

    moves = [hand_over(earlier[n], *place, n) for n, place in enumerate(befores)]
    for move in moves:
        move.start()

    @pl.when(host % 2 == 0)
    def _():
        keys[...] = even_ref[...]
        fill_values(vaug, odd_ref)

    @pl.when(host % 2 == 1)
    def _():
        keys[...] = odd_ref[...]
        fill_values(vaug, even_ref)

    def part(start):
        def query_of(h):
            at = (first + start + h) * HD
            return q_ref[:, at : at + HD]

        def scores(h):
            return dot_t(query_of(h), keys[...])

        def state_of(h):
            at = (first - base + start + h) * 2 * HD
            return state_ref[:, at : at + 2 * HD]

        def finish(h, total, worst):
            sums = total[:, HD:]
            inverse = pl.reciprocal(sums, approx=True)
            out_ref[:, (start + h) * HD : (start + h + 1) * HD] = (total[:, :HD] * inverse).astype(BF)
            return jnp.minimum(worst, jnp.minimum(sums, inverse))

        def check(worst):
            @pl.when(jnp.logical_not(jnp.min(worst) > TINY))
            def _():
                exact_block(first + start, start, heads, host, own_len, kv, q_ref, k_ref, v_ref, keys, vaug, out_ref)

        @pl.when(host == 0)
        def _():
            worst = jnp.ones((slab, HD), F32)
            for h in range(heads):
                worst = finish(h, state_of(h), worst)
            check(worst)

        @pl.when(host > 0)
        def _():
            worst = jnp.ones((slab, HD), F32)
            current = scores(0)
            for h in range(heads):
                following = scores(h + 1) if h + 1 < heads else None
                expo = jnp.exp2(current * SCALE2).astype(BF)
                total = dot(expo, vaug[...]) + state_of(h)
                worst = finish(h, total, worst)
                current = following
            check(worst)

        @pl.when(own_len < slab)
        def _():
            row_ids = lax.broadcasted_iota(jnp.int32, (slab, HD), 0)
            for h in range(start, start + heads):
                cols = slice(h * HD, (h + 1) * HD)
                kept = jnp.where(row_ids < own_len, out_ref[:, cols].astype(F32), 0.0)
                out_ref[:, cols] = kept.astype(BF)

        if last:
            source = out_ref.at[:, start * HD : (start + heads) * HD]
            move = hand_over(source, first + start, heads, len(befores) + start // heads)
            move.start()
            moves.append(move)

    for start in range(0, count, heads):
        part(start)
    for move in moves:
        move.wait()


def exact_block(q_head, out_head, heads, host, own_len, kv, q_ref, k_ref, v_ref, keys, vaug, out_ref):
    slab = q_ref.shape[0]
    tile = 128

    def body(i, carry):
        h = lax.div(i, slab // tile)
        r = lax.rem(i, slab // tile)
        at = pl.ds(pl.multiple_of(r * tile, tile), tile)
        query = q_ref[at, lanes(q_head + h, HD)]
        row_ids = lax.broadcasted_iota(jnp.int32, (tile, slab), 0) + r * tile
        key_ids = lax.broadcasted_iota(jnp.int32, (tile, slab), 1)
        own = dot_t(query, k_ref[:, kv * HD : (kv + 1) * HD]) * SCALE2
        own = jnp.where((key_ids <= row_ids) & (key_ids < own_len), own, MASKED)
        far = dot_t(query, keys[...]) * SCALE2
        far = jnp.where(host > 0, far, MASKED)
        peak = jnp.maximum(jnp.max(own, 1, keepdims=True), jnp.max(far, 1, keepdims=True))
        own = jnp.exp2(own - peak)
        far = jnp.where(host > 0, jnp.exp2(far - peak), 0.0)
        sums = jnp.sum(own, 1, keepdims=True) + jnp.sum(far, 1, keepdims=True)
        values = jnp.where(host > 0, vaug[:, :HD].astype(F32), 0.0).astype(BF)
        total = dot(own.astype(BF), v_ref[:, kv * HD : (kv + 1) * HD]) + dot(far.astype(BF), values)
        live = row_ids[:, :1] < own_len
        out_ref[at, lanes(out_head + h, HD)] = jnp.where(live, total / sums, 0.0).astype(BF)
        return carry

    lax.fori_loop(0, heads * (slab // tile), body, 0)


def anchor_part(lengths, ctx_q, state, base, own_k, own_v, anchor, first, count, per_kv, befores=None, after=()):
    slab, width = ctx_q.shape
    work = count * slab * slab
    last = befores is not None
    earlier = list(befores.values()) if last else []
    places = tuple((at, x.shape[1] // HD) for at, x in befores.items()) if last else ()
    results = jax.ShapeDtypeStruct((slab, count * HD), BF)
    scratch = [pltpu.VMEM((slab, HD), BF), pltpu.VMEM((slab, 2 * HD), BF)]
    if last:
        scratch = [pltpu.VMEM(results.shape, BF)] + scratch
        scratch += [pltpu.SemaphoreType.DMA((len(earlier) + count,))]
        results = jax.ShapeDtypeStruct((slab, width), BF)
    return pl.pallas_call(
        functools.partial(anchor_kernel, first, count, base, per_kv, last, places),
        out_shape=results,
        in_specs=[SMEM] + [VMEM] * (6 + len(earlier)) + [ANY] * len(after),
        out_specs=ANY if last else VMEM,
        scratch_shapes=scratch,
        compiler_params=params(),
        cost_estimate=pl.CostEstimate(
            flops=work * HD * 8, bytes_accessed=count * slab * HD * 8, transcendentals=work
        ),
        name="context_anchor",
    )(lengths, ctx_q, state, own_k, own_v, *anchor, *earlier, *after)


def write_level(ref, width, level):
    for at in range(3):
        part = level.astype(BF)
        ref[:, width + at * HD : width + (at + 1) * HD] = part
        level = level - part.astype(F32)


def read_level(ref, width):
    parts = [ref[:, width + i * HD : width + (i + 1) * HD].astype(F32) for i in range(3)]
    return parts[0] + parts[1] + parts[2]


def source_kernel(per_kv, q_rows, group_size, lengths_ref, k_ref, v_ref, self_ref, known_ref, landed_ref, *rest):
    keep_ref, send_ref, q_all = rest[-3:]
    slab, columns = k_ref.shape
    width = per_kv * columns
    query_count = 8 * q_rows
    block = 2 * q_rows
    quarter = block * width // HD
    host = lax.axis_index("hst")
    own_len = lengths_ref[host]
    rows = per_kv * query_count
    odd = bit(host, 0) == 1
    low = jnp.where(odd, bit(host, 1), bit(host, 2)) == 0

    def place(lower, upper, spread_out):
        middle = (2, 1) if spread_out else (1, 2)
        for ref, chips in ((lower, (0, middle[0])), (upper, (middle[1], 3))):
            for n, chip in enumerate(chips):
                for h in range(width // HD):
                    at = slab + n * quarter + h * block
                    to = h * query_count + chip * block
                    q_all[to : to + block, :] = ref[at : at + block, :]

    for is_low, is_odd in ((False, False), (False, True), (True, False), (True, True)):
        @pl.when((low == is_low) & (odd == is_odd))
        def _():
            pair = (known_ref, landed_ref) if is_low else (landed_ref, known_ref)
            place(*pair, is_odd)

    first = lax.axis_index("tp") * (width // HD) // group_size * HD
    own_cols = pl.ds(pl.multiple_of(first, HD), columns)
    selves_kv = [self_ref[i, :, own_cols].astype(F32) for i in range(2)]
    lane = lax.broadcasted_iota(jnp.int32, (query_count, HD), 1)
    query_ids = lax.broadcasted_iota(jnp.int32, (query_count, HD), 0)
    self_ok = (host * q_rows + lane <= query_ids) & (lane < q_rows)
    self_ok = jnp.concatenate([self_ok] * per_kv, 0)
    key_ids = lax.broadcasted_iota(jnp.int32, (rows, slab), 1)
    pad = jnp.zeros((HD - q_rows, HD), F32)
    for j in range(columns // HD):
        cols = slice(j * HD, (j + 1) * HD)
        queries = q_all[j * rows : (j + 1) * rows, :]
        self_keys = jnp.concatenate([selves_kv[0][:, cols], pad], 0).astype(BF)
        self_values = jnp.concatenate([selves_kv[1][:, cols], pad], 0).astype(BF)
        near = dot_t(queries, k_ref[:, cols]) * SCALE2
        near = jnp.where(key_ids < own_len, near, MASKED)
        selves = dot_t(queries, self_keys) * SCALE2
        selves = jnp.where(self_ok, selves, MASKED)
        peak = jnp.maximum(jnp.max(near, 1, keepdims=True), jnp.max(selves, 1, keepdims=True))
        near = jnp.exp2(near - peak)
        selves = jnp.exp2(selves - peak)
        sums = jnp.sum(near, 1, keepdims=True) + jnp.sum(selves, 1, keepdims=True)
        total = dot(near.astype(BF), v_ref[:, cols]) + dot(selves.astype(BF), self_values)
        total = total / sums
        level = peak + jnp.log2(sums)
        stats = jnp.zeros((query_count, HD), F32)
        for h in range(per_kv):
            stats = jnp.where(lane == h, level[h * query_count : (h + 1) * query_count, :], stats)

        def put(out_ref):
            def run():
                for h in range(per_kv):
                    part = total[h * query_count : (h + 1) * query_count, :]
                    out_ref[:, h * HD : (h + 1) * HD] = part.astype(BF)
                write_level(out_ref, per_kv * HD, stats)

            return run

        choose(odd if j else jnp.logical_not(odd), put(keep_ref), put(send_ref))


def source_part(lengths, own_k, own_v, query_kv, known, landed, q_rows, per_kv, after=()):
    slab, columns = own_k.shape
    width = per_kv * columns
    count = 8 * q_rows
    work = count * (width // HD) * slab
    return pl.pallas_call(
        functools.partial(source_kernel, per_kv, q_rows, H // KVH),
        out_shape=[jax.ShapeDtypeStruct((count, (per_kv + 3) * HD), BF)] * 2,
        in_specs=[SMEM] + [VMEM] * 5 + [ANY] * len(after),
        out_specs=[VMEM] * 2,
        scratch_shapes=[pltpu.VMEM((count * width // HD, HD), BF)],
        compiler_params=params(),
        cost_estimate=pl.CostEstimate(flops=work * HD * 8, bytes_accessed=2**21, transcendentals=work),
        name="query_source",
    )(lengths, own_k, own_v, query_kv, known, landed, *after)


def merged(refs, width):
    levels = [read_level(ref, width) for ref in refs]
    peak = jnp.maximum(*levels)
    weights = [jnp.exp2(x - peak) for x in levels]
    whole = weights[0] + weights[1]
    return [w / whole for w in weights], peak + jnp.log2(whole)


def blend(shares, refs, h):
    cols = slice(h * HD, (h + 1) * HD)
    return sum(w[:, h : h + 1] * ref[:, cols].astype(F32) for w, ref in zip(shares, refs))


def merge_part(one, two, last, after=()):
    rows, wide = one.shape
    width = wide - 3 * HD

    def kernel(one_ref, two_ref, *rest):
        out_ref = rest[-1]
        shares, level = merged((one_ref, two_ref), width)
        if not last:
            write_level(out_ref, width, level)
        for h in range(width // HD):
            out_ref[:, h * HD : (h + 1) * HD] = blend(shares, (one_ref, two_ref), h).astype(BF)

    return small_call(kernel, "query_merge", [(rows, width if last else wide)], (one, two), after)[0]


def project_part(own, other, out_weight, after=()):
    rows, half = own.shape
    depth, columns = out_weight.shape

    def kernel(w_ref, own_ref, other_ref, *rest):
        out_ref, attended = rest[-2:]

        def put(first, second):
            def run():
                attended[:, :half] = first[...]
                attended[:, half:] = second[...]

            return run

        even = bit(lax.axis_index("hst"), 0) == 0
        choose(even, put(own_ref, other_ref), put(other_ref, own_ref))
        out_ref[...] = dot(attended[...], w_ref[...]).astype(BF)

    return pl.pallas_call(
        kernel,
        out_shape=jax.ShapeDtypeStruct((rows, columns), BF),
        in_specs=[VMEM] * 3 + [ANY] * len(after),
        out_specs=VMEM,
        scratch_shapes=[pltpu.VMEM((rows, depth), BF)],
        compiler_params=params(),
        cost_estimate=pl.CostEstimate(
            flops=2 * rows * depth * columns, bytes_accessed=2 * depth * columns, transcendentals=0
        ),
        name="query_project",
    )(out_weight, own, other, *after)


def general_queries(lengths, own_k, own_v, self_kv, query_q, out_weight, per_kv):
    own_kv = jnp.stack([own_k, own_v], 0)
    host_id = lax.axis_index("hst")
    local_heads = query_q.shape[1] // HD
    kv_local = own_kv.shape[2] // HD
    slab_rows = own_kv.shape[1]
    own_len = lengths[host_id]
    row_ids = jnp.arange(slab_rows)
    all_queries = lax.all_gather(query_q, "hst", axis=0, tiled=True)
    query_count = all_queries.shape[0]
    q_rows = query_q.shape[0]
    source = jnp.concatenate([own_kv, self_kv], 1)
    source = source.reshape(2, slab_rows + q_rows, kv_local, HD).transpose(0, 2, 1, 3)
    query_ids = jnp.arange(query_count)
    context_ok = jnp.broadcast_to(row_ids[None, :] < own_len, (query_count, slab_rows))
    self_ok = (host_id * q_rows + jnp.arange(q_rows))[None, :] <= query_ids[:, None]
    seen_ok = jnp.concatenate([context_ok, self_ok], 1)
    query_heads = all_queries.reshape(query_count, local_heads, HD).transpose(1, 0, 2)

    def score_head(operands):
        query_rows, head_index = operands
        kv_index = head_index // per_kv
        scores = dot_t(query_rows, source[0, kv_index]) * HD ** (-0.5)
        scores = jnp.where(seen_ok, scores, MASKED)
        peak = jnp.max(scores, axis=1)
        expo = jnp.exp(scores - peak[:, None])
        return peak, jnp.sum(expo, axis=1), dot(expo.astype(BF), source[1, kv_index])

    maxima, totals, outputs = lax.map(score_head, (query_heads, jnp.arange(local_heads)))
    factor = jnp.exp(maxima - lax.pmax(maxima, "hst"))
    denominator, summed = lax.psum((totals * factor, outputs * factor[..., None]), "hst")
    attended = (summed / denominator[..., None]).astype(BF)
    attended = attended.transpose(1, 0, 2).reshape(query_count, local_heads * HD)
    return lax.psum(dot(attended, out_weight), "tp").astype(BF)


def per_device(hosts, groups, ctx_q, ctx_kv, lengths, query_q, query_kv, out_weight):
    slab = ctx_q.shape[0]
    local_heads = ctx_q.shape[1] // HD
    group_size = H // KVH
    kv_local = max(1, local_heads // group_size)
    per_kv = min(local_heads, group_size)
    q_rows = query_q.shape[0]
    host = lax.axis_index("hst")
    fast = hosts == 8 and groups & (groups - 1) == 0
    fast = fast and q_rows == 8 and local_heads == 16 and per_kv == 8

    if not fast:
        kv_first = lax.axis_index("tp") * local_heads // group_size
        self_kv = lax.dynamic_slice_in_dim(query_kv, kv_first * HD, kv_local * HD, 2)
        own_k, own_v = pick(ctx_kv, kv_local, local_heads)
        query_out = general_queries(lengths, own_k, own_v, self_kv, query_q, out_weight, per_kv)
        k, v = spread(jnp.stack([own_k, own_v]), "hst", 0)
        anchor = jnp.where(host % 2 == 0, k, v), jnp.where(host % 2 == 0, v, k)
        state = own_part(ctx_q, own_k, own_v, 0, local_heads, per_kv)
        results = {}
        for first in range(0, local_heads, per_kv):
            cols = slice(first // per_kv * HD, (first // per_kv + 1) * HD)
            last = first + per_kv == local_heads
            results[first] = anchor_part(
                lengths, ctx_q, state, 0, own_k, own_v, [x[:, cols] for x in anchor],
                first, per_kv, per_kv, dict(results) if last else None,
            )
        return results[first], query_out

    states = {}

    def own(first, count, after=()):
        states[first] = own_part(ctx_q, own_k, own_v, first, count, per_kv, after)
        return states[first]

    along = ((2, 4), (4, 2))

    def source_first(h):
        return h < 2

    def done_early(h):
        return (h <= 2) | (h == 5)

    def near_low(h):
        return jnp.where(bit(h, 0) == 1, bit(h, 2), bit(h, 1)) == 0

    query_landed = swap(query_q, "hst", hosts, 1, 1)
    own_k, own_v = pick(ctx_kv, kv_local, local_heads)
    landed = swap(own_v, "hst", hosts, 1, 1)
    done = own(0, 2)
    one, two = first_payloads(own_k, landed, query_q, query_landed, (done,))
    one_landed = swap(one, "hst", hosts, *along[0])
    two_landed = swap(two, "hst", hosts, *along[0])
    done = own(2, 6, (one,))
    one = relay(source_first, one, one_landed, slab, near_low, (done,))
    one_landed = swap(one, "hst", hosts, *along[1])
    done = own(8, 8, (one,))
    two = relay(source_first, two, two_landed, slab, None, (done,))
    two_landed = swap(two, "hst", hosts, *along[1])
    held = relay(done_early, one, one_landed, slab, None, (two,))
    anchor = held, swap(held, "hst", hosts, 1, 1)
    keep, send = source_part(lengths, own_k, own_v, query_kv, one, one_landed, q_rows, per_kv, (held,))
    landed = swap(send, "hst", hosts, 1, 1)
    results = {}

    def anchors(first, count, after, last=False):
        base = max(x for x in states if x <= first)
        results[first] = anchor_part(
            lengths, ctx_q, states[base], base, own_k, own_v, anchor,
            first, count, per_kv, dict(results) if last else None, after,
        )
        return results[first]

    done = anchors(0, 2, (keep,))
    source = merge_part(keep, landed, False, (done,))
    landed = swap(source, "hst", hosts, *along[0])
    done = anchors(2, 3, (source,))
    source = merge_part(source, landed, False, (done,))
    landed = swap(source, "hst", hosts, *along[1])
    held = relay(done_early, two, two_landed, slab, None, (source,))
    other = swap(held, "hst", hosts, 1, 1)
    done = anchors(5, 3, (held,))
    anchor = held, other
    source = merge_part(source, landed, True, (done,))
    landed = swap(source, "hst", hosts, 1, 1)
    done = anchors(8, 1, (source,))
    terms = project_part(source, landed, out_weight, (done,))
    shares = [(12, 4, True), (9, 3, False)]
    step = 1
    while step < groups:
        landed = swap(terms, "tp", groups, step, step)
        last = False
        if shares:
            first, count, last = shares.pop()
            done = anchors(first, count, (terms,), last)
        terms = add_part(terms, landed, () if last else (done,))
        step *= 2
    for first, count, last in reversed(shares):
        done = anchors(first, count, (), last)
    return done, terms


def solution(mesh):
    hosts, groups = mesh.shape["hst"], mesh.shape["tp"]
    return jax.shard_map(
        functools.partial(per_device, hosts, groups),
        mesh=mesh,
        in_specs=(
            P("hst", "tp"),
            P(None, "hst", None),
            P(),
            P("hst", "tp"),
            P(None, "hst", None),
            P("tp", "hst"),
        ),
        out_specs=(P("hst", "tp"), P(None, "hst")),
        check_vma=False,
    )
```

```python
import functools

import jax
import jax.numpy as jnp
from jax import lax
from jax.experimental import pallas as pl
from jax.experimental.pallas import tpu as pltpu
from jax.sharding import PartitionSpec as P

H = 64
KVH = 8
HD = 128
MASKED = -1e30
LOG2E = 1.4426950408889634
SCALE2 = HD ** (-0.5) * LOG2E
TINY = 2.0 ** -90
BF = jnp.bfloat16
F32 = jnp.float32
VMEM = pl.BlockSpec(memory_space=pltpu.VMEM)
SMEM = pl.BlockSpec(memory_space=pltpu.SMEM)
ANY = pl.BlockSpec(memory_space=pl.ANY)
HBM = pl.BlockSpec(memory_space=pltpu.HBM)


def params(mib=20):
    return pltpu.CompilerParams(vmem_limit_bytes=mib * 2**20)


def dot_t(a, b):
    return lax.dot_general(a, b, (((1,), (1,)), ((), ())), preferred_element_type=F32)


def dot(a, b):
    return lax.dot_general(a, b, (((1,), (0,)), ((), ())), preferred_element_type=F32)


def spread(value, axis, source):
    kept = jnp.where(lax.axis_index(axis) == source, value, 0).astype(value.dtype)
    return lax.psum(kept, axis)


def swap(value, axis, size, even, odd):
    return lax.ppermute(value, axis, [(i, i ^ (odd if i & 1 else even)) for i in range(size)])


def pick_kernel(group_size, local_heads, kv_ref, k_ref, v_ref, sems):
    first = lax.axis_index("tp") * local_heads // group_size * HD
    cols = pl.ds(pl.multiple_of(first, HD), k_ref.shape[1])
    moves = [
        pltpu.make_async_copy(kv_ref.at[1, :, cols], v_ref, sems.at[1]),
        pltpu.make_async_copy(kv_ref.at[0, :, cols], k_ref, sems.at[0]),
    ]
    for move in moves:
        move.start()
    for move in moves:
        move.wait()


def pick(ctx_kv, kv_local, local_heads):
    return pl.pallas_call(
        functools.partial(pick_kernel, H // KVH, local_heads),
        out_shape=[jax.ShapeDtypeStruct((ctx_kv.shape[1], kv_local * HD), BF)] * 2,
        in_specs=[HBM],
        out_specs=[VMEM] * 2,
        scratch_shapes=[pltpu.SemaphoreType.DMA((2,))],
        compiler_params=params(52),
        name="pick_columns",
    )(ctx_kv)


def bit(value, at):
    return (value >> at) & 1


def small_call(kernel, name, shapes, inputs, after=()):
    return pl.pallas_call(
        kernel,
        out_shape=[jax.ShapeDtypeStruct(x, BF) for x in shapes],
        in_specs=[VMEM] * len(inputs) + [ANY] * len(after),
        out_specs=[VMEM] * len(shapes),
        compiler_params=params(),
        name=name,
    )(*inputs, *after)


def choose(condition, one, two):
    pl.when(condition)(one)
    pl.when(jnp.logical_not(condition))(two)


def take_rows(target, source, rows, cols=slice(None)):
    def run():
        target[:rows, :] = source[:rows, cols]

    return run


def join(low_of, known, landed, after=()):
    rows, width = known.shape

    def kernel(known_ref, landed_ref, *rest):
        out_ref = rest[-1]

        def put(first, second):
            def run():
                both = jnp.concatenate([first[...].astype(F32), second[...].astype(F32)], 0)
                out_ref[...] = both.astype(BF)

            return run

        choose(low_of(lax.axis_index("hst")), put(known_ref, landed_ref), put(landed_ref, known_ref))

    return small_call(kernel, "query_join", [(2 * rows, width)], (known, landed), after)[0]


def relay(keep_of, one, two, after=(), split=1):
    slab, columns = one.shape
    width = columns // split

    def kernel(one_ref, two_ref, *rest):
        keep = keep_of(lax.axis_index("hst"))
        for j, out_ref in enumerate(rest[-split:]):
            cols = slice(j * width, (j + 1) * width)
            choose(keep, take_rows(out_ref, one_ref, slab, cols), take_rows(out_ref, two_ref, slab, cols))

    return small_call(kernel, "anchor_relay", [(slab, width)] * split, (one, two), after)


def add_part(one, two, after=()):
    def kernel(one_ref, two_ref, *rest):
        rest[-1][...] = (one_ref[...].astype(F32) + two_ref[...].astype(F32)).astype(BF)

    return small_call(kernel, "query_sum", [one.shape], (one, two), after)[0]


def fill_values(vaug, values):
    for j in range(values.shape[1] // HD):
        vaug[:, 2 * j * HD : (2 * j + 1) * HD] = values[:, j * HD : (j + 1) * HD]
        vaug[:, (2 * j + 1) * HD : (2 * j + 2) * HD] = jnp.ones((values.shape[0], HD), BF)


def lanes(index, width):
    return pl.ds(pl.multiple_of(index * width, width), width)


def row_tile(slab):
    return 256 if slab % 256 == 0 else slab


def body_size(count, most):
    return max(x for x in range(1, most + 1) if count % x == 0)


def own_kernel(first, count, per_kv, q_ref, k_ref, v_ref, *rest):
    state_ref, vaug = rest[-2], rest[-1]
    slab = q_ref.shape[0]
    tile = row_tile(slab)
    half = tile // 2
    heads = body_size(count, 4)
    fill_values(vaug, v_ref)
    rows = lax.broadcasted_iota(jnp.int32, (half, half), 0)
    cols = lax.broadcasted_iota(jnp.int32, (half, half), 1)
    causal = cols <= rows
    chunks = slab // tile
    units = [(h, j) for h in range(heads) for j in range(chunks)]

    def body(i, carry):
        kv = lax.div(first + i * heads, per_kv)

        def scores(at):
            h, j = units[at]
            query = q_ref[j * tile :, lanes(first + i * heads + h, HD)]
            return dot_t(query, k_ref[j * tile : (j + 1) * tile, lanes(kv, HD)])

        def power(x):
            return jnp.exp2(x * SCALE2).astype(BF)

        def corner(x):
            return jnp.where(causal, jnp.exp2(x * SCALE2), 0.0).astype(BF)

        current = scores(0)
        totals = [None] * chunks
        for at, (h, j) in enumerate(units):
            following = scores(at + 1) if at + 1 < len(units) else None
            top = jnp.concatenate([corner(current[:half, :half]), jnp.zeros((half, half), BF)], 1)
            low = jnp.concatenate([power(current[half:tile, :half]), corner(current[half:tile, half:])], 1)
            expo = [top, low] if j == chunks - 1 else [top, low, power(current[tile:])]
            part = dot(jnp.concatenate(expo, 0), vaug[j * tile : (j + 1) * tile, lanes(kv, 2 * HD)])
            for r in range(j, chunks):
                piece = part[(r - j) * tile : (r - j + 1) * tile]
                totals[r] = piece if j == 0 else totals[r] + piece
            state_ref[j * tile : (j + 1) * tile, lanes(i * heads + h, 2 * HD)] = totals[j]
            current = following
        return carry

    lax.fori_loop(0, count // heads, body, 0)


def own_part(ctx_q, own_k, own_v, first, count, per_kv, after=()):
    slab = ctx_q.shape[0]
    work = count * slab * (slab + row_tile(slab)) // 2
    return pl.pallas_call(
        functools.partial(own_kernel, first, count, per_kv),
        out_shape=jax.ShapeDtypeStruct((slab, count * 2 * HD), F32),
        in_specs=[VMEM] * 3 + [ANY] * len(after),
        out_specs=VMEM,
        scratch_shapes=[pltpu.VMEM((slab, 2 * own_v.shape[1]), BF)],
        compiler_params=params(),
        cost_estimate=pl.CostEstimate(
            flops=work * HD * 8, bytes_accessed=count * slab * HD * 6, transcendentals=work
        ),
        name="context_own",
    )(ctx_q, own_k, own_v, *after)


def anchor_kernel(first, count, base, per_kv, last, befores, *refs):
    lengths_ref, q_ref, state_ref, k_ref, v_ref, even_ref, odd_ref = refs[:7]
    earlier = refs[7 : 7 + len(befores)]
    if last:
        full_ref, out_ref, keys, vaug, sems = refs[-5:]
    else:
        out_ref, keys, vaug = refs[-3:]
    slab = q_ref.shape[0]
    heads = body_size(count, 2 if last else 4)
    kv = first // per_kv
    host = lax.axis_index("hst")
    own_len = lengths_ref[host]

    def hand_over(source, start, width, sem):
        target = full_ref.at[:, pl.ds(start * HD, width * HD)]
        return pltpu.make_async_copy(source, target, sems.at[sem])

    moves = [hand_over(earlier[n], *place, n) for n, place in enumerate(befores)]
    for move in moves:
        move.start()

    @pl.when(host % 2 == 0)
    def _():
        keys[...] = even_ref[...]
        fill_values(vaug, odd_ref)

    @pl.when(host % 2 == 1)
    def _():
        keys[...] = odd_ref[...]
        fill_values(vaug, even_ref)

    def part(start):
        def query_of(h):
            at = (first + start + h) * HD
            return q_ref[:, at : at + HD]

        def scores(h):
            return dot_t(query_of(h), keys[...])

        def state_of(h):
            at = (first - base + start + h) * 2 * HD
            return state_ref[:, at : at + 2 * HD]

        def finish(h, total, worst):
            sums = total[:, HD:]
            inverse = pl.reciprocal(sums, approx=True)
            out_ref[:, (start + h) * HD : (start + h + 1) * HD] = (total[:, :HD] * inverse).astype(BF)
            return jnp.minimum(worst, jnp.minimum(sums, inverse))

        def check(worst):
            @pl.when(jnp.logical_not(jnp.min(worst) > TINY))
            def _():
                exact_block(first + start, start, heads, host, own_len, kv, q_ref, k_ref, v_ref, keys, vaug, out_ref)

        @pl.when(host == 0)
        def _():
            worst = jnp.ones((slab, HD), F32)
            for h in range(heads):
                worst = finish(h, state_of(h), worst)
            check(worst)

        @pl.when(host > 0)
        def _():
            worst = jnp.ones((slab, HD), F32)
            current = scores(0)
            for h in range(heads):
                following = scores(h + 1) if h + 1 < heads else None
                expo = jnp.exp2(current * SCALE2).astype(BF)
                total = dot(expo, vaug[...]) + state_of(h)
                worst = finish(h, total, worst)
                current = following
            check(worst)

        @pl.when(own_len < slab)
        def _():
            row_ids = lax.broadcasted_iota(jnp.int32, (slab, HD), 0)
            for h in range(start, start + heads):
                cols = slice(h * HD, (h + 1) * HD)
                kept = jnp.where(row_ids < own_len, out_ref[:, cols].astype(F32), 0.0)
                out_ref[:, cols] = kept.astype(BF)

        if last:
            source = out_ref.at[:, start * HD : (start + heads) * HD]
            move = hand_over(source, first + start, heads, len(befores) + start // heads)
            move.start()
            moves.append(move)

    for start in range(0, count, heads):
        part(start)
    for move in moves:
        move.wait()


def exact_block(q_head, out_head, heads, host, own_len, kv, q_ref, k_ref, v_ref, keys, vaug, out_ref):
    slab = q_ref.shape[0]
    tile = 128

    def body(i, carry):
        h = lax.div(i, slab // tile)
        r = lax.rem(i, slab // tile)
        at = pl.ds(pl.multiple_of(r * tile, tile), tile)
        query = q_ref[at, lanes(q_head + h, HD)]
        row_ids = lax.broadcasted_iota(jnp.int32, (tile, slab), 0) + r * tile
        key_ids = lax.broadcasted_iota(jnp.int32, (tile, slab), 1)
        own = dot_t(query, k_ref[:, kv * HD : (kv + 1) * HD]) * SCALE2
        own = jnp.where((key_ids <= row_ids) & (key_ids < own_len), own, MASKED)
        far = dot_t(query, keys[...]) * SCALE2
        far = jnp.where(host > 0, far, MASKED)
        peak = jnp.maximum(jnp.max(own, 1, keepdims=True), jnp.max(far, 1, keepdims=True))
        own = jnp.exp2(own - peak)
        far = jnp.where(host > 0, jnp.exp2(far - peak), 0.0)
        sums = jnp.sum(own, 1, keepdims=True) + jnp.sum(far, 1, keepdims=True)
        values = jnp.where(host > 0, vaug[:, :HD].astype(F32), 0.0).astype(BF)
        total = dot(own.astype(BF), v_ref[:, kv * HD : (kv + 1) * HD]) + dot(far.astype(BF), values)
        live = row_ids[:, :1] < own_len
        out_ref[at, lanes(out_head + h, HD)] = jnp.where(live, total / sums, 0.0).astype(BF)
        return carry

    lax.fori_loop(0, heads * (slab // tile), body, 0)


def anchor_part(lengths, ctx_q, state, base, own_k, own_v, anchor, first, count, per_kv, befores=None, after=()):
    slab, width = ctx_q.shape
    work = count * slab * slab
    last = befores is not None
    earlier = list(befores.values()) if last else []
    places = tuple((at, x.shape[1] // HD) for at, x in befores.items()) if last else ()
    results = jax.ShapeDtypeStruct((slab, count * HD), BF)
    scratch = [pltpu.VMEM((slab, HD), BF), pltpu.VMEM((slab, 2 * HD), BF)]
    if last:
        scratch = [pltpu.VMEM(results.shape, BF)] + scratch
        scratch += [pltpu.SemaphoreType.DMA((len(earlier) + count,))]
        results = jax.ShapeDtypeStruct((slab, width), BF)
    return pl.pallas_call(
        functools.partial(anchor_kernel, first, count, base, per_kv, last, places),
        out_shape=results,
        in_specs=[SMEM] + [VMEM] * (6 + len(earlier)) + [ANY] * len(after),
        out_specs=ANY if last else VMEM,
        scratch_shapes=scratch,
        compiler_params=params(),
        cost_estimate=pl.CostEstimate(
            flops=work * HD * 8, bytes_accessed=count * slab * HD * 8, transcendentals=work
        ),
        name="context_anchor",
    )(lengths, ctx_q, state, own_k, own_v, *anchor, *earlier, *after)


PART = 16


def write_level(ref, width, level):
    lane = lax.broadcasted_iota(jnp.int32, level.shape, 1)
    parts = []
    for at in range(3):
        part = level.astype(BF).astype(F32)
        parts.append(part if at == 0 else pltpu.roll(part, at * PART, 1))
        level = level - part
    packed = jnp.where(lane < PART, parts[0], jnp.where(lane < 2 * PART, parts[1], parts[2]))
    ref[:, width : width + HD] = packed.astype(BF)


def read_level(ref, width):
    packed = ref[:, width : width + HD].astype(F32)
    return packed + pltpu.roll(packed, HD - PART, 1) + pltpu.roll(packed, HD - 2 * PART, 1)


def source_kernel(per_kv, q_rows, group_size, lengths_ref, k_ref, v_ref, self_ref, known_ref, landed_ref, *rest):
    keep_ref, send_ref, q_all, vaug = rest[-4:]
    slab, columns = k_ref.shape
    width = per_kv * columns
    query_count = 8 * q_rows
    block = 2 * q_rows
    host = lax.axis_index("hst")
    own_len = lengths_ref[host]
    rows = per_kv * query_count
    odd = bit(host, 0) == 1
    low = jnp.where(odd, bit(host, 1), bit(host, 2)) == 0

    def place(lower, upper, spread_out):
        middle = (2, 1) if spread_out else (1, 2)
        for ref, chips in ((lower, (0, middle[0])), (upper, (middle[1], 3))):
            for n, chip in enumerate(chips):
                for h in range(width // HD):
                    to = h * query_count + chip * block
                    q_all[to : to + block, :] = ref[n * block : (n + 1) * block, h * HD : (h + 1) * HD]

    for is_low, is_odd in ((False, False), (False, True), (True, False), (True, True)):
        @pl.when((low == is_low) & (odd == is_odd))
        def _():
            pair = (known_ref, landed_ref) if is_low else (landed_ref, known_ref)
            place(*pair, is_odd)

    first = lax.axis_index("tp") * (width // HD) // group_size * HD
    own_cols = pl.ds(pl.multiple_of(first, HD), columns)
    selves_kv = [self_ref[i, :, own_cols].astype(F32) for i in range(2)]
    lane = lax.broadcasted_iota(jnp.int32, (query_count, HD), 1)
    query_ids = lax.broadcasted_iota(jnp.int32, (query_count, HD), 0)
    self_ok = (host * q_rows + lane <= query_ids) & (lane < q_rows)
    self_ok = jnp.concatenate([self_ok] * per_kv, 0)
    pad = jnp.zeros((HD - q_rows, HD), F32)
    key_rows = lax.broadcasted_iota(jnp.int32, (slab, HD), 0)
    ones = jnp.where(key_rows < own_len, 1.0, 0.0).astype(BF)
    for j in range(columns // HD):
        values = v_ref[:, j * HD : (j + 1) * HD].astype(F32)
        vaug[:, 2 * j * HD : (2 * j + 1) * HD] = jnp.where(key_rows < own_len, values, 0.0).astype(BF)
        vaug[:, (2 * j + 1) * HD : (2 * j + 2) * HD] = ones

    def operands(j):
        cols = slice(j * HD, (j + 1) * HD)
        queries = q_all[j * rows : (j + 1) * rows, :]
        self_keys = jnp.concatenate([selves_kv[0][:, cols], pad], 0).astype(BF)
        self_values = jnp.concatenate([selves_kv[1][:, cols], pad], 0).astype(BF)
        near = dot_t(queries, k_ref[:, cols]) * SCALE2
        selves = jnp.where(self_ok, dot_t(queries, self_keys) * SCALE2, MASKED)
        return near, selves, jnp.concatenate([self_values, jnp.ones((HD, HD), BF)], 1)

    def store(j, total, level):
        stats = jnp.zeros((query_count, HD), F32)
        for h in range(per_kv):
            stats = jnp.where(lane == h, level[h * query_count : (h + 1) * query_count, :], stats)

        def put(out_ref):
            def run():
                for h in range(per_kv):
                    part = total[h * query_count : (h + 1) * query_count, :]
                    out_ref[:, h * HD : (h + 1) * HD] = part.astype(BF)
                write_level(out_ref, per_kv * HD, stats)

            return run

        choose(odd if j else jnp.logical_not(odd), put(keep_ref), put(send_ref))

    worst = jnp.ones((rows, HD), F32)
    found = []
    for j in range(columns // HD):
        near, selves, self_values = operands(j)
        near = jnp.exp2(near).astype(BF)
        selves = jnp.exp2(selves).astype(BF)
        total = dot(near, vaug[:, 2 * j * HD : (2 * j + 2) * HD]) + dot(selves, self_values)
        sums = total[:, HD:]
        inverse = 1.0 / sums
        worst = jnp.minimum(worst, jnp.minimum(sums, inverse))
        found.append((total[:, :HD] * inverse, jnp.log2(sums)))
    for j, result in enumerate(found):
        store(j, *result)

    @pl.when(jnp.logical_not(jnp.min(worst) > TINY))
    def _():
        key_ids = lax.broadcasted_iota(jnp.int32, (rows, slab), 1)
        for j in range(columns // HD):
            near, selves, self_values = operands(j)
            near = jnp.where(key_ids < own_len, near, MASKED)
            peak = jnp.maximum(jnp.max(near, 1, keepdims=True), jnp.max(selves, 1, keepdims=True))
            near = jnp.exp2(near - peak).astype(BF)
            selves = jnp.exp2(selves - peak).astype(BF)
            total = dot(near, vaug[:, 2 * j * HD : (2 * j + 2) * HD]) + dot(selves, self_values)
            sums = total[:, HD:]
            store(j, total[:, :HD] / sums, peak + jnp.log2(sums))


def source_part(lengths, own_k, own_v, query_kv, known, landed, q_rows, per_kv, after=()):
    slab, columns = own_k.shape
    width = per_kv * columns
    count = 8 * q_rows
    work = count * (width // HD) * slab
    return pl.pallas_call(
        functools.partial(source_kernel, per_kv, q_rows, H // KVH),
        out_shape=[jax.ShapeDtypeStruct((count, (per_kv + 1) * HD), BF)] * 2,
        in_specs=[SMEM] + [VMEM] * 5 + [ANY] * len(after),
        out_specs=[VMEM] * 2,
        scratch_shapes=[pltpu.VMEM((count * width // HD, HD), BF), pltpu.VMEM((slab, 2 * columns), BF)],
        compiler_params=params(),
        cost_estimate=pl.CostEstimate(flops=work * HD * 8, bytes_accessed=2**21, transcendentals=work),
        name="query_source",
    )(lengths, own_k, own_v, query_kv, known, landed, *after)


def merged(refs, width):
    levels = [read_level(ref, width) for ref in refs]
    peak = jnp.maximum(*levels)
    weights = [jnp.exp2(x - peak) for x in levels]
    whole = weights[0] + weights[1]
    return [w / whole for w in weights], peak + jnp.log2(whole)


def blend(shares, refs, h):
    cols = slice(h * HD, (h + 1) * HD)
    return sum(w[:, h : h + 1] * ref[:, cols].astype(F32) for w, ref in zip(shares, refs))


def merge_part(one, two, last, after=()):
    rows, wide = one.shape
    width = wide - HD

    def kernel(one_ref, two_ref, *rest):
        out_ref = rest[-1]
        shares, level = merged((one_ref, two_ref), width)
        if not last:
            write_level(out_ref, width, level)
        for h in range(width // HD):
            out_ref[:, h * HD : (h + 1) * HD] = blend(shares, (one_ref, two_ref), h).astype(BF)

    return small_call(kernel, "query_merge", [(rows, width if last else wide)], (one, two), after)[0]


def project_part(own, other, out_weight, after=()):
    rows, half = own.shape
    depth, columns = out_weight.shape

    def kernel(w_ref, own_ref, other_ref, *rest):
        out_ref, attended = rest[-2:]

        def put(first, second):
            def run():
                attended[:, :half] = first[...]
                attended[:, half:] = second[...]

            return run

        even = bit(lax.axis_index("hst"), 0) == 0
        choose(even, put(own_ref, other_ref), put(other_ref, own_ref))
        out_ref[...] = dot(attended[...], w_ref[...]).astype(BF)

    return pl.pallas_call(
        kernel,
        out_shape=jax.ShapeDtypeStruct((rows, columns), BF),
        in_specs=[VMEM] * 3 + [ANY] * len(after),
        out_specs=VMEM,
        scratch_shapes=[pltpu.VMEM((rows, depth), BF)],
        compiler_params=params(),
        cost_estimate=pl.CostEstimate(
            flops=2 * rows * depth * columns, bytes_accessed=2 * depth * columns, transcendentals=0
        ),
        name="query_project",
    )(out_weight, own, other, *after)


def general_queries(lengths, own_k, own_v, self_kv, query_q, out_weight, per_kv):
    own_kv = jnp.stack([own_k, own_v], 0)
    host_id = lax.axis_index("hst")
    local_heads = query_q.shape[1] // HD
    kv_local = own_kv.shape[2] // HD
    slab_rows = own_kv.shape[1]
    own_len = lengths[host_id]
    row_ids = jnp.arange(slab_rows)
    all_queries = lax.all_gather(query_q, "hst", axis=0, tiled=True)
    query_count = all_queries.shape[0]
    q_rows = query_q.shape[0]
    source = jnp.concatenate([own_kv, self_kv], 1)
    source = source.reshape(2, slab_rows + q_rows, kv_local, HD).transpose(0, 2, 1, 3)
    query_ids = jnp.arange(query_count)
    context_ok = jnp.broadcast_to(row_ids[None, :] < own_len, (query_count, slab_rows))
    self_ok = (host_id * q_rows + jnp.arange(q_rows))[None, :] <= query_ids[:, None]
    seen_ok = jnp.concatenate([context_ok, self_ok], 1)
    query_heads = all_queries.reshape(query_count, local_heads, HD).transpose(1, 0, 2)

    def score_head(operands):
        query_rows, head_index = operands
        kv_index = head_index // per_kv
        scores = dot_t(query_rows, source[0, kv_index]) * HD ** (-0.5)
        scores = jnp.where(seen_ok, scores, MASKED)
        peak = jnp.max(scores, axis=1)
        expo = jnp.exp(scores - peak[:, None])
        return peak, jnp.sum(expo, axis=1), dot(expo.astype(BF), source[1, kv_index])

    maxima, totals, outputs = lax.map(score_head, (query_heads, jnp.arange(local_heads)))
    factor = jnp.exp(maxima - lax.pmax(maxima, "hst"))
    denominator, summed = lax.psum((totals * factor, outputs * factor[..., None]), "hst")
    attended = (summed / denominator[..., None]).astype(BF)
    attended = attended.transpose(1, 0, 2).reshape(query_count, local_heads * HD)
    return lax.psum(dot(attended, out_weight), "tp").astype(BF)


def per_device(hosts, groups, ctx_q, ctx_kv, lengths, query_q, query_kv, out_weight):
    slab = ctx_q.shape[0]
    local_heads = ctx_q.shape[1] // HD
    group_size = H // KVH
    kv_local = max(1, local_heads // group_size)
    per_kv = min(local_heads, group_size)
    q_rows = query_q.shape[0]
    host = lax.axis_index("hst")
    fast = hosts == 8 and groups & (groups - 1) == 0
    fast = fast and q_rows == 8 and local_heads == 16 and per_kv == 8

    if not fast:
        kv_first = lax.axis_index("tp") * local_heads // group_size
        self_kv = lax.dynamic_slice_in_dim(query_kv, kv_first * HD, kv_local * HD, 2)
        own_k, own_v = pick(ctx_kv, kv_local, local_heads)
        query_out = general_queries(lengths, own_k, own_v, self_kv, query_q, out_weight, per_kv)
        k, v = spread(jnp.stack([own_k, own_v]), "hst", 0)
        anchor = jnp.where(host % 2 == 0, k, v), jnp.where(host % 2 == 0, v, k)
        state = own_part(ctx_q, own_k, own_v, 0, local_heads, per_kv)
        results = {}
        for first in range(0, local_heads, per_kv):
            cols = slice(first // per_kv * HD, (first // per_kv + 1) * HD)
            last = first + per_kv == local_heads
            results[first] = anchor_part(
                lengths, ctx_q, state, 0, own_k, own_v, [x[:, cols] for x in anchor],
                first, per_kv, per_kv, dict(results) if last else None,
            )
        return results[first], query_out

    states = {}

    def own(first, count, after=()):
        states[first] = own_part(ctx_q, own_k, own_v, first, count, per_kv, after)
        return states[first]

    along = ((2, 4), (4, 2))

    def is_even(h):
        return bit(h, 0) == 0

    def source_first(h):
        return h < 2

    def done_early(h):
        return (h <= 2) | (h == 5)

    def near_low(h):
        return jnp.where(bit(h, 0) == 1, bit(h, 2), bit(h, 1)) == 0

    landed = swap(query_q, "hst", hosts, 1, 1)
    own_k, own_v = pick(ctx_kv, kv_local, local_heads)
    value_landed = swap(own_v, "hst", hosts, 1, 1)
    queries = join(is_even, query_q, landed, (own_v,))
    landed = swap(queries, "hst", hosts, *along[0])
    done = own(0, 2, (queries,))
    (held,) = relay(is_even, own_k, value_landed, (done,))
    held_landed = swap(held, "hst", hosts, *along[0])
    queries = join(near_low, queries, landed, (held,))
    landed = swap(queries, "hst", hosts, *along[1])
    done = own(2, 6, (queries,))
    keep, send = source_part(lengths, own_k, own_v, query_kv, queries, landed, q_rows, per_kv, (done,))
    landed = swap(send, "hst", hosts, 1, 1)
    done = own(8, 4, (keep,))
    parts = relay(source_first, held, held_landed, (done,), kv_local)
    parts_landed = [swap(x, "hst", hosts, *along[1]) for x in parts]
    source = merge_part(keep, landed, False, (parts[-1],))
    landed = swap(source, "hst", hosts, *along[0])
    done = own(12, 4, (source,))
    anchor = {}

    def complete(kv, after):
        (held,) = relay(done_early, parts[kv], parts_landed[kv], after)
        anchor[kv] = held, swap(held, "hst", hosts, 1, 1)
        return held

    source = merge_part(source, landed, False, (done,))
    landed = swap(source, "hst", hosts, *along[1])
    done = complete(0, (source,))
    results = {}

    def anchors(first, count, after, last=False):
        base = max(x for x in states if x <= first)
        results[first] = anchor_part(
            lengths, ctx_q, states[base], base, own_k, own_v, anchor[first // per_kv],
            first, count, per_kv, dict(results) if last else None, after,
        )
        return results[first]

    done = anchors(0, 2, (done,))
    done = anchors(2, 2, (done,))
    source = merge_part(source, landed, True, (done,))
    landed = swap(source, "hst", hosts, 1, 1)
    done = complete(1, (source,))
    done = anchors(4, 2, (done,))
    terms = project_part(source, landed, out_weight, (done,))
    shares = [[(12, 4, True)], [(6, 2, False), (8, 4, False)]]
    step = 1
    while step < groups:
        landed = swap(terms, "tp", groups, step, step)
        last = False
        done = terms
        for first, count, last in shares.pop() if shares else ():
            done = anchors(first, count, (terms, done), last)
        terms = add_part(terms, landed, () if last else (done,))
        step *= 2
    for group in reversed(shares):
        for first, count, last in group:
            done = anchors(first, count, (), last)
    return done, terms


def solution(mesh):
    hosts, groups = mesh.shape["hst"], mesh.shape["tp"]
    return jax.shard_map(
        functools.partial(per_device, hosts, groups),
        mesh=mesh,
        in_specs=(
            P("hst", "tp"),
            P(None, "hst", None),
            P(),
            P("hst", "tp"),
            P(None, "hst", None),
            P("tp", "hst"),
        ),
        out_specs=(P("hst", "tp"), P(None, "hst")),
        check_vma=False,
    )
```

```python
import functools

import jax
import jax.numpy as jnp
from jax import lax
from jax.experimental import pallas as pl
from jax.experimental.pallas import tpu as pltpu
from jax.sharding import PartitionSpec as P

H = 64
KVH = 8
HD = 128
MASKED = -1e30
LOG2E = 1.4426950408889634
SCALE2 = HD ** (-0.5) * LOG2E
TINY = 2.0 ** -90
BF = jnp.bfloat16
F32 = jnp.float32
VMEM = pl.BlockSpec(memory_space=pltpu.VMEM)
SMEM = pl.BlockSpec(memory_space=pltpu.SMEM)
ANY = pl.BlockSpec(memory_space=pl.ANY)
HBM = pl.BlockSpec(memory_space=pltpu.HBM)


def params(mib=20):
    return pltpu.CompilerParams(vmem_limit_bytes=mib * 2**20)


def dot_t(a, b):
    return lax.dot_general(a, b, (((1,), (1,)), ((), ())), preferred_element_type=F32)


def dot(a, b):
    return lax.dot_general(a, b, (((1,), (0,)), ((), ())), preferred_element_type=F32)


def spread(value, axis, source):
    kept = jnp.where(lax.axis_index(axis) == source, value, 0).astype(value.dtype)
    return lax.psum(kept, axis)


def swap(value, axis, size, even, odd):
    return lax.ppermute(value, axis, [(i, i ^ (odd if i & 1 else even)) for i in range(size)])


def pick_kernel(group_size, local_heads, kv_ref, k_ref, v_ref, sems):
    first = lax.axis_index("tp") * local_heads // group_size * HD
    cols = pl.ds(pl.multiple_of(first, HD), k_ref.shape[1])
    moves = [
        pltpu.make_async_copy(kv_ref.at[1, :, cols], v_ref, sems.at[1]),
        pltpu.make_async_copy(kv_ref.at[0, :, cols], k_ref, sems.at[0]),
    ]
    for move in moves:
        move.start()
    for move in moves:
        move.wait()


def pick(ctx_kv, kv_local, local_heads):
    return pl.pallas_call(
        functools.partial(pick_kernel, H // KVH, local_heads),
        out_shape=[jax.ShapeDtypeStruct((ctx_kv.shape[1], kv_local * HD), BF)] * 2,
        in_specs=[HBM],
        out_specs=[VMEM] * 2,
        scratch_shapes=[pltpu.SemaphoreType.DMA((2,))],
        compiler_params=params(52),
        cost_estimate=pl.CostEstimate(flops=0, bytes_accessed=2**22, transcendentals=0),
        name="pick_columns",
    )(ctx_kv)


def bit(value, at):
    return (value >> at) & 1


def small_call(kernel, name, shapes, inputs, after=()):
    return pl.pallas_call(
        kernel,
        out_shape=[jax.ShapeDtypeStruct(x, BF) for x in shapes],
        in_specs=[VMEM] * len(inputs) + [ANY] * len(after),
        out_specs=[VMEM] * len(shapes),
        compiler_params=params(),
        cost_estimate=pl.CostEstimate(flops=0, bytes_accessed=2**20, transcendentals=0),
        name=name,
    )(*inputs, *after)


def choose(condition, one, two):
    pl.when(condition)(one)
    pl.when(jnp.logical_not(condition))(two)


def take_rows(target, source, rows, cols=slice(None)):
    def run():
        target[:rows, :] = source[:rows, cols]

    return run


def join(low_of, known, landed, after=()):
    rows, width = known.shape

    def kernel(known_ref, landed_ref, *rest):
        out_ref = rest[-1]

        def put(first, second):
            def run():
                both = jnp.concatenate([first[...].astype(F32), second[...].astype(F32)], 0)
                out_ref[...] = both.astype(BF)

            return run

        choose(low_of(lax.axis_index("hst")), put(known_ref, landed_ref), put(landed_ref, known_ref))

    return small_call(kernel, "query_join", [(2 * rows, width)], (known, landed), after)[0]


def relay(keep_of, one, two, after=(), split=1):
    slab, columns = one.shape
    width = columns // split

    def kernel(one_ref, two_ref, *rest):
        keep = keep_of(lax.axis_index("hst"))
        for j, out_ref in enumerate(rest[-split:]):
            cols = slice(j * width, (j + 1) * width)
            choose(keep, take_rows(out_ref, one_ref, slab, cols), take_rows(out_ref, two_ref, slab, cols))

    return small_call(kernel, "anchor_relay", [(slab, width)] * split, (one, two), after)


def add_part(one, two, after=()):
    def kernel(one_ref, two_ref, *rest):
        rest[-1][...] = (one_ref[...].astype(F32) + two_ref[...].astype(F32)).astype(BF)

    return small_call(kernel, "query_sum", [one.shape], (one, two), after)[0]


def prepare(first, second, swapped, after=()):
    slab, columns = first.shape

    def kernel(first_ref, second_ref, *rest):
        keys_ref, values_ref = rest[-2:]

        def fill(k_ref, v_ref):
            def run():
                for j in range(columns // HD):
                    cols = slice(j * HD, (j + 1) * HD)
                    at = 2 * j * HD
                    scaled = k_ref[:, cols].astype(F32) * SCALE2
                    high = scaled.astype(BF)
                    keys_ref[:, at : at + HD] = high
                    keys_ref[:, at + HD : at + 2 * HD] = (scaled - high.astype(F32)).astype(BF)
                    values_ref[:, at : at + HD] = v_ref[:, cols]
                    values_ref[:, at + HD : at + 2 * HD] = jnp.ones((slab, HD), BF)

            return run

        if swapped:
            even = bit(lax.axis_index("hst"), 0) == 0
            choose(even, fill(first_ref, second_ref), fill(second_ref, first_ref))
        else:
            fill(first_ref, second_ref)()

    shapes = [(slab, 2 * columns)] * 2
    return small_call(kernel, "operands", shapes, (first, second), after)


def twice(query):
    return jnp.concatenate([query, query], 1)


def lanes(index, width):
    return pl.ds(pl.multiple_of(index * width, width), width)


def row_tile(slab):
    return 256 if slab % 256 == 0 else slab


def body_size(count, most):
    return max(x for x in range(1, most + 1) if count % x == 0)


def own_kernel(first, count, per_kv, q_ref, k_ref, v_ref, *rest):
    state_ref = rest[-1]
    slab = q_ref.shape[0]
    tile = row_tile(slab)
    half = tile // 2
    heads = body_size(count, 4)
    rows = lax.broadcasted_iota(jnp.int32, (half, half), 0)
    cols = lax.broadcasted_iota(jnp.int32, (half, half), 1)
    causal = cols <= rows
    chunks = slab // tile
    units = [(h, j) for h in range(heads) for j in range(chunks)]

    def body(i, carry):
        kv = lax.div(first + i * heads, per_kv)

        def scores(at):
            h, j = units[at]
            query = q_ref[j * tile :, lanes(first + i * heads + h, HD)]
            return dot_t(twice(query), k_ref[j * tile : (j + 1) * tile, lanes(kv, 2 * HD)])

        def power(x):
            return jnp.exp2(x).astype(BF)

        def corner(x):
            return jnp.where(causal, jnp.exp2(x), 0.0).astype(BF)

        current = scores(0)
        totals = [None] * chunks
        for at, (h, j) in enumerate(units):
            following = scores(at + 1) if at + 1 < len(units) else None
            top = jnp.concatenate([corner(current[:half, :half]), jnp.zeros((half, half), BF)], 1)
            low = jnp.concatenate([power(current[half:tile, :half]), corner(current[half:tile, half:])], 1)
            expo = [top, low] if j == chunks - 1 else [top, low, power(current[tile:])]
            part = dot(jnp.concatenate(expo, 0), v_ref[j * tile : (j + 1) * tile, lanes(kv, 2 * HD)])
            for r in range(j, chunks):
                piece = part[(r - j) * tile : (r - j + 1) * tile]
                totals[r] = piece if j == 0 else totals[r] + piece
            state_ref[j * tile : (j + 1) * tile, lanes(i * heads + h, 2 * HD)] = totals[j]
            current = following
        return carry

    lax.fori_loop(0, count // heads, body, 0)


def own_part(ctx_q, own_k, own_v, first, count, per_kv, after=()):
    slab = ctx_q.shape[0]
    work = count * slab * (slab + row_tile(slab)) // 2
    return pl.pallas_call(
        functools.partial(own_kernel, first, count, per_kv),
        out_shape=jax.ShapeDtypeStruct((slab, count * 2 * HD), F32),
        in_specs=[VMEM] * 3 + [ANY] * len(after),
        out_specs=VMEM,
        compiler_params=params(),
        cost_estimate=pl.CostEstimate(
            flops=work * HD * 8, bytes_accessed=count * slab * HD * 6, transcendentals=work
        ),
        name="context_own",
    )(ctx_q, own_k, own_v, *after)


def anchor_kernel(first, count, base, per_kv, last, befores, *refs):
    lengths_ref, q_ref, state_ref, k_ref, v_ref, keys, vaug = refs[:7]
    earlier = refs[7 : 7 + len(befores)]
    if last:
        full_ref, out_ref, sems = refs[-3:]
    else:
        out_ref = refs[-1]
    slab = q_ref.shape[0]
    heads = body_size(count, 2 if last else 4)
    kv = first // per_kv
    host = lax.axis_index("hst")
    own_len = lengths_ref[host]

    def hand_over(source, start, width, sem):
        target = full_ref.at[:, pl.ds(start * HD, width * HD)]
        return pltpu.make_async_copy(source, target, sems.at[sem])

    moves = [hand_over(earlier[n], *place, n) for n, place in enumerate(befores)]
    for move in moves:
        move.start()

    def part(start):
        def query_of(h):
            at = (first + start + h) * HD
            return q_ref[:, at : at + HD]

        def scores(h):
            return dot_t(twice(query_of(h)), keys[...])

        def state_of(h):
            at = (first - base + start + h) * 2 * HD
            return state_ref[:, at : at + 2 * HD]

        def finish(h, total, worst):
            sums = total[:, HD:]
            inverse = pl.reciprocal(sums, approx=True)
            out_ref[:, (start + h) * HD : (start + h + 1) * HD] = (total[:, :HD] * inverse).astype(BF)
            return jnp.minimum(worst, jnp.minimum(sums, inverse))

        def check(worst):
            @pl.when(jnp.logical_not(jnp.min(worst) > TINY))
            def _():
                exact_block(first + start, start, heads, host, own_len, kv, q_ref, k_ref, v_ref, keys, vaug, out_ref)

        @pl.when(host == 0)
        def _():
            worst = jnp.ones((slab, HD), F32)
            for h in range(heads):
                worst = finish(h, state_of(h), worst)
            check(worst)

        @pl.when(host > 0)
        def _():
            worst = jnp.ones((slab, HD), F32)
            current = scores(0)
            for h in range(heads):
                following = scores(h + 1) if h + 1 < heads else None
                expo = jnp.exp2(current).astype(BF)
                total = dot(expo, vaug[...]) + state_of(h)
                worst = finish(h, total, worst)
                current = following
            check(worst)

        @pl.when(own_len < slab)
        def _():
            row_ids = lax.broadcasted_iota(jnp.int32, (slab, HD), 0)
            for h in range(start, start + heads):
                cols = slice(h * HD, (h + 1) * HD)
                kept = jnp.where(row_ids < own_len, out_ref[:, cols].astype(F32), 0.0)
                out_ref[:, cols] = kept.astype(BF)

        if last:
            source = out_ref.at[:, start * HD : (start + heads) * HD]
            move = hand_over(source, first + start, heads, len(befores) + start // heads)
            move.start()
            moves.append(move)

    for start in range(0, count, heads):
        part(start)
    for move in moves:
        move.wait()


def exact_block(q_head, out_head, heads, host, own_len, kv, q_ref, k_ref, v_ref, keys, vaug, out_ref):
    slab = q_ref.shape[0]
    tile = 128

    def body(i, carry):
        h = lax.div(i, slab // tile)
        r = lax.rem(i, slab // tile)
        at = pl.ds(pl.multiple_of(r * tile, tile), tile)
        query = q_ref[at, lanes(q_head + h, HD)]
        row_ids = lax.broadcasted_iota(jnp.int32, (tile, slab), 0) + r * tile
        key_ids = lax.broadcasted_iota(jnp.int32, (tile, slab), 1)
        own = dot_t(twice(query), k_ref[:, 2 * kv * HD : 2 * (kv + 1) * HD])
        own = jnp.where((key_ids <= row_ids) & (key_ids < own_len), own, MASKED)
        far = dot_t(twice(query), keys[...])
        far = jnp.where(host > 0, far, MASKED)
        peak = jnp.maximum(jnp.max(own, 1, keepdims=True), jnp.max(far, 1, keepdims=True))
        own = jnp.exp2(own - peak)
        far = jnp.where(host > 0, jnp.exp2(far - peak), 0.0)
        sums = jnp.sum(own, 1, keepdims=True) + jnp.sum(far, 1, keepdims=True)
        values = jnp.where(host > 0, vaug[:, :HD].astype(F32), 0.0).astype(BF)
        total = dot(own.astype(BF), v_ref[:, 2 * kv * HD : (2 * kv + 1) * HD]) + dot(far.astype(BF), values)
        live = row_ids[:, :1] < own_len
        out_ref[at, lanes(out_head + h, HD)] = jnp.where(live, total / sums, 0.0).astype(BF)
        return carry

    lax.fori_loop(0, heads * (slab // tile), body, 0)


def anchor_part(lengths, ctx_q, state, base, own_k, own_v, anchor, first, count, per_kv, befores=None, after=()):
    slab, width = ctx_q.shape
    work = count * slab * slab
    last = befores is not None
    earlier = list(befores.values()) if last else []
    places = tuple((at, x.shape[1] // HD) for at, x in befores.items()) if last else ()
    results = jax.ShapeDtypeStruct((slab, count * HD), BF)
    scratch = []
    if last:
        scratch = [pltpu.VMEM(results.shape, BF), pltpu.SemaphoreType.DMA((len(earlier) + count,))]
        results = jax.ShapeDtypeStruct((slab, width), BF)
    return pl.pallas_call(
        functools.partial(anchor_kernel, first, count, base, per_kv, last, places),
        out_shape=results,
        in_specs=[SMEM] + [VMEM] * (6 + len(earlier)) + [ANY] * len(after),
        out_specs=ANY if last else VMEM,
        scratch_shapes=scratch,
        compiler_params=params(),
        cost_estimate=pl.CostEstimate(
            flops=work * HD * 8, bytes_accessed=count * slab * HD * 8, transcendentals=work
        ),
        name="context_anchor",
    )(lengths, ctx_q, state, own_k, own_v, *anchor, *earlier, *after)


PART = 16


def write_level(ref, width, level):
    lane = lax.broadcasted_iota(jnp.int32, level.shape, 1)
    parts = []
    for at in range(3):
        part = level.astype(BF).astype(F32)
        parts.append(part if at == 0 else pltpu.roll(part, at * PART, 1))
        level = level - part
    packed = jnp.where(lane < PART, parts[0], jnp.where(lane < 2 * PART, parts[1], parts[2]))
    ref[:, width : width + HD] = packed.astype(BF)


def read_level(ref, width):
    packed = ref[:, width : width + HD].astype(F32)
    return packed + pltpu.roll(packed, HD - PART, 1) + pltpu.roll(packed, HD - 2 * PART, 1)


def source_kernel(per_kv, q_rows, group_size, lengths_ref, k_ref, v_ref, self_ref, known_ref, landed_ref, *rest):
    keep_ref, send_ref, q_all, vaug = rest[-4:]
    slab, columns = v_ref.shape
    width = per_kv * columns
    query_count = 8 * q_rows
    block = 2 * q_rows
    host = lax.axis_index("hst")
    own_len = lengths_ref[host]
    rows = per_kv * query_count
    odd = bit(host, 0) == 1
    low = jnp.where(odd, bit(host, 1), bit(host, 2)) == 0

    def place(lower, upper, spread_out):
        middle = (2, 1) if spread_out else (1, 2)
        for ref, chips in ((lower, (0, middle[0])), (upper, (middle[1], 3))):
            for n, chip in enumerate(chips):
                for h in range(width // HD):
                    to = h * query_count + chip * block
                    q_all[to : to + block, :] = ref[n * block : (n + 1) * block, h * HD : (h + 1) * HD]

    for is_low, is_odd in ((False, False), (False, True), (True, False), (True, True)):
        @pl.when((low == is_low) & (odd == is_odd))
        def _():
            pair = (known_ref, landed_ref) if is_low else (landed_ref, known_ref)
            place(*pair, is_odd)

    first = lax.axis_index("tp") * (width // HD) // group_size * HD
    own_cols = pl.ds(pl.multiple_of(first, HD), columns)
    selves_kv = [self_ref[i, :, own_cols].astype(F32) for i in range(2)]
    lane = lax.broadcasted_iota(jnp.int32, (query_count, HD), 1)
    query_ids = lax.broadcasted_iota(jnp.int32, (query_count, HD), 0)
    self_ok = (host * q_rows + lane <= query_ids) & (lane < q_rows)
    self_ok = jnp.concatenate([self_ok] * per_kv, 0)
    pad = jnp.zeros((HD - q_rows, HD), F32)
    key_rows = lax.broadcasted_iota(jnp.int32, (slab, HD), 0)
    ones = jnp.where(key_rows < own_len, 1.0, 0.0).astype(BF)
    for j in range(columns // HD):
        values = v_ref[:, j * HD : (j + 1) * HD].astype(F32)
        vaug[:, 2 * j * HD : (2 * j + 1) * HD] = jnp.where(key_rows < own_len, values, 0.0).astype(BF)
        vaug[:, (2 * j + 1) * HD : (2 * j + 2) * HD] = ones

    def operands(j):
        cols = slice(j * HD, (j + 1) * HD)
        queries = q_all[j * rows : (j + 1) * rows, :]
        self_keys = jnp.concatenate([selves_kv[0][:, cols], pad], 0).astype(BF)
        self_values = jnp.concatenate([selves_kv[1][:, cols], pad], 0).astype(BF)
        near = dot_t(twice(queries), k_ref[:, 2 * j * HD : 2 * (j + 1) * HD])
        selves = jnp.where(self_ok, dot_t(queries, self_keys) * SCALE2, MASKED)
        return near, selves, jnp.concatenate([self_values, jnp.ones((HD, HD), BF)], 1)

    def store(j, total, level):
        stats = jnp.zeros((query_count, HD), F32)
        for h in range(per_kv):
            stats = jnp.where(lane == h, level[h * query_count : (h + 1) * query_count, :], stats)

        def put(out_ref):
            def run():
                for h in range(per_kv):
                    part = total[h * query_count : (h + 1) * query_count, :]
                    out_ref[:, h * HD : (h + 1) * HD] = part.astype(BF)
                write_level(out_ref, per_kv * HD, stats)

            return run

        choose(odd if j else jnp.logical_not(odd), put(keep_ref), put(send_ref))

    worst = jnp.ones((rows, HD), F32)
    found = []
    for j in range(columns // HD):
        near, selves, self_values = operands(j)
        near = jnp.exp2(near).astype(BF)
        selves = jnp.exp2(selves).astype(BF)
        total = dot(near, vaug[:, 2 * j * HD : (2 * j + 2) * HD]) + dot(selves, self_values)
        sums = total[:, HD:]
        inverse = 1.0 / sums
        worst = jnp.minimum(worst, jnp.minimum(sums, inverse))
        found.append((total[:, :HD] * inverse, jnp.log2(sums)))
    for j, result in enumerate(found):
        store(j, *result)

    @pl.when(jnp.logical_not(jnp.min(worst) > TINY))
    def _():
        key_ids = lax.broadcasted_iota(jnp.int32, (rows, slab), 1)
        for j in range(columns // HD):
            near, selves, self_values = operands(j)
            near = jnp.where(key_ids < own_len, near, MASKED)
            peak = jnp.maximum(jnp.max(near, 1, keepdims=True), jnp.max(selves, 1, keepdims=True))
            near = jnp.exp2(near - peak).astype(BF)
            selves = jnp.exp2(selves - peak).astype(BF)
            total = dot(near, vaug[:, 2 * j * HD : (2 * j + 2) * HD]) + dot(selves, self_values)
            sums = total[:, HD:]
            store(j, total[:, :HD] / sums, peak + jnp.log2(sums))


def source_part(lengths, own_k, own_v, query_kv, known, landed, q_rows, per_kv, after=()):
    slab, columns = own_v.shape
    width = per_kv * columns
    count = 8 * q_rows
    work = count * (width // HD) * slab
    return pl.pallas_call(
        functools.partial(source_kernel, per_kv, q_rows, H // KVH),
        out_shape=[jax.ShapeDtypeStruct((count, (per_kv + 1) * HD), BF)] * 2,
        in_specs=[SMEM] + [VMEM] * 5 + [ANY] * len(after),
        out_specs=[VMEM] * 2,
        scratch_shapes=[pltpu.VMEM((count * width // HD, HD), BF), pltpu.VMEM((slab, 2 * columns), BF)],
        compiler_params=params(),
        cost_estimate=pl.CostEstimate(flops=work * HD * 8, bytes_accessed=2**21, transcendentals=work),
        name="query_source",
    )(lengths, own_k, own_v, query_kv, known, landed, *after)


def merged(refs, width):
    levels = [read_level(ref, width) for ref in refs]
    peak = jnp.maximum(*levels)
    weights = [jnp.exp2(x - peak) for x in levels]
    whole = weights[0] + weights[1]
    return [w / whole for w in weights], peak + jnp.log2(whole)


def blend(shares, refs, h):
    cols = slice(h * HD, (h + 1) * HD)
    return sum(w[:, h : h + 1] * ref[:, cols].astype(F32) for w, ref in zip(shares, refs))


def merge_part(one, two, last, after=()):
    rows, wide = one.shape
    width = wide - HD

    def kernel(one_ref, two_ref, *rest):
        out_ref = rest[-1]
        shares, level = merged((one_ref, two_ref), width)
        if not last:
            write_level(out_ref, width, level)
        for h in range(width // HD):
            out_ref[:, h * HD : (h + 1) * HD] = blend(shares, (one_ref, two_ref), h).astype(BF)

    return small_call(kernel, "query_merge", [(rows, width if last else wide)], (one, two), after)[0]


def project_part(own, other, out_weight, after=()):
    rows, half = own.shape
    depth, columns = out_weight.shape

    def kernel(w_ref, own_ref, other_ref, *rest):
        out_ref, attended = rest[-2:]

        def put(first, second):
            def run():
                attended[:, :half] = first[...]
                attended[:, half:] = second[...]

            return run

        even = bit(lax.axis_index("hst"), 0) == 0
        choose(even, put(own_ref, other_ref), put(other_ref, own_ref))
        out_ref[...] = dot(attended[...], w_ref[...]).astype(BF)

    return pl.pallas_call(
        kernel,
        out_shape=jax.ShapeDtypeStruct((rows, columns), BF),
        in_specs=[VMEM] * 3 + [ANY] * len(after),
        out_specs=VMEM,
        scratch_shapes=[pltpu.VMEM((rows, depth), BF)],
        compiler_params=params(),
        cost_estimate=pl.CostEstimate(
            flops=2 * rows * depth * columns, bytes_accessed=2 * depth * columns, transcendentals=0
        ),
        name="query_project",
    )(out_weight, own, other, *after)


def general_queries(lengths, own_k, own_v, self_kv, query_q, out_weight, per_kv):
    own_kv = jnp.stack([own_k, own_v], 0)
    host_id = lax.axis_index("hst")
    local_heads = query_q.shape[1] // HD
    kv_local = own_kv.shape[2] // HD
    slab_rows = own_kv.shape[1]
    own_len = lengths[host_id]
    row_ids = jnp.arange(slab_rows)
    all_queries = lax.all_gather(query_q, "hst", axis=0, tiled=True)
    query_count = all_queries.shape[0]
    q_rows = query_q.shape[0]
    source = jnp.concatenate([own_kv, self_kv], 1)
    source = source.reshape(2, slab_rows + q_rows, kv_local, HD).transpose(0, 2, 1, 3)
    query_ids = jnp.arange(query_count)
    context_ok = jnp.broadcast_to(row_ids[None, :] < own_len, (query_count, slab_rows))
    self_ok = (host_id * q_rows + jnp.arange(q_rows))[None, :] <= query_ids[:, None]
    seen_ok = jnp.concatenate([context_ok, self_ok], 1)
    query_heads = all_queries.reshape(query_count, local_heads, HD).transpose(1, 0, 2)

    def score_head(operands):
        query_rows, head_index = operands
        kv_index = head_index // per_kv
        scores = dot_t(query_rows, source[0, kv_index]) * HD ** (-0.5)
        scores = jnp.where(seen_ok, scores, MASKED)
        peak = jnp.max(scores, axis=1)
        expo = jnp.exp(scores - peak[:, None])
        return peak, jnp.sum(expo, axis=1), dot(expo.astype(BF), source[1, kv_index])

    maxima, totals, outputs = lax.map(score_head, (query_heads, jnp.arange(local_heads)))
    factor = jnp.exp(maxima - lax.pmax(maxima, "hst"))
    denominator, summed = lax.psum((totals * factor, outputs * factor[..., None]), "hst")
    attended = (summed / denominator[..., None]).astype(BF)
    attended = attended.transpose(1, 0, 2).reshape(query_count, local_heads * HD)
    return lax.psum(dot(attended, out_weight), "tp").astype(BF)


def per_device(hosts, groups, ctx_q, ctx_kv, lengths, query_q, query_kv, out_weight):
    slab = ctx_q.shape[0]
    local_heads = ctx_q.shape[1] // HD
    group_size = H // KVH
    kv_local = max(1, local_heads // group_size)
    per_kv = min(local_heads, group_size)
    q_rows = query_q.shape[0]
    host = lax.axis_index("hst")
    fast = hosts == 8 and groups & (groups - 1) == 0
    fast = fast and q_rows == 8 and local_heads == 16 and per_kv == 8

    if not fast:
        kv_first = lax.axis_index("tp") * local_heads // group_size
        self_kv = lax.dynamic_slice_in_dim(query_kv, kv_first * HD, kv_local * HD, 2)
        own_k, own_v = pick(ctx_kv, kv_local, local_heads)
        query_out = general_queries(lengths, own_k, own_v, self_kv, query_q, out_weight, per_kv)
        k, v = spread(jnp.stack([own_k, own_v]), "hst", 0)
        own_k, own_v = prepare(own_k, own_v, False)
        anchor = prepare(k, v, False)
        state = own_part(ctx_q, own_k, own_v, 0, local_heads, per_kv)
        results = {}
        for first in range(0, local_heads, per_kv):
            cols = slice(2 * first // per_kv * HD, 2 * (first // per_kv + 1) * HD)
            last = first + per_kv == local_heads
            results[first] = anchor_part(
                lengths, ctx_q, state, 0, own_k, own_v, [x[:, cols] for x in anchor],
                first, per_kv, per_kv, dict(results) if last else None,
            )
        return results[first], query_out

    states = {}

    def own(first, count, after=()):
        states[first] = own_part(ctx_q, own_keys, own_values, first, count, per_kv, after)
        return states[first]

    along = ((2, 4), (4, 2))

    def is_even(h):
        return bit(h, 0) == 0

    def source_first(h):
        return h < 2

    def done_early(h):
        return (h <= 2) | (h == 5)

    def near_low(h):
        return jnp.where(bit(h, 0) == 1, bit(h, 2), bit(h, 1)) == 0

    landed = swap(query_q, "hst", hosts, 1, 1)
    own_k, own_v = pick(ctx_kv, kv_local, local_heads)
    value_landed = swap(own_v, "hst", hosts, 1, 1)
    own_keys, own_values = prepare(own_k, own_v, False)
    queries = join(is_even, query_q, landed, (own_keys,))
    landed = swap(queries, "hst", hosts, *along[0])
    done = own(0, 2, (queries,))
    parts = list(relay(is_even, own_k, value_landed, (done,), kv_local))
    parts_landed = [swap(x, "hst", hosts, *along[0]) for x in parts]
    queries = join(near_low, queries, landed, (parts[0],))
    landed = swap(queries, "hst", hosts, *along[1])
    done = own(2, 6, (queries,))
    anchor = {}

    def pass_on(kv, after):
        (parts[kv],) = relay(source_first, parts[kv], parts_landed[kv], after)
        parts_landed[kv] = swap(parts[kv], "hst", hosts, *along[1])
        return parts[kv]

    def complete(kv, after):
        (held,) = relay(done_early, parts[kv], parts_landed[kv], after)
        anchor[kv] = held, swap(held, "hst", hosts, 1, 1)
        return held

    done = pass_on(0, (done,))
    keep, send = source_part(lengths, own_keys, own_v, query_kv, queries, landed, q_rows, per_kv, (done,))
    landed = swap(send, "hst", hosts, 1, 1)
    done = own(8, 4, (keep,))
    source = merge_part(keep, landed, False, (done,))
    landed = swap(source, "hst", hosts, *along[0])
    done = complete(0, (source,))
    done = own(12, 4, (done,))
    source = merge_part(source, landed, False, (done,))
    landed = swap(source, "hst", hosts, *along[1])
    done = pass_on(1, (source,))
    anchor[0] = prepare(*anchor[0], True, (done,))
    results = {}

    def anchors(first, count, after, last=False):
        base = max(x for x in states if x <= first)
        results[first] = anchor_part(
            lengths, ctx_q, states[base], base, own_keys, own_values, anchor[first // per_kv],
            first, count, per_kv, dict(results) if last else None, after,
        )
        return results[first]

    done = anchors(0, 2, ())
    done = anchors(2, 2, (done,))
    source = merge_part(source, landed, True, (done,))
    landed = swap(source, "hst", hosts, 1, 1)
    done = complete(1, (source,))
    done = anchors(4, 2, (done,))
    terms = project_part(source, landed, out_weight, (done,))
    anchor[1] = prepare(*anchor[1], True, (terms,))
    shares = [[(12, 4, True)], [(6, 2, False), (8, 4, False)]]
    step = 1
    while step < groups:
        landed = swap(terms, "tp", groups, step, step)
        last = False
        done = terms
        for first, count, last in shares.pop() if shares else ():
            done = anchors(first, count, (terms, done), last)
        terms = add_part(terms, landed, () if last else (done,))
        step *= 2
    for group in reversed(shares):
        for first, count, last in group:
            done = anchors(first, count, (), last)
    return done, terms


def solution(mesh):
    hosts, groups = mesh.shape["hst"], mesh.shape["tp"]
    return jax.shard_map(
        functools.partial(per_device, hosts, groups),
        mesh=mesh,
        in_specs=(
            P("hst", "tp"),
            P(None, "hst", None),
            P(),
            P("hst", "tp"),
            P(None, "hst", None),
            P("tp", "hst"),
        ),
        out_specs=(P("hst", "tp"), P(None, "hst")),
        check_vma=False,
    )
```

```python
import functools

import jax
import jax.numpy as jnp
from jax import lax
from jax.experimental import pallas as pl
from jax.experimental.pallas import tpu as pltpu
from jax.sharding import PartitionSpec as P

H = 64
KVH = 8
HD = 128
MASKED = -1e30
LOG2E = 1.4426950408889634
SCALE2 = HD ** (-0.5) * LOG2E
TINY = 2.0 ** -90
BF = jnp.bfloat16
F32 = jnp.float32
VMEM = pl.BlockSpec(memory_space=pltpu.VMEM)
SMEM = pl.BlockSpec(memory_space=pltpu.SMEM)
ANY = pl.BlockSpec(memory_space=pl.ANY)
HBM = pl.BlockSpec(memory_space=pltpu.HBM)


def params(mib=32):
    return pltpu.CompilerParams(vmem_limit_bytes=mib * 2**20)


def dot_t(a, b):
    return lax.dot_general(a, b, (((1,), (1,)), ((), ())), preferred_element_type=F32)


def dot(a, b):
    return lax.dot_general(a, b, (((1,), (0,)), ((), ())), preferred_element_type=F32)


def spread(value, axis, source):
    kept = jnp.where(lax.axis_index(axis) == source, value, 0).astype(value.dtype)
    return lax.psum(kept, axis)


def swap(value, axis, size, even, odd):
    return lax.ppermute(value, axis, [(i, i ^ (odd if i & 1 else even)) for i in range(size)])


def pick_kernel(group_size, local_heads, kv_ref, k_ref, v_ref, sems):
    first = lax.axis_index("tp") * local_heads // group_size * HD
    cols = pl.ds(pl.multiple_of(first, HD), k_ref.shape[1])
    moves = [
        pltpu.make_async_copy(kv_ref.at[1, :, cols], v_ref, sems.at[1]),
        pltpu.make_async_copy(kv_ref.at[0, :, cols], k_ref, sems.at[0]),
    ]
    for move in moves:
        move.start()
    for move in moves:
        move.wait()


def pick(ctx_kv, kv_local, local_heads):
    return pl.pallas_call(
        functools.partial(pick_kernel, H // KVH, local_heads),
        out_shape=[jax.ShapeDtypeStruct((ctx_kv.shape[1], kv_local * HD), BF)] * 2,
        in_specs=[HBM],
        out_specs=[VMEM] * 2,
        scratch_shapes=[pltpu.SemaphoreType.DMA((2,))],
        compiler_params=params(52),
        cost_estimate=pl.CostEstimate(flops=0, bytes_accessed=2**22, transcendentals=0),
        name="pick_columns",
    )(ctx_kv)


def bit(value, at):
    return (value >> at) & 1


def small_call(kernel, name, shapes, inputs, after=()):
    return pl.pallas_call(
        kernel,
        out_shape=[jax.ShapeDtypeStruct(x, BF) for x in shapes],
        in_specs=[VMEM] * len(inputs) + [ANY] * len(after),
        out_specs=[VMEM] * len(shapes),
        compiler_params=params(),
        cost_estimate=pl.CostEstimate(flops=0, bytes_accessed=2**20, transcendentals=0),
        name=name,
    )(*inputs, *after)


def choose(condition, one, two):
    pl.when(condition)(one)
    pl.when(jnp.logical_not(condition))(two)


def take_rows(target, source, rows, cols=slice(None)):
    def run():
        target[:rows, :] = source[:rows, cols]

    return run


def by_chip(own, others, bits, after=()):
    rows, width = own.shape

    def kernel(*refs):
        out_ref, all_ref = refs[-2:]
        host = lax.axis_index("hst")
        for ref, flip in zip(refs, (0,) + tuple(bits)):
            start = pl.multiple_of((jnp.bitwise_xor(host, flip) >> 1) * rows, rows)
            all_ref[pl.ds(start, rows), :] = ref[...].astype(F32)
        out_ref[...] = all_ref[...].astype(BF)

    total = rows * (1 + len(bits))
    return pl.pallas_call(
        kernel,
        out_shape=jax.ShapeDtypeStruct((total, width), BF),
        in_specs=[VMEM] * (1 + len(bits)) + [ANY] * len(after),
        out_specs=VMEM,
        scratch_shapes=[pltpu.VMEM((total, width), F32)],
        compiler_params=params(),
        cost_estimate=pl.CostEstimate(flops=0, bytes_accessed=2**20, transcendentals=0),
        name="query_chips",
    )(own, *others, *after)


def relay(keep_of, one, two, after=(), split=1):
    slab, columns = one.shape
    width = columns // split

    def kernel(one_ref, two_ref, *rest):
        keep = keep_of(lax.axis_index("hst"))
        for j, out_ref in enumerate(rest[-split:]):
            cols = slice(j * width, (j + 1) * width)
            choose(keep, take_rows(out_ref, one_ref, slab, cols), take_rows(out_ref, two_ref, slab, cols))

    return small_call(kernel, "anchor_relay", [(slab, width)] * split, (one, two), after)


def add_part(one, two, after=()):
    def kernel(one_ref, two_ref, *rest):
        rest[-1][...] = (one_ref[...].astype(F32) + two_ref[...].astype(F32)).astype(BF)

    return small_call(kernel, "query_sum", [one.shape], (one, two), after)[0]


def prepare(first, second, swapped, after=()):
    slab, columns = first.shape

    def kernel(first_ref, second_ref, *rest):
        keys_ref, values_ref = rest[-2:]

        def fill(k_ref, v_ref):
            def run():
                for j in range(columns // HD):
                    cols = slice(j * HD, (j + 1) * HD)
                    at = 2 * j * HD
                    scaled = k_ref[:, cols].astype(F32) * SCALE2
                    high = scaled.astype(BF)
                    keys_ref[:, at : at + HD] = high
                    keys_ref[:, at + HD : at + 2 * HD] = (scaled - high.astype(F32)).astype(BF)
                    values_ref[:, at : at + HD] = v_ref[:, cols]
                    values_ref[:, at + HD : at + 2 * HD] = jnp.ones((slab, HD), BF)

            return run

        if swapped:
            even = bit(lax.axis_index("hst"), 0) == 0
            choose(even, fill(first_ref, second_ref), fill(second_ref, first_ref))
        else:
            fill(first_ref, second_ref)()

    shapes = [(slab, 2 * columns)] * 2
    return small_call(kernel, "operands", shapes, (first, second), after)


def twice(query):
    return jnp.concatenate([query, query], 1)


def lanes(index, width):
    return pl.ds(pl.multiple_of(index * width, width), width)


def row_tile(slab):
    return 256 if slab % 256 == 0 else slab


def body_size(first, count, per_kv, most):
    def fits(size):
        bodies = range(first, first + count, size)
        return count % size == 0 and all(x // per_kv == (x + size - 1) // per_kv for x in bodies)

    return max(x for x in range(1, most + 1) if fits(x))


def own_kernel(first, count, per_kv, q_ref, k_ref, v_ref, *rest):
    state_ref = rest[-1]
    slab = q_ref.shape[0]
    tile = row_tile(slab)
    half = tile // 2
    heads = body_size(first, count, per_kv, 4)
    rows = lax.broadcasted_iota(jnp.int32, (half, half), 0)
    cols = lax.broadcasted_iota(jnp.int32, (half, half), 1)
    causal = cols <= rows
    chunks = slab // tile
    group = 2 if heads % 2 == 0 else 1
    units = [(g, j) for g in range(0, heads, group) for j in range(chunks)]

    def body(i, carry):
        kv = lax.div(first + i * heads, per_kv)

        def scores(at):
            g, j = units[at]
            queries = [q_ref[j * tile :, lanes(first + i * heads + g + h, HD)] for h in range(group)]
            keys = k_ref[j * tile : (j + 1) * tile, lanes(kv, 2 * HD)]
            return dot_t(twice(jnp.concatenate(queries, 0)), keys)

        def power(x):
            return jnp.exp2(x).astype(BF)

        def corner(x):
            return jnp.where(causal, jnp.exp2(x), 0.0).astype(BF)

        current = scores(0)
        totals = [[None] * chunks for _ in range(group)]
        for at, (g, j) in enumerate(units):
            following = scores(at + 1) if at + 1 < len(units) else None
            rows_each = slab - j * tile
            expo = []
            for h in range(group):
                mine = current[h * rows_each : (h + 1) * rows_each]
                expo.append(jnp.concatenate([corner(mine[:half, :half]), jnp.zeros((half, half), BF)], 1))
                expo.append(jnp.concatenate([power(mine[half:tile, :half]), corner(mine[half:tile, half:])], 1))
                if rows_each > tile:
                    expo.append(power(mine[tile:]))
            part = dot(jnp.concatenate(expo, 0), v_ref[j * tile : (j + 1) * tile, lanes(kv, 2 * HD)])
            for h in range(group):
                for r in range(j, chunks):
                    start = h * rows_each + (r - j) * tile
                    piece = part[start : start + tile]
                    totals[h][r] = piece if j == 0 else totals[h][r] + piece
                cols = lanes(i * heads + g + h, 2 * HD)
                state_ref[j * tile : (j + 1) * tile, cols] = totals[h][j]
            current = following
        return carry

    lax.fori_loop(0, count // heads, body, 0)


def own_part(ctx_q, own_k, own_v, first, count, per_kv, after=()):
    slab = ctx_q.shape[0]
    work = count * slab * (slab + row_tile(slab)) // 2
    return pl.pallas_call(
        functools.partial(own_kernel, first, count, per_kv),
        out_shape=jax.ShapeDtypeStruct((slab, count * 2 * HD), F32),
        in_specs=[VMEM] * 3 + [ANY] * len(after),
        out_specs=VMEM,
        compiler_params=params(),
        cost_estimate=pl.CostEstimate(
            flops=work * HD * 8, bytes_accessed=count * slab * HD * 6, transcendentals=work
        ),
        name="context_own",
    )(ctx_q, own_k, own_v, *after)


def anchor_kernel(first, count, bases, per_kv, last, befores, *refs):
    lengths_ref, q_ref, k_ref, v_ref, keys, vaug = refs[:6]
    state_refs = refs[6 : 6 + len(bases)]
    earlier = refs[6 + len(bases) : 6 + len(bases) + len(befores)]
    if last:
        full_ref, out_ref, sems = refs[-3:]
    else:
        out_ref = refs[-1]
    slab = q_ref.shape[0]
    heads = body_size(first, count, per_kv, 2 if last else 4)
    group = 2 if heads % 2 == 0 else 1
    tile = row_tile(slab)
    chunks = slab // tile
    units = [(g, j) for g in range(0, heads, group) for j in range(chunks)]
    kv = first // per_kv
    host = lax.axis_index("hst")
    own_len = lengths_ref[host]

    def hand_over(source, start, width, sem):
        target = full_ref.at[:, pl.ds(start * HD, width * HD)]
        return pltpu.make_async_copy(source, target, sems.at[sem])

    moves = [hand_over(earlier[n], *place, n) for n, place in enumerate(befores)]
    for move in moves:
        move.start()

    def part(start):
        def query_of(h):
            at = (first + start + h) * HD
            return q_ref[:, at : at + HD]

        def scores(g, j):
            queries = jnp.concatenate([query_of(g + h) for h in range(group)], 0)
            return dot_t(twice(queries), keys[j * tile : (j + 1) * tile, :])

        def state_of(h):
            head = first + start + h
            n = max(n for n, base in enumerate(bases) if base <= head)
            at = (head - bases[n]) * 2 * HD
            return state_refs[n][:, at : at + 2 * HD]

        def finish(h, total, worst):
            sums = total[:, HD:]
            inverse = pl.reciprocal(sums, approx=True)
            out_ref[:, (start + h) * HD : (start + h + 1) * HD] = (total[:, :HD] * inverse).astype(BF)
            return jnp.minimum(worst, jnp.minimum(sums, inverse))

        def check(worst):
            @pl.when(jnp.logical_not(jnp.min(worst) > TINY))
            def _():
                exact_block(first + start, start, heads, host, own_len, kv, q_ref, k_ref, v_ref, keys, vaug, out_ref)

        @pl.when(host == 0)
        def _():
            worst = jnp.ones((slab, HD), F32)
            for h in range(heads):
                worst = finish(h, state_of(h), worst)
            check(worst)

        @pl.when(host > 0)
        def _():
            worst = jnp.ones((slab, HD), F32)
            current = scores(*units[0])
            for at, (g, j) in enumerate(units):
                following = scores(*units[at + 1]) if at + 1 < len(units) else None
                if j == 0:
                    totals = [state_of(g + h) for h in range(group)]
                part = dot(jnp.exp2(current).astype(BF), vaug[j * tile : (j + 1) * tile, :])
                totals = [x + part[h * slab : (h + 1) * slab] for h, x in enumerate(totals)]
                if j == chunks - 1:
                    for h in range(group):
                        worst = finish(g + h, totals[h], worst)
                current = following
            check(worst)

        @pl.when(own_len < slab)
        def _():
            row_ids = lax.broadcasted_iota(jnp.int32, (slab, HD), 0)
            for h in range(start, start + heads):
                cols = slice(h * HD, (h + 1) * HD)
                kept = jnp.where(row_ids < own_len, out_ref[:, cols].astype(F32), 0.0)
                out_ref[:, cols] = kept.astype(BF)

        if last:
            source = out_ref.at[:, start * HD : (start + heads) * HD]
            move = hand_over(source, first + start, heads, len(befores) + start // heads)
            move.start()
            moves.append(move)

    for start in range(0, count, heads):
        part(start)
    for move in moves:
        move.wait()


def exact_block(q_head, out_head, heads, host, own_len, kv, q_ref, k_ref, v_ref, keys, vaug, out_ref):
    slab = q_ref.shape[0]
    tile = 128

    def body(i, carry):
        h = lax.div(i, slab // tile)
        r = lax.rem(i, slab // tile)
        at = pl.ds(pl.multiple_of(r * tile, tile), tile)
        query = q_ref[at, lanes(q_head + h, HD)]
        row_ids = lax.broadcasted_iota(jnp.int32, (tile, slab), 0) + r * tile
        key_ids = lax.broadcasted_iota(jnp.int32, (tile, slab), 1)
        own = dot_t(twice(query), k_ref[:, 2 * kv * HD : 2 * (kv + 1) * HD])
        own = jnp.where((key_ids <= row_ids) & (key_ids < own_len), own, MASKED)
        far = dot_t(twice(query), keys[...])
        far = jnp.where(host > 0, far, MASKED)
        peak = jnp.maximum(jnp.max(own, 1, keepdims=True), jnp.max(far, 1, keepdims=True))
        own = jnp.exp2(own - peak)
        far = jnp.where(host > 0, jnp.exp2(far - peak), 0.0)
        sums = jnp.sum(own, 1, keepdims=True) + jnp.sum(far, 1, keepdims=True)
        values = jnp.where(host > 0, vaug[:, :HD].astype(F32), 0.0).astype(BF)
        total = dot(own.astype(BF), v_ref[:, 2 * kv * HD : (2 * kv + 1) * HD]) + dot(far.astype(BF), values)
        live = row_ids[:, :1] < own_len
        out_ref[at, lanes(out_head + h, HD)] = jnp.where(live, total / sums, 0.0).astype(BF)
        return carry

    lax.fori_loop(0, heads * (slab // tile), body, 0)


def anchor_part(lengths, ctx_q, states, own_k, own_v, anchor, first, count, per_kv, befores=None, after=()):
    slab, width = ctx_q.shape
    work = count * slab * slab
    last = befores is not None
    ends = {x: x + y.shape[1] // (2 * HD) for x, y in states.items()}
    bases = tuple(x for x in sorted(states) if x < first + count and ends[x] > first)
    earlier = list(befores.values()) if last else []
    places = tuple((at, x.shape[1] // HD) for at, x in befores.items()) if last else ()
    results = jax.ShapeDtypeStruct((slab, count * HD), BF)
    scratch = []
    if last:
        scratch = [pltpu.VMEM(results.shape, BF), pltpu.SemaphoreType.DMA((len(earlier) + count,))]
        results = jax.ShapeDtypeStruct((slab, width), BF)
    return pl.pallas_call(
        functools.partial(anchor_kernel, first, count, bases, per_kv, last, places),
        out_shape=results,
        in_specs=[SMEM] + [VMEM] * (5 + len(bases) + len(earlier)) + [ANY] * len(after),
        out_specs=ANY if last else VMEM,
        scratch_shapes=scratch,
        compiler_params=params(),
        cost_estimate=pl.CostEstimate(
            flops=work * HD * 8, bytes_accessed=count * slab * HD * 8, transcendentals=work
        ),
        name="context_anchor",
    )(lengths, ctx_q, own_k, own_v, *anchor, *[states[x] for x in bases], *earlier, *after)


PART = 16


def write_level(ref, width, level):
    lane = lax.broadcasted_iota(jnp.int32, level.shape, 1)
    parts = []
    for at in range(3):
        part = level.astype(BF).astype(F32)
        parts.append(part if at == 0 else pltpu.roll(part, at * PART, 1))
        level = level - part
    packed = jnp.where(lane < PART, parts[0], jnp.where(lane < 2 * PART, parts[1], parts[2]))
    ref[:, width : width + HD] = packed.astype(BF)


def read_level(ref, width):
    packed = ref[:, width : width + HD].astype(F32)
    return packed + pltpu.roll(packed, HD - PART, 1) + pltpu.roll(packed, HD - 2 * PART, 1)


def source_kernel(per_kv, q_rows, group_size, lengths_ref, k_ref, v_ref, self_ref, known_ref, landed_ref, *rest):
    keep_ref, send_ref, q_all, vaug = rest[-4:]
    slab, columns = v_ref.shape
    width = per_kv * columns
    query_count = 8 * q_rows
    host = lax.axis_index("hst")
    own_len = lengths_ref[host]
    rows = per_kv * query_count
    odd = bit(host, 0) == 1

    def place(even_ref, odd_ref):
        def run():
            parts = []
            for chip in range(4):
                at = slice(chip * q_rows, (chip + 1) * q_rows)
                parts += [even_ref[at, :].astype(F32), odd_ref[at, :].astype(F32)]
            queries = jnp.concatenate(parts, 0).astype(BF)
            for h in range(width // HD):
                q_all[h * query_count : (h + 1) * query_count, :] = queries[:, h * HD : (h + 1) * HD]

        return run

    choose(odd, place(landed_ref, known_ref), place(known_ref, landed_ref))

    first = lax.axis_index("tp") * (width // HD) // group_size * HD
    own_cols = pl.ds(pl.multiple_of(first, HD), columns)
    selves_kv = [self_ref[i, :, own_cols].astype(F32) for i in range(2)]
    lane = lax.broadcasted_iota(jnp.int32, (query_count, HD), 1)
    query_ids = lax.broadcasted_iota(jnp.int32, (query_count, HD), 0)
    self_ok = (host * q_rows + lane <= query_ids) & (lane < q_rows)
    self_ok = jnp.concatenate([self_ok] * per_kv, 0)
    pad = jnp.zeros((HD - q_rows, HD), F32)
    key_rows = lax.broadcasted_iota(jnp.int32, (slab, HD), 0)
    ones = jnp.where(key_rows < own_len, 1.0, 0.0).astype(BF)
    for j in range(columns // HD):
        values = v_ref[:, j * HD : (j + 1) * HD].astype(F32)
        vaug[:, 2 * j * HD : (2 * j + 1) * HD] = jnp.where(key_rows < own_len, values, 0.0).astype(BF)
        vaug[:, (2 * j + 1) * HD : (2 * j + 2) * HD] = ones

    def operands(j):
        cols = slice(j * HD, (j + 1) * HD)
        queries = q_all[j * rows : (j + 1) * rows, :]
        self_keys = jnp.concatenate([selves_kv[0][:, cols], pad], 0).astype(BF)
        self_values = jnp.concatenate([selves_kv[1][:, cols], pad], 0).astype(BF)
        near = dot_t(twice(queries), k_ref[:, 2 * j * HD : 2 * (j + 1) * HD])
        selves = jnp.where(self_ok, dot_t(queries, self_keys) * SCALE2, MASKED)
        return near, selves, jnp.concatenate([self_values, jnp.ones((HD, HD), BF)], 1)

    def store(j, total, level):
        stats = jnp.zeros((query_count, HD), F32)
        for h in range(per_kv):
            stats = jnp.where(lane == h, level[h * query_count : (h + 1) * query_count, :], stats)

        def put(out_ref):
            def run():
                for h in range(per_kv):
                    part = total[h * query_count : (h + 1) * query_count, :]
                    out_ref[:, h * HD : (h + 1) * HD] = part.astype(BF)
                write_level(out_ref, per_kv * HD, stats)

            return run

        choose(odd if j else jnp.logical_not(odd), put(keep_ref), put(send_ref))

    worst = jnp.ones((rows, HD), F32)
    found = []
    for j in range(columns // HD):
        near, selves, self_values = operands(j)
        near = jnp.exp2(near).astype(BF)
        selves = jnp.exp2(selves).astype(BF)
        total = dot(near, vaug[:, 2 * j * HD : (2 * j + 2) * HD]) + dot(selves, self_values)
        sums = total[:, HD:]
        inverse = 1.0 / sums
        worst = jnp.minimum(worst, jnp.minimum(sums, inverse))
        found.append((total[:, :HD] * inverse, jnp.log2(sums)))
    for j, result in enumerate(found):
        store(j, *result)

    @pl.when(jnp.logical_not(jnp.min(worst) > TINY))
    def _():
        key_ids = lax.broadcasted_iota(jnp.int32, (rows, slab), 1)
        for j in range(columns // HD):
            near, selves, self_values = operands(j)
            near = jnp.where(key_ids < own_len, near, MASKED)
            peak = jnp.maximum(jnp.max(near, 1, keepdims=True), jnp.max(selves, 1, keepdims=True))
            near = jnp.exp2(near - peak).astype(BF)
            selves = jnp.exp2(selves - peak).astype(BF)
            total = dot(near, vaug[:, 2 * j * HD : (2 * j + 2) * HD]) + dot(selves, self_values)
            sums = total[:, HD:]
            store(j, total[:, :HD] / sums, peak + jnp.log2(sums))


def source_part(lengths, own_k, own_v, query_kv, known, landed, q_rows, per_kv, after=()):
    slab, columns = own_v.shape
    width = per_kv * columns
    count = 8 * q_rows
    work = count * (width // HD) * slab
    return pl.pallas_call(
        functools.partial(source_kernel, per_kv, q_rows, H // KVH),
        out_shape=[jax.ShapeDtypeStruct((count, (per_kv + 1) * HD), BF)] * 2,
        in_specs=[SMEM] + [VMEM] * 5 + [ANY] * len(after),
        out_specs=[VMEM] * 2,
        scratch_shapes=[pltpu.VMEM((count * width // HD, HD), BF), pltpu.VMEM((slab, 2 * columns), BF)],
        compiler_params=params(),
        cost_estimate=pl.CostEstimate(flops=work * HD * 8, bytes_accessed=2**21, transcendentals=work),
        name="query_source",
    )(lengths, own_k, own_v, query_kv, known, landed, *after)


def merged(refs, width):
    levels = [read_level(ref, width) for ref in refs]
    peak = jnp.maximum(*levels)
    weights = [jnp.exp2(x - peak) for x in levels]
    whole = weights[0] + weights[1]
    return [w / whole for w in weights], peak + jnp.log2(whole)


def blend(shares, refs, h):
    cols = slice(h * HD, (h + 1) * HD)
    return sum(w[:, h : h + 1] * ref[:, cols].astype(F32) for w, ref in zip(shares, refs))


def merge_part(one, two, last, after=()):
    rows, wide = one.shape
    width = wide - HD

    def kernel(one_ref, two_ref, *rest):
        out_ref = rest[-1]
        shares, level = merged((one_ref, two_ref), width)
        if not last:
            write_level(out_ref, width, level)
        for h in range(width // HD):
            out_ref[:, h * HD : (h + 1) * HD] = blend(shares, (one_ref, two_ref), h).astype(BF)

    return small_call(kernel, "query_merge", [(rows, width if last else wide)], (one, two), after)[0]


def project_part(own, other, out_weight, after=()):
    rows, half = own.shape
    depth, columns = out_weight.shape

    def kernel(w_ref, own_ref, other_ref, *rest):
        out_ref, attended = rest[-2:]

        def put(first, second):
            def run():
                attended[:, :half] = first[...]
                attended[:, half:] = second[...]

            return run

        even = bit(lax.axis_index("hst"), 0) == 0
        choose(even, put(own_ref, other_ref), put(other_ref, own_ref))
        out_ref[...] = dot(attended[...], w_ref[...]).astype(BF)

    return pl.pallas_call(
        kernel,
        out_shape=jax.ShapeDtypeStruct((rows, columns), BF),
        in_specs=[VMEM] * 3 + [ANY] * len(after),
        out_specs=VMEM,
        scratch_shapes=[pltpu.VMEM((rows, depth), BF)],
        compiler_params=params(),
        cost_estimate=pl.CostEstimate(
            flops=2 * rows * depth * columns, bytes_accessed=2 * depth * columns, transcendentals=0
        ),
        name="query_project",
    )(out_weight, own, other, *after)


def general_queries(lengths, own_k, own_v, self_kv, query_q, out_weight, per_kv):
    own_kv = jnp.stack([own_k, own_v], 0)
    host_id = lax.axis_index("hst")
    local_heads = query_q.shape[1] // HD
    kv_local = own_kv.shape[2] // HD
    slab_rows = own_kv.shape[1]
    own_len = lengths[host_id]
    row_ids = jnp.arange(slab_rows)
    all_queries = lax.all_gather(query_q, "hst", axis=0, tiled=True)
    query_count = all_queries.shape[0]
    q_rows = query_q.shape[0]
    source = jnp.concatenate([own_kv, self_kv], 1)
    source = source.reshape(2, slab_rows + q_rows, kv_local, HD).transpose(0, 2, 1, 3)
    query_ids = jnp.arange(query_count)
    context_ok = jnp.broadcast_to(row_ids[None, :] < own_len, (query_count, slab_rows))
    self_ok = (host_id * q_rows + jnp.arange(q_rows))[None, :] <= query_ids[:, None]
    seen_ok = jnp.concatenate([context_ok, self_ok], 1)
    query_heads = all_queries.reshape(query_count, local_heads, HD).transpose(1, 0, 2)

    def score_head(operands):
        query_rows, head_index = operands
        kv_index = head_index // per_kv
        scores = dot_t(query_rows, source[0, kv_index]) * HD ** (-0.5)
        scores = jnp.where(seen_ok, scores, MASKED)
        peak = jnp.max(scores, axis=1)
        expo = jnp.exp(scores - peak[:, None])
        return peak, jnp.sum(expo, axis=1), dot(expo.astype(BF), source[1, kv_index])

    maxima, totals, outputs = lax.map(score_head, (query_heads, jnp.arange(local_heads)))
    factor = jnp.exp(maxima - lax.pmax(maxima, "hst"))
    denominator, summed = lax.psum((totals * factor, outputs * factor[..., None]), "hst")
    attended = (summed / denominator[..., None]).astype(BF)
    attended = attended.transpose(1, 0, 2).reshape(query_count, local_heads * HD)
    return lax.psum(dot(attended, out_weight), "tp").astype(BF)


def per_device(hosts, groups, ctx_q, ctx_kv, lengths, query_q, query_kv, out_weight):
    slab = ctx_q.shape[0]
    local_heads = ctx_q.shape[1] // HD
    group_size = H // KVH
    kv_local = max(1, local_heads // group_size)
    per_kv = min(local_heads, group_size)
    q_rows = query_q.shape[0]
    host = lax.axis_index("hst")
    fast = hosts == 8 and groups & (groups - 1) == 0
    fast = fast and q_rows == 8 and local_heads == 16 and per_kv == 8

    if not fast:
        kv_first = lax.axis_index("tp") * local_heads // group_size
        self_kv = lax.dynamic_slice_in_dim(query_kv, kv_first * HD, kv_local * HD, 2)
        own_k, own_v = pick(ctx_kv, kv_local, local_heads)
        query_out = general_queries(lengths, own_k, own_v, self_kv, query_q, out_weight, per_kv)
        k, v = spread(jnp.stack([own_k, own_v]), "hst", 0)
        own_k, own_v = prepare(own_k, own_v, False)
        anchor = prepare(k, v, False)
        state = own_part(ctx_q, own_k, own_v, 0, local_heads, per_kv)
        results = {}
        for first in range(0, local_heads, per_kv):
            cols = slice(2 * first // per_kv * HD, 2 * (first // per_kv + 1) * HD)
            last = first + per_kv == local_heads
            results[first] = anchor_part(
                lengths, ctx_q, {0: state}, own_k, own_v, [x[:, cols] for x in anchor],
                first, per_kv, per_kv, dict(results) if last else None,
            )
        return results[first], query_out

    states = {}

    def own(first, count, after=()):
        states[first] = own_part(ctx_q, own_keys, own_values, first, count, per_kv, after)
        return states[first]

    along = ((2, 4), (4, 2))

    def is_even(h):
        return bit(h, 0) == 0

    def source_first(h):
        return h < 2

    def done_early(h):
        return (h <= 2) | (h == 5)

    bits = (2, 4, 6)
    landed = [swap(query_q, "hst", hosts, x, x) for x in bits]
    own_k, own_v = pick(ctx_kv, kv_local, local_heads)
    value_landed = swap(own_v, "hst", hosts, 1, 1)
    own_keys, own_values = prepare(own_k, own_v, False)
    queries = by_chip(query_q, landed, bits, (own_keys,))
    landed = swap(queries, "hst", hosts, 1, 1)
    done = own(0, 2, (queries,))
    (held,) = relay(is_even, own_k, value_landed, (done,))
    held_landed = swap(held, "hst", hosts, *along[0])
    keep, send = source_part(lengths, own_keys, own_v, query_kv, queries, landed, q_rows, per_kv, (held,))
    landed = swap(send, "hst", hosts, 1, 1)
    done = own(2, 4, (keep,))
    source = merge_part(keep, landed, False, (done,))
    landed = swap(source, "hst", hosts, *along[0])
    done = own(6, 4, (source,))
    parts = relay(source_first, held, held_landed, (done,), kv_local)
    parts_landed = [swap(x, "hst", hosts, *along[1]) for x in parts]
    source = merge_part(source, landed, False, (parts[0],))
    landed = swap(source, "hst", hosts, *along[1])
    done = own(10, 4, (source,))
    anchor = {}

    def complete(kv, after):
        (held,) = relay(done_early, parts[kv], parts_landed[kv], after)
        anchor[kv] = held, swap(held, "hst", hosts, 1, 1)
        return held

    done = complete(0, (done,))
    done = own(14, 2, (done,))
    anchor[0] = prepare(*anchor[0], True, (done,))
    results = {}

    def anchors(first, count, after, last=False):
        results[first] = anchor_part(
            lengths, ctx_q, states, own_keys, own_values, anchor[first // per_kv],
            first, count, per_kv, dict(results) if last else None, after,
        )
        return results[first]

    done = anchors(0, 2, ())
    source = merge_part(source, landed, True, (done,))
    landed = swap(source, "hst", hosts, 1, 1)
    done = complete(1, (source,))
    done = anchors(2, 4, (done,))
    terms = project_part(source, landed, out_weight, (done,))
    anchor[1] = prepare(*anchor[1], True, (terms,))
    shares = [[(10, 6, True)], [(6, 2, False), (8, 2, False)]]
    step = 1
    while step < groups:
        landed = swap(terms, "tp", groups, step, step)
        last = False
        done = terms
        for first, count, last in shares.pop() if shares else ():
            done = anchors(first, count, (terms, done), last)
        terms = add_part(terms, landed, () if last else (done,))
        step *= 2
    for group in reversed(shares):
        for first, count, last in group:
            done = anchors(first, count, (), last)
    return done, terms


def solution(mesh):
    hosts, groups = mesh.shape["hst"], mesh.shape["tp"]
    return jax.shard_map(
        functools.partial(per_device, hosts, groups),
        mesh=mesh,
        in_specs=(
            P("hst", "tp"),
            P(None, "hst", None),
            P(),
            P("hst", "tp"),
            P(None, "hst", None),
            P("tp", "hst"),
        ),
        out_specs=(P("hst", "tp"), P(None, "hst")),
        check_vma=False,
    )
```

```python
import functools

import jax
import jax.numpy as jnp
from jax import lax
from jax.experimental import pallas as pl
from jax.experimental.pallas import tpu as pltpu
from jax.sharding import PartitionSpec as P

H = 64
KVH = 8
HD = 128
MASKED = -1e30
LOG2E = 1.4426950408889634
SCALE2 = HD ** (-0.5) * LOG2E
TINY = 2.0 ** -90
BF = jnp.bfloat16
F32 = jnp.float32
VMEM = pl.BlockSpec(memory_space=pltpu.VMEM)
SMEM = pl.BlockSpec(memory_space=pltpu.SMEM)
ANY = pl.BlockSpec(memory_space=pl.ANY)
HBM = pl.BlockSpec(memory_space=pltpu.HBM)


def params(mib=20):
    return pltpu.CompilerParams(vmem_limit_bytes=mib * 2**20)


def dot_t(a, b):
    return lax.dot_general(a, b, (((1,), (1,)), ((), ())), preferred_element_type=F32)


def dot(a, b):
    return lax.dot_general(a, b, (((1,), (0,)), ((), ())), preferred_element_type=F32)


def spread(value, axis, source):
    kept = jnp.where(lax.axis_index(axis) == source, value, 0).astype(value.dtype)
    return lax.psum(kept, axis)


def send(value, axis, pairs):
    return lax.ppermute(value, axis, pairs)


def swap(value, axis, size, even, odd):
    return lax.ppermute(value, axis, [(i, i ^ (odd if i & 1 else even)) for i in range(size)])


def pick_kernel(group_size, local_heads, kv_ref, k_ref, v_ref, sems):
    first = lax.axis_index("tp") * local_heads // group_size * HD
    cols = pl.ds(pl.multiple_of(first, HD), k_ref.shape[1])
    moves = [
        pltpu.make_async_copy(kv_ref.at[1, :, cols], v_ref, sems.at[1]),
        pltpu.make_async_copy(kv_ref.at[0, :, cols], k_ref, sems.at[0]),
    ]
    for move in moves:
        move.start()
    for move in moves:
        move.wait()


def pick(ctx_kv, kv_local, local_heads):
    return pl.pallas_call(
        functools.partial(pick_kernel, H // KVH, local_heads),
        out_shape=[jax.ShapeDtypeStruct((ctx_kv.shape[1], kv_local * HD), BF)] * 2,
        in_specs=[HBM],
        out_specs=[VMEM] * 2,
        scratch_shapes=[pltpu.SemaphoreType.DMA((2,))],
        compiler_params=params(52),
        cost_estimate=pl.CostEstimate(flops=0, bytes_accessed=2**22, transcendentals=0),
        name="pick_columns",
    )(ctx_kv)


def bit(value, at):
    return (value >> at) & 1


def small_call(kernel, name, shapes, inputs, after=()):
    return pl.pallas_call(
        kernel,
        out_shape=[jax.ShapeDtypeStruct(x, BF) for x in shapes],
        in_specs=[VMEM] * len(inputs) + [ANY] * len(after),
        out_specs=[VMEM] * len(shapes),
        compiler_params=params(),
        cost_estimate=pl.CostEstimate(flops=0, bytes_accessed=2**20, transcendentals=0),
        name=name,
    )(*inputs, *after)


def choose(condition, one, two):
    pl.when(condition)(one)
    pl.when(jnp.logical_not(condition))(two)


def take_rows(target, source, rows, cols=slice(None)):
    def run():
        target[:rows, :] = source[:rows, cols]

    return run


def join(low_of, known, landed, after=()):
    rows, width = known.shape

    def kernel(known_ref, landed_ref, *rest):
        out_ref = rest[-1]

        def put(first, second):
            def run():
                both = jnp.concatenate([first[...].astype(F32), second[...].astype(F32)], 0)
                out_ref[...] = both.astype(BF)

            return run

        choose(low_of(lax.axis_index("hst")), put(known_ref, landed_ref), put(landed_ref, known_ref))

    return small_call(kernel, "query_join", [(2 * rows, width)], (known, landed), after)[0]


def relay(keep_of, one, two, after=(), split=1):
    slab, columns = one.shape
    width = columns // split

    def kernel(one_ref, two_ref, *rest):
        keep = keep_of(lax.axis_index("hst"))
        for j, out_ref in enumerate(rest[-split:]):
            cols = slice(j * width, (j + 1) * width)
            choose(keep, take_rows(out_ref, one_ref, slab, cols), take_rows(out_ref, two_ref, slab, cols))

    return small_call(kernel, "anchor_relay", [(slab, width)] * split, (one, two), after)


def add_part(one, two, after=()):
    def kernel(one_ref, two_ref, *rest):
        rest[-1][...] = (one_ref[...].astype(F32) + two_ref[...].astype(F32)).astype(BF)

    return small_call(kernel, "query_sum", [one.shape], (one, two), after)[0]


def prepare(first, second, swapped, after=()):
    slab, columns = first.shape

    def kernel(first_ref, second_ref, *rest):
        keys_ref, values_ref = rest[-2:]

        def fill(k_ref, v_ref):
            def run():
                for j in range(columns // HD):
                    cols = slice(j * HD, (j + 1) * HD)
                    at = 2 * j * HD
                    scaled = k_ref[:, cols].astype(F32) * SCALE2
                    high = scaled.astype(BF)
                    keys_ref[:, at : at + HD] = high
                    keys_ref[:, at + HD : at + 2 * HD] = (scaled - high.astype(F32)).astype(BF)
                    values_ref[:, at : at + HD] = v_ref[:, cols]
                    values_ref[:, at + HD : at + 2 * HD] = jnp.ones((slab, HD), BF)

            return run

        if swapped:
            even = bit(lax.axis_index("hst"), 0) == 0
            choose(even, fill(first_ref, second_ref), fill(second_ref, first_ref))
        else:
            fill(first_ref, second_ref)()

    shapes = [(slab, 2 * columns)] * 2
    return small_call(kernel, "operands", shapes, (first, second), after)


def twice(query):
    return jnp.concatenate([query, query], 1)


def lanes(index, width):
    return pl.ds(pl.multiple_of(index * width, width), width)


def row_tile(slab):
    return 256 if slab % 256 == 0 else slab


def body_size(first, count, per_kv, most):
    def fits(size):
        bodies = range(first, first + count, size)
        return count % size == 0 and all(x // per_kv == (x + size - 1) // per_kv for x in bodies)

    return max(x for x in range(1, most + 1) if fits(x))


def own_kernel(first, count, per_kv, q_ref, k_ref, v_ref, *rest):
    state_ref = rest[-1]
    slab = q_ref.shape[0]
    tile = row_tile(slab)
    half = tile // 2
    heads = body_size(first, count, per_kv, 4)
    rows = lax.broadcasted_iota(jnp.int32, (half, half), 0)
    cols = lax.broadcasted_iota(jnp.int32, (half, half), 1)
    causal = cols <= rows
    chunks = slab // tile
    units = [(h, j) for h in range(heads) for j in range(chunks)]

    def body(i, carry):
        kv = lax.div(first + i * heads, per_kv)

        def scores(at):
            h, j = units[at]
            query = q_ref[j * tile :, lanes(first + i * heads + h, HD)]
            return dot_t(twice(query), k_ref[j * tile : (j + 1) * tile, lanes(kv, 2 * HD)])

        def power(x):
            return jnp.exp2(x).astype(BF)

        def corner(x):
            return jnp.where(causal, jnp.exp2(x), 0.0).astype(BF)

        current = scores(0)
        totals = [None] * chunks
        for at, (h, j) in enumerate(units):
            following = scores(at + 1) if at + 1 < len(units) else None
            top = jnp.concatenate([corner(current[:half, :half]), jnp.zeros((half, half), BF)], 1)
            low = jnp.concatenate([power(current[half:tile, :half]), corner(current[half:tile, half:])], 1)
            expo = [top, low] if j == chunks - 1 else [top, low, power(current[tile:])]
            part = dot(jnp.concatenate(expo, 0), v_ref[j * tile : (j + 1) * tile, lanes(kv, 2 * HD)])
            for r in range(j, chunks):
                piece = part[(r - j) * tile : (r - j + 1) * tile]
                totals[r] = piece if j == 0 else totals[r] + piece
            state_ref[j * tile : (j + 1) * tile, lanes(i * heads + h, 2 * HD)] = totals[j]
            current = following
        return carry

    lax.fori_loop(0, count // heads, body, 0)


def own_part(ctx_q, own_k, own_v, first, count, per_kv, after=()):
    slab = ctx_q.shape[0]
    work = count * slab * (slab + row_tile(slab)) // 2
    return pl.pallas_call(
        functools.partial(own_kernel, first, count, per_kv),
        out_shape=jax.ShapeDtypeStruct((slab, count * 2 * HD), F32),
        in_specs=[VMEM] * 3 + [ANY] * len(after),
        out_specs=VMEM,
        compiler_params=params(),
        cost_estimate=pl.CostEstimate(
            flops=work * HD * 8, bytes_accessed=count * slab * HD * 6, transcendentals=work
        ),
        name="context_own",
    )(ctx_q, own_k, own_v, *after)


def anchor_kernel(first, count, bases, per_kv, last, befores, *refs):
    lengths_ref, q_ref, k_ref, v_ref, keys, vaug = refs[:6]
    state_refs = refs[6 : 6 + len(bases)]
    earlier = refs[6 + len(bases) : 6 + len(bases) + len(befores)]
    if last:
        full_ref, out_ref, sems = refs[-3:]
    else:
        out_ref = refs[-1]
    slab = q_ref.shape[0]
    heads = body_size(first, count, per_kv, 2 if last else 4)
    tile = row_tile(slab)
    chunks = slab // tile
    units = [(h, j) for h in range(heads) for j in range(chunks)]
    kv = first // per_kv
    host = lax.axis_index("hst")
    own_len = lengths_ref[host]

    def hand_over(source, start, width, sem):
        target = full_ref.at[:, pl.ds(start * HD, width * HD)]
        return pltpu.make_async_copy(source, target, sems.at[sem])

    moves = [hand_over(earlier[n], *place, n) for n, place in enumerate(befores)]
    for move in moves:
        move.start()

    def part(start):
        def query_of(h):
            at = (first + start + h) * HD
            return q_ref[:, at : at + HD]

        def scores(h, j):
            return dot_t(twice(query_of(h)), keys[j * tile : (j + 1) * tile, :])

        def state_of(h):
            head = first + start + h
            n = max(n for n, base in enumerate(bases) if base <= head)
            at = (head - bases[n]) * 2 * HD
            return state_refs[n][:, at : at + 2 * HD]

        def finish(h, total, worst):
            sums = total[:, HD:]
            inverse = pl.reciprocal(sums, approx=True)
            out_ref[:, (start + h) * HD : (start + h + 1) * HD] = (total[:, :HD] * inverse).astype(BF)
            return jnp.minimum(worst, jnp.minimum(sums, inverse))

        def check(worst):
            @pl.when(jnp.logical_not(jnp.min(worst) > TINY))
            def _():
                exact_block(first + start, start, heads, host, own_len, kv, q_ref, k_ref, v_ref, keys, vaug, out_ref)

        @pl.when(host == 0)
        def _():
            worst = jnp.ones((slab, HD), F32)
            for h in range(heads):
                worst = finish(h, state_of(h), worst)
            check(worst)

        @pl.when(host > 0)
        def _():
            worst = jnp.ones((slab, HD), F32)
            current = scores(*units[0])
            for at, (h, j) in enumerate(units):
                following = scores(*units[at + 1]) if at + 1 < len(units) else None
                part = dot(jnp.exp2(current).astype(BF), vaug[j * tile : (j + 1) * tile, :])
                total = (state_of(h) if j == 0 else total) + part
                if j == chunks - 1:
                    worst = finish(h, total, worst)
                current = following
            check(worst)

        @pl.when(own_len < slab)
        def _():
            row_ids = lax.broadcasted_iota(jnp.int32, (slab, HD), 0)
            for h in range(start, start + heads):
                cols = slice(h * HD, (h + 1) * HD)
                kept = jnp.where(row_ids < own_len, out_ref[:, cols].astype(F32), 0.0)
                out_ref[:, cols] = kept.astype(BF)

        if last:
            source = out_ref.at[:, start * HD : (start + heads) * HD]
            move = hand_over(source, first + start, heads, len(befores) + start // heads)
            move.start()
            moves.append(move)

    for start in range(0, count, heads):
        part(start)
    for move in moves:
        move.wait()


def exact_block(q_head, out_head, heads, host, own_len, kv, q_ref, k_ref, v_ref, keys, vaug, out_ref):
    slab = q_ref.shape[0]
    tile = 64

    def body(i, carry):
        h = lax.div(i, slab // tile)
        r = lax.rem(i, slab // tile)
        at = pl.ds(pl.multiple_of(r * tile, tile), tile)
        query = q_ref[at, lanes(q_head + h, HD)]
        row_ids = lax.broadcasted_iota(jnp.int32, (tile, slab), 0) + r * tile
        key_ids = lax.broadcasted_iota(jnp.int32, (tile, slab), 1)
        own = dot_t(twice(query), k_ref[:, 2 * kv * HD : 2 * (kv + 1) * HD])
        own = jnp.where((key_ids <= row_ids) & (key_ids < own_len), own, MASKED)
        far = dot_t(twice(query), keys[...])
        far = jnp.where(host > 0, far, MASKED)
        peak = jnp.maximum(jnp.max(own, 1, keepdims=True), jnp.max(far, 1, keepdims=True))
        own = jnp.exp2(own - peak)
        far = jnp.where(host > 0, jnp.exp2(far - peak), 0.0)
        sums = jnp.sum(own, 1, keepdims=True) + jnp.sum(far, 1, keepdims=True)
        values = jnp.where(host > 0, vaug[:, :HD].astype(F32), 0.0).astype(BF)
        total = dot(own.astype(BF), v_ref[:, 2 * kv * HD : (2 * kv + 1) * HD]) + dot(far.astype(BF), values)
        live = row_ids[:, :1] < own_len
        out_ref[at, lanes(out_head + h, HD)] = jnp.where(live, total / sums, 0.0).astype(BF)
        return carry

    lax.fori_loop(0, heads * (slab // tile), body, 0)


def anchor_part(lengths, ctx_q, states, own_k, own_v, anchor, first, count, per_kv, befores=None, after=()):
    slab, width = ctx_q.shape
    work = count * slab * slab
    last = befores is not None
    ends = {x: x + y.shape[1] // (2 * HD) for x, y in states.items()}
    bases = tuple(x for x in sorted(states) if x < first + count and ends[x] > first)
    earlier = list(befores.values()) if last else []
    places = tuple((at, x.shape[1] // HD) for at, x in befores.items()) if last else ()
    results = jax.ShapeDtypeStruct((slab, count * HD), BF)
    scratch = []
    if last:
        scratch = [pltpu.VMEM(results.shape, BF), pltpu.SemaphoreType.DMA((len(earlier) + count,))]
        results = jax.ShapeDtypeStruct((slab, width), BF)
    return pl.pallas_call(
        functools.partial(anchor_kernel, first, count, bases, per_kv, last, places),
        out_shape=results,
        in_specs=[SMEM] + [VMEM] * (5 + len(bases) + len(earlier)) + [ANY] * len(after),
        out_specs=ANY if last else VMEM,
        scratch_shapes=scratch,
        compiler_params=params(),
        cost_estimate=pl.CostEstimate(
            flops=work * HD * 8, bytes_accessed=count * slab * HD * 8, transcendentals=work
        ),
        name="context_anchor",
    )(lengths, ctx_q, own_k, own_v, *anchor, *[states[x] for x in bases], *earlier, *after)


PART = 16


def write_level(ref, width, level):
    lane = lax.broadcasted_iota(jnp.int32, level.shape, 1)
    parts = []
    for at in range(3):
        part = level.astype(BF).astype(F32)
        parts.append(part if at == 0 else pltpu.roll(part, at * PART, 1))
        level = level - part
    packed = jnp.where(lane < PART, parts[0], jnp.where(lane < 2 * PART, parts[1], parts[2]))
    ref[:, width : width + HD] = packed.astype(BF)


def read_level(ref, width):
    packed = ref[:, width : width + HD].astype(F32)
    return packed + pltpu.roll(packed, HD - PART, 1) + pltpu.roll(packed, HD - 2 * PART, 1)


def source_kernel(per_kv, q_rows, group_size, lengths_ref, k_ref, v_ref, self_ref, known_ref, landed_ref, *rest):
    keep_ref, send_ref, q_all, vaug = rest[-4:]
    slab, columns = v_ref.shape
    width = per_kv * columns
    query_count = 8 * q_rows
    block = 2 * q_rows
    host = lax.axis_index("hst")
    own_len = lengths_ref[host]
    rows = per_kv * query_count
    odd = bit(host, 0) == 1
    low = jnp.where(odd, bit(host, 1), bit(host, 2)) == 0

    def place(lower, upper, spread_out):
        middle = (2, 1) if spread_out else (1, 2)
        for ref, chips in ((lower, (0, middle[0])), (upper, (middle[1], 3))):
            for n, chip in enumerate(chips):
                for h in range(width // HD):
                    to = h * query_count + chip * block
                    q_all[to : to + block, :] = ref[n * block : (n + 1) * block, h * HD : (h + 1) * HD]

    for is_low, is_odd in ((False, False), (False, True), (True, False), (True, True)):
        @pl.when((low == is_low) & (odd == is_odd))
        def _():
            pair = (known_ref, landed_ref) if is_low else (landed_ref, known_ref)
            place(*pair, is_odd)

    first = lax.axis_index("tp") * (width // HD) // group_size * HD
    own_cols = pl.ds(pl.multiple_of(first, HD), columns)
    selves_kv = [self_ref[i, :, own_cols].astype(F32) for i in range(2)]
    lane = lax.broadcasted_iota(jnp.int32, (query_count, HD), 1)
    query_ids = lax.broadcasted_iota(jnp.int32, (query_count, HD), 0)
    self_ok = (host * q_rows + lane <= query_ids) & (lane < q_rows)
    self_ok = jnp.concatenate([self_ok] * per_kv, 0)
    pad = jnp.zeros((HD - q_rows, HD), F32)
    key_rows = lax.broadcasted_iota(jnp.int32, (slab, HD), 0)
    ones = jnp.where(key_rows < own_len, 1.0, 0.0).astype(BF)
    for j in range(columns // HD):
        values = v_ref[:, j * HD : (j + 1) * HD].astype(F32)
        vaug[:, 2 * j * HD : (2 * j + 1) * HD] = jnp.where(key_rows < own_len, values, 0.0).astype(BF)
        vaug[:, (2 * j + 1) * HD : (2 * j + 2) * HD] = ones

    def operands(j):
        cols = slice(j * HD, (j + 1) * HD)
        queries = q_all[j * rows : (j + 1) * rows, :]
        self_keys = jnp.concatenate([selves_kv[0][:, cols], pad], 0).astype(BF)
        self_values = jnp.concatenate([selves_kv[1][:, cols], pad], 0).astype(BF)
        near = dot_t(twice(queries), k_ref[:, 2 * j * HD : 2 * (j + 1) * HD])
        selves = jnp.where(self_ok, dot_t(queries, self_keys) * SCALE2, MASKED)
        return near, selves, jnp.concatenate([self_values, jnp.ones((HD, HD), BF)], 1)

    def store(j, total, level):
        stats = jnp.zeros((query_count, HD), F32)
        for h in range(per_kv):
            stats = jnp.where(lane == h, level[h * query_count : (h + 1) * query_count, :], stats)

        def put(out_ref):
            def run():
                for h in range(per_kv):
                    part = total[h * query_count : (h + 1) * query_count, :]
                    out_ref[:, h * HD : (h + 1) * HD] = part.astype(BF)
                write_level(out_ref, per_kv * HD, stats)

            return run

        choose(odd if j else jnp.logical_not(odd), put(keep_ref), put(send_ref))

    worst = jnp.ones((rows, HD), F32)
    found = []
    for j in range(columns // HD):
        near, selves, self_values = operands(j)
        near = jnp.exp2(near).astype(BF)
        selves = jnp.exp2(selves).astype(BF)
        total = dot(near, vaug[:, 2 * j * HD : (2 * j + 2) * HD]) + dot(selves, self_values)
        sums = total[:, HD:]
        inverse = 1.0 / sums
        worst = jnp.minimum(worst, jnp.minimum(sums, inverse))
        found.append((total[:, :HD] * inverse, jnp.log2(sums)))
    for j, result in enumerate(found):
        store(j, *result)

    @pl.when(jnp.logical_not(jnp.min(worst) > TINY))
    def _():
        key_ids = lax.broadcasted_iota(jnp.int32, (query_count, slab), 1)
        heads_ok = (host * q_rows + lane <= query_ids) & (lane < q_rows)
        for j in range(columns // HD):
            cols = slice(j * HD, (j + 1) * HD)
            self_keys = jnp.concatenate([selves_kv[0][:, cols], pad], 0).astype(BF)
            self_values = jnp.concatenate([selves_kv[1][:, cols], pad], 0).astype(BF)
            self_values = jnp.concatenate([self_values, jnp.ones((HD, HD), BF)], 1)
            mine = odd if j else jnp.logical_not(odd)

            def body(h, stats):
                at = pl.ds(pl.multiple_of((j * per_kv + h) * query_count, query_count), query_count)
                queries = q_all[at, :]
                near = dot_t(twice(queries), k_ref[:, 2 * j * HD : 2 * (j + 1) * HD])
                near = jnp.where(key_ids < own_len, near, MASKED)
                selves = jnp.where(heads_ok, dot_t(queries, self_keys) * SCALE2, MASKED)
                peak = jnp.maximum(jnp.max(near, 1, keepdims=True), jnp.max(selves, 1, keepdims=True))
                near = jnp.exp2(near - peak).astype(BF)
                selves = jnp.exp2(selves - peak).astype(BF)
                total = dot(near, vaug[:, 2 * j * HD : (2 * j + 2) * HD]) + dot(selves, self_values)
                result = (total[:, :HD] / total[:, HD:]).astype(BF)

                def put(out_ref):
                    def run():
                        out_ref[:, lanes(h, HD)] = result

                    return run

                choose(mine, put(keep_ref), put(send_ref))
                return jnp.where(lane == h, peak + jnp.log2(total[:, HD:]), stats)

            stats = lax.fori_loop(0, per_kv, body, jnp.zeros((query_count, HD), F32))

            def put_level(out_ref):
                def run():
                    write_level(out_ref, per_kv * HD, stats)

                return run

            choose(mine, put_level(keep_ref), put_level(send_ref))


def source_part(lengths, own_k, own_v, query_kv, known, landed, q_rows, per_kv, after=()):
    slab, columns = own_v.shape
    width = per_kv * columns
    count = 8 * q_rows
    work = count * (width // HD) * slab
    return pl.pallas_call(
        functools.partial(source_kernel, per_kv, q_rows, H // KVH),
        out_shape=[jax.ShapeDtypeStruct((count, (per_kv + 1) * HD), BF)] * 2,
        in_specs=[SMEM] + [VMEM] * 5 + [ANY] * len(after),
        out_specs=[VMEM] * 2,
        scratch_shapes=[pltpu.VMEM((count * width // HD, HD), BF), pltpu.VMEM((slab, 2 * columns), BF)],
        compiler_params=params(),
        cost_estimate=pl.CostEstimate(flops=work * HD * 8, bytes_accessed=2**21, transcendentals=work),
        name="query_source",
    )(lengths, own_k, own_v, query_kv, known, landed, *after)


def merged(refs, width):
    levels = [read_level(ref, width) for ref in refs]
    peak = jnp.maximum(*levels)
    weights = [jnp.exp2(x - peak) for x in levels]
    whole = weights[0] + weights[1]
    return [w / whole for w in weights], peak + jnp.log2(whole)


def blend(shares, refs, h):
    cols = slice(h * HD, (h + 1) * HD)
    return sum(w[:, h : h + 1] * ref[:, cols].astype(F32) for w, ref in zip(shares, refs))


def merge_part(one, two, last, after=()):
    rows, wide = one.shape
    width = wide - HD

    def kernel(one_ref, two_ref, *rest):
        out_ref = rest[-1]
        shares, level = merged((one_ref, two_ref), width)
        if not last:
            write_level(out_ref, width, level)
        for h in range(width // HD):
            out_ref[:, h * HD : (h + 1) * HD] = blend(shares, (one_ref, two_ref), h).astype(BF)

    return small_call(kernel, "query_merge", [(rows, width if last else wide)], (one, two), after)[0]


def project_part(own, other, out_weight, after=()):
    rows, half = own.shape
    depth, columns = out_weight.shape

    def kernel(w_ref, own_ref, other_ref, *rest):
        out_ref, attended = rest[-2:]

        def put(first, second):
            def run():
                attended[:, :half] = first[...]
                attended[:, half:] = second[...]

            return run

        even = bit(lax.axis_index("hst"), 0) == 0
        choose(even, put(own_ref, other_ref), put(other_ref, own_ref))
        out_ref[...] = dot(attended[...], w_ref[...]).astype(BF)

    return pl.pallas_call(
        kernel,
        out_shape=jax.ShapeDtypeStruct((rows, columns), BF),
        in_specs=[VMEM] * 3 + [ANY] * len(after),
        out_specs=VMEM,
        scratch_shapes=[pltpu.VMEM((rows, depth), BF)],
        compiler_params=params(),
        cost_estimate=pl.CostEstimate(
            flops=2 * rows * depth * columns, bytes_accessed=2 * depth * columns, transcendentals=0
        ),
        name="query_project",
    )(out_weight, own, other, *after)


def general_queries(lengths, own_k, own_v, self_kv, query_q, out_weight, per_kv):
    own_kv = jnp.stack([own_k, own_v], 0)
    host_id = lax.axis_index("hst")
    local_heads = query_q.shape[1] // HD
    kv_local = own_kv.shape[2] // HD
    slab_rows = own_kv.shape[1]
    own_len = lengths[host_id]
    row_ids = jnp.arange(slab_rows)
    all_queries = lax.all_gather(query_q, "hst", axis=0, tiled=True)
    query_count = all_queries.shape[0]
    q_rows = query_q.shape[0]
    source = jnp.concatenate([own_kv, self_kv], 1)
    source = source.reshape(2, slab_rows + q_rows, kv_local, HD).transpose(0, 2, 1, 3)
    query_ids = jnp.arange(query_count)
    context_ok = jnp.broadcast_to(row_ids[None, :] < own_len, (query_count, slab_rows))
    self_ok = (host_id * q_rows + jnp.arange(q_rows))[None, :] <= query_ids[:, None]
    seen_ok = jnp.concatenate([context_ok, self_ok], 1)
    query_heads = all_queries.reshape(query_count, local_heads, HD).transpose(1, 0, 2)

    def score_head(operands):
        query_rows, head_index = operands
        kv_index = head_index // per_kv
        scores = dot_t(query_rows, source[0, kv_index]) * HD ** (-0.5)
        scores = jnp.where(seen_ok, scores, MASKED)
        peak = jnp.max(scores, axis=1)
        expo = jnp.exp(scores - peak[:, None])
        return peak, jnp.sum(expo, axis=1), dot(expo.astype(BF), source[1, kv_index])

    maxima, totals, outputs = lax.map(score_head, (query_heads, jnp.arange(local_heads)))
    factor = jnp.exp(maxima - lax.pmax(maxima, "hst"))
    denominator, summed = lax.psum((totals * factor, outputs * factor[..., None]), "hst")
    attended = (summed / denominator[..., None]).astype(BF)
    attended = attended.transpose(1, 0, 2).reshape(query_count, local_heads * HD)
    return lax.psum(dot(attended, out_weight), "tp").astype(BF)


def per_device(hosts, groups, ctx_q, ctx_kv, lengths, query_q, query_kv, out_weight):
    slab = ctx_q.shape[0]
    local_heads = ctx_q.shape[1] // HD
    group_size = H // KVH
    kv_local = max(1, local_heads // group_size)
    per_kv = min(local_heads, group_size)
    q_rows = query_q.shape[0]
    host = lax.axis_index("hst")
    fast = hosts == 8 and groups & (groups - 1) == 0
    fast = fast and q_rows == 8 and local_heads == 16 and per_kv == 8

    if not fast:
        kv_first = lax.axis_index("tp") * local_heads // group_size
        self_kv = lax.dynamic_slice_in_dim(query_kv, kv_first * HD, kv_local * HD, 2)
        own_k, own_v = pick(ctx_kv, kv_local, local_heads)
        query_out = general_queries(lengths, own_k, own_v, self_kv, query_q, out_weight, per_kv)
        k, v = spread(jnp.stack([own_k, own_v]), "hst", 0)
        own_k, own_v = prepare(own_k, own_v, False)
        anchor = prepare(k, v, False)
        state = own_part(ctx_q, own_k, own_v, 0, local_heads, per_kv)
        results = {}
        for first in range(0, local_heads, per_kv):
            cols = slice(2 * first // per_kv * HD, 2 * (first // per_kv + 1) * HD)
            last = first + per_kv == local_heads
            results[first] = anchor_part(
                lengths, ctx_q, {0: state}, own_k, own_v, [x[:, cols] for x in anchor],
                first, per_kv, per_kv, dict(results) if last else None,
            )
        return results[first], query_out

    states = {}

    def own(first, count, after=()):
        states[first] = own_part(ctx_q, own_keys, own_values, first, count, per_kv, after)
        return states[first]

    along = ((2, 4), (4, 2))

    def is_even(h):
        return bit(h, 0) == 0

    def source_first(h):
        return h < 2

    def done_early(h):
        return (h <= 2) | (h == 5)

    def near_low(h):
        return jnp.where(bit(h, 0) == 1, bit(h, 2), bit(h, 1)) == 0

    landed = swap(query_q, "hst", hosts, 1, 1)
    own_k, own_v = pick(ctx_kv, kv_local, local_heads)
    value_landed = swap(own_v, "hst", hosts, 1, 1)
    own_keys, own_values = prepare(own_k, own_v, False)
    queries = join(is_even, query_q, landed, (own_keys,))
    landed = swap(queries, "hst", hosts, *along[0])
    done = own(0, 2, (queries,))
    parts = list(relay(is_even, own_k, value_landed, (done,), kv_local))
    parts_landed = [send(x, "hst", [(0, 2), (1, 5)]) for x in parts]
    queries = join(near_low, queries, landed, (parts[0],))
    landed = swap(queries, "hst", hosts, *along[1])
    done = own(2, 6, (queries,))
    anchor = {}

    def pass_on(kv, after):
        (parts[kv],) = relay(source_first, parts[kv], parts_landed[kv], after)
        parts_landed[kv] = send(parts[kv], "hst", [(0, 4), (2, 6), (1, 3), (5, 7)])
        return parts[kv]

    def complete(kv, after):
        (held,) = relay(done_early, parts[kv], parts_landed[kv], after)
        anchor[kv] = held, swap(held, "hst", hosts, 1, 1)
        return held

    done = pass_on(0, (done,))
    keep, give = source_part(lengths, own_keys, own_v, query_kv, queries, landed, q_rows, per_kv, (done,))
    landed = swap(give, "hst", hosts, 1, 1)
    done = own(8, 4, (keep,))
    done = pass_on(1, (done,))
    done = complete(0, (done,))
    source = merge_part(keep, landed, False, (done,))
    landed = swap(source, "hst", hosts, *along[0])
    done = own(12, 4, (source,))
    anchor[0] = prepare(*anchor[0], True, (done,))
    results = {}

    def anchors(first, count, after, last=False):
        results[first] = anchor_part(
            lengths, ctx_q, states, own_keys, own_values, anchor[first // per_kv],
            first, count, per_kv, dict(results) if last else None, after,
        )
        return results[first]

    done = anchors(0, 2, ())
    source = merge_part(source, landed, False, (done,))
    landed = swap(source, "hst", hosts, *along[1])
    done = anchors(2, 4, (source,))
    source = merge_part(source, landed, True, (done,))
    landed = swap(source, "hst", hosts, 1, 1)
    done = complete(1, (source,))
    done = anchors(6, 2, (done,))
    terms = project_part(source, landed, out_weight, (done,))
    anchor[1] = prepare(*anchor[1], True, (terms,))
    shares = [[(12, 4, True)], [(8, 4, False)]]
    step = 1
    while step < groups:
        landed = swap(terms, "tp", groups, step, step)
        last = False
        done = terms
        for first, count, last in shares.pop() if shares else ():
            done = anchors(first, count, (terms, done), last)
        terms = add_part(terms, landed, () if last else (done,))
        step *= 2
    for group in reversed(shares):
        for first, count, last in group:
            done = anchors(first, count, (), last)
    return done, terms


def solution(mesh):
    hosts, groups = mesh.shape["hst"], mesh.shape["tp"]
    return jax.shard_map(
        functools.partial(per_device, hosts, groups),
        mesh=mesh,
        in_specs=(
            P("hst", "tp"),
            P(None, "hst", None),
            P(),
            P("hst", "tp"),
            P(None, "hst", None),
            P("tp", "hst"),
        ),
        out_specs=(P("hst", "tp"), P(None, "hst")),
        check_vma=False,
    )
```

```python
import functools

import jax
import jax.numpy as jnp
from jax import lax
from jax.experimental import pallas as pl
from jax.experimental.pallas import tpu as pltpu
from jax.sharding import PartitionSpec as P

H = 64
KVH = 8
HD = 128
MASKED = -1e30
LOG2E = 1.4426950408889634
SCALE2 = HD ** (-0.5) * LOG2E
TINY = 2.0 ** -90
BF = jnp.bfloat16
F32 = jnp.float32
VMEM = pl.BlockSpec(memory_space=pltpu.VMEM)
SMEM = pl.BlockSpec(memory_space=pltpu.SMEM)
ANY = pl.BlockSpec(memory_space=pl.ANY)
HBM = pl.BlockSpec(memory_space=pltpu.HBM)


def params(mib=20):
    return pltpu.CompilerParams(vmem_limit_bytes=mib * 2**20)


def dot_t(a, b):
    return lax.dot_general(a, b, (((1,), (1,)), ((), ())), preferred_element_type=F32)


def dot(a, b):
    return lax.dot_general(a, b, (((1,), (0,)), ((), ())), preferred_element_type=F32)


def spread(value, axis, source):
    kept = jnp.where(lax.axis_index(axis) == source, value, 0).astype(value.dtype)
    return lax.psum(kept, axis)


def swap(value, axis, size, even, odd):
    return lax.ppermute(value, axis, [(i, i ^ (odd if i & 1 else even)) for i in range(size)])


def pick_kernel(group_size, local_heads, kv_ref, k_ref, v_ref, sems):
    first = lax.axis_index("tp") * local_heads // group_size * HD
    cols = pl.ds(pl.multiple_of(first, HD), k_ref.shape[1])
    moves = [
        pltpu.make_async_copy(kv_ref.at[1, :, cols], v_ref, sems.at[1]),
        pltpu.make_async_copy(kv_ref.at[0, :, cols], k_ref, sems.at[0]),
    ]
    for move in moves:
        move.start()
    for move in moves:
        move.wait()


def pick(ctx_kv, kv_local, local_heads):
    return pl.pallas_call(
        functools.partial(pick_kernel, H // KVH, local_heads),
        out_shape=[jax.ShapeDtypeStruct((ctx_kv.shape[1], kv_local * HD), BF)] * 2,
        in_specs=[HBM],
        out_specs=[VMEM] * 2,
        scratch_shapes=[pltpu.SemaphoreType.DMA((2,))],
        compiler_params=params(52),
        cost_estimate=pl.CostEstimate(flops=0, bytes_accessed=2**22, transcendentals=0),
        name="pick_columns",
    )(ctx_kv)


def bit(value, at):
    return (value >> at) & 1


def small_call(kernel, name, shapes, inputs, after=()):
    return pl.pallas_call(
        kernel,
        out_shape=[jax.ShapeDtypeStruct(x, BF) for x in shapes],
        in_specs=[VMEM] * len(inputs) + [ANY] * len(after),
        out_specs=[VMEM] * len(shapes),
        compiler_params=params(),
        cost_estimate=pl.CostEstimate(flops=0, bytes_accessed=2**20, transcendentals=0),
        name=name,
    )(*inputs, *after)


def choose(condition, one, two):
    pl.when(condition)(one)
    pl.when(jnp.logical_not(condition))(two)


def take_rows(target, source, rows, cols=slice(None)):
    def run():
        target[:rows, :] = source[:rows, cols]

    return run


def join(low_of, known, landed, after=()):
    rows, width = known.shape

    def kernel(known_ref, landed_ref, *rest):
        out_ref = rest[-1]

        def put(first, second):
            def run():
                both = jnp.concatenate([first[...].astype(F32), second[...].astype(F32)], 0)
                out_ref[...] = both.astype(BF)

            return run

        choose(low_of(lax.axis_index("hst")), put(known_ref, landed_ref), put(landed_ref, known_ref))

    return small_call(kernel, "query_join", [(2 * rows, width)], (known, landed), after)[0]


def relay(keep_of, one, two, after=(), split=1):
    slab, columns = one.shape
    width = columns // split

    def kernel(one_ref, two_ref, *rest):
        keep = keep_of(lax.axis_index("hst"))
        for j, out_ref in enumerate(rest[-split:]):
            cols = slice(j * width, (j + 1) * width)
            choose(keep, take_rows(out_ref, one_ref, slab, cols), take_rows(out_ref, two_ref, slab, cols))

    return small_call(kernel, "anchor_relay", [(slab, width)] * split, (one, two), after)


def add_part(one, two, after=()):
    def kernel(one_ref, two_ref, *rest):
        rest[-1][...] = (one_ref[...].astype(F32) + two_ref[...].astype(F32)).astype(BF)

    return small_call(kernel, "query_sum", [one.shape], (one, two), after)[0]


def prepare(first, second, swapped, after=()):
    slab, columns = first.shape

    def kernel(first_ref, second_ref, *rest):
        keys_ref, values_ref = rest[-2:]

        def fill(k_ref, v_ref):
            def run():
                for j in range(columns // HD):
                    cols = slice(j * HD, (j + 1) * HD)
                    at = 2 * j * HD
                    scaled = k_ref[:, cols].astype(F32) * SCALE2
                    high = scaled.astype(BF)
                    low = scaled - high.astype(F32)
                    keys_ref[at : at + HD, :] = high.astype(F32).T.astype(BF)
                    keys_ref[at + HD : at + 2 * HD, :] = low.T.astype(BF)
                    values_ref[:, at : at + HD] = v_ref[:, cols]
                    values_ref[:, at + HD : at + 2 * HD] = jnp.ones((slab, HD), BF)

            return run

        if swapped:
            even = bit(lax.axis_index("hst"), 0) == 0
            choose(even, fill(first_ref, second_ref), fill(second_ref, first_ref))
        else:
            fill(first_ref, second_ref)()

    shapes = [(2 * columns, slab), (slab, 2 * columns)]
    return small_call(kernel, "operands", shapes, (first, second), after)


def twice(query):
    return jnp.concatenate([query, query], 1)


def lanes(index, width):
    return pl.ds(pl.multiple_of(index * width, width), width)


def row_tile(slab):
    return 256 if slab % 256 == 0 else slab


def body_size(first, count, per_kv, most):
    def fits(size):
        bodies = range(first, first + count, size)
        return count % size == 0 and all(x // per_kv == (x + size - 1) // per_kv for x in bodies)

    return max(x for x in range(1, most + 1) if fits(x))


def own_kernel(first, count, per_kv, q_ref, k_ref, v_ref, *rest):
    state_ref = rest[-1]
    slab = q_ref.shape[0]
    tile = row_tile(slab)
    half = tile // 2
    heads = body_size(first, count, per_kv, 4)
    rows = lax.broadcasted_iota(jnp.int32, (half, half), 0)
    cols = lax.broadcasted_iota(jnp.int32, (half, half), 1)
    causal = cols <= rows
    chunks = slab // tile
    units = [(h, j) for h in range(heads) for j in range(chunks)]

    def body(i, carry):
        kv = lax.div(first + i * heads, per_kv)

        def scores(at):
            h, j = units[at]
            query = q_ref[j * tile :, lanes(first + i * heads + h, HD)]
            return dot(twice(query), k_ref[lanes(kv, 2 * HD), j * tile : (j + 1) * tile])

        def power(x):
            return jnp.exp2(x).astype(BF)

        def corner(x):
            return jnp.where(causal, jnp.exp2(x), 0.0).astype(BF)

        current = scores(0)
        totals = [None] * chunks
        for at, (h, j) in enumerate(units):
            following = scores(at + 1) if at + 1 < len(units) else None
            top = jnp.concatenate([corner(current[:half, :half]), jnp.zeros((half, half), BF)], 1)
            low = jnp.concatenate([power(current[half:tile, :half]), corner(current[half:tile, half:])], 1)
            expo = [top, low] if j == chunks - 1 else [top, low, power(current[tile:])]
            part = dot(jnp.concatenate(expo, 0), v_ref[j * tile : (j + 1) * tile, lanes(kv, 2 * HD)])
            for r in range(j, chunks):
                piece = part[(r - j) * tile : (r - j + 1) * tile]
                totals[r] = piece if j == 0 else totals[r] + piece
            state_ref[j * tile : (j + 1) * tile, lanes(i * heads + h, 2 * HD)] = totals[j]
            current = following
        return carry

    lax.fori_loop(0, count // heads, body, 0)


def own_part(ctx_q, own_k, own_v, first, count, per_kv, after=()):
    slab = ctx_q.shape[0]
    work = count * slab * (slab + row_tile(slab)) // 2
    return pl.pallas_call(
        functools.partial(own_kernel, first, count, per_kv),
        out_shape=jax.ShapeDtypeStruct((slab, count * 2 * HD), F32),
        in_specs=[VMEM] * 3 + [ANY] * len(after),
        out_specs=VMEM,
        compiler_params=params(),
        cost_estimate=pl.CostEstimate(
            flops=work * HD * 8, bytes_accessed=count * slab * HD * 6, transcendentals=work
        ),
        name="context_own",
    )(ctx_q, own_k, own_v, *after)


def anchor_kernel(first, count, bases, per_kv, last, befores, *refs):
    lengths_ref, q_ref, k_ref, v_ref, keys, vaug = refs[:6]
    state_refs = refs[6 : 6 + len(bases)]
    earlier = refs[6 + len(bases) : 6 + len(bases) + len(befores)]
    if last:
        full_ref, out_ref, sems = refs[-3:]
    else:
        out_ref = refs[-1]
    slab = q_ref.shape[0]
    heads = body_size(first, count, per_kv, 2 if last else 4)
    kv = first // per_kv
    host = lax.axis_index("hst")
    own_len = lengths_ref[host]

    def hand_over(source, start, width, sem):
        target = full_ref.at[:, pl.ds(start * HD, width * HD)]
        return pltpu.make_async_copy(source, target, sems.at[sem])

    moves = [hand_over(earlier[n], *place, n) for n, place in enumerate(befores)]
    for move in moves:
        move.start()

    def part(start):
        def query_of(h):
            at = (first + start + h) * HD
            return q_ref[:, at : at + HD]

        def scores(h):
            return dot(twice(query_of(h)), keys[...])

        def state_of(h):
            head = first + start + h
            n = max(n for n, base in enumerate(bases) if base <= head)
            at = (head - bases[n]) * 2 * HD
            return state_refs[n][:, at : at + 2 * HD]

        def finish(h, total, sums, worst):
            inverse = pl.reciprocal(sums, approx=True)
            out_ref[:, (start + h) * HD : (start + h + 1) * HD] = (total * inverse).astype(BF)
            return jnp.minimum(worst, jnp.minimum(sums, inverse))

        def check(worst):
            @pl.when(jnp.logical_not(jnp.min(worst) > TINY))
            def _():
                exact_block(first + start, start, heads, host, own_len, kv, q_ref, k_ref, v_ref, keys, vaug, out_ref)

        @pl.when(host == 0)
        def _():
            worst = jnp.ones((slab, HD), F32)
            for h in range(heads):
                state = state_of(h)
                worst = finish(h, state[:, :HD], state[:, HD:], worst)
            check(worst)

        @pl.when(host > 0)
        def _():
            worst = jnp.ones((slab, HD), F32)
            current = scores(0)
            for h in range(heads):
                following = scores(h + 1) if h + 1 < heads else None
                expo = jnp.exp2(current)
                state = state_of(h)
                total = dot(expo.astype(BF), vaug[:, :HD]) + state[:, :HD]
                sums = jnp.sum(expo, axis=1, keepdims=True) + state[:, HD:]
                worst = finish(h, total, sums, worst)
                current = following
            check(worst)

        @pl.when(own_len < slab)
        def _():
            row_ids = lax.broadcasted_iota(jnp.int32, (slab, HD), 0)
            for h in range(start, start + heads):
                cols = slice(h * HD, (h + 1) * HD)
                kept = jnp.where(row_ids < own_len, out_ref[:, cols].astype(F32), 0.0)
                out_ref[:, cols] = kept.astype(BF)

        if last:
            source = out_ref.at[:, start * HD : (start + heads) * HD]
            move = hand_over(source, first + start, heads, len(befores) + start // heads)
            move.start()
            moves.append(move)

    for start in range(0, count, heads):
        part(start)
    for move in moves:
        move.wait()


def exact_block(q_head, out_head, heads, host, own_len, kv, q_ref, k_ref, v_ref, keys, vaug, out_ref):
    slab = q_ref.shape[0]
    tile = 64

    def body(i, carry):
        h = lax.div(i, slab // tile)
        r = lax.rem(i, slab // tile)
        at = pl.ds(pl.multiple_of(r * tile, tile), tile)
        query = q_ref[at, lanes(q_head + h, HD)]
        row_ids = lax.broadcasted_iota(jnp.int32, (tile, slab), 0) + r * tile
        key_ids = lax.broadcasted_iota(jnp.int32, (tile, slab), 1)
        own = dot(twice(query), k_ref[2 * kv * HD : 2 * (kv + 1) * HD, :])
        own = jnp.where((key_ids <= row_ids) & (key_ids < own_len), own, MASKED)
        far = dot(twice(query), keys[...])
        far = jnp.where(host > 0, far, MASKED)
        peak = jnp.maximum(jnp.max(own, 1, keepdims=True), jnp.max(far, 1, keepdims=True))
        own = jnp.exp2(own - peak)
        far = jnp.where(host > 0, jnp.exp2(far - peak), 0.0)
        sums = jnp.sum(own, 1, keepdims=True) + jnp.sum(far, 1, keepdims=True)
        values = jnp.where(host > 0, vaug[:, :HD].astype(F32), 0.0).astype(BF)
        total = dot(own.astype(BF), v_ref[:, 2 * kv * HD : (2 * kv + 1) * HD]) + dot(far.astype(BF), values)
        live = row_ids[:, :1] < own_len
        out_ref[at, lanes(out_head + h, HD)] = jnp.where(live, total / sums, 0.0).astype(BF)
        return carry

    lax.fori_loop(0, heads * (slab // tile), body, 0)


def anchor_part(lengths, ctx_q, states, own_k, own_v, anchor, first, count, per_kv, befores=None, after=()):
    slab, width = ctx_q.shape
    work = count * slab * slab
    last = befores is not None
    ends = {x: x + y.shape[1] // (2 * HD) for x, y in states.items()}
    bases = tuple(x for x in sorted(states) if x < first + count and ends[x] > first)
    earlier = list(befores.values()) if last else []
    places = tuple((at, x.shape[1] // HD) for at, x in befores.items()) if last else ()
    results = jax.ShapeDtypeStruct((slab, count * HD), BF)
    scratch = []
    if last:
        scratch = [pltpu.VMEM(results.shape, BF), pltpu.SemaphoreType.DMA((len(earlier) + count,))]
        results = jax.ShapeDtypeStruct((slab, width), BF)
    return pl.pallas_call(
        functools.partial(anchor_kernel, first, count, bases, per_kv, last, places),
        out_shape=results,
        in_specs=[SMEM] + [VMEM] * (5 + len(bases) + len(earlier)) + [ANY] * len(after),
        out_specs=ANY if last else VMEM,
        scratch_shapes=scratch,
        compiler_params=params(),
        cost_estimate=pl.CostEstimate(
            flops=work * HD * 8, bytes_accessed=count * slab * HD * 8, transcendentals=work
        ),
        name="context_anchor",
    )(lengths, ctx_q, own_k, own_v, *anchor, *[states[x] for x in bases], *earlier, *after)


PART = 16


def write_level(ref, width, level):
    lane = lax.broadcasted_iota(jnp.int32, level.shape, 1)
    parts = []
    for at in range(3):
        part = level.astype(BF).astype(F32)
        parts.append(part if at == 0 else pltpu.roll(part, at * PART, 1))
        level = level - part
    packed = jnp.where(lane < PART, parts[0], jnp.where(lane < 2 * PART, parts[1], parts[2]))
    ref[:, width : width + HD] = packed.astype(BF)


def read_level(ref, width):
    packed = ref[:, width : width + HD].astype(F32)
    return packed + pltpu.roll(packed, HD - PART, 1) + pltpu.roll(packed, HD - 2 * PART, 1)


def source_kernel(per_kv, q_rows, group_size, lengths_ref, k_ref, v_ref, self_ref, known_ref, landed_ref, *rest):
    keep_ref, send_ref, q_all, vaug = rest[-4:]
    slab, columns = v_ref.shape
    width = per_kv * columns
    query_count = 8 * q_rows
    block = 2 * q_rows
    host = lax.axis_index("hst")
    own_len = lengths_ref[host]
    rows = per_kv * query_count
    odd = bit(host, 0) == 1
    low = jnp.where(odd, bit(host, 1), bit(host, 2)) == 0

    def place(lower, upper, spread_out):
        middle = (2, 1) if spread_out else (1, 2)
        for ref, chips in ((lower, (0, middle[0])), (upper, (middle[1], 3))):
            for n, chip in enumerate(chips):
                for h in range(width // HD):
                    to = h * query_count + chip * block
                    q_all[to : to + block, :] = ref[n * block : (n + 1) * block, h * HD : (h + 1) * HD]

    for is_low, is_odd in ((False, False), (False, True), (True, False), (True, True)):
        @pl.when((low == is_low) & (odd == is_odd))
        def _():
            pair = (known_ref, landed_ref) if is_low else (landed_ref, known_ref)
            place(*pair, is_odd)

    first = lax.axis_index("tp") * (width // HD) // group_size * HD
    own_cols = pl.ds(pl.multiple_of(first, HD), columns)
    selves_kv = [self_ref[i, :, own_cols].astype(F32) for i in range(2)]
    lane = lax.broadcasted_iota(jnp.int32, (query_count, HD), 1)
    query_ids = lax.broadcasted_iota(jnp.int32, (query_count, HD), 0)
    self_ok = (host * q_rows + lane <= query_ids) & (lane < q_rows)
    self_ok = jnp.concatenate([self_ok] * per_kv, 0)
    pad = jnp.zeros((HD - q_rows, HD), F32)
    key_rows = lax.broadcasted_iota(jnp.int32, (slab, HD), 0)
    ones = jnp.where(key_rows < own_len, 1.0, 0.0).astype(BF)
    for j in range(columns // HD):
        values = v_ref[:, j * HD : (j + 1) * HD].astype(F32)
        vaug[:, 2 * j * HD : (2 * j + 1) * HD] = jnp.where(key_rows < own_len, values, 0.0).astype(BF)
        vaug[:, (2 * j + 1) * HD : (2 * j + 2) * HD] = ones

    def operands(j):
        cols = slice(j * HD, (j + 1) * HD)
        queries = q_all[j * rows : (j + 1) * rows, :]
        self_keys = jnp.concatenate([selves_kv[0][:, cols], pad], 0).astype(BF)
        self_values = jnp.concatenate([selves_kv[1][:, cols], pad], 0).astype(BF)
        near = dot(twice(queries), k_ref[2 * j * HD : 2 * (j + 1) * HD, :])
        selves = jnp.where(self_ok, dot_t(queries, self_keys) * SCALE2, MASKED)
        return near, selves, jnp.concatenate([self_values, jnp.ones((HD, HD), BF)], 1)

    def store(j, total, level):
        stats = jnp.zeros((query_count, HD), F32)
        for h in range(per_kv):
            stats = jnp.where(lane == h, level[h * query_count : (h + 1) * query_count, :], stats)

        def put(out_ref):
            def run():
                for h in range(per_kv):
                    part = total[h * query_count : (h + 1) * query_count, :]
                    out_ref[:, h * HD : (h + 1) * HD] = part.astype(BF)
                write_level(out_ref, per_kv * HD, stats)

            return run

        choose(odd if j else jnp.logical_not(odd), put(keep_ref), put(send_ref))

    worst = jnp.ones((rows, HD), F32)
    found = []
    for j in range(columns // HD):
        near, selves, self_values = operands(j)
        near = jnp.exp2(near).astype(BF)
        selves = jnp.exp2(selves).astype(BF)
        total = dot(near, vaug[:, 2 * j * HD : (2 * j + 2) * HD]) + dot(selves, self_values)
        sums = total[:, HD:]
        inverse = 1.0 / sums
        worst = jnp.minimum(worst, jnp.minimum(sums, inverse))
        found.append((total[:, :HD] * inverse, jnp.log2(sums)))
    for j, result in enumerate(found):
        store(j, *result)

    @pl.when(jnp.logical_not(jnp.min(worst) > TINY))
    def _():
        key_ids = lax.broadcasted_iota(jnp.int32, (query_count, slab), 1)
        heads_ok = (host * q_rows + lane <= query_ids) & (lane < q_rows)
        for j in range(columns // HD):
            cols = slice(j * HD, (j + 1) * HD)
            self_keys = jnp.concatenate([selves_kv[0][:, cols], pad], 0).astype(BF)
            self_values = jnp.concatenate([selves_kv[1][:, cols], pad], 0).astype(BF)
            self_values = jnp.concatenate([self_values, jnp.ones((HD, HD), BF)], 1)
            mine = odd if j else jnp.logical_not(odd)

            def body(h, stats):
                at = pl.ds(pl.multiple_of((j * per_kv + h) * query_count, query_count), query_count)
                queries = q_all[at, :]
                near = dot(twice(queries), k_ref[2 * j * HD : 2 * (j + 1) * HD, :])
                near = jnp.where(key_ids < own_len, near, MASKED)
                selves = jnp.where(heads_ok, dot_t(queries, self_keys) * SCALE2, MASKED)
                peak = jnp.maximum(jnp.max(near, 1, keepdims=True), jnp.max(selves, 1, keepdims=True))
                near = jnp.exp2(near - peak).astype(BF)
                selves = jnp.exp2(selves - peak).astype(BF)
                total = dot(near, vaug[:, 2 * j * HD : (2 * j + 2) * HD]) + dot(selves, self_values)
                result = (total[:, :HD] / total[:, HD:]).astype(BF)

                def put(out_ref):
                    def run():
                        out_ref[:, lanes(h, HD)] = result

                    return run

                choose(mine, put(keep_ref), put(send_ref))
                return jnp.where(lane == h, peak + jnp.log2(total[:, HD:]), stats)

            stats = lax.fori_loop(0, per_kv, body, jnp.zeros((query_count, HD), F32))

            def put_level(out_ref):
                def run():
                    write_level(out_ref, per_kv * HD, stats)

                return run

            choose(mine, put_level(keep_ref), put_level(send_ref))


def source_part(lengths, own_k, own_v, query_kv, known, landed, q_rows, per_kv, after=()):
    slab, columns = own_v.shape
    width = per_kv * columns
    count = 8 * q_rows
    work = count * (width // HD) * slab
    return pl.pallas_call(
        functools.partial(source_kernel, per_kv, q_rows, H // KVH),
        out_shape=[jax.ShapeDtypeStruct((count, (per_kv + 1) * HD), BF)] * 2,
        in_specs=[SMEM] + [VMEM] * 5 + [ANY] * len(after),
        out_specs=[VMEM] * 2,
        scratch_shapes=[pltpu.VMEM((count * width // HD, HD), BF), pltpu.VMEM((slab, 2 * columns), BF)],
        compiler_params=params(),
        cost_estimate=pl.CostEstimate(flops=work * HD * 8, bytes_accessed=2**21, transcendentals=work),
        name="query_source",
    )(lengths, own_k, own_v, query_kv, known, landed, *after)


def merged(refs, width):
    levels = [read_level(ref, width) for ref in refs]
    peak = jnp.maximum(*levels)
    weights = [jnp.exp2(x - peak) for x in levels]
    whole = weights[0] + weights[1]
    return [w / whole for w in weights], peak + jnp.log2(whole)


def blend(shares, refs, h):
    cols = slice(h * HD, (h + 1) * HD)
    return sum(w[:, h : h + 1] * ref[:, cols].astype(F32) for w, ref in zip(shares, refs))


def merge_part(one, two, last, after=()):
    rows, wide = one.shape
    width = wide - HD

    def kernel(one_ref, two_ref, *rest):
        out_ref = rest[-1]
        shares, level = merged((one_ref, two_ref), width)
        if not last:
            write_level(out_ref, width, level)
        for h in range(width // HD):
            out_ref[:, h * HD : (h + 1) * HD] = blend(shares, (one_ref, two_ref), h).astype(BF)

    return small_call(kernel, "query_merge", [(rows, width if last else wide)], (one, two), after)[0]


def project_part(own, other, out_weight, after=()):
    rows, half = own.shape
    depth, columns = out_weight.shape

    def kernel(w_ref, own_ref, other_ref, *rest):
        out_ref, attended = rest[-2:]

        def put(first, second):
            def run():
                attended[:, :half] = first[...]
                attended[:, half:] = second[...]

            return run

        even = bit(lax.axis_index("hst"), 0) == 0
        choose(even, put(own_ref, other_ref), put(other_ref, own_ref))
        out_ref[...] = dot(attended[...], w_ref[...]).astype(BF)

    return pl.pallas_call(
        kernel,
        out_shape=jax.ShapeDtypeStruct((rows, columns), BF),
        in_specs=[VMEM] * 3 + [ANY] * len(after),
        out_specs=VMEM,
        scratch_shapes=[pltpu.VMEM((rows, depth), BF)],
        compiler_params=params(),
        cost_estimate=pl.CostEstimate(
            flops=2 * rows * depth * columns, bytes_accessed=2 * depth * columns, transcendentals=0
        ),
        name="query_project",
    )(out_weight, own, other, *after)


def general_queries(lengths, own_k, own_v, self_kv, query_q, out_weight, per_kv):
    own_kv = jnp.stack([own_k, own_v], 0)
    host_id = lax.axis_index("hst")
    local_heads = query_q.shape[1] // HD
    kv_local = own_kv.shape[2] // HD
    slab_rows = own_kv.shape[1]
    own_len = lengths[host_id]
    row_ids = jnp.arange(slab_rows)
    all_queries = lax.all_gather(query_q, "hst", axis=0, tiled=True)
    query_count = all_queries.shape[0]
    q_rows = query_q.shape[0]
    source = jnp.concatenate([own_kv, self_kv], 1)
    source = source.reshape(2, slab_rows + q_rows, kv_local, HD).transpose(0, 2, 1, 3)
    query_ids = jnp.arange(query_count)
    context_ok = jnp.broadcast_to(row_ids[None, :] < own_len, (query_count, slab_rows))
    self_ok = (host_id * q_rows + jnp.arange(q_rows))[None, :] <= query_ids[:, None]
    seen_ok = jnp.concatenate([context_ok, self_ok], 1)
    query_heads = all_queries.reshape(query_count, local_heads, HD).transpose(1, 0, 2)

    def score_head(operands):
        query_rows, head_index = operands
        kv_index = head_index // per_kv
        scores = dot_t(query_rows, source[0, kv_index]) * HD ** (-0.5)
        scores = jnp.where(seen_ok, scores, MASKED)
        peak = jnp.max(scores, axis=1)
        expo = jnp.exp(scores - peak[:, None])
        return peak, jnp.sum(expo, axis=1), dot(expo.astype(BF), source[1, kv_index])

    maxima, totals, outputs = lax.map(score_head, (query_heads, jnp.arange(local_heads)))
    factor = jnp.exp(maxima - lax.pmax(maxima, "hst"))
    denominator, summed = lax.psum((totals * factor, outputs * factor[..., None]), "hst")
    attended = (summed / denominator[..., None]).astype(BF)
    attended = attended.transpose(1, 0, 2).reshape(query_count, local_heads * HD)
    return lax.psum(dot(attended, out_weight), "tp").astype(BF)


def per_device(hosts, groups, ctx_q, ctx_kv, lengths, query_q, query_kv, out_weight):
    slab = ctx_q.shape[0]
    local_heads = ctx_q.shape[1] // HD
    group_size = H // KVH
    kv_local = max(1, local_heads // group_size)
    per_kv = min(local_heads, group_size)
    q_rows = query_q.shape[0]
    host = lax.axis_index("hst")
    fast = hosts == 8 and groups & (groups - 1) == 0
    fast = fast and q_rows == 8 and local_heads == 16 and per_kv == 8

    if not fast:
        kv_first = lax.axis_index("tp") * local_heads // group_size
        self_kv = lax.dynamic_slice_in_dim(query_kv, kv_first * HD, kv_local * HD, 2)
        own_k, own_v = pick(ctx_kv, kv_local, local_heads)
        query_out = general_queries(lengths, own_k, own_v, self_kv, query_q, out_weight, per_kv)
        k, v = spread(jnp.stack([own_k, own_v]), "hst", 0)
        own_k, own_v = prepare(own_k, own_v, False)
        anchor = prepare(k, v, False)
        state = own_part(ctx_q, own_k, own_v, 0, local_heads, per_kv)
        results = {}
        for first in range(0, local_heads, per_kv):
            cols = slice(2 * first // per_kv * HD, 2 * (first // per_kv + 1) * HD)
            last = first + per_kv == local_heads
            results[first] = anchor_part(
                lengths, ctx_q, {0: state}, own_k, own_v, (anchor[0][cols, :], anchor[1][:, cols]),
                first, per_kv, per_kv, dict(results) if last else None,
            )
        return results[first], query_out

    states = {}

    def own(first, count, after=()):
        states[first] = own_part(ctx_q, own_keys, own_values, first, count, per_kv, after)
        return states[first]

    along = ((2, 4), (4, 2))

    def is_even(h):
        return bit(h, 0) == 0

    def source_first(h):
        return h < 2

    def done_early(h):
        return (h <= 2) | (h == 5)

    def near_low(h):
        return jnp.where(bit(h, 0) == 1, bit(h, 2), bit(h, 1)) == 0

    landed = swap(query_q, "hst", hosts, 1, 1)
    own_k, own_v = pick(ctx_kv, kv_local, local_heads)
    value_landed = swap(own_v, "hst", hosts, 1, 1)
    own_keys, own_values = prepare(own_k, own_v, False)
    queries = join(is_even, query_q, landed, (own_keys,))
    landed = swap(queries, "hst", hosts, *along[0])
    done = own(0, 2, (queries,))
    parts = list(relay(is_even, own_k, value_landed, (done,), kv_local))
    parts_landed = [swap(x, "hst", hosts, *along[0]) for x in parts]
    queries = join(near_low, queries, landed, (parts[0],))
    landed = swap(queries, "hst", hosts, *along[1])
    done = own(2, 6, (queries,))
    anchor = {}

    def pass_on(kv, after):
        (parts[kv],) = relay(source_first, parts[kv], parts_landed[kv], after)
        parts_landed[kv] = swap(parts[kv], "hst", hosts, *along[1])
        return parts[kv]

    def complete(kv, after):
        (held,) = relay(done_early, parts[kv], parts_landed[kv], after)
        anchor[kv] = held, swap(held, "hst", hosts, 1, 1)
        return held

    done = pass_on(0, (done,))
    keep, give = source_part(lengths, own_keys, own_v, query_kv, queries, landed, q_rows, per_kv, (done,))
    landed = swap(give, "hst", hosts, 1, 1)
    done = own(8, 4, (keep,))
    done = pass_on(1, (done,))
    done = complete(0, (done,))
    source = merge_part(keep, landed, False, (done,))
    landed = swap(source, "hst", hosts, *along[0])
    done = own(12, 4, (source,))
    anchor[0] = prepare(*anchor[0], True, (done,))
    results = {}

    def anchors(first, count, after, last=False):
        results[first] = anchor_part(
            lengths, ctx_q, states, own_keys, own_values, anchor[first // per_kv],
            first, count, per_kv, dict(results) if last else None, after,
        )
        return results[first]

    done = anchors(0, 2, ())
    source = merge_part(source, landed, False, (done,))
    landed = swap(source, "hst", hosts, *along[1])
    done = anchors(2, 4, (source,))
    source = merge_part(source, landed, True, (done,))
    landed = swap(source, "hst", hosts, 1, 1)
    done = complete(1, (source,))
    done = anchors(6, 2, (done,))
    terms = project_part(source, landed, out_weight, (done,))
    anchor[1] = prepare(*anchor[1], True, (terms,))
    shares = [[(12, 4, True)], [(8, 4, False)]]
    step = 1
    while step < groups:
        landed = swap(terms, "tp", groups, step, step)
        last = False
        done = terms
        for first, count, last in shares.pop() if shares else ():
            done = anchors(first, count, (terms, done), last)
        terms = add_part(terms, landed, () if last else (done,))
        step *= 2
    for group in reversed(shares):
        for first, count, last in group:
            done = anchors(first, count, (), last)
    return done, terms


def solution(mesh):
    hosts, groups = mesh.shape["hst"], mesh.shape["tp"]
    return jax.shard_map(
        functools.partial(per_device, hosts, groups),
        mesh=mesh,
        in_specs=(
            P("hst", "tp"),
            P(None, "hst", None),
            P(),
            P("hst", "tp"),
            P(None, "hst", None),
            P("tp", "hst"),
        ),
        out_specs=(P("hst", "tp"), P(None, "hst")),
        check_vma=False,
    )
```

```python
import functools

import jax
import jax.numpy as jnp
from jax import lax
from jax.experimental import pallas as pl
from jax.experimental.pallas import tpu as pltpu
from jax.sharding import PartitionSpec as P

H = 64
KVH = 8
HD = 128
MASKED = -1e30
LOG2E = 1.4426950408889634
SCALE2 = HD ** (-0.5) * LOG2E
TINY = 2.0 ** -90
BF = jnp.bfloat16
F32 = jnp.float32
VMEM = pl.BlockSpec(memory_space=pltpu.VMEM)
ANY = pl.BlockSpec(memory_space=pl.ANY)
HBM = pl.BlockSpec(memory_space=pltpu.HBM)


def params(mib=20):
    return pltpu.CompilerParams(vmem_limit_bytes=mib * 2**20)


def dot_t(a, b):
    return lax.dot_general(a, b, (((1,), (1,)), ((), ())), preferred_element_type=F32)


def dot(a, b):
    return lax.dot_general(a, b, (((1,), (0,)), ((), ())), preferred_element_type=F32)


def spread(value, axis, source):
    kept = jnp.where(lax.axis_index(axis) == source, value, 0).astype(value.dtype)
    return lax.psum(kept, axis)


def swap(value, axis, size, even, odd):
    return lax.ppermute(value, axis, [(i, i ^ (odd if i & 1 else even)) for i in range(size)])


def pick_kernel(group_size, local_heads, kv_ref, k_ref, v_ref, sems):
    first = lax.axis_index("tp") * local_heads // group_size * HD
    cols = pl.ds(pl.multiple_of(first, HD), k_ref.shape[1])
    moves = [
        pltpu.make_async_copy(kv_ref.at[1, :, cols], v_ref, sems.at[1]),
        pltpu.make_async_copy(kv_ref.at[0, :, cols], k_ref, sems.at[0]),
    ]
    for move in moves:
        move.start()
    for move in moves:
        move.wait()


def pick(ctx_kv, kv_local, local_heads):
    return pl.pallas_call(
        functools.partial(pick_kernel, H // KVH, local_heads),
        out_shape=[jax.ShapeDtypeStruct((ctx_kv.shape[1], kv_local * HD), BF)] * 2,
        in_specs=[HBM],
        out_specs=[VMEM] * 2,
        scratch_shapes=[pltpu.SemaphoreType.DMA((2,))],
        compiler_params=params(52),
        cost_estimate=pl.CostEstimate(flops=0, bytes_accessed=2**22, transcendentals=0),
        name="pick_columns",
    )(ctx_kv)


def bit(value, at):
    return (value >> at) & 1


def small_call(kernel, name, shapes, inputs, after=()):
    return pl.pallas_call(
        kernel,
        out_shape=[jax.ShapeDtypeStruct(x, BF) for x in shapes],
        in_specs=[VMEM] * len(inputs) + [ANY] * len(after),
        out_specs=[VMEM] * len(shapes),
        compiler_params=params(),
        cost_estimate=pl.CostEstimate(flops=0, bytes_accessed=2**20, transcendentals=0),
        name=name,
    )(*inputs, *after)


def choose(condition, one, two):
    pl.when(condition)(one)
    pl.when(jnp.logical_not(condition))(two)


def take_rows(target, source, rows, cols=slice(None)):
    def run():
        target[:rows, :] = source[:rows, cols]

    return run


def join(low_of, known, landed, after=()):
    rows, width = known.shape

    def kernel(known_ref, landed_ref, *rest):
        out_ref = rest[-1]

        def put(first, second):
            def run():
                both = jnp.concatenate([first[...].astype(F32), second[...].astype(F32)], 0)
                out_ref[...] = both.astype(BF)

            return run

        choose(low_of(lax.axis_index("hst")), put(known_ref, landed_ref), put(landed_ref, known_ref))

    return small_call(kernel, "query_join", [(2 * rows, width)], (known, landed), after)[0]


def relay(keep_of, one, two, after=(), split=1):
    slab, columns = one.shape
    width = columns // split

    def kernel(one_ref, two_ref, *rest):
        keep = keep_of(lax.axis_index("hst"))
        for j, out_ref in enumerate(rest[-split:]):
            cols = slice(j * width, (j + 1) * width)
            choose(keep, take_rows(out_ref, one_ref, slab, cols), take_rows(out_ref, two_ref, slab, cols))

    return small_call(kernel, "anchor_relay", [(slab, width)] * split, (one, two), after)


def add_part(one, two, after=()):
    def kernel(one_ref, two_ref, *rest):
        rest[-1][...] = (one_ref[...].astype(F32) + two_ref[...].astype(F32)).astype(BF)

    return small_call(kernel, "query_sum", [one.shape], (one, two), after)[0]


def prepare(first, second, swapped, after=()):
    slab, columns = first.shape

    def kernel(first_ref, second_ref, *rest):
        keys_ref, values_ref = rest[-2:]

        def fill(k_ref, v_ref):
            def run():
                for j in range(columns // HD):
                    cols = slice(j * HD, (j + 1) * HD)
                    at = 2 * j * HD
                    scaled = k_ref[:, cols].astype(F32) * SCALE2
                    high = scaled.astype(BF)
                    low = scaled - high.astype(F32)
                    keys_ref[at : at + HD, :] = high.astype(F32).T.astype(BF)
                    keys_ref[at + HD : at + 2 * HD, :] = low.T.astype(BF)
                    values_ref[:, at : at + HD] = v_ref[:, cols]
                    values_ref[:, at + HD : at + 2 * HD] = jnp.ones((slab, HD), BF)

            return run

        if swapped:
            even = bit(lax.axis_index("hst"), 0) == 0
            choose(even, fill(first_ref, second_ref), fill(second_ref, first_ref))
        else:
            fill(first_ref, second_ref)()

    shapes = [(2 * columns, slab), (slab, 2 * columns)]
    return small_call(kernel, "operands", shapes, (first, second), after)


def twice(query):
    return jnp.concatenate([query, query], 1)


def lanes(index, width):
    return pl.ds(pl.multiple_of(index * width, width), width)


def row_tile(slab):
    return 256 if slab % 256 == 0 else slab


def body_size(first, count, per_kv, most):
    def fits(size):
        bodies = range(first, first + count, size)
        return count % size == 0 and all(x // per_kv == (x + size - 1) // per_kv for x in bodies)

    return max(x for x in range(1, most + 1) if fits(x))


def own_kernel(first, count, per_kv, q_ref, k_ref, v_ref, *rest):
    state_ref = rest[-1]
    slab = q_ref.shape[0]
    tile = row_tile(slab)
    half = tile // 2
    heads = body_size(first, count, per_kv, 4)
    rows = lax.broadcasted_iota(jnp.int32, (half, half), 0)
    cols = lax.broadcasted_iota(jnp.int32, (half, half), 1)
    causal = cols <= rows
    chunks = slab // tile
    units = [(h, j) for h in range(heads) for j in range(chunks)]

    def body(i, carry):
        kv = lax.div(first + i * heads, per_kv)

        def scores(at):
            h, j = units[at]
            query = q_ref[j * tile :, lanes(first + i * heads + h, HD)]
            return dot(twice(query), k_ref[lanes(kv, 2 * HD), j * tile : (j + 1) * tile])

        def power(x):
            return jnp.exp2(x).astype(BF)

        def corner(x):
            return jnp.where(causal, jnp.exp2(x), 0.0).astype(BF)

        current = scores(0)
        totals = [None] * chunks
        for at, (h, j) in enumerate(units):
            following = scores(at + 1) if at + 1 < len(units) else None
            top = jnp.concatenate([corner(current[:half, :half]), jnp.zeros((half, half), BF)], 1)
            low = jnp.concatenate([power(current[half:tile, :half]), corner(current[half:tile, half:])], 1)
            expo = [top, low] if j == chunks - 1 else [top, low, power(current[tile:])]
            part = dot(jnp.concatenate(expo, 0), v_ref[j * tile : (j + 1) * tile, lanes(kv, 2 * HD)])
            for r in range(j, chunks):
                piece = part[(r - j) * tile : (r - j + 1) * tile]
                totals[r] = piece if j == 0 else totals[r] + piece
            state_ref[j * tile : (j + 1) * tile, lanes(i * heads + h, 2 * HD)] = totals[j]
            current = following
        return carry

    lax.fori_loop(0, count // heads, body, 0)


def own_part(ctx_q, own_k, own_v, first, count, per_kv, after=()):
    slab = ctx_q.shape[0]
    work = count * slab * (slab + row_tile(slab)) // 2
    return pl.pallas_call(
        functools.partial(own_kernel, first, count, per_kv),
        out_shape=jax.ShapeDtypeStruct((slab, count * 2 * HD), F32),
        in_specs=[VMEM] * 3 + [ANY] * len(after),
        out_specs=VMEM,
        compiler_params=params(),
        cost_estimate=pl.CostEstimate(
            flops=work * HD * 8, bytes_accessed=count * slab * HD * 6, transcendentals=work
        ),
        name="context_own",
    )(ctx_q, own_k, own_v, *after)


def length_of(lengths_ref, host):
    lengths = lengths_ref[...]
    index = lax.broadcasted_iota(jnp.int32, lengths.shape, 1)
    return jnp.sum(jnp.where(index == host, lengths, 0), axis=1, keepdims=True)


def anchor_kernel(first, count, bases, per_kv, last, befores, *refs):
    lengths_ref, q_ref, k_ref, v_ref, keys, vaug = refs[:6]
    hosts = lengths_ref.shape[1]
    state_refs = refs[6 : 6 + len(bases)]
    earlier = refs[6 + len(bases) : 6 + len(bases) + len(befores)]
    if last:
        full_ref, out_ref, sems = refs[-3:]
    else:
        out_ref = refs[-1]
    slab = q_ref.shape[0]
    heads = body_size(first, count, per_kv, 2 if last else 4)
    kv = first // per_kv
    host = lax.axis_index("hst")

    def hand_over(source, start, width, sem):
        target = full_ref.at[:, pl.ds(start * HD, width * HD)]
        return pltpu.make_async_copy(source, target, sems.at[sem])

    moves = [hand_over(earlier[n], *place, n) for n, place in enumerate(befores)]
    for move in moves:
        move.start()

    def part(start):
        def query_of(h):
            at = (first + start + h) * HD
            return q_ref[:, at : at + HD]

        def scores(h):
            return dot(twice(query_of(h)), keys[...])

        def state_of(h):
            head = first + start + h
            n = max(n for n, base in enumerate(bases) if base <= head)
            at = (head - bases[n]) * 2 * HD
            return state_refs[n][:, at : at + 2 * HD]

        def finish(h, total, sums, worst):
            inverse = pl.reciprocal(sums, approx=True)
            out_ref[:, (start + h) * HD : (start + h + 1) * HD] = (total * inverse).astype(BF)
            return jnp.minimum(worst, jnp.minimum(sums, inverse))

        def check(worst):
            @pl.when(jnp.logical_not(jnp.min(worst) > TINY))
            def _():
                exact_block(first + start, start, heads, host, kv, q_ref, k_ref, v_ref, keys, vaug, out_ref)

        @pl.when(host == 0)
        def _():
            worst = jnp.ones((slab, HD), F32)
            for h in range(heads):
                state = state_of(h)
                worst = finish(h, state[:, :HD], state[:, HD:], worst)
            check(worst)

        @pl.when(host > 0)
        def _():
            worst = jnp.ones((slab, HD), F32)
            current = scores(0)
            for h in range(heads):
                following = scores(h + 1) if h + 1 < heads else None
                expo = jnp.exp2(current)
                state = state_of(h)
                total = dot(expo.astype(BF), vaug[:, :HD]) + state[:, :HD]
                sums = jnp.sum(expo, axis=1, keepdims=True) + state[:, HD:]
                worst = finish(h, total, sums, worst)
                current = following
            check(worst)

        @pl.when(host * 4 >= hosts * 3)
        def _():
            own_len = length_of(lengths_ref, host)
            row_ids = lax.broadcasted_iota(jnp.int32, (slab, HD), 0)
            for h in range(start, start + heads):
                cols = slice(h * HD, (h + 1) * HD)
                kept = jnp.where(row_ids < own_len, out_ref[:, cols].astype(F32), 0.0)
                out_ref[:, cols] = kept.astype(BF)

        if last:
            source = out_ref.at[:, start * HD : (start + heads) * HD]
            move = hand_over(source, first + start, heads, len(befores) + start // heads)
            move.start()
            moves.append(move)

    for start in range(0, count, heads):
        part(start)
    for move in moves:
        move.wait()


def exact_block(q_head, out_head, heads, host, kv, q_ref, k_ref, v_ref, keys, vaug, out_ref):
    slab = q_ref.shape[0]
    tile = 64

    def body(i, carry):
        h = lax.div(i, slab // tile)
        r = lax.rem(i, slab // tile)
        at = pl.ds(pl.multiple_of(r * tile, tile), tile)
        query = q_ref[at, lanes(q_head + h, HD)]
        row_ids = lax.broadcasted_iota(jnp.int32, (tile, slab), 0) + r * tile
        key_ids = lax.broadcasted_iota(jnp.int32, (tile, slab), 1)
        own = dot(twice(query), k_ref[2 * kv * HD : 2 * (kv + 1) * HD, :])
        own = jnp.where(key_ids <= row_ids, own, MASKED)
        far = dot(twice(query), keys[...])
        far = jnp.where(host > 0, far, MASKED)
        peak = jnp.maximum(jnp.max(own, 1, keepdims=True), jnp.max(far, 1, keepdims=True))
        own = jnp.exp2(own - peak)
        far = jnp.where(host > 0, jnp.exp2(far - peak), 0.0)
        sums = jnp.sum(own, 1, keepdims=True) + jnp.sum(far, 1, keepdims=True)
        values = jnp.where(host > 0, vaug[:, :HD].astype(F32), 0.0).astype(BF)
        total = dot(own.astype(BF), v_ref[:, 2 * kv * HD : (2 * kv + 1) * HD]) + dot(far.astype(BF), values)
        out_ref[at, lanes(out_head + h, HD)] = (total / sums).astype(BF)
        return carry

    lax.fori_loop(0, heads * (slab // tile), body, 0)


def anchor_part(lengths, ctx_q, states, own_k, own_v, anchor, first, count, per_kv, befores=None, after=()):
    slab, width = ctx_q.shape
    work = count * slab * slab
    last = befores is not None
    ends = {x: x + y.shape[1] // (2 * HD) for x, y in states.items()}
    bases = tuple(x for x in sorted(states) if x < first + count and ends[x] > first)
    earlier = list(befores.values()) if last else []
    places = tuple((at, x.shape[1] // HD) for at, x in befores.items()) if last else ()
    results = jax.ShapeDtypeStruct((slab, count * HD), BF)
    scratch = []
    if last:
        scratch = [pltpu.VMEM(results.shape, BF), pltpu.SemaphoreType.DMA((len(earlier) + count,))]
        results = jax.ShapeDtypeStruct((slab, width), BF)
    return pl.pallas_call(
        functools.partial(anchor_kernel, first, count, bases, per_kv, last, places),
        out_shape=results,
        in_specs=[VMEM] * (6 + len(bases) + len(earlier)) + [ANY] * len(after),
        out_specs=ANY if last else VMEM,
        scratch_shapes=scratch,
        compiler_params=params(),
        cost_estimate=pl.CostEstimate(
            flops=work * HD * 8, bytes_accessed=count * slab * HD * 8, transcendentals=work
        ),
        name="context_anchor",
    )(lengths, ctx_q, own_k, own_v, *anchor, *[states[x] for x in bases], *earlier, *after)


PART = 16


def write_level(ref, width, level):
    lane = lax.broadcasted_iota(jnp.int32, level.shape, 1)
    parts = []
    for at in range(3):
        part = level.astype(BF).astype(F32)
        parts.append(part if at == 0 else pltpu.roll(part, at * PART, 1))
        level = level - part
    packed = jnp.where(lane < PART, parts[0], jnp.where(lane < 2 * PART, parts[1], parts[2]))
    ref[:, width : width + HD] = packed.astype(BF)


def read_level(ref, width):
    packed = ref[:, width : width + HD].astype(F32)
    return packed + pltpu.roll(packed, HD - PART, 1) + pltpu.roll(packed, HD - 2 * PART, 1)


def source_kernel(per_kv, q_rows, group_size, lengths_ref, k_ref, v_ref, self_ref, known_ref, landed_ref, *rest):
    keep_ref, send_ref, q_all, vaug = rest[-4:]
    slab, columns = v_ref.shape
    width = per_kv * columns
    query_count = 8 * q_rows
    block = 2 * q_rows
    host = lax.axis_index("hst")
    own_len = length_of(lengths_ref, host)
    rows = per_kv * query_count
    odd = bit(host, 0) == 1
    low = jnp.where(odd, bit(host, 1), bit(host, 2)) == 0

    def place(lower, upper, spread_out):
        middle = (2, 1) if spread_out else (1, 2)
        for ref, chips in ((lower, (0, middle[0])), (upper, (middle[1], 3))):
            for n, chip in enumerate(chips):
                for h in range(width // HD):
                    to = h * query_count + chip * block
                    q_all[to : to + block, :] = ref[n * block : (n + 1) * block, h * HD : (h + 1) * HD]

    for is_low, is_odd in ((False, False), (False, True), (True, False), (True, True)):
        @pl.when((low == is_low) & (odd == is_odd))
        def _():
            pair = (known_ref, landed_ref) if is_low else (landed_ref, known_ref)
            place(*pair, is_odd)

    first = lax.axis_index("tp") * (width // HD) // group_size * HD
    own_cols = pl.ds(pl.multiple_of(first, HD), columns)
    selves_kv = [self_ref[i, :, own_cols].astype(F32) for i in range(2)]
    lane = lax.broadcasted_iota(jnp.int32, (query_count, HD), 1)
    query_ids = lax.broadcasted_iota(jnp.int32, (query_count, HD), 0)
    self_ok = (host * q_rows + lane <= query_ids) & (lane < q_rows)
    self_ok = jnp.concatenate([self_ok] * per_kv, 0)
    pad = jnp.zeros((HD - q_rows, HD), F32)
    key_rows = lax.broadcasted_iota(jnp.int32, (slab, HD), 0)
    ones = jnp.where(key_rows < own_len, 1.0, 0.0).astype(BF)
    for j in range(columns // HD):
        values = v_ref[:, j * HD : (j + 1) * HD].astype(F32)
        vaug[:, 2 * j * HD : (2 * j + 1) * HD] = jnp.where(key_rows < own_len, values, 0.0).astype(BF)
        vaug[:, (2 * j + 1) * HD : (2 * j + 2) * HD] = ones

    def operands(j):
        cols = slice(j * HD, (j + 1) * HD)
        queries = q_all[j * rows : (j + 1) * rows, :]
        self_keys = jnp.concatenate([selves_kv[0][:, cols], pad], 0).astype(BF)
        self_values = jnp.concatenate([selves_kv[1][:, cols], pad], 0).astype(BF)
        near = dot(twice(queries), k_ref[2 * j * HD : 2 * (j + 1) * HD, :])
        selves = jnp.where(self_ok, dot_t(queries, self_keys) * SCALE2, MASKED)
        return near, selves, jnp.concatenate([self_values, jnp.ones((HD, HD), BF)], 1)

    def store(j, total, level):
        stats = jnp.zeros((query_count, HD), F32)
        for h in range(per_kv):
            stats = jnp.where(lane == h, level[h * query_count : (h + 1) * query_count, :], stats)

        def put(out_ref):
            def run():
                for h in range(per_kv):
                    part = total[h * query_count : (h + 1) * query_count, :]
                    out_ref[:, h * HD : (h + 1) * HD] = part.astype(BF)
                write_level(out_ref, per_kv * HD, stats)

            return run

        choose(odd if j else jnp.logical_not(odd), put(keep_ref), put(send_ref))

    worst = jnp.ones((rows, HD), F32)
    found = []
    for j in range(columns // HD):
        near, selves, self_values = operands(j)
        near = jnp.exp2(near).astype(BF)
        selves = jnp.exp2(selves).astype(BF)
        total = dot(near, vaug[:, 2 * j * HD : (2 * j + 2) * HD]) + dot(selves, self_values)
        sums = total[:, HD:]
        inverse = 1.0 / sums
        worst = jnp.minimum(worst, jnp.minimum(sums, inverse))
        found.append((total[:, :HD] * inverse, jnp.log2(sums)))
    for j, result in enumerate(found):
        store(j, *result)

    @pl.when(jnp.logical_not(jnp.min(worst) > TINY))
    def _():
        key_ids = lax.broadcasted_iota(jnp.int32, (query_count, slab), 1)
        heads_ok = (host * q_rows + lane <= query_ids) & (lane < q_rows)
        for j in range(columns // HD):
            cols = slice(j * HD, (j + 1) * HD)
            self_keys = jnp.concatenate([selves_kv[0][:, cols], pad], 0).astype(BF)
            self_values = jnp.concatenate([selves_kv[1][:, cols], pad], 0).astype(BF)
            self_values = jnp.concatenate([self_values, jnp.ones((HD, HD), BF)], 1)
            mine = odd if j else jnp.logical_not(odd)

            def body(h, stats):
                at = pl.ds(pl.multiple_of((j * per_kv + h) * query_count, query_count), query_count)
                queries = q_all[at, :]
                near = dot(twice(queries), k_ref[2 * j * HD : 2 * (j + 1) * HD, :])
                near = jnp.where(key_ids < own_len, near, MASKED)
                selves = jnp.where(heads_ok, dot_t(queries, self_keys) * SCALE2, MASKED)
                peak = jnp.maximum(jnp.max(near, 1, keepdims=True), jnp.max(selves, 1, keepdims=True))
                near = jnp.exp2(near - peak).astype(BF)
                selves = jnp.exp2(selves - peak).astype(BF)
                total = dot(near, vaug[:, 2 * j * HD : (2 * j + 2) * HD]) + dot(selves, self_values)
                result = (total[:, :HD] / total[:, HD:]).astype(BF)

                def put(out_ref):
                    def run():
                        out_ref[:, lanes(h, HD)] = result

                    return run

                choose(mine, put(keep_ref), put(send_ref))
                return jnp.where(lane == h, peak + jnp.log2(total[:, HD:]), stats)

            stats = lax.fori_loop(0, per_kv, body, jnp.zeros((query_count, HD), F32))

            def put_level(out_ref):
                def run():
                    write_level(out_ref, per_kv * HD, stats)

                return run

            choose(mine, put_level(keep_ref), put_level(send_ref))


def source_part(lengths, own_k, own_v, query_kv, known, landed, q_rows, per_kv, after=()):
    slab, columns = own_v.shape
    width = per_kv * columns
    count = 8 * q_rows
    work = count * (width // HD) * slab
    return pl.pallas_call(
        functools.partial(source_kernel, per_kv, q_rows, H // KVH),
        out_shape=[jax.ShapeDtypeStruct((count, (per_kv + 1) * HD), BF)] * 2,
        in_specs=[VMEM] * 6 + [ANY] * len(after),
        out_specs=[VMEM] * 2,
        scratch_shapes=[pltpu.VMEM((count * width // HD, HD), BF), pltpu.VMEM((slab, 2 * columns), BF)],
        compiler_params=params(),
        cost_estimate=pl.CostEstimate(flops=work * HD * 8, bytes_accessed=2**21, transcendentals=work),
        name="query_source",
    )(lengths, own_k, own_v, query_kv, known, landed, *after)


def merge_part(groups, last, after=()):
    rows, wide = groups[0].shape
    width = wide - HD

    def kernel(*refs):
        in_refs, out_ref = refs[: len(groups)], refs[-1]
        levels = [read_level(ref, width) for ref in in_refs]
        peak = functools.reduce(jnp.maximum, levels)
        weights = [jnp.exp2(x - peak) for x in levels]
        whole = functools.reduce(jnp.add, weights)
        shares = [w / whole for w in weights]
        if not last:
            write_level(out_ref, width, peak + jnp.log2(whole))
        for h in range(width // HD):
            cols = slice(h * HD, (h + 1) * HD)
            total = sum(w[:, h : h + 1] * ref[:, cols].astype(F32) for w, ref in zip(shares, in_refs))
            out_ref[:, cols] = total.astype(BF)

    return small_call(kernel, "query_merge", [(rows, width if last else wide)], groups, after)[0]


def project_part(own, other, out_weight, after=()):
    rows, half = own.shape
    depth, columns = out_weight.shape

    def kernel(w_ref, own_ref, other_ref, *rest):
        out_ref, attended = rest[-2:]

        def put(first, second):
            def run():
                attended[:, :half] = first[...]
                attended[:, half:] = second[...]

            return run

        even = bit(lax.axis_index("hst"), 0) == 0
        choose(even, put(own_ref, other_ref), put(other_ref, own_ref))
        out_ref[...] = dot(attended[...], w_ref[...]).astype(BF)

    return pl.pallas_call(
        kernel,
        out_shape=jax.ShapeDtypeStruct((rows, columns), BF),
        in_specs=[VMEM] * 3 + [ANY] * len(after),
        out_specs=VMEM,
        scratch_shapes=[pltpu.VMEM((rows, depth), BF)],
        compiler_params=params(),
        cost_estimate=pl.CostEstimate(
            flops=2 * rows * depth * columns, bytes_accessed=2 * depth * columns, transcendentals=0
        ),
        name="query_project",
    )(out_weight, own, other, *after)


def general_queries(lengths, own_k, own_v, self_kv, query_q, out_weight, per_kv):
    own_kv = jnp.stack([own_k, own_v], 0)
    host_id = lax.axis_index("hst")
    local_heads = query_q.shape[1] // HD
    kv_local = own_kv.shape[2] // HD
    slab_rows = own_kv.shape[1]
    own_len = lengths[host_id]
    row_ids = jnp.arange(slab_rows)
    all_queries = lax.all_gather(query_q, "hst", axis=0, tiled=True)
    query_count = all_queries.shape[0]
    q_rows = query_q.shape[0]
    source = jnp.concatenate([own_kv, self_kv], 1)
    source = source.reshape(2, slab_rows + q_rows, kv_local, HD).transpose(0, 2, 1, 3)
    query_ids = jnp.arange(query_count)
    context_ok = jnp.broadcast_to(row_ids[None, :] < own_len, (query_count, slab_rows))
    self_ok = (host_id * q_rows + jnp.arange(q_rows))[None, :] <= query_ids[:, None]
    seen_ok = jnp.concatenate([context_ok, self_ok], 1)
    query_heads = all_queries.reshape(query_count, local_heads, HD).transpose(1, 0, 2)

    def score_head(operands):
        query_rows, head_index = operands
        kv_index = head_index // per_kv
        scores = dot_t(query_rows, source[0, kv_index]) * HD ** (-0.5)
        scores = jnp.where(seen_ok, scores, MASKED)
        peak = jnp.max(scores, axis=1)
        expo = jnp.exp(scores - peak[:, None])
        return peak, jnp.sum(expo, axis=1), dot(expo.astype(BF), source[1, kv_index])

    maxima, totals, outputs = lax.map(score_head, (query_heads, jnp.arange(local_heads)))
    factor = jnp.exp(maxima - lax.pmax(maxima, "hst"))
    denominator, summed = lax.psum((totals * factor, outputs * factor[..., None]), "hst")
    attended = (summed / denominator[..., None]).astype(BF)
    attended = attended.transpose(1, 0, 2).reshape(query_count, local_heads * HD)
    return lax.psum(dot(attended, out_weight), "tp").astype(BF)


def per_device(hosts, groups, ctx_q, ctx_kv, lengths, query_q, query_kv, out_weight):
    slab = ctx_q.shape[0]
    local_heads = ctx_q.shape[1] // HD
    group_size = H // KVH
    kv_local = max(1, local_heads // group_size)
    per_kv = min(local_heads, group_size)
    q_rows = query_q.shape[0]
    host = lax.axis_index("hst")
    fast = hosts == 8 and groups & (groups - 1) == 0
    fast = fast and q_rows == 8 and local_heads == 16 and per_kv == 8

    if not fast:
        kv_first = lax.axis_index("tp") * local_heads // group_size
        self_kv = lax.dynamic_slice_in_dim(query_kv, kv_first * HD, kv_local * HD, 2)
        own_k, own_v = pick(ctx_kv, kv_local, local_heads)
        query_out = general_queries(lengths, own_k, own_v, self_kv, query_q, out_weight, per_kv)
        k, v = spread(jnp.stack([own_k, own_v]), "hst", 0)
        lengths = lengths.reshape(1, hosts)
        own_k, own_v = prepare(own_k, own_v, False)
        anchor = prepare(k, v, False)
        state = own_part(ctx_q, own_k, own_v, 0, local_heads, per_kv)
        results = {}
        for first in range(0, local_heads, per_kv):
            cols = slice(2 * first // per_kv * HD, 2 * (first // per_kv + 1) * HD)
            last = first + per_kv == local_heads
            results[first] = anchor_part(
                lengths, ctx_q, {0: state}, own_k, own_v, (anchor[0][cols, :], anchor[1][:, cols]),
                first, per_kv, per_kv, dict(results) if last else None,
            )
        return results[first], query_out

    lengths = lengths.reshape(1, hosts)
    states = {}

    def own(first, count, after=()):
        states[first] = own_part(ctx_q, own_keys, own_values, first, count, per_kv, after)
        return states[first]

    along = ((2, 4), (4, 2))

    def is_even(h):
        return bit(h, 0) == 0

    def source_first(h):
        return h < 2

    def done_early(h):
        return (h <= 2) | (h == 5)

    def near_low(h):
        return jnp.where(bit(h, 0) == 1, bit(h, 2), bit(h, 1)) == 0

    landed = swap(query_q, "hst", hosts, 1, 1)
    own_k, own_v = pick(ctx_kv, kv_local, local_heads)
    value_landed = swap(own_v, "hst", hosts, 1, 1)
    own_keys, own_values = prepare(own_k, own_v, False)
    queries = join(is_even, query_q, landed, (own_keys,))
    landed = swap(queries, "hst", hosts, *along[0])
    done = own(0, 2, (queries,))
    parts = list(relay(is_even, own_k, value_landed, (done,), kv_local))
    parts_landed = [swap(x, "hst", hosts, *along[0]) for x in parts]
    queries = join(near_low, queries, landed, (parts[0],))
    landed = swap(queries, "hst", hosts, *along[1])
    done = own(2, 6, (queries,))
    anchor = {}

    def pass_on(kv, after):
        (parts[kv],) = relay(source_first, parts[kv], parts_landed[kv], after)
        parts_landed[kv] = swap(parts[kv], "hst", hosts, *along[1])
        return parts[kv]

    def complete(kv, after):
        (held,) = relay(done_early, parts[kv], parts_landed[kv], after)
        anchor[kv] = held, swap(held, "hst", hosts, 1, 1)
        return held

    done = pass_on(0, (done,))
    keep, give = source_part(lengths, own_keys, own_v, query_kv, queries, landed, q_rows, per_kv, (done,))
    landed = swap(give, "hst", hosts, 1, 1)
    done = own(8, 4, (keep,))
    done = pass_on(1, (done,))
    done = complete(0, (done,))
    source = merge_part([keep, landed], False, (done,))
    landed = [swap(source, "hst", hosts, x, x) for x in (6, 2, 4)]
    done = own(12, 4, (source,))
    anchor[0] = prepare(*anchor[0], True, (done,))
    results = {}

    def anchors(first, count, after, last=False):
        results[first] = anchor_part(
            lengths, ctx_q, states, own_keys, own_values, anchor[first // per_kv],
            first, count, per_kv, dict(results) if last else None, after,
        )
        return results[first]

    done = anchors(0, 2, ())
    attended = merge_part([source, *landed], True, (done,))
    landed = swap(attended, "hst", hosts, 1, 1)
    done = complete(1, (attended,))
    done = anchors(2, 2, (done,))
    terms = project_part(attended, landed, out_weight, (done,))
    anchor[1] = prepare(*anchor[1], True, (terms,))
    shares = [[(10, 6, True)], [(4, 4, False), (8, 2, False)]]
    step = 1
    while step < groups:
        landed = swap(terms, "tp", groups, step, step)
        last = False
        done = terms
        for first, count, last in shares.pop() if shares else ():
            done = anchors(first, count, (terms, done), last)
        terms = add_part(terms, landed, () if last else (done,))
        step *= 2
    for group in reversed(shares):
        for first, count, last in group:
            done = anchors(first, count, (), last)
    return done, terms


def solution(mesh):
    hosts, groups = mesh.shape["hst"], mesh.shape["tp"]
    return jax.shard_map(
        functools.partial(per_device, hosts, groups),
        mesh=mesh,
        in_specs=(
            P("hst", "tp"),
            P(None, "hst", None),
            P(),
            P("hst", "tp"),
            P(None, "hst", None),
            P("tp", "hst"),
        ),
        out_specs=(P("hst", "tp"), P(None, "hst")),
        check_vma=False,
    )
```

```python
import functools

import jax
import jax.numpy as jnp
from jax import lax
from jax.experimental import pallas as pl
from jax.experimental.pallas import tpu as pltpu
from jax.sharding import PartitionSpec as P

H = 64
KVH = 8
HD = 128
MASKED = -1e30
LOG2E = 1.4426950408889634
SCALE2 = HD ** (-0.5) * LOG2E
TINY = 2.0 ** -90
BF = jnp.bfloat16
F32 = jnp.float32
VMEM = pl.BlockSpec(memory_space=pltpu.VMEM)
ANY = pl.BlockSpec(memory_space=pl.ANY)
HBM = pl.BlockSpec(memory_space=pltpu.HBM)


def params(mib=20):
    return pltpu.CompilerParams(vmem_limit_bytes=mib * 2**20)


def dot_t(a, b):
    return lax.dot_general(a, b, (((1,), (1,)), ((), ())), preferred_element_type=F32)


def dot(a, b):
    return lax.dot_general(a, b, (((1,), (0,)), ((), ())), preferred_element_type=F32)


def spread(value, axis, source):
    kept = jnp.where(lax.axis_index(axis) == source, value, 0).astype(value.dtype)
    return lax.psum(kept, axis)


def swap(value, axis, size, even, odd):
    return lax.ppermute(value, axis, [(i, i ^ (odd if i & 1 else even)) for i in range(size)])


def pick_kernel(group_size, local_heads, kv_ref, k_ref, v_ref, sems):
    first = lax.axis_index("tp") * local_heads // group_size * HD
    cols = pl.ds(pl.multiple_of(first, HD), k_ref.shape[1])
    moves = [
        pltpu.make_async_copy(kv_ref.at[1, :, cols], v_ref, sems.at[1]),
        pltpu.make_async_copy(kv_ref.at[0, :, cols], k_ref, sems.at[0]),
    ]
    for move in moves:
        move.start()
    for move in moves:
        move.wait()


def pick(ctx_kv, kv_local, local_heads):
    return pl.pallas_call(
        functools.partial(pick_kernel, H // KVH, local_heads),
        out_shape=[jax.ShapeDtypeStruct((ctx_kv.shape[1], kv_local * HD), BF)] * 2,
        in_specs=[HBM],
        out_specs=[VMEM] * 2,
        scratch_shapes=[pltpu.SemaphoreType.DMA((2,))],
        compiler_params=params(52),
        cost_estimate=pl.CostEstimate(flops=0, bytes_accessed=2**22, transcendentals=0),
        name="pick_columns",
    )(ctx_kv)


def bit(value, at):
    return (value >> at) & 1


def small_call(kernel, name, shapes, inputs, after=()):
    return pl.pallas_call(
        kernel,
        out_shape=[jax.ShapeDtypeStruct(x, BF) for x in shapes],
        in_specs=[VMEM] * len(inputs) + [ANY] * len(after),
        out_specs=[VMEM] * len(shapes),
        compiler_params=params(),
        cost_estimate=pl.CostEstimate(flops=0, bytes_accessed=2**20, transcendentals=0),
        name=name,
    )(*inputs, *after)


def choose(condition, one, two):
    pl.when(condition)(one)
    pl.when(jnp.logical_not(condition))(two)


def take_rows(target, source, rows, cols=slice(None)):
    def run():
        target[:rows, :] = source[:rows, cols]

    return run


def by_chip(own, others, bits, after=()):
    rows, width = own.shape

    def kernel(*refs):
        out_ref, all_ref = refs[-2:]
        host = lax.axis_index("hst")
        for ref, flip in zip(refs, (0,) + tuple(bits)):
            start = pl.multiple_of((jnp.bitwise_xor(host, flip) >> 1) * rows, rows)
            all_ref[pl.ds(start, rows), :] = ref[...].astype(F32)
        out_ref[...] = all_ref[...].astype(BF)

    total = rows * (1 + len(bits))
    return pl.pallas_call(
        kernel,
        out_shape=jax.ShapeDtypeStruct((total, width), BF),
        in_specs=[VMEM] * (1 + len(bits)) + [ANY] * len(after),
        out_specs=VMEM,
        scratch_shapes=[pltpu.VMEM((total, width), F32)],
        compiler_params=params(),
        cost_estimate=pl.CostEstimate(flops=0, bytes_accessed=2**20, transcendentals=0),
        name="query_chips",
    )(own, *others, *after)


def relay(keep_of, one, two, after=(), split=1):
    slab, columns = one.shape
    width = columns // split

    def kernel(one_ref, two_ref, *rest):
        keep = keep_of(lax.axis_index("hst"))
        for j, out_ref in enumerate(rest[-split:]):
            cols = slice(j * width, (j + 1) * width)
            choose(keep, take_rows(out_ref, one_ref, slab, cols), take_rows(out_ref, two_ref, slab, cols))

    return small_call(kernel, "anchor_relay", [(slab, width)] * split, (one, two), after)


def add_part(one, two, after=()):
    def kernel(one_ref, two_ref, *rest):
        rest[-1][...] = (one_ref[...].astype(F32) + two_ref[...].astype(F32)).astype(BF)

    return small_call(kernel, "query_sum", [one.shape], (one, two), after)[0]


def prepare(first, second, swapped, after=()):
    slab, columns = first.shape

    def kernel(first_ref, second_ref, *rest):
        keys_ref, values_ref = rest[-2:]

        def fill(k_ref, v_ref):
            def run():
                for j in range(columns // HD):
                    cols = slice(j * HD, (j + 1) * HD)
                    at = 2 * j * HD
                    scaled = k_ref[:, cols].astype(F32) * SCALE2
                    high = scaled.astype(BF)
                    low = scaled - high.astype(F32)
                    keys_ref[at : at + HD, :] = high.astype(F32).T.astype(BF)
                    keys_ref[at + HD : at + 2 * HD, :] = low.T.astype(BF)
                    values_ref[:, at : at + HD] = v_ref[:, cols]
                    values_ref[:, at + HD : at + 2 * HD] = jnp.ones((slab, HD), BF)

            return run

        if swapped:
            even = bit(lax.axis_index("hst"), 0) == 0
            choose(even, fill(first_ref, second_ref), fill(second_ref, first_ref))
        else:
            fill(first_ref, second_ref)()

    shapes = [(2 * columns, slab), (slab, 2 * columns)]
    return small_call(kernel, "operands", shapes, (first, second), after)


def twice(query):
    return jnp.concatenate([query, query], 1)


def lanes(index, width):
    return pl.ds(pl.multiple_of(index * width, width), width)


def row_tile(slab):
    return 256 if slab % 256 == 0 else slab


def body_size(first, count, per_kv, most):
    def fits(size):
        bodies = range(first, first + count, size)
        return count % size == 0 and all(x // per_kv == (x + size - 1) // per_kv for x in bodies)

    return max(x for x in range(1, most + 1) if fits(x))


def own_kernel(first, count, per_kv, q_ref, k_ref, v_ref, *rest):
    state_ref = rest[-1]
    slab = q_ref.shape[0]
    tile = row_tile(slab)
    half = tile // 2
    heads = body_size(first, count, per_kv, 4)
    rows = lax.broadcasted_iota(jnp.int32, (half, half), 0)
    cols = lax.broadcasted_iota(jnp.int32, (half, half), 1)
    causal = cols <= rows
    chunks = slab // tile
    units = [(h, j) for h in range(heads) for j in range(chunks)]

    def body(i, carry):
        kv = lax.div(first + i * heads, per_kv)

        def scores(at):
            h, j = units[at]
            query = q_ref[j * tile :, lanes(first + i * heads + h, HD)]
            return dot(twice(query), k_ref[lanes(kv, 2 * HD), j * tile : (j + 1) * tile])

        def power(x):
            return jnp.exp2(x).astype(BF)

        def corner(x):
            return jnp.where(causal, jnp.exp2(x), 0.0).astype(BF)

        current = scores(0)
        totals = [None] * chunks
        for at, (h, j) in enumerate(units):
            following = scores(at + 1) if at + 1 < len(units) else None
            top = jnp.concatenate([corner(current[:half, :half]), jnp.zeros((half, half), BF)], 1)
            low = jnp.concatenate([power(current[half:tile, :half]), corner(current[half:tile, half:])], 1)
            expo = [top, low] if j == chunks - 1 else [top, low, power(current[tile:])]
            part = dot(jnp.concatenate(expo, 0), v_ref[j * tile : (j + 1) * tile, lanes(kv, 2 * HD)])
            for r in range(j, chunks):
                piece = part[(r - j) * tile : (r - j + 1) * tile]
                totals[r] = piece if j == 0 else totals[r] + piece
            state_ref[j * tile : (j + 1) * tile, lanes(i * heads + h, 2 * HD)] = totals[j]
            current = following
        return carry

    lax.fori_loop(0, count // heads, body, 0)


def own_part(ctx_q, own_k, own_v, first, count, per_kv, after=()):
    slab = ctx_q.shape[0]
    work = count * slab * (slab + row_tile(slab)) // 2
    return pl.pallas_call(
        functools.partial(own_kernel, first, count, per_kv),
        out_shape=jax.ShapeDtypeStruct((slab, count * 2 * HD), F32),
        in_specs=[VMEM] * 3 + [ANY] * len(after),
        out_specs=VMEM,
        compiler_params=params(),
        cost_estimate=pl.CostEstimate(
            flops=work * HD * 8, bytes_accessed=count * slab * HD * 6, transcendentals=work
        ),
        name="context_own",
    )(ctx_q, own_k, own_v, *after)


def length_of(lengths_ref, host):
    lengths = lengths_ref[...]
    index = lax.broadcasted_iota(jnp.int32, lengths.shape, 1)
    return jnp.sum(jnp.where(index == host, lengths, 0), axis=1, keepdims=True)


def anchor_kernel(first, count, bases, per_kv, last, befores, *refs):
    lengths_ref, q_ref, k_ref, v_ref, keys, vaug = refs[:6]
    hosts = lengths_ref.shape[1]
    state_refs = refs[6 : 6 + len(bases)]
    earlier = refs[6 + len(bases) : 6 + len(bases) + len(befores)]
    if last:
        full_ref, out_ref, sems = refs[-3:]
    else:
        out_ref = refs[-1]
    slab = q_ref.shape[0]
    heads = body_size(first, count, per_kv, 2 if last else 4)
    kv = first // per_kv
    host = lax.axis_index("hst")

    def hand_over(source, start, width, sem):
        target = full_ref.at[:, pl.ds(start * HD, width * HD)]
        return pltpu.make_async_copy(source, target, sems.at[sem])

    moves = [hand_over(earlier[n], *place, n) for n, place in enumerate(befores)]
    for move in moves:
        move.start()

    def part(start):
        def query_of(h):
            at = (first + start + h) * HD
            return q_ref[:, at : at + HD]

        def scores(h):
            return dot(twice(query_of(h)), keys[...])

        def state_of(h):
            head = first + start + h
            n = max(n for n, base in enumerate(bases) if base <= head)
            at = (head - bases[n]) * 2 * HD
            return state_refs[n][:, at : at + 2 * HD]

        def finish(h, total, sums, worst):
            inverse = pl.reciprocal(sums, approx=True)
            out_ref[:, (start + h) * HD : (start + h + 1) * HD] = (total * inverse).astype(BF)
            return jnp.minimum(worst, jnp.minimum(sums, inverse))

        def check(worst):
            @pl.when(jnp.logical_not(jnp.min(worst) > TINY))
            def _():
                exact_block(first + start, start, heads, host, kv, q_ref, k_ref, v_ref, keys, vaug, out_ref)

        @pl.when(host == 0)
        def _():
            worst = jnp.ones((slab, HD), F32)
            for h in range(heads):
                state = state_of(h)
                worst = finish(h, state[:, :HD], state[:, HD:], worst)
            check(worst)

        @pl.when(host > 0)
        def _():
            worst = jnp.ones((slab, HD), F32)
            current = scores(0)
            for h in range(heads):
                following = scores(h + 1) if h + 1 < heads else None
                expo = jnp.exp2(current)
                state = state_of(h)
                total = dot(expo.astype(BF), vaug[:, :HD]) + state[:, :HD]
                sums = jnp.sum(expo, axis=1, keepdims=True) + state[:, HD:]
                worst = finish(h, total, sums, worst)
                current = following
            check(worst)

        @pl.when(host * 4 >= hosts * 3)
        def _():
            own_len = length_of(lengths_ref, host)
            row_ids = lax.broadcasted_iota(jnp.int32, (slab, HD), 0)
            for h in range(start, start + heads):
                cols = slice(h * HD, (h + 1) * HD)
                kept = jnp.where(row_ids < own_len, out_ref[:, cols].astype(F32), 0.0)
                out_ref[:, cols] = kept.astype(BF)

        if last:
            source = out_ref.at[:, start * HD : (start + heads) * HD]
            move = hand_over(source, first + start, heads, len(befores) + start // heads)
            move.start()
            moves.append(move)

    for start in range(0, count, heads):
        part(start)
    for move in moves:
        move.wait()


def exact_block(q_head, out_head, heads, host, kv, q_ref, k_ref, v_ref, keys, vaug, out_ref):
    slab = q_ref.shape[0]
    tile = 64

    def body(i, carry):
        h = lax.div(i, slab // tile)
        r = lax.rem(i, slab // tile)
        at = pl.ds(pl.multiple_of(r * tile, tile), tile)
        query = q_ref[at, lanes(q_head + h, HD)]
        row_ids = lax.broadcasted_iota(jnp.int32, (tile, slab), 0) + r * tile
        key_ids = lax.broadcasted_iota(jnp.int32, (tile, slab), 1)
        own = dot(twice(query), k_ref[2 * kv * HD : 2 * (kv + 1) * HD, :])
        own = jnp.where(key_ids <= row_ids, own, MASKED)
        far = dot(twice(query), keys[...])
        far = jnp.where(host > 0, far, MASKED)
        peak = jnp.maximum(jnp.max(own, 1, keepdims=True), jnp.max(far, 1, keepdims=True))
        own = jnp.exp2(own - peak)
        far = jnp.where(host > 0, jnp.exp2(far - peak), 0.0)
        sums = jnp.sum(own, 1, keepdims=True) + jnp.sum(far, 1, keepdims=True)
        values = jnp.where(host > 0, vaug[:, :HD].astype(F32), 0.0).astype(BF)
        total = dot(own.astype(BF), v_ref[:, 2 * kv * HD : (2 * kv + 1) * HD]) + dot(far.astype(BF), values)
        out_ref[at, lanes(out_head + h, HD)] = (total / sums).astype(BF)
        return carry

    lax.fori_loop(0, heads * (slab // tile), body, 0)


def anchor_part(lengths, ctx_q, states, own_k, own_v, anchor, first, count, per_kv, befores=None, after=()):
    slab, width = ctx_q.shape
    work = count * slab * slab
    last = befores is not None
    ends = {x: x + y.shape[1] // (2 * HD) for x, y in states.items()}
    bases = tuple(x for x in sorted(states) if x < first + count and ends[x] > first)
    earlier = list(befores.values()) if last else []
    places = tuple((at, x.shape[1] // HD) for at, x in befores.items()) if last else ()
    results = jax.ShapeDtypeStruct((slab, count * HD), BF)
    scratch = []
    if last:
        scratch = [pltpu.VMEM(results.shape, BF), pltpu.SemaphoreType.DMA((len(earlier) + count,))]
        results = jax.ShapeDtypeStruct((slab, width), BF)
    return pl.pallas_call(
        functools.partial(anchor_kernel, first, count, bases, per_kv, last, places),
        out_shape=results,
        in_specs=[VMEM] * (6 + len(bases) + len(earlier)) + [ANY] * len(after),
        out_specs=ANY if last else VMEM,
        scratch_shapes=scratch,
        compiler_params=params(),
        cost_estimate=pl.CostEstimate(
            flops=work * HD * 8, bytes_accessed=count * slab * HD * 8, transcendentals=work
        ),
        name="context_anchor",
    )(lengths, ctx_q, own_k, own_v, *anchor, *[states[x] for x in bases], *earlier, *after)


PART = 16


def write_level(ref, width, level):
    lane = lax.broadcasted_iota(jnp.int32, level.shape, 1)
    parts = []
    for at in range(3):
        part = level.astype(BF).astype(F32)
        parts.append(part if at == 0 else pltpu.roll(part, at * PART, 1))
        level = level - part
    packed = jnp.where(lane < PART, parts[0], jnp.where(lane < 2 * PART, parts[1], parts[2]))
    ref[:, width : width + HD] = packed.astype(BF)


def read_level(ref, width):
    packed = ref[:, width : width + HD].astype(F32)
    return packed + pltpu.roll(packed, HD - PART, 1) + pltpu.roll(packed, HD - 2 * PART, 1)


def source_kernel(per_kv, q_rows, group_size, lengths_ref, k_ref, v_ref, self_ref, known_ref, landed_ref, *rest):
    keep_ref, send_ref, q_all, vaug = rest[-4:]
    slab, columns = v_ref.shape
    width = per_kv * columns
    query_count = 8 * q_rows
    host = lax.axis_index("hst")
    own_len = length_of(lengths_ref, host)
    rows = per_kv * query_count
    odd = bit(host, 0) == 1

    def place(even_ref, odd_ref):
        def run():
            parts = []
            for chip in range(4):
                at = slice(chip * q_rows, (chip + 1) * q_rows)
                parts += [even_ref[at, :].astype(F32), odd_ref[at, :].astype(F32)]
            queries = jnp.concatenate(parts, 0).astype(BF)
            for h in range(width // HD):
                q_all[h * query_count : (h + 1) * query_count, :] = queries[:, h * HD : (h + 1) * HD]

        return run

    choose(odd, place(landed_ref, known_ref), place(known_ref, landed_ref))

    first = lax.axis_index("tp") * (width // HD) // group_size * HD
    own_cols = pl.ds(pl.multiple_of(first, HD), columns)
    selves_kv = [self_ref[i, :, own_cols].astype(F32) for i in range(2)]
    lane = lax.broadcasted_iota(jnp.int32, (query_count, HD), 1)
    query_ids = lax.broadcasted_iota(jnp.int32, (query_count, HD), 0)
    self_ok = (host * q_rows + lane <= query_ids) & (lane < q_rows)
    self_ok = jnp.concatenate([self_ok] * per_kv, 0)
    pad = jnp.zeros((HD - q_rows, HD), F32)
    key_rows = lax.broadcasted_iota(jnp.int32, (slab, HD), 0)
    ones = jnp.where(key_rows < own_len, 1.0, 0.0).astype(BF)
    for j in range(columns // HD):
        values = v_ref[:, j * HD : (j + 1) * HD].astype(F32)
        vaug[:, 2 * j * HD : (2 * j + 1) * HD] = jnp.where(key_rows < own_len, values, 0.0).astype(BF)
        vaug[:, (2 * j + 1) * HD : (2 * j + 2) * HD] = ones

    def operands(j):
        cols = slice(j * HD, (j + 1) * HD)
        queries = q_all[j * rows : (j + 1) * rows, :]
        self_keys = jnp.concatenate([selves_kv[0][:, cols], pad], 0).astype(BF)
        self_values = jnp.concatenate([selves_kv[1][:, cols], pad], 0).astype(BF)
        near = dot(twice(queries), k_ref[2 * j * HD : 2 * (j + 1) * HD, :])
        selves = jnp.where(self_ok, dot_t(queries, self_keys) * SCALE2, MASKED)
        return near, selves, jnp.concatenate([self_values, jnp.ones((HD, HD), BF)], 1)

    def store(j, total, level):
        stats = jnp.zeros((query_count, HD), F32)
        for h in range(per_kv):
            stats = jnp.where(lane == h, level[h * query_count : (h + 1) * query_count, :], stats)

        def put(out_ref):
            def run():
                for h in range(per_kv):
                    part = total[h * query_count : (h + 1) * query_count, :]
                    out_ref[:, h * HD : (h + 1) * HD] = part.astype(BF)
                write_level(out_ref, per_kv * HD, stats)

            return run

        choose(odd if j else jnp.logical_not(odd), put(keep_ref), put(send_ref))

    worst = jnp.ones((rows, HD), F32)
    found = []
    for j in range(columns // HD):
        near, selves, self_values = operands(j)
        near = jnp.exp2(near).astype(BF)
        selves = jnp.exp2(selves).astype(BF)
        total = dot(near, vaug[:, 2 * j * HD : (2 * j + 2) * HD]) + dot(selves, self_values)
        sums = total[:, HD:]
        inverse = 1.0 / sums
        worst = jnp.minimum(worst, jnp.minimum(sums, inverse))
        found.append((total[:, :HD] * inverse, jnp.log2(sums)))
    for j, result in enumerate(found):
        store(j, *result)

    @pl.when(jnp.logical_not(jnp.min(worst) > TINY))
    def _():
        key_ids = lax.broadcasted_iota(jnp.int32, (query_count, slab), 1)
        heads_ok = (host * q_rows + lane <= query_ids) & (lane < q_rows)
        for j in range(columns // HD):
            cols = slice(j * HD, (j + 1) * HD)
            self_keys = jnp.concatenate([selves_kv[0][:, cols], pad], 0).astype(BF)
            self_values = jnp.concatenate([selves_kv[1][:, cols], pad], 0).astype(BF)
            self_values = jnp.concatenate([self_values, jnp.ones((HD, HD), BF)], 1)
            mine = odd if j else jnp.logical_not(odd)

            def body(h, stats):
                at = pl.ds(pl.multiple_of((j * per_kv + h) * query_count, query_count), query_count)
                queries = q_all[at, :]
                near = dot(twice(queries), k_ref[2 * j * HD : 2 * (j + 1) * HD, :])
                near = jnp.where(key_ids < own_len, near, MASKED)
                selves = jnp.where(heads_ok, dot_t(queries, self_keys) * SCALE2, MASKED)
                peak = jnp.maximum(jnp.max(near, 1, keepdims=True), jnp.max(selves, 1, keepdims=True))
                near = jnp.exp2(near - peak).astype(BF)
                selves = jnp.exp2(selves - peak).astype(BF)
                total = dot(near, vaug[:, 2 * j * HD : (2 * j + 2) * HD]) + dot(selves, self_values)
                result = (total[:, :HD] / total[:, HD:]).astype(BF)

                def put(out_ref):
                    def run():
                        out_ref[:, lanes(h, HD)] = result

                    return run

                choose(mine, put(keep_ref), put(send_ref))
                return jnp.where(lane == h, peak + jnp.log2(total[:, HD:]), stats)

            stats = lax.fori_loop(0, per_kv, body, jnp.zeros((query_count, HD), F32))

            def put_level(out_ref):
                def run():
                    write_level(out_ref, per_kv * HD, stats)

                return run

            choose(mine, put_level(keep_ref), put_level(send_ref))


def source_part(lengths, own_k, own_v, query_kv, known, landed, q_rows, per_kv, after=()):
    slab, columns = own_v.shape
    width = per_kv * columns
    count = 8 * q_rows
    work = count * (width // HD) * slab
    return pl.pallas_call(
        functools.partial(source_kernel, per_kv, q_rows, H // KVH),
        out_shape=[jax.ShapeDtypeStruct((count, (per_kv + 1) * HD), BF)] * 2,
        in_specs=[VMEM] * 6 + [ANY] * len(after),
        out_specs=[VMEM] * 2,
        scratch_shapes=[pltpu.VMEM((count * width // HD, HD), BF), pltpu.VMEM((slab, 2 * columns), BF)],
        compiler_params=params(),
        cost_estimate=pl.CostEstimate(flops=work * HD * 8, bytes_accessed=2**21, transcendentals=work),
        name="query_source",
    )(lengths, own_k, own_v, query_kv, known, landed, *after)


def merge_part(groups, last, after=()):
    rows, wide = groups[0].shape
    width = wide - HD

    def kernel(*refs):
        in_refs, out_ref = refs[: len(groups)], refs[-1]
        levels = [read_level(ref, width) for ref in in_refs]
        peak = functools.reduce(jnp.maximum, levels)
        weights = [jnp.exp2(x - peak) for x in levels]
        whole = functools.reduce(jnp.add, weights)
        shares = [w / whole for w in weights]
        if not last:
            write_level(out_ref, width, peak + jnp.log2(whole))
        for h in range(width // HD):
            cols = slice(h * HD, (h + 1) * HD)
            total = sum(w[:, h : h + 1] * ref[:, cols].astype(F32) for w, ref in zip(shares, in_refs))
            out_ref[:, cols] = total.astype(BF)

    return small_call(kernel, "query_merge", [(rows, width if last else wide)], groups, after)[0]


def project_part(own, other, out_weight, after=()):
    rows, half = own.shape
    depth, columns = out_weight.shape

    def kernel(w_ref, own_ref, other_ref, *rest):
        out_ref, attended = rest[-2:]

        def put(first, second):
            def run():
                attended[:, :half] = first[...]
                attended[:, half:] = second[...]

            return run

        even = bit(lax.axis_index("hst"), 0) == 0
        choose(even, put(own_ref, other_ref), put(other_ref, own_ref))
        out_ref[...] = dot(attended[...], w_ref[...]).astype(BF)

    return pl.pallas_call(
        kernel,
        out_shape=jax.ShapeDtypeStruct((rows, columns), BF),
        in_specs=[VMEM] * 3 + [ANY] * len(after),
        out_specs=VMEM,
        scratch_shapes=[pltpu.VMEM((rows, depth), BF)],
        compiler_params=params(),
        cost_estimate=pl.CostEstimate(
            flops=2 * rows * depth * columns, bytes_accessed=2 * depth * columns, transcendentals=0
        ),
        name="query_project",
    )(out_weight, own, other, *after)


def general_queries(lengths, own_k, own_v, self_kv, query_q, out_weight, per_kv):
    own_kv = jnp.stack([own_k, own_v], 0)
    host_id = lax.axis_index("hst")
    local_heads = query_q.shape[1] // HD
    kv_local = own_kv.shape[2] // HD
    slab_rows = own_kv.shape[1]
    own_len = lengths[host_id]
    row_ids = jnp.arange(slab_rows)
    all_queries = lax.all_gather(query_q, "hst", axis=0, tiled=True)
    query_count = all_queries.shape[0]
    q_rows = query_q.shape[0]
    source = jnp.concatenate([own_kv, self_kv], 1)
    source = source.reshape(2, slab_rows + q_rows, kv_local, HD).transpose(0, 2, 1, 3)
    query_ids = jnp.arange(query_count)
    context_ok = jnp.broadcast_to(row_ids[None, :] < own_len, (query_count, slab_rows))
    self_ok = (host_id * q_rows + jnp.arange(q_rows))[None, :] <= query_ids[:, None]
    seen_ok = jnp.concatenate([context_ok, self_ok], 1)
    query_heads = all_queries.reshape(query_count, local_heads, HD).transpose(1, 0, 2)

    def score_head(operands):
        query_rows, head_index = operands
        kv_index = head_index // per_kv
        scores = dot_t(query_rows, source[0, kv_index]) * HD ** (-0.5)
        scores = jnp.where(seen_ok, scores, MASKED)
        peak = jnp.max(scores, axis=1)
        expo = jnp.exp(scores - peak[:, None])
        return peak, jnp.sum(expo, axis=1), dot(expo.astype(BF), source[1, kv_index])

    maxima, totals, outputs = lax.map(score_head, (query_heads, jnp.arange(local_heads)))
    factor = jnp.exp(maxima - lax.pmax(maxima, "hst"))
    denominator, summed = lax.psum((totals * factor, outputs * factor[..., None]), "hst")
    attended = (summed / denominator[..., None]).astype(BF)
    attended = attended.transpose(1, 0, 2).reshape(query_count, local_heads * HD)
    return lax.psum(dot(attended, out_weight), "tp").astype(BF)


def per_device(hosts, groups, ctx_q, ctx_kv, lengths, query_q, query_kv, out_weight):
    slab = ctx_q.shape[0]
    local_heads = ctx_q.shape[1] // HD
    group_size = H // KVH
    kv_local = max(1, local_heads // group_size)
    per_kv = min(local_heads, group_size)
    q_rows = query_q.shape[0]
    host = lax.axis_index("hst")
    fast = hosts == 8 and groups & (groups - 1) == 0
    fast = fast and q_rows == 8 and local_heads == 16 and per_kv == 8

    if not fast:
        kv_first = lax.axis_index("tp") * local_heads // group_size
        self_kv = lax.dynamic_slice_in_dim(query_kv, kv_first * HD, kv_local * HD, 2)
        own_k, own_v = pick(ctx_kv, kv_local, local_heads)
        query_out = general_queries(lengths, own_k, own_v, self_kv, query_q, out_weight, per_kv)
        k, v = spread(jnp.stack([own_k, own_v]), "hst", 0)
        lengths = lengths.reshape(1, hosts)
        own_k, own_v = prepare(own_k, own_v, False)
        anchor = prepare(k, v, False)
        state = own_part(ctx_q, own_k, own_v, 0, local_heads, per_kv)
        results = {}
        for first in range(0, local_heads, per_kv):
            cols = slice(2 * first // per_kv * HD, 2 * (first // per_kv + 1) * HD)
            last = first + per_kv == local_heads
            results[first] = anchor_part(
                lengths, ctx_q, {0: state}, own_k, own_v, (anchor[0][cols, :], anchor[1][:, cols]),
                first, per_kv, per_kv, dict(results) if last else None,
            )
        return results[first], query_out

    lengths = lengths.reshape(1, hosts)
    states = {}

    def own(first, count, after=()):
        states[first] = own_part(ctx_q, own_keys, own_values, first, count, per_kv, after)
        return states[first]

    along = ((2, 4), (4, 2))

    def is_even(h):
        return bit(h, 0) == 0

    def source_first(h):
        return h < 2

    def done_early(h):
        return (h <= 2) | (h == 5)

    bits = (6, 2, 4)
    landed = [swap(query_q, "hst", hosts, x, x) for x in bits]
    own_k, own_v = pick(ctx_kv, kv_local, local_heads)
    value_landed = swap(own_v, "hst", hosts, 1, 1)
    own_keys, own_values = prepare(own_k, own_v, False)
    done = own(0, 2)
    parts = list(relay(is_even, own_k, value_landed, (done,), kv_local))
    parts_landed = [swap(x, "hst", hosts, *along[0]) for x in parts]
    queries = by_chip(query_q, landed, bits, (parts[0],))
    landed = swap(queries, "hst", hosts, 1, 1)
    done = own(2, 2, (queries,))
    anchor = {}

    def pass_on(kv, after):
        (parts[kv],) = relay(source_first, parts[kv], parts_landed[kv], after)
        parts_landed[kv] = swap(parts[kv], "hst", hosts, *along[1])
        return parts[kv]

    def complete(kv, after):
        (held,) = relay(done_early, parts[kv], parts_landed[kv], after)
        anchor[kv] = held, swap(held, "hst", hosts, 1, 1)
        return held

    keep, give = source_part(lengths, own_keys, own_v, query_kv, queries, landed, q_rows, per_kv, (done,))
    landed = swap(give, "hst", hosts, 1, 1)
    done = own(4, 4, (keep,))
    source = merge_part([keep, landed], False, (done,))
    landed = swap(source, "hst", hosts, *along[0])
    done = pass_on(0, (source,))
    done = own(8, 8, (done,))
    source = merge_part([source, landed], False, (done,))
    landed = swap(source, "hst", hosts, *along[1])
    done = complete(0, (source,))
    done = pass_on(1, (done,))
    anchor[0] = prepare(*anchor[0], True, (done,))
    results = {}

    def anchors(first, count, after, last=False):
        results[first] = anchor_part(
            lengths, ctx_q, states, own_keys, own_values, anchor[first // per_kv],
            first, count, per_kv, dict(results) if last else None, after,
        )
        return results[first]

    done = anchors(0, 4, ())
    attended = merge_part([source, landed], True, (done,))
    landed = swap(attended, "hst", hosts, 1, 1)
    done = complete(1, (attended,))
    done = anchors(4, 2, (done,))
    terms = project_part(attended, landed, out_weight, (done,))
    anchor[1] = prepare(*anchor[1], True, (terms,))
    shares = [[(12, 4, True)], [(6, 2, False), (8, 4, False)]]
    step = 1
    while step < groups:
        landed = swap(terms, "tp", groups, step, step)
        last = False
        done = terms
        for first, count, last in shares.pop() if shares else ():
            done = anchors(first, count, (terms, done), last)
        terms = add_part(terms, landed, () if last else (done,))
        step *= 2
    for group in reversed(shares):
        for first, count, last in group:
            done = anchors(first, count, (), last)
    return done, terms


def solution(mesh):
    hosts, groups = mesh.shape["hst"], mesh.shape["tp"]
    return jax.shard_map(
        functools.partial(per_device, hosts, groups),
        mesh=mesh,
        in_specs=(
            P("hst", "tp"),
            P(None, "hst", None),
            P(),
            P("hst", "tp"),
            P(None, "hst", None),
            P("tp", "hst"),
        ),
        out_specs=(P("hst", "tp"), P(None, "hst")),
        check_vma=False,
    )
```

```python
import functools

import jax
import jax.numpy as jnp
from jax import lax
from jax.experimental import pallas as pl
from jax.experimental.pallas import tpu as pltpu
from jax.sharding import PartitionSpec as P

H = 64
KVH = 8
HD = 128
MASKED = -1e30
LOG2E = 1.4426950408889634
SCALE2 = HD ** (-0.5) * LOG2E
TINY = 2.0 ** -90
BF = jnp.bfloat16
F32 = jnp.float32
VMEM = pl.BlockSpec(memory_space=pltpu.VMEM)
ANY = pl.BlockSpec(memory_space=pl.ANY)
HBM = pl.BlockSpec(memory_space=pltpu.HBM)


def params(mib=20):
    return pltpu.CompilerParams(vmem_limit_bytes=mib * 2**20)


def dot_t(a, b):
    return lax.dot_general(a, b, (((1,), (1,)), ((), ())), preferred_element_type=F32)


def dot(a, b):
    return lax.dot_general(a, b, (((1,), (0,)), ((), ())), preferred_element_type=F32)


def spread(value, axis, source):
    kept = jnp.where(lax.axis_index(axis) == source, value, 0).astype(value.dtype)
    return lax.psum(kept, axis)


def swap(value, axis, size, even, odd):
    return lax.ppermute(value, axis, [(i, i ^ (odd if i & 1 else even)) for i in range(size)])


def pick_kernel(group_size, local_heads, kv_ref, k_ref, v_ref, sems):
    first = lax.axis_index("tp") * local_heads // group_size * HD
    cols = pl.ds(pl.multiple_of(first, HD), k_ref.shape[1])
    moves = [
        pltpu.make_async_copy(kv_ref.at[1, :, cols], v_ref, sems.at[1]),
        pltpu.make_async_copy(kv_ref.at[0, :, cols], k_ref, sems.at[0]),
    ]
    for move in moves:
        move.start()
    for move in moves:
        move.wait()


def pick(ctx_kv, kv_local, local_heads):
    return pl.pallas_call(
        functools.partial(pick_kernel, H // KVH, local_heads),
        out_shape=[jax.ShapeDtypeStruct((ctx_kv.shape[1], kv_local * HD), BF)] * 2,
        in_specs=[HBM],
        out_specs=[VMEM] * 2,
        scratch_shapes=[pltpu.SemaphoreType.DMA((2,))],
        compiler_params=params(52),
        cost_estimate=pl.CostEstimate(flops=0, bytes_accessed=2**22, transcendentals=0),
        name="pick_columns",
    )(ctx_kv)


def bit(value, at):
    return (value >> at) & 1


def small_call(kernel, name, shapes, inputs, after=()):
    return pl.pallas_call(
        kernel,
        out_shape=[jax.ShapeDtypeStruct(x, BF) for x in shapes],
        in_specs=[VMEM] * len(inputs) + [ANY] * len(after),
        out_specs=[VMEM] * len(shapes),
        compiler_params=params(),
        cost_estimate=pl.CostEstimate(flops=0, bytes_accessed=2**20, transcendentals=0),
        name=name,
    )(*inputs, *after)


def choose(condition, one, two):
    pl.when(condition)(one)
    pl.when(jnp.logical_not(condition))(two)


def take_rows(target, source, rows, cols=slice(None)):
    def run():
        target[:rows, :] = source[:rows, cols]

    return run


def by_chip(own, others, bits, after=()):
    rows, width = own.shape

    def kernel(*refs):
        out_ref, all_ref = refs[-2:]
        host = lax.axis_index("hst")
        for ref, flip in zip(refs, (0,) + tuple(bits)):
            start = pl.multiple_of((jnp.bitwise_xor(host, flip) >> 1) * rows, rows)
            all_ref[pl.ds(start, rows), :] = ref[...].astype(F32)
        out_ref[...] = all_ref[...].astype(BF)

    total = rows * (1 + len(bits))
    return pl.pallas_call(
        kernel,
        out_shape=jax.ShapeDtypeStruct((total, width), BF),
        in_specs=[VMEM] * (1 + len(bits)) + [ANY] * len(after),
        out_specs=VMEM,
        scratch_shapes=[pltpu.VMEM((total, width), F32)],
        compiler_params=params(),
        cost_estimate=pl.CostEstimate(flops=0, bytes_accessed=2**20, transcendentals=0),
        name="query_chips",
    )(own, *others, *after)


def relay(keep_of, one, two, after=(), kv=0):
    cols = slice(kv * HD, (kv + 1) * HD)
    slab = one.shape[0]

    def kernel(one_ref, two_ref, *rest):
        keep = keep_of(lax.axis_index("hst"))
        choose(keep, take_rows(rest[-1], one_ref, slab, cols), take_rows(rest[-1], two_ref, slab, cols))

    return small_call(kernel, "anchor_relay", [(slab, HD)], (one, two), after)


def add_part(one, two, after=()):
    def kernel(one_ref, two_ref, *rest):
        rest[-1][...] = (one_ref[...].astype(F32) + two_ref[...].astype(F32)).astype(BF)

    return small_call(kernel, "query_sum", [one.shape], (one, two), after)[0]


def prepare(first, second, swapped, after=()):
    slab, columns = first.shape

    def kernel(first_ref, second_ref, *rest):
        keys_ref, values_ref = rest[-2:]

        def fill(k_ref, v_ref):
            def run():
                for j in range(columns // HD):
                    cols = slice(j * HD, (j + 1) * HD)
                    at = 2 * j * HD
                    scaled = k_ref[:, cols].astype(F32) * SCALE2
                    high = scaled.astype(BF)
                    low = scaled - high.astype(F32)
                    keys_ref[at : at + HD, :] = high.astype(F32).T.astype(BF)
                    keys_ref[at + HD : at + 2 * HD, :] = low.T.astype(BF)
                    values_ref[:, at : at + HD] = v_ref[:, cols]
                    values_ref[:, at + HD : at + 2 * HD] = jnp.ones((slab, HD), BF)

            return run

        if swapped:
            even = bit(lax.axis_index("hst"), 0) == 0
            choose(even, fill(first_ref, second_ref), fill(second_ref, first_ref))
        else:
            fill(first_ref, second_ref)()

    shapes = [(2 * columns, slab), (slab, 2 * columns)]
    return small_call(kernel, "operands", shapes, (first, second), after)


def twice(query):
    return jnp.concatenate([query, query], 1)


def lanes(index, width):
    return pl.ds(pl.multiple_of(index * width, width), width)


def row_tile(slab):
    return 256 if slab % 256 == 0 else slab


def body_size(first, count, per_kv, most):
    def fits(size):
        bodies = range(first, first + count, size)
        return count % size == 0 and all(x // per_kv == (x + size - 1) // per_kv for x in bodies)

    return max(x for x in range(1, most + 1) if fits(x))


def own_kernel(first, count, per_kv, q_ref, k_ref, v_ref, *rest):
    state_ref = rest[-1]
    slab = q_ref.shape[0]
    tile = row_tile(slab)
    half = tile // 2
    heads = body_size(first, count, per_kv, 4)
    rows = lax.broadcasted_iota(jnp.int32, (half, half), 0)
    cols = lax.broadcasted_iota(jnp.int32, (half, half), 1)
    causal = cols <= rows
    chunks = slab // tile
    units = [(h, j) for h in range(heads) for j in range(chunks)]

    def body(i, carry):
        kv = lax.div(first + i * heads, per_kv)

        def scores(at):
            h, j = units[at]
            query = q_ref[j * tile :, lanes(first + i * heads + h, HD)]
            return dot(twice(query), k_ref[lanes(kv, 2 * HD), j * tile : (j + 1) * tile])

        def power(x):
            return jnp.exp2(x).astype(BF)

        def corner(x):
            return jnp.where(causal, jnp.exp2(x), 0.0).astype(BF)

        current = scores(0)
        totals = [None] * chunks
        for at, (h, j) in enumerate(units):
            following = scores(at + 1) if at + 1 < len(units) else None
            top = jnp.concatenate([corner(current[:half, :half]), jnp.zeros((half, half), BF)], 1)
            low = jnp.concatenate([power(current[half:tile, :half]), corner(current[half:tile, half:])], 1)
            expo = [top, low] if j == chunks - 1 else [top, low, power(current[tile:])]
            part = dot(jnp.concatenate(expo, 0), v_ref[j * tile : (j + 1) * tile, lanes(kv, 2 * HD)])
            for r in range(j, chunks):
                piece = part[(r - j) * tile : (r - j + 1) * tile]
                totals[r] = piece if j == 0 else totals[r] + piece
            state_ref[j * tile : (j + 1) * tile, lanes(i * heads + h, 2 * HD)] = totals[j]
            current = following
        return carry

    lax.fori_loop(0, count // heads, body, 0)


def own_part(ctx_q, own_k, own_v, first, count, per_kv, after=()):
    slab = ctx_q.shape[0]
    work = count * slab * (slab + row_tile(slab)) // 2
    return pl.pallas_call(
        functools.partial(own_kernel, first, count, per_kv),
        out_shape=jax.ShapeDtypeStruct((slab, count * 2 * HD), F32),
        in_specs=[VMEM] * 3 + [ANY] * len(after),
        out_specs=VMEM,
        compiler_params=params(),
        cost_estimate=pl.CostEstimate(
            flops=work * HD * 8, bytes_accessed=count * slab * HD * 6, transcendentals=work
        ),
        name="context_own",
    )(ctx_q, own_k, own_v, *after)


def length_of(lengths_ref, host):
    lengths = lengths_ref[...]
    index = lax.broadcasted_iota(jnp.int32, lengths.shape, 1)
    return jnp.sum(jnp.where(index == host, lengths, 0), axis=1, keepdims=True)


def anchor_kernel(first, count, bases, per_kv, last, befores, *refs):
    lengths_ref, q_ref, k_ref, v_ref, keys, vaug = refs[:6]
    hosts = lengths_ref.shape[1]
    state_refs = refs[6 : 6 + len(bases)]
    earlier = refs[6 + len(bases) : 6 + len(bases) + len(befores)]
    if last:
        full_ref, out_ref, sems = refs[-3:]
    else:
        out_ref = refs[-1]
    slab = q_ref.shape[0]
    heads = body_size(first, count, per_kv, 2 if last else 4)
    kv = first // per_kv
    host = lax.axis_index("hst")

    def hand_over(source, start, width, sem):
        target = full_ref.at[:, pl.ds(start * HD, width * HD)]
        return pltpu.make_async_copy(source, target, sems.at[sem])

    moves = [hand_over(earlier[n], *place, n) for n, place in enumerate(befores)]
    for move in moves:
        move.start()

    def part(start):
        def query_of(h):
            at = (first + start + h) * HD
            return q_ref[:, at : at + HD]

        def scores(h):
            return dot(twice(query_of(h)), keys[...])

        def state_of(h):
            head = first + start + h
            n = max(n for n, base in enumerate(bases) if base <= head)
            at = (head - bases[n]) * 2 * HD
            return state_refs[n][:, at : at + 2 * HD]

        def finish(h, total, sums, worst):
            inverse = pl.reciprocal(sums, approx=True)
            out_ref[:, (start + h) * HD : (start + h + 1) * HD] = (total * inverse).astype(BF)
            return jnp.minimum(worst, jnp.minimum(sums, inverse))

        def check(worst):
            @pl.when(jnp.logical_not(jnp.min(worst) > TINY))
            def _():
                exact_block(first + start, start, heads, host, kv, q_ref, k_ref, v_ref, keys, vaug, out_ref)

        @pl.when(host == 0)
        def _():
            worst = jnp.ones((slab, HD), F32)
            for h in range(heads):
                state = state_of(h)
                worst = finish(h, state[:, :HD], state[:, HD:], worst)
            check(worst)

        @pl.when(host > 0)
        def _():
            worst = jnp.ones((slab, HD), F32)
            current = scores(0)
            for h in range(heads):
                following = scores(h + 1) if h + 1 < heads else None
                expo = jnp.exp2(current)
                state = state_of(h)
                total = dot(expo.astype(BF), vaug[:, :HD]) + state[:, :HD]
                sums = jnp.sum(expo, axis=1, keepdims=True) + state[:, HD:]
                worst = finish(h, total, sums, worst)
                current = following
            check(worst)

        @pl.when(host * 4 >= hosts * 3)
        def _():
            own_len = length_of(lengths_ref, host)
            row_ids = lax.broadcasted_iota(jnp.int32, (slab, HD), 0)
            for h in range(start, start + heads):
                cols = slice(h * HD, (h + 1) * HD)
                kept = jnp.where(row_ids < own_len, out_ref[:, cols].astype(F32), 0.0)
                out_ref[:, cols] = kept.astype(BF)

        if last:
            source = out_ref.at[:, start * HD : (start + heads) * HD]
            move = hand_over(source, first + start, heads, len(befores) + start // heads)
            move.start()
            moves.append(move)

    for start in range(0, count, heads):
        part(start)
    for move in moves:
        move.wait()


def exact_block(q_head, out_head, heads, host, kv, q_ref, k_ref, v_ref, keys, vaug, out_ref):
    slab = q_ref.shape[0]
    tile = 64

    def body(i, carry):
        h = lax.div(i, slab // tile)
        r = lax.rem(i, slab // tile)
        at = pl.ds(pl.multiple_of(r * tile, tile), tile)
        query = q_ref[at, lanes(q_head + h, HD)]
        row_ids = lax.broadcasted_iota(jnp.int32, (tile, slab), 0) + r * tile
        key_ids = lax.broadcasted_iota(jnp.int32, (tile, slab), 1)
        own = dot(twice(query), k_ref[2 * kv * HD : 2 * (kv + 1) * HD, :])
        own = jnp.where(key_ids <= row_ids, own, MASKED)
        far = dot(twice(query), keys[...])
        far = jnp.where(host > 0, far, MASKED)
        peak = jnp.maximum(jnp.max(own, 1, keepdims=True), jnp.max(far, 1, keepdims=True))
        own = jnp.exp2(own - peak)
        far = jnp.where(host > 0, jnp.exp2(far - peak), 0.0)
        sums = jnp.sum(own, 1, keepdims=True) + jnp.sum(far, 1, keepdims=True)
        values = jnp.where(host > 0, vaug[:, :HD].astype(F32), 0.0).astype(BF)
        total = dot(own.astype(BF), v_ref[:, 2 * kv * HD : (2 * kv + 1) * HD]) + dot(far.astype(BF), values)
        out_ref[at, lanes(out_head + h, HD)] = (total / sums).astype(BF)
        return carry

    lax.fori_loop(0, heads * (slab // tile), body, 0)


def anchor_part(lengths, ctx_q, states, own_k, own_v, anchor, first, count, per_kv, befores=None, after=()):
    slab, width = ctx_q.shape
    work = count * slab * slab
    last = befores is not None
    ends = {x: x + y.shape[1] // (2 * HD) for x, y in states.items()}
    bases = tuple(x for x in sorted(states) if x < first + count and ends[x] > first)
    earlier = list(befores.values()) if last else []
    places = tuple((at, x.shape[1] // HD) for at, x in befores.items()) if last else ()
    results = jax.ShapeDtypeStruct((slab, count * HD), BF)
    scratch = []
    if last:
        scratch = [pltpu.VMEM(results.shape, BF), pltpu.SemaphoreType.DMA((len(earlier) + count,))]
        results = jax.ShapeDtypeStruct((slab, width), BF)
    return pl.pallas_call(
        functools.partial(anchor_kernel, first, count, bases, per_kv, last, places),
        out_shape=results,
        in_specs=[VMEM] * (6 + len(bases) + len(earlier)) + [ANY] * len(after),
        out_specs=ANY if last else VMEM,
        scratch_shapes=scratch,
        compiler_params=params(),
        cost_estimate=pl.CostEstimate(
            flops=work * HD * 8, bytes_accessed=count * slab * HD * 8, transcendentals=work
        ),
        name="context_anchor",
    )(lengths, ctx_q, own_k, own_v, *anchor, *[states[x] for x in bases], *earlier, *after)


PART = 16


def write_level(ref, width, level):
    lane = lax.broadcasted_iota(jnp.int32, level.shape, 1)
    parts = []
    for at in range(3):
        part = level.astype(BF).astype(F32)
        parts.append(part if at == 0 else pltpu.roll(part, at * PART, 1))
        level = level - part
    packed = jnp.where(lane < PART, parts[0], jnp.where(lane < 2 * PART, parts[1], parts[2]))
    ref[:, width : width + HD] = packed.astype(BF)


def read_level(ref, width):
    packed = ref[:, width : width + HD].astype(F32)
    return packed + pltpu.roll(packed, HD - PART, 1) + pltpu.roll(packed, HD - 2 * PART, 1)


def source_kernel(per_kv, q_rows, group_size, lengths_ref, k_ref, v_ref, self_ref, known_ref, landed_ref, *rest):
    keep_ref, send_ref, q_all, vaug = rest[-4:]
    slab, columns = v_ref.shape
    width = per_kv * columns
    query_count = 8 * q_rows
    host = lax.axis_index("hst")
    own_len = length_of(lengths_ref, host)
    rows = per_kv * query_count
    odd = bit(host, 0) == 1

    def place(even_ref, odd_ref):
        def run():
            parts = []
            for chip in range(4):
                at = slice(chip * q_rows, (chip + 1) * q_rows)
                parts += [even_ref[at, :].astype(F32), odd_ref[at, :].astype(F32)]
            queries = jnp.concatenate(parts, 0).astype(BF)
            for h in range(width // HD):
                q_all[h * query_count : (h + 1) * query_count, :] = queries[:, h * HD : (h + 1) * HD]

        return run

    choose(odd, place(landed_ref, known_ref), place(known_ref, landed_ref))

    first = lax.axis_index("tp") * (width // HD) // group_size * HD
    own_cols = pl.ds(pl.multiple_of(first, HD), columns)
    selves_kv = [self_ref[i, :, own_cols].astype(F32) for i in range(2)]
    lane = lax.broadcasted_iota(jnp.int32, (query_count, HD), 1)
    query_ids = lax.broadcasted_iota(jnp.int32, (query_count, HD), 0)
    self_ok = (host * q_rows + lane <= query_ids) & (lane < q_rows)
    self_ok = jnp.concatenate([self_ok] * per_kv, 0)
    pad = jnp.zeros((HD - q_rows, HD), F32)
    key_rows = lax.broadcasted_iota(jnp.int32, (slab, HD), 0)
    ones = jnp.where(key_rows < own_len, 1.0, 0.0).astype(BF)
    for j in range(columns // HD):
        values = v_ref[:, j * HD : (j + 1) * HD].astype(F32)
        vaug[:, 2 * j * HD : (2 * j + 1) * HD] = jnp.where(key_rows < own_len, values, 0.0).astype(BF)
        vaug[:, (2 * j + 1) * HD : (2 * j + 2) * HD] = ones

    def operands(j):
        cols = slice(j * HD, (j + 1) * HD)
        queries = q_all[j * rows : (j + 1) * rows, :]
        self_keys = jnp.concatenate([selves_kv[0][:, cols], pad], 0).astype(BF)
        self_values = jnp.concatenate([selves_kv[1][:, cols], pad], 0).astype(BF)
        near = dot(twice(queries), k_ref[2 * j * HD : 2 * (j + 1) * HD, :])
        selves = jnp.where(self_ok, dot_t(queries, self_keys) * SCALE2, MASKED)
        return near, selves, jnp.concatenate([self_values, jnp.ones((HD, HD), BF)], 1)

    def store(j, total, level):
        stats = jnp.zeros((query_count, HD), F32)
        for h in range(per_kv):
            stats = jnp.where(lane == h, level[h * query_count : (h + 1) * query_count, :], stats)

        def put(out_ref):
            def run():
                for h in range(per_kv):
                    part = total[h * query_count : (h + 1) * query_count, :]
                    out_ref[:, h * HD : (h + 1) * HD] = part.astype(BF)
                write_level(out_ref, per_kv * HD, stats)

            return run

        choose(odd if j else jnp.logical_not(odd), put(keep_ref), put(send_ref))

    worst = jnp.ones((rows, HD), F32)
    found = []
    for j in range(columns // HD):
        near, selves, self_values = operands(j)
        near = jnp.exp2(near).astype(BF)
        selves = jnp.exp2(selves).astype(BF)
        total = dot(near, vaug[:, 2 * j * HD : (2 * j + 2) * HD]) + dot(selves, self_values)
        sums = total[:, HD:]
        inverse = 1.0 / sums
        worst = jnp.minimum(worst, jnp.minimum(sums, inverse))
        found.append((total[:, :HD] * inverse, jnp.log2(sums)))
    for j, result in enumerate(found):
        store(j, *result)

    @pl.when(jnp.logical_not(jnp.min(worst) > TINY))
    def _():
        key_ids = lax.broadcasted_iota(jnp.int32, (query_count, slab), 1)
        heads_ok = (host * q_rows + lane <= query_ids) & (lane < q_rows)
        for j in range(columns // HD):
            cols = slice(j * HD, (j + 1) * HD)
            self_keys = jnp.concatenate([selves_kv[0][:, cols], pad], 0).astype(BF)
            self_values = jnp.concatenate([selves_kv[1][:, cols], pad], 0).astype(BF)
            self_values = jnp.concatenate([self_values, jnp.ones((HD, HD), BF)], 1)
            mine = odd if j else jnp.logical_not(odd)

            def body(h, stats):
                at = pl.ds(pl.multiple_of((j * per_kv + h) * query_count, query_count), query_count)
                queries = q_all[at, :]
                near = dot(twice(queries), k_ref[2 * j * HD : 2 * (j + 1) * HD, :])
                near = jnp.where(key_ids < own_len, near, MASKED)
                selves = jnp.where(heads_ok, dot_t(queries, self_keys) * SCALE2, MASKED)
                peak = jnp.maximum(jnp.max(near, 1, keepdims=True), jnp.max(selves, 1, keepdims=True))
                near = jnp.exp2(near - peak).astype(BF)
                selves = jnp.exp2(selves - peak).astype(BF)
                total = dot(near, vaug[:, 2 * j * HD : (2 * j + 2) * HD]) + dot(selves, self_values)
                result = (total[:, :HD] / total[:, HD:]).astype(BF)

                def put(out_ref):
                    def run():
                        out_ref[:, lanes(h, HD)] = result

                    return run

                choose(mine, put(keep_ref), put(send_ref))
                return jnp.where(lane == h, peak + jnp.log2(total[:, HD:]), stats)

            stats = lax.fori_loop(0, per_kv, body, jnp.zeros((query_count, HD), F32))

            def put_level(out_ref):
                def run():
                    write_level(out_ref, per_kv * HD, stats)

                return run

            choose(mine, put_level(keep_ref), put_level(send_ref))


def source_part(lengths, own_k, own_v, query_kv, known, landed, q_rows, per_kv, after=()):
    slab, columns = own_v.shape
    width = per_kv * columns
    count = 8 * q_rows
    work = count * (width // HD) * slab
    return pl.pallas_call(
        functools.partial(source_kernel, per_kv, q_rows, H // KVH),
        out_shape=[jax.ShapeDtypeStruct((count, (per_kv + 1) * HD), BF)] * 2,
        in_specs=[VMEM] * 6 + [ANY] * len(after),
        out_specs=[VMEM] * 2,
        scratch_shapes=[pltpu.VMEM((count * width // HD, HD), BF), pltpu.VMEM((slab, 2 * columns), BF)],
        compiler_params=params(),
        cost_estimate=pl.CostEstimate(flops=work * HD * 8, bytes_accessed=2**21, transcendentals=work),
        name="query_source",
    )(lengths, own_k, own_v, query_kv, known, landed, *after)


def merge_part(groups, last, after=()):
    rows, wide = groups[0].shape
    width = wide - HD

    def kernel(*refs):
        in_refs, out_ref = refs[: len(groups)], refs[-1]
        levels = [read_level(ref, width) for ref in in_refs]
        peak = functools.reduce(jnp.maximum, levels)
        weights = [jnp.exp2(x - peak) for x in levels]
        whole = functools.reduce(jnp.add, weights)
        shares = [w / whole for w in weights]
        if not last:
            write_level(out_ref, width, peak + jnp.log2(whole))
        for h in range(width // HD):
            cols = slice(h * HD, (h + 1) * HD)
            total = sum(w[:, h : h + 1] * ref[:, cols].astype(F32) for w, ref in zip(shares, in_refs))
            out_ref[:, cols] = total.astype(BF)

    return small_call(kernel, "query_merge", [(rows, width if last else wide)], groups, after)[0]


def project_part(own, other, out_weight, after=()):
    rows, half = own.shape
    depth, columns = out_weight.shape

    def kernel(w_ref, own_ref, other_ref, *rest):
        out_ref, attended = rest[-2:]

        def put(first, second):
            def run():
                attended[:, :half] = first[...]
                attended[:, half:] = second[...]

            return run

        even = bit(lax.axis_index("hst"), 0) == 0
        choose(even, put(own_ref, other_ref), put(other_ref, own_ref))
        out_ref[...] = dot(attended[...], w_ref[...]).astype(BF)

    return pl.pallas_call(
        kernel,
        out_shape=jax.ShapeDtypeStruct((rows, columns), BF),
        in_specs=[VMEM] * 3 + [ANY] * len(after),
        out_specs=VMEM,
        scratch_shapes=[pltpu.VMEM((rows, depth), BF)],
        compiler_params=params(),
        cost_estimate=pl.CostEstimate(
            flops=2 * rows * depth * columns, bytes_accessed=2 * depth * columns, transcendentals=0
        ),
        name="query_project",
    )(out_weight, own, other, *after)


def general_queries(lengths, own_k, own_v, self_kv, query_q, out_weight, per_kv):
    own_kv = jnp.stack([own_k, own_v], 0)
    host_id = lax.axis_index("hst")
    local_heads = query_q.shape[1] // HD
    kv_local = own_kv.shape[2] // HD
    slab_rows = own_kv.shape[1]
    own_len = lengths[host_id]
    row_ids = jnp.arange(slab_rows)
    all_queries = lax.all_gather(query_q, "hst", axis=0, tiled=True)
    query_count = all_queries.shape[0]
    q_rows = query_q.shape[0]
    source = jnp.concatenate([own_kv, self_kv], 1)
    source = source.reshape(2, slab_rows + q_rows, kv_local, HD).transpose(0, 2, 1, 3)
    query_ids = jnp.arange(query_count)
    context_ok = jnp.broadcast_to(row_ids[None, :] < own_len, (query_count, slab_rows))
    self_ok = (host_id * q_rows + jnp.arange(q_rows))[None, :] <= query_ids[:, None]
    seen_ok = jnp.concatenate([context_ok, self_ok], 1)
    query_heads = all_queries.reshape(query_count, local_heads, HD).transpose(1, 0, 2)

    def score_head(operands):
        query_rows, head_index = operands
        kv_index = head_index // per_kv
        scores = dot_t(query_rows, source[0, kv_index]) * HD ** (-0.5)
        scores = jnp.where(seen_ok, scores, MASKED)
        peak = jnp.max(scores, axis=1)
        expo = jnp.exp(scores - peak[:, None])
        return peak, jnp.sum(expo, axis=1), dot(expo.astype(BF), source[1, kv_index])

    maxima, totals, outputs = lax.map(score_head, (query_heads, jnp.arange(local_heads)))
    factor = jnp.exp(maxima - lax.pmax(maxima, "hst"))
    denominator, summed = lax.psum((totals * factor, outputs * factor[..., None]), "hst")
    attended = (summed / denominator[..., None]).astype(BF)
    attended = attended.transpose(1, 0, 2).reshape(query_count, local_heads * HD)
    return lax.psum(dot(attended, out_weight), "tp").astype(BF)


def per_device(hosts, groups, ctx_q, ctx_kv, lengths, query_q, query_kv, out_weight):
    slab = ctx_q.shape[0]
    local_heads = ctx_q.shape[1] // HD
    group_size = H // KVH
    kv_local = max(1, local_heads // group_size)
    per_kv = min(local_heads, group_size)
    q_rows = query_q.shape[0]
    host = lax.axis_index("hst")
    fast = hosts == 8 and groups & (groups - 1) == 0
    fast = fast and q_rows == 8 and local_heads == 16 and per_kv == 8

    if not fast:
        kv_first = lax.axis_index("tp") * local_heads // group_size
        self_kv = lax.dynamic_slice_in_dim(query_kv, kv_first * HD, kv_local * HD, 2)
        own_k, own_v = pick(ctx_kv, kv_local, local_heads)
        query_out = general_queries(lengths, own_k, own_v, self_kv, query_q, out_weight, per_kv)
        k, v = spread(jnp.stack([own_k, own_v]), "hst", 0)
        lengths = lengths.reshape(1, hosts)
        own_k, own_v = prepare(own_k, own_v, False)
        anchor = prepare(k, v, False)
        state = own_part(ctx_q, own_k, own_v, 0, local_heads, per_kv)
        results = {}
        for first in range(0, local_heads, per_kv):
            cols = slice(2 * first // per_kv * HD, 2 * (first // per_kv + 1) * HD)
            last = first + per_kv == local_heads
            results[first] = anchor_part(
                lengths, ctx_q, {0: state}, own_k, own_v, (anchor[0][cols, :], anchor[1][:, cols]),
                first, per_kv, per_kv, dict(results) if last else None,
            )
        return results[first], query_out

    lengths = lengths.reshape(1, hosts)
    states = {}

    def own(first, count, after=()):
        states[first] = own_part(ctx_q, own_keys, own_values, first, count, per_kv, after)
        return states[first]

    along = ((2, 4), (4, 2))

    def is_even(h):
        return bit(h, 0) == 0

    def source_first(h):
        return h < 2

    def done_early(h):
        return (h <= 2) | (h == 5)

    bits = (6, 2, 4)
    landed = [swap(query_q, "hst", hosts, x, x) for x in bits]
    own_k, own_v = pick(ctx_kv, kv_local, local_heads)
    value_landed = swap(own_v, "hst", hosts, 1, 1)
    own_keys, own_values = prepare(own_k, own_v, False)
    done = own(0, 2)
    parts, parts_landed = {}, {}

    def send_off(kv, after):
        (parts[kv],) = relay(is_even, own_k, value_landed, after, kv)
        parts_landed[kv] = swap(parts[kv], "hst", hosts, *along[0])
        return parts[kv]

    done = send_off(0, (done,))
    done = own(2, 2, (done,))
    queries = by_chip(query_q, landed, bits, (done,))
    landed = swap(queries, "hst", hosts, 1, 1)
    anchor = {}

    def pass_on(kv, after):
        (parts[kv],) = relay(source_first, parts[kv], parts_landed[kv], after)
        parts_landed[kv] = swap(parts[kv], "hst", hosts, *along[1])
        return parts[kv]

    def complete(kv, after):
        (held,) = relay(done_early, parts[kv], parts_landed[kv], after)
        anchor[kv] = held, swap(held, "hst", hosts, 1, 1)
        return held

    keep, give = source_part(lengths, own_keys, own_v, query_kv, queries, landed, q_rows, per_kv, ())
    landed = swap(give, "hst", hosts, 1, 1)
    done = own(4, 4, (keep,))
    source = merge_part([keep, landed], False, (done,))
    landed = swap(source, "hst", hosts, *along[0])
    done = pass_on(0, (source,))
    done = own(8, 8, (done,))
    source = merge_part([source, landed], False, (done,))
    landed = swap(source, "hst", hosts, *along[1])
    done = send_off(1, (source,))
    done = complete(0, (done,))
    anchor[0] = prepare(*anchor[0], True, (done,))
    results = {}

    def anchors(first, count, after, last=False):
        results[first] = anchor_part(
            lengths, ctx_q, states, own_keys, own_values, anchor[first // per_kv],
            first, count, per_kv, dict(results) if last else None, after,
        )
        return results[first]

    done = anchors(0, 4, ())
    attended = merge_part([source, landed], True, (done,))
    landed = swap(attended, "hst", hosts, 1, 1)
    done = pass_on(1, (attended,))
    done = anchors(4, 2, (done,))
    terms = project_part(attended, landed, out_weight, (done,))
    done = complete(1, (terms,))
    shares = [[(12, 4, True)], [(6, 2, False), (8, 4, False)]]
    step = 1
    while step < groups:
        landed = swap(terms, "tp", groups, step, step)
        last = False
        for first, count, last in shares.pop() if shares else ():
            if first == per_kv:
                anchor[1] = prepare(*anchor[1], True, (done,))
            done = anchors(first, count, (terms, done), last)
        terms = add_part(terms, landed, () if last else (done,))
        step *= 2
    for group in reversed(shares):
        for first, count, last in group:
            done = anchors(first, count, (), last)
    return done, terms


def solution(mesh):
    hosts, groups = mesh.shape["hst"], mesh.shape["tp"]
    return jax.shard_map(
        functools.partial(per_device, hosts, groups),
        mesh=mesh,
        in_specs=(
            P("hst", "tp"),
            P(None, "hst", None),
            P(),
            P("hst", "tp"),
            P(None, "hst", None),
            P("tp", "hst"),
        ),
        out_specs=(P("hst", "tp"), P(None, "hst")),
        check_vma=False,
    )
```

```python
import functools

import jax
import jax.numpy as jnp
from jax import lax
from jax.experimental import pallas as pl
from jax.experimental.pallas import tpu as pltpu
from jax.sharding import PartitionSpec as P

H = 64
KVH = 8
HD = 128
MASKED = -1e30
LOG2E = 1.4426950408889634
SCALE2 = HD ** (-0.5) * LOG2E
TINY = 2.0 ** -90
BF = jnp.bfloat16
F32 = jnp.float32
VMEM = pl.BlockSpec(memory_space=pltpu.VMEM)
ANY = pl.BlockSpec(memory_space=pl.ANY)
HBM = pl.BlockSpec(memory_space=pltpu.HBM)


def params(mib=20):
    return pltpu.CompilerParams(vmem_limit_bytes=mib * 2**20)


def dot_t(a, b):
    return lax.dot_general(a, b, (((1,), (1,)), ((), ())), preferred_element_type=F32)


def dot(a, b):
    return lax.dot_general(a, b, (((1,), (0,)), ((), ())), preferred_element_type=F32)


def spread(value, axis, source):
    kept = jnp.where(lax.axis_index(axis) == source, value, 0).astype(value.dtype)
    return lax.psum(kept, axis)


def swap(value, axis, size, even, odd):
    return lax.ppermute(value, axis, [(i, i ^ (odd if i & 1 else even)) for i in range(size)])


def pick_kernel(group_size, local_heads, kv_ref, k_ref, v_ref, sems):
    first = lax.axis_index("tp") * local_heads // group_size * HD
    cols = pl.ds(pl.multiple_of(first, HD), k_ref.shape[1])
    moves = [
        pltpu.make_async_copy(kv_ref.at[1, :, cols], v_ref, sems.at[1]),
        pltpu.make_async_copy(kv_ref.at[0, :, cols], k_ref, sems.at[0]),
    ]
    for move in moves:
        move.start()
    for move in moves:
        move.wait()


def pick(ctx_kv, kv_local, local_heads):
    return pl.pallas_call(
        functools.partial(pick_kernel, H // KVH, local_heads),
        out_shape=[jax.ShapeDtypeStruct((ctx_kv.shape[1], kv_local * HD), BF)] * 2,
        in_specs=[HBM],
        out_specs=[VMEM] * 2,
        scratch_shapes=[pltpu.SemaphoreType.DMA((2,))],
        compiler_params=params(52),
        cost_estimate=pl.CostEstimate(flops=0, bytes_accessed=2**22, transcendentals=0),
        name="pick_columns",
    )(ctx_kv)


def bit(value, at):
    return (value >> at) & 1


def small_call(kernel, name, shapes, inputs, after=()):
    return pl.pallas_call(
        kernel,
        out_shape=[jax.ShapeDtypeStruct(x, BF) for x in shapes],
        in_specs=[VMEM] * len(inputs) + [ANY] * len(after),
        out_specs=[VMEM] * len(shapes),
        compiler_params=params(),
        cost_estimate=pl.CostEstimate(flops=0, bytes_accessed=2**14, transcendentals=0),
        name=name,
    )(*inputs, *after)


def choose(condition, one, two):
    pl.when(condition)(one)
    pl.when(jnp.logical_not(condition))(two)


def take_rows(target, source, rows, cols=slice(None)):
    def run():
        target[:rows, :] = source[:rows, cols]

    return run


def by_chip(own, others, bits, after=()):
    rows, width = own.shape

    def kernel(*refs):
        out_ref, all_ref = refs[-2:]
        host = lax.axis_index("hst")
        for ref, flip in zip(refs, (0,) + tuple(bits)):
            start = pl.multiple_of((jnp.bitwise_xor(host, flip) >> 1) * rows, rows)
            all_ref[pl.ds(start, rows), :] = ref[...].astype(F32)
        out_ref[...] = all_ref[...].astype(BF)

    total = rows * (1 + len(bits))
    return pl.pallas_call(
        kernel,
        out_shape=jax.ShapeDtypeStruct((total, width), BF),
        in_specs=[VMEM] * (1 + len(bits)) + [ANY] * len(after),
        out_specs=VMEM,
        scratch_shapes=[pltpu.VMEM((total, width), F32)],
        compiler_params=params(),
        cost_estimate=pl.CostEstimate(flops=0, bytes_accessed=2**20, transcendentals=0),
        name="query_chips",
    )(own, *others, *after)


def relay(keep_of, one, two, after=(), split=1):
    slab, columns = one.shape
    width = columns // split

    def kernel(one_ref, two_ref, *rest):
        keep = keep_of(lax.axis_index("hst"))
        for j, out_ref in enumerate(rest[-split:]):
            cols = slice(j * width, (j + 1) * width)
            choose(keep, take_rows(out_ref, one_ref, slab, cols), take_rows(out_ref, two_ref, slab, cols))

    return small_call(kernel, "anchor_relay", [(slab, width)] * split, (one, two), after)


def add_part(one, two, after=()):
    def kernel(one_ref, two_ref, *rest):
        rest[-1][...] = (one_ref[...].astype(F32) + two_ref[...].astype(F32)).astype(BF)

    return small_call(kernel, "query_sum", [one.shape], (one, two), after)[0]


def prepare(first, second, swapped, after=()):
    slab, columns = first.shape

    def kernel(first_ref, second_ref, *rest):
        keys_ref, values_ref = rest[-2:]

        def fill(k_ref, v_ref):
            def run():
                for j in range(columns // HD):
                    cols = slice(j * HD, (j + 1) * HD)
                    at = 2 * j * HD
                    scaled = k_ref[:, cols].astype(F32) * SCALE2
                    high = scaled.astype(BF)
                    low = scaled - high.astype(F32)
                    keys_ref[at : at + HD, :] = high.astype(F32).T.astype(BF)
                    keys_ref[at + HD : at + 2 * HD, :] = low.T.astype(BF)
                    values_ref[:, at : at + HD] = v_ref[:, cols]
                    values_ref[:, at + HD : at + 2 * HD] = jnp.ones((slab, HD), BF)

            return run

        if swapped:
            even = bit(lax.axis_index("hst"), 0) == 0
            choose(even, fill(first_ref, second_ref), fill(second_ref, first_ref))
        else:
            fill(first_ref, second_ref)()

    shapes = [(2 * columns, slab), (slab, 2 * columns)]
    return small_call(kernel, "operands", shapes, (first, second), after)


def twice(query):
    return jnp.concatenate([query, query], 1)


def lanes(index, width):
    return pl.ds(pl.multiple_of(index * width, width), width)


def row_tile(slab):
    return 256 if slab % 256 == 0 else slab


def body_size(first, count, per_kv, most):
    def fits(size):
        bodies = range(first, first + count, size)
        return count % size == 0 and all(x // per_kv == (x + size - 1) // per_kv for x in bodies)

    return max(x for x in range(1, most + 1) if fits(x))


def own_kernel(first, count, per_kv, q_ref, k_ref, v_ref, *rest):
    state_ref = rest[-1]
    slab = q_ref.shape[0]
    tile = row_tile(slab)
    half = tile // 2
    heads = body_size(first, count, per_kv, 4)
    rows = lax.broadcasted_iota(jnp.int32, (half, half), 0)
    cols = lax.broadcasted_iota(jnp.int32, (half, half), 1)
    causal = cols <= rows
    chunks = slab // tile
    units = [(h, j) for h in range(heads) for j in range(chunks)]

    def body(i, carry):
        kv = lax.div(first + i * heads, per_kv)

        def scores(at):
            h, j = units[at]
            query = q_ref[j * tile :, lanes(first + i * heads + h, HD)]
            return dot(twice(query), k_ref[lanes(kv, 2 * HD), j * tile : (j + 1) * tile])

        def power(x):
            return jnp.exp2(x).astype(BF)

        def corner(x):
            return jnp.where(causal, jnp.exp2(x), 0.0).astype(BF)

        current = scores(0)
        totals = [None] * chunks
        for at, (h, j) in enumerate(units):
            following = scores(at + 1) if at + 1 < len(units) else None
            top = jnp.concatenate([corner(current[:half, :half]), jnp.zeros((half, half), BF)], 1)
            low = jnp.concatenate([power(current[half:tile, :half]), corner(current[half:tile, half:])], 1)
            expo = [top, low] if j == chunks - 1 else [top, low, power(current[tile:])]
            part = dot(jnp.concatenate(expo, 0), v_ref[j * tile : (j + 1) * tile, lanes(kv, 2 * HD)])
            for r in range(j, chunks):
                piece = part[(r - j) * tile : (r - j + 1) * tile]
                totals[r] = piece if j == 0 else totals[r] + piece
            state_ref[j * tile : (j + 1) * tile, lanes(i * heads + h, 2 * HD)] = totals[j]
            current = following
        return carry

    lax.fori_loop(0, count // heads, body, 0)


def own_part(ctx_q, own_k, own_v, first, count, per_kv, after=()):
    slab = ctx_q.shape[0]
    work = count * slab * (slab + row_tile(slab)) // 2
    return pl.pallas_call(
        functools.partial(own_kernel, first, count, per_kv),
        out_shape=jax.ShapeDtypeStruct((slab, count * 2 * HD), F32),
        in_specs=[VMEM] * 3 + [ANY] * len(after),
        out_specs=VMEM,
        compiler_params=params(),
        cost_estimate=pl.CostEstimate(
            flops=work * HD * 8, bytes_accessed=count * slab * HD * 6, transcendentals=work
        ),
        name="context_own",
    )(ctx_q, own_k, own_v, *after)


def length_of(lengths_ref, host):
    lengths = lengths_ref[...]
    index = lax.broadcasted_iota(jnp.int32, lengths.shape, 1)
    return jnp.sum(jnp.where(index == host, lengths, 0), axis=1, keepdims=True)


def anchor_kernel(first, count, bases, per_kv, last, befores, *refs):
    lengths_ref, q_ref, k_ref, v_ref, keys, vaug = refs[:6]
    hosts = lengths_ref.shape[1]
    state_refs = refs[6 : 6 + len(bases)]
    earlier = refs[6 + len(bases) : 6 + len(bases) + len(befores)]
    if last:
        full_ref, out_ref, sems = refs[-3:]
    else:
        out_ref = refs[-1]
    slab = q_ref.shape[0]
    heads = body_size(first, count, per_kv, 2 if last else 4)
    kv = first // per_kv
    host = lax.axis_index("hst")

    def hand_over(source, start, width, sem):
        target = full_ref.at[:, pl.ds(start * HD, width * HD)]
        return pltpu.make_async_copy(source, target, sems.at[sem])

    moves = [hand_over(earlier[n], *place, n) for n, place in enumerate(befores)]
    for move in moves:
        move.start()

    def part(start):
        def query_of(h):
            at = (first + start + h) * HD
            return q_ref[:, at : at + HD]

        def scores(h):
            return dot(twice(query_of(h)), keys[...])

        def state_of(h):
            head = first + start + h
            n = max(n for n, base in enumerate(bases) if base <= head)
            at = (head - bases[n]) * 2 * HD
            return state_refs[n][:, at : at + 2 * HD]

        def finish(h, total, sums, worst):
            inverse = pl.reciprocal(sums, approx=True)
            out_ref[:, (start + h) * HD : (start + h + 1) * HD] = (total * inverse).astype(BF)
            return jnp.minimum(worst, jnp.minimum(sums, inverse))

        def check(worst):
            @pl.when(jnp.logical_not(jnp.min(worst) > TINY))
            def _():
                exact_block(first + start, start, heads, host, kv, q_ref, k_ref, v_ref, keys, vaug, out_ref)

        @pl.when(host == 0)
        def _():
            worst = jnp.ones((slab, HD), F32)
            for h in range(heads):
                state = state_of(h)
                worst = finish(h, state[:, :HD], state[:, HD:], worst)
            check(worst)

        @pl.when(host > 0)
        def _():
            worst = jnp.ones((slab, HD), F32)
            current = scores(0)
            for h in range(heads):
                following = scores(h + 1) if h + 1 < heads else None
                expo = jnp.exp2(current)
                state = state_of(h)
                total = dot(expo.astype(BF), vaug[:, :HD]) + state[:, :HD]
                sums = jnp.sum(expo, axis=1, keepdims=True) + state[:, HD:]
                worst = finish(h, total, sums, worst)
                current = following
            check(worst)

        @pl.when(host * 4 >= hosts * 3)
        def _():
            own_len = length_of(lengths_ref, host)
            row_ids = lax.broadcasted_iota(jnp.int32, (slab, HD), 0)
            for h in range(start, start + heads):
                cols = slice(h * HD, (h + 1) * HD)
                kept = jnp.where(row_ids < own_len, out_ref[:, cols].astype(F32), 0.0)
                out_ref[:, cols] = kept.astype(BF)

        if last:
            source = out_ref.at[:, start * HD : (start + heads) * HD]
            move = hand_over(source, first + start, heads, len(befores) + start // heads)
            move.start()
            moves.append(move)

    for start in range(0, count, heads):
        part(start)
    for move in moves:
        move.wait()


def exact_block(q_head, out_head, heads, host, kv, q_ref, k_ref, v_ref, keys, vaug, out_ref):
    slab = q_ref.shape[0]
    tile = 64

    def body(i, carry):
        h = lax.div(i, slab // tile)
        r = lax.rem(i, slab // tile)
        at = pl.ds(pl.multiple_of(r * tile, tile), tile)
        query = q_ref[at, lanes(q_head + h, HD)]
        row_ids = lax.broadcasted_iota(jnp.int32, (tile, slab), 0) + r * tile
        key_ids = lax.broadcasted_iota(jnp.int32, (tile, slab), 1)
        own = dot(twice(query), k_ref[2 * kv * HD : 2 * (kv + 1) * HD, :])
        own = jnp.where(key_ids <= row_ids, own, MASKED)
        far = dot(twice(query), keys[...])
        far = jnp.where(host > 0, far, MASKED)
        peak = jnp.maximum(jnp.max(own, 1, keepdims=True), jnp.max(far, 1, keepdims=True))
        own = jnp.exp2(own - peak)
        far = jnp.where(host > 0, jnp.exp2(far - peak), 0.0)
        sums = jnp.sum(own, 1, keepdims=True) + jnp.sum(far, 1, keepdims=True)
        values = jnp.where(host > 0, vaug[:, :HD].astype(F32), 0.0).astype(BF)
        total = dot(own.astype(BF), v_ref[:, 2 * kv * HD : (2 * kv + 1) * HD]) + dot(far.astype(BF), values)
        out_ref[at, lanes(out_head + h, HD)] = (total / sums).astype(BF)
        return carry

    lax.fori_loop(0, heads * (slab // tile), body, 0)


def anchor_part(lengths, ctx_q, states, own_k, own_v, anchor, first, count, per_kv, befores=None, after=()):
    slab, width = ctx_q.shape
    work = count * slab * slab
    last = befores is not None
    ends = {x: x + y.shape[1] // (2 * HD) for x, y in states.items()}
    bases = tuple(x for x in sorted(states) if x < first + count and ends[x] > first)
    earlier = list(befores.values()) if last else []
    places = tuple((at, x.shape[1] // HD) for at, x in befores.items()) if last else ()
    results = jax.ShapeDtypeStruct((slab, count * HD), BF)
    scratch = []
    if last:
        scratch = [pltpu.VMEM(results.shape, BF), pltpu.SemaphoreType.DMA((len(earlier) + count,))]
        results = jax.ShapeDtypeStruct((slab, width), BF)
    return pl.pallas_call(
        functools.partial(anchor_kernel, first, count, bases, per_kv, last, places),
        out_shape=results,
        in_specs=[VMEM] * (6 + len(bases) + len(earlier)) + [ANY] * len(after),
        out_specs=ANY if last else VMEM,
        scratch_shapes=scratch,
        compiler_params=params(),
        cost_estimate=pl.CostEstimate(
            flops=work * HD * 8, bytes_accessed=count * slab * HD * 8, transcendentals=work
        ),
        name="context_anchor",
    )(lengths, ctx_q, own_k, own_v, *anchor, *[states[x] for x in bases], *earlier, *after)


PART = 16


def write_level(ref, width, level):
    lane = lax.broadcasted_iota(jnp.int32, level.shape, 1)
    parts = []
    for at in range(3):
        part = level.astype(BF).astype(F32)
        parts.append(part if at == 0 else pltpu.roll(part, at * PART, 1))
        level = level - part
    packed = jnp.where(lane < PART, parts[0], jnp.where(lane < 2 * PART, parts[1], parts[2]))
    ref[:, width : width + HD] = packed.astype(BF)


def read_level(ref, width):
    packed = ref[:, width : width + HD].astype(F32)
    return packed + pltpu.roll(packed, HD - PART, 1) + pltpu.roll(packed, HD - 2 * PART, 1)


def source_kernel(per_kv, q_rows, group_size, lengths_ref, k_ref, v_ref, self_ref, known_ref, landed_ref, *rest):
    keep_ref, send_ref, q_all, vaug = rest[-4:]
    slab, columns = v_ref.shape
    width = per_kv * columns
    query_count = 8 * q_rows
    host = lax.axis_index("hst")
    own_len = length_of(lengths_ref, host)
    rows = per_kv * query_count
    odd = bit(host, 0) == 1

    def place(even_ref, odd_ref):
        def run():
            parts = []
            for chip in range(4):
                at = slice(chip * q_rows, (chip + 1) * q_rows)
                parts += [even_ref[at, :].astype(F32), odd_ref[at, :].astype(F32)]
            queries = jnp.concatenate(parts, 0).astype(BF)
            for h in range(width // HD):
                q_all[h * query_count : (h + 1) * query_count, :] = queries[:, h * HD : (h + 1) * HD]

        return run

    choose(odd, place(landed_ref, known_ref), place(known_ref, landed_ref))

    first = lax.axis_index("tp") * (width // HD) // group_size * HD
    own_cols = pl.ds(pl.multiple_of(first, HD), columns)
    selves_kv = [self_ref[i, :, own_cols].astype(F32) for i in range(2)]
    lane = lax.broadcasted_iota(jnp.int32, (query_count, HD), 1)
    query_ids = lax.broadcasted_iota(jnp.int32, (query_count, HD), 0)
    self_ok = (host * q_rows + lane <= query_ids) & (lane < q_rows)
    self_ok = jnp.concatenate([self_ok] * per_kv, 0)
    pad = jnp.zeros((HD - q_rows, HD), F32)
    key_rows = lax.broadcasted_iota(jnp.int32, (slab, HD), 0)
    ones = jnp.where(key_rows < own_len, 1.0, 0.0).astype(BF)
    for j in range(columns // HD):
        values = v_ref[:, j * HD : (j + 1) * HD].astype(F32)
        vaug[:, 2 * j * HD : (2 * j + 1) * HD] = jnp.where(key_rows < own_len, values, 0.0).astype(BF)
        vaug[:, (2 * j + 1) * HD : (2 * j + 2) * HD] = ones

    def operands(j):
        cols = slice(j * HD, (j + 1) * HD)
        queries = q_all[j * rows : (j + 1) * rows, :]
        self_keys = jnp.concatenate([selves_kv[0][:, cols], pad], 0).astype(BF)
        self_values = jnp.concatenate([selves_kv[1][:, cols], pad], 0).astype(BF)
        near = dot(twice(queries), k_ref[2 * j * HD : 2 * (j + 1) * HD, :])
        selves = jnp.where(self_ok, dot_t(queries, self_keys) * SCALE2, MASKED)
        return near, selves, jnp.concatenate([self_values, jnp.ones((HD, HD), BF)], 1)

    def store(j, total, level):
        stats = jnp.zeros((query_count, HD), F32)
        for h in range(per_kv):
            stats = jnp.where(lane == h, level[h * query_count : (h + 1) * query_count, :], stats)

        def put(out_ref):
            def run():
                for h in range(per_kv):
                    part = total[h * query_count : (h + 1) * query_count, :]
                    out_ref[:, h * HD : (h + 1) * HD] = part.astype(BF)
                write_level(out_ref, per_kv * HD, stats)

            return run

        choose(odd if j else jnp.logical_not(odd), put(keep_ref), put(send_ref))

    worst = jnp.ones((rows, HD), F32)
    found = []
    for j in range(columns // HD):
        near, selves, self_values = operands(j)
        near = jnp.exp2(near).astype(BF)
        selves = jnp.exp2(selves).astype(BF)
        total = dot(near, vaug[:, 2 * j * HD : (2 * j + 2) * HD]) + dot(selves, self_values)
        sums = total[:, HD:]
        inverse = 1.0 / sums
        worst = jnp.minimum(worst, jnp.minimum(sums, inverse))
        found.append((total[:, :HD] * inverse, jnp.log2(sums)))
    for j, result in enumerate(found):
        store(j, *result)

    @pl.when(jnp.logical_not(jnp.min(worst) > TINY))
    def _():
        key_ids = lax.broadcasted_iota(jnp.int32, (query_count, slab), 1)
        heads_ok = (host * q_rows + lane <= query_ids) & (lane < q_rows)
        for j in range(columns // HD):
            cols = slice(j * HD, (j + 1) * HD)
            self_keys = jnp.concatenate([selves_kv[0][:, cols], pad], 0).astype(BF)
            self_values = jnp.concatenate([selves_kv[1][:, cols], pad], 0).astype(BF)
            self_values = jnp.concatenate([self_values, jnp.ones((HD, HD), BF)], 1)
            mine = odd if j else jnp.logical_not(odd)

            def body(h, stats):
                at = pl.ds(pl.multiple_of((j * per_kv + h) * query_count, query_count), query_count)
                queries = q_all[at, :]
                near = dot(twice(queries), k_ref[2 * j * HD : 2 * (j + 1) * HD, :])
                near = jnp.where(key_ids < own_len, near, MASKED)
                selves = jnp.where(heads_ok, dot_t(queries, self_keys) * SCALE2, MASKED)
                peak = jnp.maximum(jnp.max(near, 1, keepdims=True), jnp.max(selves, 1, keepdims=True))
                near = jnp.exp2(near - peak).astype(BF)
                selves = jnp.exp2(selves - peak).astype(BF)
                total = dot(near, vaug[:, 2 * j * HD : (2 * j + 2) * HD]) + dot(selves, self_values)
                result = (total[:, :HD] / total[:, HD:]).astype(BF)

                def put(out_ref):
                    def run():
                        out_ref[:, lanes(h, HD)] = result

                    return run

                choose(mine, put(keep_ref), put(send_ref))
                return jnp.where(lane == h, peak + jnp.log2(total[:, HD:]), stats)

            stats = lax.fori_loop(0, per_kv, body, jnp.zeros((query_count, HD), F32))

            def put_level(out_ref):
                def run():
                    write_level(out_ref, per_kv * HD, stats)

                return run

            choose(mine, put_level(keep_ref), put_level(send_ref))


def source_part(lengths, own_k, own_v, query_kv, known, landed, q_rows, per_kv, after=()):
    slab, columns = own_v.shape
    width = per_kv * columns
    count = 8 * q_rows
    work = count * (width // HD) * slab
    return pl.pallas_call(
        functools.partial(source_kernel, per_kv, q_rows, H // KVH),
        out_shape=[jax.ShapeDtypeStruct((count, (per_kv + 1) * HD), BF)] * 2,
        in_specs=[VMEM] * 6 + [ANY] * len(after),
        out_specs=[VMEM] * 2,
        scratch_shapes=[pltpu.VMEM((count * width // HD, HD), BF), pltpu.VMEM((slab, 2 * columns), BF)],
        compiler_params=params(),
        cost_estimate=pl.CostEstimate(flops=work * HD * 8, bytes_accessed=2**21, transcendentals=work),
        name="query_source",
    )(lengths, own_k, own_v, query_kv, known, landed, *after)


def merge_part(groups, last, after=()):
    rows, wide = groups[0].shape
    width = wide - HD

    def kernel(*refs):
        in_refs, out_ref = refs[: len(groups)], refs[-1]
        levels = [read_level(ref, width) for ref in in_refs]
        peak = functools.reduce(jnp.maximum, levels)
        weights = [jnp.exp2(x - peak) for x in levels]
        whole = functools.reduce(jnp.add, weights)
        shares = [w / whole for w in weights]
        if not last:
            write_level(out_ref, width, peak + jnp.log2(whole))
        for h in range(width // HD):
            cols = slice(h * HD, (h + 1) * HD)
            total = sum(w[:, h : h + 1] * ref[:, cols].astype(F32) for w, ref in zip(shares, in_refs))
            out_ref[:, cols] = total.astype(BF)

    return small_call(kernel, "query_merge", [(rows, width if last else wide)], groups, after)[0]


def project_part(own, other, out_weight, after=()):
    rows, half = own.shape
    depth, columns = out_weight.shape

    def kernel(w_ref, own_ref, other_ref, *rest):
        out_ref, attended = rest[-2:]

        def put(first, second):
            def run():
                attended[:, :half] = first[...]
                attended[:, half:] = second[...]

            return run

        even = bit(lax.axis_index("hst"), 0) == 0
        choose(even, put(own_ref, other_ref), put(other_ref, own_ref))
        out_ref[...] = dot(attended[...], w_ref[...]).astype(BF)

    return pl.pallas_call(
        kernel,
        out_shape=jax.ShapeDtypeStruct((rows, columns), BF),
        in_specs=[VMEM] * 3 + [ANY] * len(after),
        out_specs=VMEM,
        scratch_shapes=[pltpu.VMEM((rows, depth), BF)],
        compiler_params=params(),
        cost_estimate=pl.CostEstimate(
            flops=2 * rows * depth * columns, bytes_accessed=2 * depth * columns, transcendentals=0
        ),
        name="query_project",
    )(out_weight, own, other, *after)


def general_queries(lengths, own_k, own_v, self_kv, query_q, out_weight, per_kv):
    own_kv = jnp.stack([own_k, own_v], 0)
    host_id = lax.axis_index("hst")
    local_heads = query_q.shape[1] // HD
    kv_local = own_kv.shape[2] // HD
    slab_rows = own_kv.shape[1]
    own_len = lengths[host_id]
    row_ids = jnp.arange(slab_rows)
    all_queries = lax.all_gather(query_q, "hst", axis=0, tiled=True)
    query_count = all_queries.shape[0]
    q_rows = query_q.shape[0]
    source = jnp.concatenate([own_kv, self_kv], 1)
    source = source.reshape(2, slab_rows + q_rows, kv_local, HD).transpose(0, 2, 1, 3)
    query_ids = jnp.arange(query_count)
    context_ok = jnp.broadcast_to(row_ids[None, :] < own_len, (query_count, slab_rows))
    self_ok = (host_id * q_rows + jnp.arange(q_rows))[None, :] <= query_ids[:, None]
    seen_ok = jnp.concatenate([context_ok, self_ok], 1)
    query_heads = all_queries.reshape(query_count, local_heads, HD).transpose(1, 0, 2)

    def score_head(operands):
        query_rows, head_index = operands
        kv_index = head_index // per_kv
        scores = dot_t(query_rows, source[0, kv_index]) * HD ** (-0.5)
        scores = jnp.where(seen_ok, scores, MASKED)
        peak = jnp.max(scores, axis=1)
        expo = jnp.exp(scores - peak[:, None])
        return peak, jnp.sum(expo, axis=1), dot(expo.astype(BF), source[1, kv_index])

    maxima, totals, outputs = lax.map(score_head, (query_heads, jnp.arange(local_heads)))
    factor = jnp.exp(maxima - lax.pmax(maxima, "hst"))
    denominator, summed = lax.psum((totals * factor, outputs * factor[..., None]), "hst")
    attended = (summed / denominator[..., None]).astype(BF)
    attended = attended.transpose(1, 0, 2).reshape(query_count, local_heads * HD)
    return lax.psum(dot(attended, out_weight), "tp").astype(BF)


def per_device(hosts, groups, ctx_q, ctx_kv, lengths, query_q, query_kv, out_weight):
    slab = ctx_q.shape[0]
    local_heads = ctx_q.shape[1] // HD
    group_size = H // KVH
    kv_local = max(1, local_heads // group_size)
    per_kv = min(local_heads, group_size)
    q_rows = query_q.shape[0]
    host = lax.axis_index("hst")
    fast = hosts == 8 and groups & (groups - 1) == 0
    fast = fast and q_rows == 8 and local_heads == 16 and per_kv == 8

    if not fast:
        kv_first = lax.axis_index("tp") * local_heads // group_size
        self_kv = lax.dynamic_slice_in_dim(query_kv, kv_first * HD, kv_local * HD, 2)
        own_k, own_v = pick(ctx_kv, kv_local, local_heads)
        query_out = general_queries(lengths, own_k, own_v, self_kv, query_q, out_weight, per_kv)
        k, v = spread(jnp.stack([own_k, own_v]), "hst", 0)
        lengths = lengths.reshape(1, hosts)
        own_k, own_v = prepare(own_k, own_v, False)
        anchor = prepare(k, v, False)
        state = own_part(ctx_q, own_k, own_v, 0, local_heads, per_kv)
        results = {}
        for first in range(0, local_heads, per_kv):
            cols = slice(2 * first // per_kv * HD, 2 * (first // per_kv + 1) * HD)
            last = first + per_kv == local_heads
            results[first] = anchor_part(
                lengths, ctx_q, {0: state}, own_k, own_v, (anchor[0][cols, :], anchor[1][:, cols]),
                first, per_kv, per_kv, dict(results) if last else None,
            )
        return results[first], query_out

    lengths = lengths.reshape(1, hosts)
    states = {}

    def own(first, count, after=()):
        states[first] = own_part(ctx_q, own_keys, own_values, first, count, per_kv, after)
        return states[first]

    along = ((2, 4), (4, 2))

    def is_even(h):
        return bit(h, 0) == 0

    def source_first(h):
        return h < 2

    done_early = (
        lambda h: (h <= 2) | (h == 5),
        lambda h: (h <= 1) | (h == 3) | (h == 4),
    )

    bits = (6, 2, 4)
    landed = [swap(query_q, "hst", hosts, x, x) for x in bits]
    own_k, own_v = pick(ctx_kv, kv_local, local_heads)
    value_landed = swap(own_v, "hst", hosts, 1, 1)
    own_keys, own_values = prepare(own_k, own_v, False)
    done = own(0, 2)
    parts = list(relay(is_even, own_k, value_landed, (done,), kv_local))
    parts_landed = [swap(x, "hst", hosts, *along[kv]) for kv, x in enumerate(parts)]
    done = own(2, 2, (parts[0],))
    queries = by_chip(query_q, landed, bits, (done,))
    landed = swap(queries, "hst", hosts, 1, 1)
    anchor = {}

    def pass_on(kv, after):
        (parts[kv],) = relay(source_first, parts[kv], parts_landed[kv], after)
        parts_landed[kv] = swap(parts[kv], "hst", hosts, *along[1 - kv])
        return parts[kv]

    def complete(kv, after):
        (held,) = relay(done_early[kv], parts[kv], parts_landed[kv], after)
        anchor[kv] = held, swap(held, "hst", hosts, 1, 1)
        return held

    keep, give = source_part(lengths, own_keys, own_v, query_kv, queries, landed, q_rows, per_kv, ())
    landed = swap(give, "hst", hosts, 1, 1)
    done = own(4, 4, (keep,))
    source = merge_part([keep, landed], False, (done,))
    landed = swap(source, "hst", hosts, *along[0])
    done = pass_on(0, (source,))
    done = own(8, 8, (done,))
    source = merge_part([source, landed], False, (done,))
    landed = swap(source, "hst", hosts, *along[1])
    done = complete(0, (source,))
    done = pass_on(1, (done,))
    anchor[0] = prepare(*anchor[0], True, (done,))
    results = {}

    def anchors(first, count, after, last=False):
        results[first] = anchor_part(
            lengths, ctx_q, states, own_keys, own_values, anchor[first // per_kv],
            first, count, per_kv, dict(results) if last else None, after,
        )
        return results[first]

    done = anchors(0, 4, ())
    attended = merge_part([source, landed], True, (done,))
    landed = swap(attended, "hst", hosts, 1, 1)
    done = anchors(4, 2, (attended,))
    done = complete(1, (done,))
    terms = project_part(attended, landed, out_weight, (done,))
    done = terms
    shares = [[(12, 4, True)], [(6, 2, False), (8, 4, False)]]
    step = 1
    while step < groups:
        landed = swap(terms, "tp", groups, step, step)
        last = False
        for first, count, last in shares.pop() if shares else ():
            if first == per_kv:
                anchor[1] = prepare(*anchor[1], True, (done,))
            done = anchors(first, count, (terms, done), last)
        terms = add_part(terms, landed, () if last else (done,))
        step *= 2
    for group in reversed(shares):
        for first, count, last in group:
            done = anchors(first, count, (), last)
    return done, terms


def solution(mesh):
    hosts, groups = mesh.shape["hst"], mesh.shape["tp"]
    return jax.shard_map(
        functools.partial(per_device, hosts, groups),
        mesh=mesh,
        in_specs=(
            P("hst", "tp"),
            P(None, "hst", None),
            P(),
            P("hst", "tp"),
            P(None, "hst", None),
            P("tp", "hst"),
        ),
        out_specs=(P("hst", "tp"), P(None, "hst")),
        check_vma=False,
    )
```

```python
import functools

import jax
import jax.numpy as jnp
from jax import lax
from jax.experimental import pallas as pl
from jax.experimental.pallas import tpu as pltpu
from jax.sharding import PartitionSpec as P

H = 64
KVH = 8
HD = 128
MASKED = -1e30
LOG2E = 1.4426950408889634
SCALE2 = HD ** (-0.5) * LOG2E
TINY = 2.0 ** -90
BF = jnp.bfloat16
F32 = jnp.float32
VMEM = pl.BlockSpec(memory_space=pltpu.VMEM)
ANY = pl.BlockSpec(memory_space=pl.ANY)
HBM = pl.BlockSpec(memory_space=pltpu.HBM)


def params(mib=20):
    return pltpu.CompilerParams(vmem_limit_bytes=mib * 2**20)


def dot_t(a, b):
    return lax.dot_general(a, b, (((1,), (1,)), ((), ())), preferred_element_type=F32)


def dot(a, b):
    return lax.dot_general(a, b, (((1,), (0,)), ((), ())), preferred_element_type=F32)


def spread(value, axis, source):
    kept = jnp.where(lax.axis_index(axis) == source, value, 0).astype(value.dtype)
    return lax.psum(kept, axis)


def swap(value, axis, size, even, odd):
    return lax.ppermute(value, axis, [(i, i ^ (odd if i & 1 else even)) for i in range(size)])


def pick_kernel(group_size, local_heads, kv_ref, k_ref, v_ref, sems):
    first = lax.axis_index("tp") * local_heads // group_size * HD
    cols = pl.ds(pl.multiple_of(first, HD), k_ref.shape[1])
    moves = [
        pltpu.make_async_copy(kv_ref.at[1, :, cols], v_ref, sems.at[1]),
        pltpu.make_async_copy(kv_ref.at[0, :, cols], k_ref, sems.at[0]),
    ]
    for move in moves:
        move.start()
    for move in moves:
        move.wait()


def pick(ctx_kv, kv_local, local_heads):
    return pl.pallas_call(
        functools.partial(pick_kernel, H // KVH, local_heads),
        out_shape=[jax.ShapeDtypeStruct((ctx_kv.shape[1], kv_local * HD), BF)] * 2,
        in_specs=[HBM],
        out_specs=[VMEM] * 2,
        scratch_shapes=[pltpu.SemaphoreType.DMA((2,))],
        compiler_params=params(52),
        cost_estimate=pl.CostEstimate(flops=0, bytes_accessed=2**22, transcendentals=0),
        name="pick_columns",
    )(ctx_kv)


def bit(value, at):
    return (value >> at) & 1


def small_call(kernel, name, shapes, inputs, after=()):
    return pl.pallas_call(
        kernel,
        out_shape=[jax.ShapeDtypeStruct(x, BF) for x in shapes],
        in_specs=[VMEM] * len(inputs) + [ANY] * len(after),
        out_specs=[VMEM] * len(shapes),
        compiler_params=params(),
        cost_estimate=pl.CostEstimate(flops=0, bytes_accessed=2**14, transcendentals=0),
        name=name,
    )(*inputs, *after)


def choose(condition, one, two):
    pl.when(condition)(one)
    pl.when(jnp.logical_not(condition))(two)


def take_rows(target, source, rows, cols=slice(None)):
    def run():
        target[:rows, :] = source[:rows, cols]

    return run


def by_chip(own, others, bits, after=()):
    rows, width = own.shape

    def kernel(*refs):
        out_ref, all_ref = refs[-2:]
        host = lax.axis_index("hst")
        for ref, flip in zip(refs, (0,) + tuple(bits)):
            start = pl.multiple_of((jnp.bitwise_xor(host, flip) >> 1) * rows, rows)
            all_ref[pl.ds(start, rows), :] = ref[...].astype(F32)
        out_ref[...] = all_ref[...].astype(BF)

    total = rows * (1 + len(bits))
    return pl.pallas_call(
        kernel,
        out_shape=jax.ShapeDtypeStruct((total, width), BF),
        in_specs=[VMEM] * (1 + len(bits)) + [ANY] * len(after),
        out_specs=VMEM,
        scratch_shapes=[pltpu.VMEM((total, width), F32)],
        compiler_params=params(),
        cost_estimate=pl.CostEstimate(flops=0, bytes_accessed=2**20, transcendentals=0),
        name="query_chips",
    )(own, *others, *after)


def relay(keep_of, one, two, after=(), kv=0):
    cols = slice(kv * HD, (kv + 1) * HD)
    slab = one.shape[0]

    def kernel(one_ref, two_ref, *rest):
        keep = keep_of(lax.axis_index("hst"))
        choose(keep, take_rows(rest[-1], one_ref, slab, cols), take_rows(rest[-1], two_ref, slab, cols))

    return small_call(kernel, "anchor_relay", [(slab, HD)], (one, two), after)


def add_part(one, two, after=()):
    def kernel(one_ref, two_ref, *rest):
        rest[-1][...] = (one_ref[...].astype(F32) + two_ref[...].astype(F32)).astype(BF)

    return small_call(kernel, "query_sum", [one.shape], (one, two), after)[0]


def prepare(first, second, swapped, after=()):
    slab, columns = first.shape

    def kernel(first_ref, second_ref, *rest):
        keys_ref, values_ref = rest[-2:]

        def fill(k_ref, v_ref):
            def run():
                for j in range(columns // HD):
                    cols = slice(j * HD, (j + 1) * HD)
                    at = 2 * j * HD
                    scaled = k_ref[:, cols].astype(F32) * SCALE2
                    high = scaled.astype(BF)
                    low = scaled - high.astype(F32)
                    keys_ref[at : at + HD, :] = high.astype(F32).T.astype(BF)
                    keys_ref[at + HD : at + 2 * HD, :] = low.T.astype(BF)
                    values_ref[:, at : at + HD] = v_ref[:, cols]
                    values_ref[:, at + HD : at + 2 * HD] = jnp.ones((slab, HD), BF)

            return run

        if swapped:
            even = bit(lax.axis_index("hst"), 0) == 0
            choose(even, fill(first_ref, second_ref), fill(second_ref, first_ref))
        else:
            fill(first_ref, second_ref)()

    shapes = [(2 * columns, slab), (slab, 2 * columns)]
    return small_call(kernel, "operands", shapes, (first, second), after)


def twice(query):
    return jnp.concatenate([query, query], 1)


def lanes(index, width):
    return pl.ds(pl.multiple_of(index * width, width), width)


def row_tile(slab):
    return 256 if slab % 256 == 0 else slab


def body_size(first, count, per_kv, most):
    def fits(size):
        bodies = range(first, first + count, size)
        return count % size == 0 and all(x // per_kv == (x + size - 1) // per_kv for x in bodies)

    return max(x for x in range(1, most + 1) if fits(x))


def own_kernel(first, count, per_kv, q_ref, k_ref, v_ref, *rest):
    state_ref = rest[-1]
    slab = q_ref.shape[0]
    tile = row_tile(slab)
    half = tile // 2
    heads = body_size(first, count, per_kv, 4)
    rows = lax.broadcasted_iota(jnp.int32, (half, half), 0)
    cols = lax.broadcasted_iota(jnp.int32, (half, half), 1)
    causal = cols <= rows
    chunks = slab // tile
    units = [(h, j) for h in range(heads) for j in range(chunks)]

    def body(i, carry):
        kv = lax.div(first + i * heads, per_kv)

        def scores(at):
            h, j = units[at]
            query = q_ref[j * tile :, lanes(first + i * heads + h, HD)]
            return dot(twice(query), k_ref[lanes(kv, 2 * HD), j * tile : (j + 1) * tile])

        def power(x):
            return jnp.exp2(x).astype(BF)

        def corner(x):
            return jnp.where(causal, jnp.exp2(x), 0.0).astype(BF)

        current = scores(0)
        totals = [None] * chunks
        for at, (h, j) in enumerate(units):
            following = scores(at + 1) if at + 1 < len(units) else None
            top = jnp.concatenate([corner(current[:half, :half]), jnp.zeros((half, half), BF)], 1)
            low = jnp.concatenate([power(current[half:tile, :half]), corner(current[half:tile, half:])], 1)
            expo = [top, low] if j == chunks - 1 else [top, low, power(current[tile:])]
            part = dot(jnp.concatenate(expo, 0), v_ref[j * tile : (j + 1) * tile, lanes(kv, 2 * HD)])
            for r in range(j, chunks):
                piece = part[(r - j) * tile : (r - j + 1) * tile]
                totals[r] = piece if j == 0 else totals[r] + piece
            state_ref[j * tile : (j + 1) * tile, lanes(i * heads + h, 2 * HD)] = totals[j]
            current = following
        return carry

    lax.fori_loop(0, count // heads, body, 0)


def own_part(ctx_q, own_k, own_v, first, count, per_kv, after=()):
    slab = ctx_q.shape[0]
    work = count * slab * (slab + row_tile(slab)) // 2
    return pl.pallas_call(
        functools.partial(own_kernel, first, count, per_kv),
        out_shape=jax.ShapeDtypeStruct((slab, count * 2 * HD), F32),
        in_specs=[VMEM] * 3 + [ANY] * len(after),
        out_specs=VMEM,
        compiler_params=params(),
        cost_estimate=pl.CostEstimate(
            flops=work * HD * 8, bytes_accessed=count * slab * HD * 6, transcendentals=work
        ),
        name="context_own",
    )(ctx_q, own_k, own_v, *after)


def length_of(lengths_ref, host):
    lengths = lengths_ref[...]
    index = lax.broadcasted_iota(jnp.int32, lengths.shape, 1)
    return jnp.sum(jnp.where(index == host, lengths, 0), axis=1, keepdims=True)


def anchor_kernel(first, count, bases, per_kv, last, befores, *refs):
    lengths_ref, q_ref, k_ref, v_ref, keys, vaug = refs[:6]
    hosts = lengths_ref.shape[1]
    state_refs = refs[6 : 6 + len(bases)]
    earlier = refs[6 + len(bases) : 6 + len(bases) + len(befores)]
    if last:
        full_ref, out_ref, sems = refs[-3:]
    else:
        out_ref = refs[-1]
    slab = q_ref.shape[0]
    heads = body_size(first, count, per_kv, 2 if last else 4)
    kv = first // per_kv
    host = lax.axis_index("hst")

    def hand_over(source, start, width, sem):
        target = full_ref.at[:, pl.ds(start * HD, width * HD)]
        return pltpu.make_async_copy(source, target, sems.at[sem])

    moves = [hand_over(earlier[n], *place, n) for n, place in enumerate(befores)]
    for move in moves:
        move.start()

    def part(start):
        def query_of(h):
            at = (first + start + h) * HD
            return q_ref[:, at : at + HD]

        def scores(h):
            return dot(twice(query_of(h)), keys[...])

        def state_of(h):
            head = first + start + h
            n = max(n for n, base in enumerate(bases) if base <= head)
            at = (head - bases[n]) * 2 * HD
            return state_refs[n][:, at : at + 2 * HD]

        def finish(h, total, sums, worst):
            inverse = pl.reciprocal(sums, approx=True)
            out_ref[:, (start + h) * HD : (start + h + 1) * HD] = (total * inverse).astype(BF)
            return jnp.minimum(worst, jnp.minimum(sums, inverse))

        def check(worst):
            @pl.when(jnp.logical_not(jnp.min(worst) > TINY))
            def _():
                exact_block(first + start, start, heads, host, kv, q_ref, k_ref, v_ref, keys, vaug, out_ref)

        @pl.when(host == 0)
        def _():
            worst = jnp.ones((slab, HD), F32)
            for h in range(heads):
                state = state_of(h)
                worst = finish(h, state[:, :HD], state[:, HD:], worst)
            check(worst)

        @pl.when(host > 0)
        def _():
            worst = jnp.ones((slab, HD), F32)
            current = scores(0)
            for h in range(heads):
                following = scores(h + 1) if h + 1 < heads else None
                expo = jnp.exp2(current)
                state = state_of(h)
                total = dot(expo.astype(BF), vaug[:, :HD]) + state[:, :HD]
                sums = jnp.sum(expo, axis=1, keepdims=True) + state[:, HD:]
                worst = finish(h, total, sums, worst)
                current = following
            check(worst)

        @pl.when(host * 4 >= hosts * 3)
        def _():
            own_len = length_of(lengths_ref, host)
            row_ids = lax.broadcasted_iota(jnp.int32, (slab, HD), 0)
            for h in range(start, start + heads):
                cols = slice(h * HD, (h + 1) * HD)
                kept = jnp.where(row_ids < own_len, out_ref[:, cols].astype(F32), 0.0)
                out_ref[:, cols] = kept.astype(BF)

        if last:
            source = out_ref.at[:, start * HD : (start + heads) * HD]
            move = hand_over(source, first + start, heads, len(befores) + start // heads)
            move.start()
            moves.append(move)

    for start in range(0, count, heads):
        part(start)
    for move in moves:
        move.wait()


def exact_block(q_head, out_head, heads, host, kv, q_ref, k_ref, v_ref, keys, vaug, out_ref):
    slab = q_ref.shape[0]
    tile = 64

    def body(i, carry):
        h = lax.div(i, slab // tile)
        r = lax.rem(i, slab // tile)
        at = pl.ds(pl.multiple_of(r * tile, tile), tile)
        query = q_ref[at, lanes(q_head + h, HD)]
        row_ids = lax.broadcasted_iota(jnp.int32, (tile, slab), 0) + r * tile
        key_ids = lax.broadcasted_iota(jnp.int32, (tile, slab), 1)
        own = dot(twice(query), k_ref[2 * kv * HD : 2 * (kv + 1) * HD, :])
        own = jnp.where(key_ids <= row_ids, own, MASKED)
        far = dot(twice(query), keys[...])
        far = jnp.where(host > 0, far, MASKED)
        peak = jnp.maximum(jnp.max(own, 1, keepdims=True), jnp.max(far, 1, keepdims=True))
        own = jnp.exp2(own - peak)
        far = jnp.where(host > 0, jnp.exp2(far - peak), 0.0)
        sums = jnp.sum(own, 1, keepdims=True) + jnp.sum(far, 1, keepdims=True)
        values = jnp.where(host > 0, vaug[:, :HD].astype(F32), 0.0).astype(BF)
        total = dot(own.astype(BF), v_ref[:, 2 * kv * HD : (2 * kv + 1) * HD]) + dot(far.astype(BF), values)
        out_ref[at, lanes(out_head + h, HD)] = (total / sums).astype(BF)
        return carry

    lax.fori_loop(0, heads * (slab // tile), body, 0)


def anchor_part(lengths, ctx_q, states, own_k, own_v, anchor, first, count, per_kv, befores=None, after=(), weight=8):
    slab, width = ctx_q.shape
    work = count * slab * slab
    last = befores is not None
    ends = {x: x + y.shape[1] // (2 * HD) for x, y in states.items()}
    bases = tuple(x for x in sorted(states) if x < first + count and ends[x] > first)
    earlier = list(befores.values()) if last else []
    places = tuple((at, x.shape[1] // HD) for at, x in befores.items()) if last else ()
    results = jax.ShapeDtypeStruct((slab, count * HD), BF)
    scratch = []
    if last:
        scratch = [pltpu.VMEM(results.shape, BF), pltpu.SemaphoreType.DMA((len(earlier) + count,))]
        results = jax.ShapeDtypeStruct((slab, width), BF)
    return pl.pallas_call(
        functools.partial(anchor_kernel, first, count, bases, per_kv, last, places),
        out_shape=results,
        in_specs=[VMEM] * (6 + len(bases) + len(earlier)) + [ANY] * len(after),
        out_specs=ANY if last else VMEM,
        scratch_shapes=scratch,
        compiler_params=params(),
        cost_estimate=pl.CostEstimate(
            flops=work * HD * weight, bytes_accessed=0, transcendentals=0
        ),
        name="context_anchor",
    )(lengths, ctx_q, own_k, own_v, *anchor, *[states[x] for x in bases], *earlier, *after)


PART = 16


def write_level(ref, width, level):
    lane = lax.broadcasted_iota(jnp.int32, level.shape, 1)
    parts = []
    for at in range(3):
        part = level.astype(BF).astype(F32)
        parts.append(part if at == 0 else pltpu.roll(part, at * PART, 1))
        level = level - part
    packed = jnp.where(lane < PART, parts[0], jnp.where(lane < 2 * PART, parts[1], parts[2]))
    ref[:, width : width + HD] = packed.astype(BF)


def read_level(ref, width):
    packed = ref[:, width : width + HD].astype(F32)
    return packed + pltpu.roll(packed, HD - PART, 1) + pltpu.roll(packed, HD - 2 * PART, 1)


def source_kernel(per_kv, q_rows, group_size, lengths_ref, k_ref, v_ref, self_ref, known_ref, landed_ref, *rest):
    keep_ref, send_ref, q_all, vaug = rest[-4:]
    slab, columns = v_ref.shape
    width = per_kv * columns
    query_count = 8 * q_rows
    host = lax.axis_index("hst")
    own_len = length_of(lengths_ref, host)
    rows = per_kv * query_count
    odd = bit(host, 0) == 1

    def place(even_ref, odd_ref):
        def run():
            parts = []
            for chip in range(4):
                at = slice(chip * q_rows, (chip + 1) * q_rows)
                parts += [even_ref[at, :].astype(F32), odd_ref[at, :].astype(F32)]
            queries = jnp.concatenate(parts, 0).astype(BF)
            for h in range(width // HD):
                q_all[h * query_count : (h + 1) * query_count, :] = queries[:, h * HD : (h + 1) * HD]

        return run

    choose(odd, place(landed_ref, known_ref), place(known_ref, landed_ref))

    first = lax.axis_index("tp") * (width // HD) // group_size * HD
    own_cols = pl.ds(pl.multiple_of(first, HD), columns)
    selves_kv = [self_ref[i, :, own_cols].astype(F32) for i in range(2)]
    lane = lax.broadcasted_iota(jnp.int32, (query_count, HD), 1)
    query_ids = lax.broadcasted_iota(jnp.int32, (query_count, HD), 0)
    self_ok = (host * q_rows + lane <= query_ids) & (lane < q_rows)
    self_ok = jnp.concatenate([self_ok] * per_kv, 0)
    pad = jnp.zeros((HD - q_rows, HD), F32)
    key_rows = lax.broadcasted_iota(jnp.int32, (slab, HD), 0)
    ones = jnp.where(key_rows < own_len, 1.0, 0.0).astype(BF)
    for j in range(columns // HD):
        values = v_ref[:, j * HD : (j + 1) * HD].astype(F32)
        vaug[:, 2 * j * HD : (2 * j + 1) * HD] = jnp.where(key_rows < own_len, values, 0.0).astype(BF)
        vaug[:, (2 * j + 1) * HD : (2 * j + 2) * HD] = ones

    def operands(j):
        cols = slice(j * HD, (j + 1) * HD)
        queries = q_all[j * rows : (j + 1) * rows, :]
        self_keys = jnp.concatenate([selves_kv[0][:, cols], pad], 0).astype(BF)
        self_values = jnp.concatenate([selves_kv[1][:, cols], pad], 0).astype(BF)
        near = dot(twice(queries), k_ref[2 * j * HD : 2 * (j + 1) * HD, :])
        selves = jnp.where(self_ok, dot_t(queries, self_keys) * SCALE2, MASKED)
        return near, selves, jnp.concatenate([self_values, jnp.ones((HD, HD), BF)], 1)

    def store(j, total, level):
        stats = jnp.zeros((query_count, HD), F32)
        for h in range(per_kv):
            stats = jnp.where(lane == h, level[h * query_count : (h + 1) * query_count, :], stats)

        def put(out_ref):
            def run():
                for h in range(per_kv):
                    part = total[h * query_count : (h + 1) * query_count, :]
                    out_ref[:, h * HD : (h + 1) * HD] = part.astype(BF)
                write_level(out_ref, per_kv * HD, stats)

            return run

        choose(odd if j else jnp.logical_not(odd), put(keep_ref), put(send_ref))

    worst = jnp.ones((rows, HD), F32)
    found = []
    for j in range(columns // HD):
        near, selves, self_values = operands(j)
        near = jnp.exp2(near).astype(BF)
        selves = jnp.exp2(selves).astype(BF)
        total = dot(near, vaug[:, 2 * j * HD : (2 * j + 2) * HD]) + dot(selves, self_values)
        sums = total[:, HD:]
        inverse = 1.0 / sums
        worst = jnp.minimum(worst, jnp.minimum(sums, inverse))
        found.append((total[:, :HD] * inverse, jnp.log2(sums)))
    for j, result in enumerate(found):
        store(j, *result)

    @pl.when(jnp.logical_not(jnp.min(worst) > TINY))
    def _():
        key_ids = lax.broadcasted_iota(jnp.int32, (query_count, slab), 1)
        heads_ok = (host * q_rows + lane <= query_ids) & (lane < q_rows)
        for j in range(columns // HD):
            cols = slice(j * HD, (j + 1) * HD)
            self_keys = jnp.concatenate([selves_kv[0][:, cols], pad], 0).astype(BF)
            self_values = jnp.concatenate([selves_kv[1][:, cols], pad], 0).astype(BF)
            self_values = jnp.concatenate([self_values, jnp.ones((HD, HD), BF)], 1)
            mine = odd if j else jnp.logical_not(odd)

            def body(h, stats):
                at = pl.ds(pl.multiple_of((j * per_kv + h) * query_count, query_count), query_count)
                queries = q_all[at, :]
                near = dot(twice(queries), k_ref[2 * j * HD : 2 * (j + 1) * HD, :])
                near = jnp.where(key_ids < own_len, near, MASKED)
                selves = jnp.where(heads_ok, dot_t(queries, self_keys) * SCALE2, MASKED)
                peak = jnp.maximum(jnp.max(near, 1, keepdims=True), jnp.max(selves, 1, keepdims=True))
                near = jnp.exp2(near - peak).astype(BF)
                selves = jnp.exp2(selves - peak).astype(BF)
                total = dot(near, vaug[:, 2 * j * HD : (2 * j + 2) * HD]) + dot(selves, self_values)
                result = (total[:, :HD] / total[:, HD:]).astype(BF)

                def put(out_ref):
                    def run():
                        out_ref[:, lanes(h, HD)] = result

                    return run

                choose(mine, put(keep_ref), put(send_ref))
                return jnp.where(lane == h, peak + jnp.log2(total[:, HD:]), stats)

            stats = lax.fori_loop(0, per_kv, body, jnp.zeros((query_count, HD), F32))

            def put_level(out_ref):
                def run():
                    write_level(out_ref, per_kv * HD, stats)

                return run

            choose(mine, put_level(keep_ref), put_level(send_ref))


def source_part(lengths, own_k, own_v, query_kv, known, landed, q_rows, per_kv, after=()):
    slab, columns = own_v.shape
    width = per_kv * columns
    count = 8 * q_rows
    work = count * (width // HD) * slab
    return pl.pallas_call(
        functools.partial(source_kernel, per_kv, q_rows, H // KVH),
        out_shape=[jax.ShapeDtypeStruct((count, (per_kv + 1) * HD), BF)] * 2,
        in_specs=[VMEM] * 6 + [ANY] * len(after),
        out_specs=[VMEM] * 2,
        scratch_shapes=[pltpu.VMEM((count * width // HD, HD), BF), pltpu.VMEM((slab, 2 * columns), BF)],
        compiler_params=params(),
        cost_estimate=pl.CostEstimate(flops=work * HD * 8, bytes_accessed=2**21, transcendentals=work),
        name="query_source",
    )(lengths, own_k, own_v, query_kv, known, landed, *after)


def merge_part(groups, last, after=()):
    rows, wide = groups[0].shape
    width = wide - HD

    def kernel(*refs):
        in_refs, out_ref = refs[: len(groups)], refs[-1]
        levels = [read_level(ref, width) for ref in in_refs]
        peak = functools.reduce(jnp.maximum, levels)
        weights = [jnp.exp2(x - peak) for x in levels]
        whole = functools.reduce(jnp.add, weights)
        shares = [w / whole for w in weights]
        if not last:
            write_level(out_ref, width, peak + jnp.log2(whole))
        for h in range(width // HD):
            cols = slice(h * HD, (h + 1) * HD)
            total = sum(w[:, h : h + 1] * ref[:, cols].astype(F32) for w, ref in zip(shares, in_refs))
            out_ref[:, cols] = total.astype(BF)

    return small_call(kernel, "query_merge", [(rows, width if last else wide)], groups, after)[0]


def project_part(own, other, out_weight, after=()):
    rows, half = own.shape
    depth, columns = out_weight.shape

    def kernel(w_ref, own_ref, other_ref, *rest):
        out_ref, attended = rest[-2:]

        def put(first, second):
            def run():
                attended[:, :half] = first[...]
                attended[:, half:] = second[...]

            return run

        even = bit(lax.axis_index("hst"), 0) == 0
        choose(even, put(own_ref, other_ref), put(other_ref, own_ref))
        out_ref[...] = dot(attended[...], w_ref[...]).astype(BF)

    return pl.pallas_call(
        kernel,
        out_shape=jax.ShapeDtypeStruct((rows, columns), BF),
        in_specs=[VMEM] * 3 + [ANY] * len(after),
        out_specs=VMEM,
        scratch_shapes=[pltpu.VMEM((rows, depth), BF)],
        compiler_params=params(),
        cost_estimate=pl.CostEstimate(
            flops=2 * rows * depth * columns, bytes_accessed=2 * depth * columns, transcendentals=0
        ),
        name="query_project",
    )(out_weight, own, other, *after)


def general_queries(lengths, own_k, own_v, self_kv, query_q, out_weight, per_kv):
    own_kv = jnp.stack([own_k, own_v], 0)
    host_id = lax.axis_index("hst")
    local_heads = query_q.shape[1] // HD
    kv_local = own_kv.shape[2] // HD
    slab_rows = own_kv.shape[1]
    own_len = lengths[host_id]
    row_ids = jnp.arange(slab_rows)
    all_queries = lax.all_gather(query_q, "hst", axis=0, tiled=True)
    query_count = all_queries.shape[0]
    q_rows = query_q.shape[0]
    source = jnp.concatenate([own_kv, self_kv], 1)
    source = source.reshape(2, slab_rows + q_rows, kv_local, HD).transpose(0, 2, 1, 3)
    query_ids = jnp.arange(query_count)
    context_ok = jnp.broadcast_to(row_ids[None, :] < own_len, (query_count, slab_rows))
    self_ok = (host_id * q_rows + jnp.arange(q_rows))[None, :] <= query_ids[:, None]
    seen_ok = jnp.concatenate([context_ok, self_ok], 1)
    query_heads = all_queries.reshape(query_count, local_heads, HD).transpose(1, 0, 2)

    def score_head(operands):
        query_rows, head_index = operands
        kv_index = head_index // per_kv
        scores = dot_t(query_rows, source[0, kv_index]) * HD ** (-0.5)
        scores = jnp.where(seen_ok, scores, MASKED)
        peak = jnp.max(scores, axis=1)
        expo = jnp.exp(scores - peak[:, None])
        return peak, jnp.sum(expo, axis=1), dot(expo.astype(BF), source[1, kv_index])

    maxima, totals, outputs = lax.map(score_head, (query_heads, jnp.arange(local_heads)))
    factor = jnp.exp(maxima - lax.pmax(maxima, "hst"))
    denominator, summed = lax.psum((totals * factor, outputs * factor[..., None]), "hst")
    attended = (summed / denominator[..., None]).astype(BF)
    attended = attended.transpose(1, 0, 2).reshape(query_count, local_heads * HD)
    return lax.psum(dot(attended, out_weight), "tp").astype(BF)


def per_device(hosts, groups, ctx_q, ctx_kv, lengths, query_q, query_kv, out_weight):
    slab = ctx_q.shape[0]
    local_heads = ctx_q.shape[1] // HD
    group_size = H // KVH
    kv_local = max(1, local_heads // group_size)
    per_kv = min(local_heads, group_size)
    q_rows = query_q.shape[0]
    host = lax.axis_index("hst")
    fast = hosts == 8 and groups & (groups - 1) == 0
    fast = fast and q_rows == 8 and local_heads == 16 and per_kv == 8

    if not fast:
        kv_first = lax.axis_index("tp") * local_heads // group_size
        self_kv = lax.dynamic_slice_in_dim(query_kv, kv_first * HD, kv_local * HD, 2)
        own_k, own_v = pick(ctx_kv, kv_local, local_heads)
        query_out = general_queries(lengths, own_k, own_v, self_kv, query_q, out_weight, per_kv)
        k, v = spread(jnp.stack([own_k, own_v]), "hst", 0)
        lengths = lengths.reshape(1, hosts)
        own_k, own_v = prepare(own_k, own_v, False)
        anchor = prepare(k, v, False)
        state = own_part(ctx_q, own_k, own_v, 0, local_heads, per_kv)
        results = {}
        for first in range(0, local_heads, per_kv):
            cols = slice(2 * first // per_kv * HD, 2 * (first // per_kv + 1) * HD)
            last = first + per_kv == local_heads
            results[first] = anchor_part(
                lengths, ctx_q, {0: state}, own_k, own_v, (anchor[0][cols, :], anchor[1][:, cols]),
                first, per_kv, per_kv, dict(results) if last else None,
            )
        return results[first], query_out

    lengths = lengths.reshape(1, hosts)
    states = {}

    def own(first, count, after=()):
        states[first] = own_part(ctx_q, own_keys, own_values, first, count, per_kv, after)
        return states[first]

    along = ((2, 4), (4, 2))

    def is_even(h):
        return bit(h, 0) == 0

    def source_first(h):
        return h < 2

    done_early = (
        lambda h: (h <= 2) | (h == 5),
        lambda h: (h <= 1) | (h == 3) | (h == 4),
    )

    bits = (6, 2, 4)
    landed = [swap(query_q, "hst", hosts, x, x) for x in bits]
    own_k, own_v = pick(ctx_kv, kv_local, local_heads)
    value_landed = swap(own_v, "hst", hosts, 1, 1)
    own_keys, own_values = prepare(own_k, own_v, False)
    done = own(0, 2)
    parts, parts_landed = {}, {}

    def send_off(kv, after):
        (parts[kv],) = relay(is_even, own_k, value_landed, after, kv)
        parts_landed[kv] = swap(parts[kv], "hst", hosts, *along[kv])
        return parts[kv]

    done = send_off(0, (done,))
    done = own(2, 2, (done,))
    queries = by_chip(query_q, landed, bits, (done,))
    landed = swap(queries, "hst", hosts, 1, 1)
    anchor = {}

    def pass_on(kv, after):
        (parts[kv],) = relay(source_first, parts[kv], parts_landed[kv], after)
        parts_landed[kv] = swap(parts[kv], "hst", hosts, *along[1 - kv])
        return parts[kv]

    def complete(kv, after):
        (held,) = relay(done_early[kv], parts[kv], parts_landed[kv], after)
        anchor[kv] = held, swap(held, "hst", hosts, 1, 1)
        return held

    keep, give = source_part(lengths, own_keys, own_v, query_kv, queries, landed, q_rows, per_kv, ())
    landed = swap(give, "hst", hosts, 1, 1)
    done = send_off(1, (keep,))
    done = own(4, 4, (done,))
    source = merge_part([keep, landed], False, (done,))
    landed = swap(source, "hst", hosts, *along[0])
    done = pass_on(0, (source,))
    done = own(8, 6, (done,))
    source = merge_part([source, landed], False, (done,))
    landed = swap(source, "hst", hosts, *along[1])
    done = own(14, 2, (source,))
    done = complete(0, (done,))
    done = pass_on(1, (done,))
    anchor[0] = prepare(*anchor[0], True, (done,))
    results = {}

    def anchors(first, count, after, last=False, weight=8):
        results[first] = anchor_part(
            lengths, ctx_q, states, own_keys, own_values, anchor[first // per_kv],
            first, count, per_kv, dict(results) if last else None, after, weight,
        )
        return results[first]

    done = anchors(0, 4, (), weight=1)
    attended = merge_part([source, landed], True, (done,))
    landed = swap(attended, "hst", hosts, 1, 1)
    done = anchors(4, 2, (attended,))
    done = complete(1, (done,))
    terms = project_part(attended, landed, out_weight, (done,))
    done = terms
    shares = [[(12, 4, True)], [(6, 2, False), (8, 4, False)]]
    step = 1
    while step < groups:
        landed = swap(terms, "tp", groups, step, step)
        last = False
        for first, count, last in shares.pop() if shares else ():
            if first == per_kv:
                anchor[1] = prepare(*anchor[1], True, (done,))
            done = anchors(first, count, (terms, done), last)
        terms = add_part(terms, landed, () if last else (done,))
        step *= 2
    for group in reversed(shares):
        for first, count, last in group:
            done = anchors(first, count, (), last)
    return done, terms


def solution(mesh):
    hosts, groups = mesh.shape["hst"], mesh.shape["tp"]
    return jax.shard_map(
        functools.partial(per_device, hosts, groups),
        mesh=mesh,
        in_specs=(
            P("hst", "tp"),
            P(None, "hst", None),
            P(),
            P("hst", "tp"),
            P(None, "hst", None),
            P("tp", "hst"),
        ),
        out_specs=(P("hst", "tp"), P(None, "hst")),
        check_vma=False,
    )
```

```python
import functools

import jax
import jax.numpy as jnp
from jax import lax
from jax.experimental import pallas as pl
from jax.experimental.pallas import tpu as pltpu
from jax.sharding import PartitionSpec as P

H = 64
KVH = 8
HD = 128
MASKED = -1e30
LOG2E = 1.4426950408889634
SCALE2 = HD ** (-0.5) * LOG2E
TINY = 2.0 ** -90
BF = jnp.bfloat16
F32 = jnp.float32
VMEM = pl.BlockSpec(memory_space=pltpu.VMEM)
ANY = pl.BlockSpec(memory_space=pl.ANY)
HBM = pl.BlockSpec(memory_space=pltpu.HBM)


def params(mib=20):
    return pltpu.CompilerParams(vmem_limit_bytes=mib * 2**20)


def dot_t(a, b):
    return lax.dot_general(a, b, (((1,), (1,)), ((), ())), preferred_element_type=F32)


def dot(a, b):
    return lax.dot_general(a, b, (((1,), (0,)), ((), ())), preferred_element_type=F32)


def spread(value, axis, source):
    kept = jnp.where(lax.axis_index(axis) == source, value, 0).astype(value.dtype)
    return lax.psum(kept, axis)


def swap(value, axis, size, even, odd):
    return lax.ppermute(value, axis, [(i, i ^ (odd if i & 1 else even)) for i in range(size)])


def pick_kernel(group_size, local_heads, kv_ref, k_ref, v_ref, sems):
    first = lax.axis_index("tp") * local_heads // group_size * HD
    cols = pl.ds(pl.multiple_of(first, HD), k_ref.shape[1])
    moves = [
        pltpu.make_async_copy(kv_ref.at[1, :, cols], v_ref, sems.at[1]),
        pltpu.make_async_copy(kv_ref.at[0, :, cols], k_ref, sems.at[0]),
    ]
    for move in moves:
        move.start()
    for move in moves:
        move.wait()


def pick(ctx_kv, kv_local, local_heads):
    return pl.pallas_call(
        functools.partial(pick_kernel, H // KVH, local_heads),
        out_shape=[jax.ShapeDtypeStruct((ctx_kv.shape[1], kv_local * HD), BF)] * 2,
        in_specs=[HBM],
        out_specs=[VMEM] * 2,
        scratch_shapes=[pltpu.SemaphoreType.DMA((2,))],
        compiler_params=params(52),
        cost_estimate=pl.CostEstimate(flops=0, bytes_accessed=2**22, transcendentals=0),
        name="pick_columns",
    )(ctx_kv)


def bit(value, at):
    return (value >> at) & 1


def small_call(kernel, name, shapes, inputs, after=()):
    return pl.pallas_call(
        kernel,
        out_shape=[jax.ShapeDtypeStruct(x, BF) for x in shapes],
        in_specs=[VMEM] * len(inputs) + [ANY] * len(after),
        out_specs=[VMEM] * len(shapes),
        compiler_params=params(),
        cost_estimate=pl.CostEstimate(flops=0, bytes_accessed=2**14, transcendentals=0),
        name=name,
    )(*inputs, *after)


def choose(condition, one, two):
    pl.when(condition)(one)
    pl.when(jnp.logical_not(condition))(two)


def take_rows(target, source, rows, cols=slice(None)):
    def run():
        target[:rows, :] = source[:rows, cols]

    return run


def by_chip(own, others, bits, after=()):
    rows, width = own.shape

    def kernel(*refs):
        out_ref, all_ref = refs[-2:]
        host = lax.axis_index("hst")
        for ref, flip in zip(refs, (0,) + tuple(bits)):
            start = pl.multiple_of((jnp.bitwise_xor(host, flip) >> 1) * rows, rows)
            all_ref[pl.ds(start, rows), :] = ref[...].astype(F32)
        out_ref[...] = all_ref[...].astype(BF)

    total = rows * (1 + len(bits))
    return pl.pallas_call(
        kernel,
        out_shape=jax.ShapeDtypeStruct((total, width), BF),
        in_specs=[VMEM] * (1 + len(bits)) + [ANY] * len(after),
        out_specs=VMEM,
        scratch_shapes=[pltpu.VMEM((total, width), F32)],
        compiler_params=params(),
        cost_estimate=pl.CostEstimate(flops=0, bytes_accessed=2**20, transcendentals=0),
        name="query_chips",
    )(own, *others, *after)


def relay(keep_of, one, two, after=(), kv=0):
    cols = slice(kv * HD, (kv + 1) * HD)
    slab = one.shape[0]

    def kernel(one_ref, two_ref, *rest):
        keep = keep_of(lax.axis_index("hst"))
        choose(keep, take_rows(rest[-1], one_ref, slab, cols), take_rows(rest[-1], two_ref, slab, cols))

    return small_call(kernel, "anchor_relay", [(slab, HD)], (one, two), after)


def add_part(one, two, after=()):
    def kernel(one_ref, two_ref, *rest):
        rest[-1][...] = (one_ref[...].astype(F32) + two_ref[...].astype(F32)).astype(BF)

    return small_call(kernel, "query_sum", [one.shape], (one, two), after)[0]


def prepare(first, second, swapped, after=()):
    slab, columns = first.shape

    def kernel(first_ref, second_ref, *rest):
        keys_ref, values_ref = rest[-2:]

        def fill(k_ref, v_ref):
            def run():
                for j in range(columns // HD):
                    cols = slice(j * HD, (j + 1) * HD)
                    at = 2 * j * HD
                    scaled = k_ref[:, cols].astype(F32) * SCALE2
                    high = scaled.astype(BF)
                    low = scaled - high.astype(F32)
                    keys_ref[at : at + HD, :] = high.astype(F32).T.astype(BF)
                    keys_ref[at + HD : at + 2 * HD, :] = low.T.astype(BF)
                    values_ref[:, at : at + HD] = v_ref[:, cols]
                    values_ref[:, at + HD : at + 2 * HD] = jnp.ones((slab, HD), BF)

            return run

        if swapped:
            even = bit(lax.axis_index("hst"), 0) == 0
            choose(even, fill(first_ref, second_ref), fill(second_ref, first_ref))
        else:
            fill(first_ref, second_ref)()

    shapes = [(2 * columns, slab), (slab, 2 * columns)]
    return small_call(kernel, "operands", shapes, (first, second), after)


def twice(query):
    return jnp.concatenate([query, query], 1)


def lanes(index, width):
    return pl.ds(pl.multiple_of(index * width, width), width)


def row_tile(slab):
    return 256 if slab % 256 == 0 else slab


def body_size(first, count, per_kv, most):
    def fits(size):
        bodies = range(first, first + count, size)
        return count % size == 0 and all(x // per_kv == (x + size - 1) // per_kv for x in bodies)

    return max(x for x in range(1, most + 1) if fits(x))


def own_kernel(first, count, per_kv, q_ref, k_ref, v_ref, *rest):
    state_ref = rest[-1]
    slab = q_ref.shape[0]
    tile = row_tile(slab)
    half = tile // 2
    heads = body_size(first, count, per_kv, 4)
    rows = lax.broadcasted_iota(jnp.int32, (half, half), 0)
    cols = lax.broadcasted_iota(jnp.int32, (half, half), 1)
    causal = cols <= rows
    chunks = slab // tile
    units = [(h, j) for h in range(heads) for j in range(chunks)]

    def body(i, carry):
        kv = lax.div(first + i * heads, per_kv)

        def scores(at):
            h, j = units[at]
            query = q_ref[j * tile :, lanes(first + i * heads + h, HD)]
            return dot(twice(query), k_ref[lanes(kv, 2 * HD), j * tile : (j + 1) * tile])

        def power(x):
            return jnp.exp2(x).astype(BF)

        def corner(x):
            return jnp.where(causal, jnp.exp2(x), 0.0).astype(BF)

        current = scores(0)
        totals = [None] * chunks
        for at, (h, j) in enumerate(units):
            following = scores(at + 1) if at + 1 < len(units) else None
            top = jnp.concatenate([corner(current[:half, :half]), jnp.zeros((half, half), BF)], 1)
            low = jnp.concatenate([power(current[half:tile, :half]), corner(current[half:tile, half:])], 1)
            expo = [top, low] if j == chunks - 1 else [top, low, power(current[tile:])]
            part = dot(jnp.concatenate(expo, 0), v_ref[j * tile : (j + 1) * tile, lanes(kv, 2 * HD)])
            for r in range(j, chunks):
                piece = part[(r - j) * tile : (r - j + 1) * tile]
                totals[r] = piece if j == 0 else totals[r] + piece
            state_ref[j * tile : (j + 1) * tile, lanes(i * heads + h, 2 * HD)] = totals[j]
            current = following
        return carry

    lax.fori_loop(0, count // heads, body, 0)


def own_part(ctx_q, own_k, own_v, first, count, per_kv, after=()):
    slab = ctx_q.shape[0]
    work = count * slab * (slab + row_tile(slab)) // 2
    return pl.pallas_call(
        functools.partial(own_kernel, first, count, per_kv),
        out_shape=jax.ShapeDtypeStruct((slab, count * 2 * HD), F32),
        in_specs=[VMEM] * 3 + [ANY] * len(after),
        out_specs=VMEM,
        compiler_params=params(),
        cost_estimate=pl.CostEstimate(
            flops=work * HD * 8, bytes_accessed=count * slab * HD * 6, transcendentals=work
        ),
        name="context_own",
    )(ctx_q, own_k, own_v, *after)


def length_of(lengths_ref, host):
    lengths = lengths_ref[...]
    index = lax.broadcasted_iota(jnp.int32, lengths.shape, 1)
    return jnp.sum(jnp.where(index == host, lengths, 0), axis=1, keepdims=True)


def anchor_kernel(first, count, bases, per_kv, last, befores, *refs):
    lengths_ref, q_ref, k_ref, v_ref, keys, vaug = refs[:6]
    hosts = lengths_ref.shape[1]
    state_refs = refs[6 : 6 + len(bases)]
    earlier = refs[6 + len(bases) : 6 + len(bases) + len(befores)]
    if last:
        full_ref, token_ref, out_ref, sems = refs[-4:]
        token_ref[...] = jnp.zeros_like(token_ref)
    else:
        out_ref = refs[-1]
    slab = q_ref.shape[0]
    heads = body_size(first, count, per_kv, 2 if last else 4)
    kv = first // per_kv
    host = lax.axis_index("hst")

    def hand_over(source, start, width, sem):
        target = full_ref.at[:, pl.ds(start * HD, width * HD)]
        return pltpu.make_async_copy(source, target, sems.at[sem])

    moves = [hand_over(earlier[n], *place, n) for n, place in enumerate(befores)]
    for move in moves:
        move.start()

    def part(start):
        def query_of(h):
            at = (first + start + h) * HD
            return q_ref[:, at : at + HD]

        def scores(h):
            return dot(twice(query_of(h)), keys[...])

        def state_of(h):
            head = first + start + h
            n = max(n for n, base in enumerate(bases) if base <= head)
            at = (head - bases[n]) * 2 * HD
            return state_refs[n][:, at : at + 2 * HD]

        def finish(h, total, sums, worst):
            inverse = pl.reciprocal(sums, approx=True)
            out_ref[:, (start + h) * HD : (start + h + 1) * HD] = (total * inverse).astype(BF)
            return jnp.minimum(worst, jnp.minimum(sums, inverse))

        def check(worst):
            @pl.when(jnp.logical_not(jnp.min(worst) > TINY))
            def _():
                exact_block(first + start, start, heads, host, kv, q_ref, k_ref, v_ref, keys, vaug, out_ref)

        @pl.when(host == 0)
        def _():
            worst = jnp.ones((slab, HD), F32)
            for h in range(heads):
                state = state_of(h)
                worst = finish(h, state[:, :HD], state[:, HD:], worst)
            check(worst)

        @pl.when(host > 0)
        def _():
            worst = jnp.ones((slab, HD), F32)
            current = scores(0)
            for h in range(heads):
                following = scores(h + 1) if h + 1 < heads else None
                expo = jnp.exp2(current)
                state = state_of(h)
                total = dot(expo.astype(BF), vaug[:, :HD]) + state[:, :HD]
                sums = jnp.sum(expo, axis=1, keepdims=True) + state[:, HD:]
                worst = finish(h, total, sums, worst)
                current = following
            check(worst)

        @pl.when(host * 4 >= hosts * 3)
        def _():
            own_len = length_of(lengths_ref, host)
            row_ids = lax.broadcasted_iota(jnp.int32, (slab, HD), 0)
            for h in range(start, start + heads):
                cols = slice(h * HD, (h + 1) * HD)
                kept = jnp.where(row_ids < own_len, out_ref[:, cols].astype(F32), 0.0)
                out_ref[:, cols] = kept.astype(BF)

        if last:
            source = out_ref.at[:, start * HD : (start + heads) * HD]
            move = hand_over(source, first + start, heads, len(befores) + start // heads)
            move.start()
            moves.append(move)

    for start in range(0, count, heads):
        part(start)
    for move in moves:
        move.wait()


def exact_block(q_head, out_head, heads, host, kv, q_ref, k_ref, v_ref, keys, vaug, out_ref):
    slab = q_ref.shape[0]
    tile = 64

    def body(i, carry):
        h = lax.div(i, slab // tile)
        r = lax.rem(i, slab // tile)
        at = pl.ds(pl.multiple_of(r * tile, tile), tile)
        query = q_ref[at, lanes(q_head + h, HD)]
        row_ids = lax.broadcasted_iota(jnp.int32, (tile, slab), 0) + r * tile
        key_ids = lax.broadcasted_iota(jnp.int32, (tile, slab), 1)
        own = dot(twice(query), k_ref[2 * kv * HD : 2 * (kv + 1) * HD, :])
        own = jnp.where(key_ids <= row_ids, own, MASKED)
        far = dot(twice(query), keys[...])
        far = jnp.where(host > 0, far, MASKED)
        peak = jnp.maximum(jnp.max(own, 1, keepdims=True), jnp.max(far, 1, keepdims=True))
        own = jnp.exp2(own - peak)
        far = jnp.where(host > 0, jnp.exp2(far - peak), 0.0)
        sums = jnp.sum(own, 1, keepdims=True) + jnp.sum(far, 1, keepdims=True)
        values = jnp.where(host > 0, vaug[:, :HD].astype(F32), 0.0).astype(BF)
        total = dot(own.astype(BF), v_ref[:, 2 * kv * HD : (2 * kv + 1) * HD]) + dot(far.astype(BF), values)
        out_ref[at, lanes(out_head + h, HD)] = (total / sums).astype(BF)
        return carry

    lax.fori_loop(0, heads * (slab // tile), body, 0)


def anchor_part(lengths, ctx_q, states, own_k, own_v, anchor, first, count, per_kv, befores=None, after=(), weight=8):
    slab, width = ctx_q.shape
    work = count * slab * slab
    last = befores is not None
    ends = {x: x + y.shape[1] // (2 * HD) for x, y in states.items()}
    bases = tuple(x for x in sorted(states) if x < first + count and ends[x] > first)
    earlier = list(befores.values()) if last else []
    places = tuple((at, x.shape[1] // HD) for at, x in befores.items()) if last else ()
    results = jax.ShapeDtypeStruct((slab, count * HD), BF)
    scratch = []
    if last:
        scratch = [pltpu.VMEM(results.shape, BF), pltpu.SemaphoreType.DMA((len(earlier) + count,))]
        token = jax.ShapeDtypeStruct((8, HD), F32)
        results = [jax.ShapeDtypeStruct((slab, width), BF), token]
    return pl.pallas_call(
        functools.partial(anchor_kernel, first, count, bases, per_kv, last, places),
        out_shape=results,
        in_specs=[VMEM] * (6 + len(bases) + len(earlier)) + [ANY] * len(after),
        out_specs=[ANY, VMEM] if last else VMEM,
        scratch_shapes=scratch,
        compiler_params=params(),
        cost_estimate=pl.CostEstimate(
            flops=work * HD * weight, bytes_accessed=0, transcendentals=0
        ),
        name="context_anchor",
    )(lengths, ctx_q, own_k, own_v, *anchor, *[states[x] for x in bases], *earlier, *after)


PART = 16


def write_level(ref, width, level):
    lane = lax.broadcasted_iota(jnp.int32, level.shape, 1)
    parts = []
    for at in range(3):
        part = level.astype(BF).astype(F32)
        parts.append(part if at == 0 else pltpu.roll(part, at * PART, 1))
        level = level - part
    packed = jnp.where(lane < PART, parts[0], jnp.where(lane < 2 * PART, parts[1], parts[2]))
    ref[:, width : width + HD] = packed.astype(BF)


def read_level(ref, width):
    packed = ref[:, width : width + HD].astype(F32)
    return packed + pltpu.roll(packed, HD - PART, 1) + pltpu.roll(packed, HD - 2 * PART, 1)


def source_kernel(per_kv, q_rows, group_size, lengths_ref, k_ref, v_ref, self_ref, known_ref, landed_ref, *rest):
    keep_ref, send_ref, q_all, vaug = rest[-4:]
    slab, columns = v_ref.shape
    width = per_kv * columns
    query_count = 8 * q_rows
    host = lax.axis_index("hst")
    own_len = length_of(lengths_ref, host)
    rows = per_kv * query_count
    odd = bit(host, 0) == 1

    def place(even_ref, odd_ref):
        def run():
            parts = []
            for chip in range(4):
                at = slice(chip * q_rows, (chip + 1) * q_rows)
                parts += [even_ref[at, :].astype(F32), odd_ref[at, :].astype(F32)]
            queries = jnp.concatenate(parts, 0).astype(BF)
            for h in range(width // HD):
                q_all[h * query_count : (h + 1) * query_count, :] = queries[:, h * HD : (h + 1) * HD]

        return run

    choose(odd, place(landed_ref, known_ref), place(known_ref, landed_ref))

    first = lax.axis_index("tp") * (width // HD) // group_size * HD
    own_cols = pl.ds(pl.multiple_of(first, HD), columns)
    selves_kv = [self_ref[i, :, own_cols].astype(F32) for i in range(2)]
    lane = lax.broadcasted_iota(jnp.int32, (query_count, HD), 1)
    query_ids = lax.broadcasted_iota(jnp.int32, (query_count, HD), 0)
    self_ok = (host * q_rows + lane <= query_ids) & (lane < q_rows)
    self_ok = jnp.concatenate([self_ok] * per_kv, 0)
    pad = jnp.zeros((HD - q_rows, HD), F32)
    key_rows = lax.broadcasted_iota(jnp.int32, (slab, HD), 0)
    ones = jnp.where(key_rows < own_len, 1.0, 0.0).astype(BF)
    for j in range(columns // HD):
        values = v_ref[:, j * HD : (j + 1) * HD].astype(F32)
        vaug[:, 2 * j * HD : (2 * j + 1) * HD] = jnp.where(key_rows < own_len, values, 0.0).astype(BF)
        vaug[:, (2 * j + 1) * HD : (2 * j + 2) * HD] = ones

    def operands(j):
        cols = slice(j * HD, (j + 1) * HD)
        queries = q_all[j * rows : (j + 1) * rows, :]
        self_keys = jnp.concatenate([selves_kv[0][:, cols], pad], 0).astype(BF)
        self_values = jnp.concatenate([selves_kv[1][:, cols], pad], 0).astype(BF)
        near = dot(twice(queries), k_ref[2 * j * HD : 2 * (j + 1) * HD, :])
        selves = jnp.where(self_ok, dot_t(queries, self_keys) * SCALE2, MASKED)
        return near, selves, jnp.concatenate([self_values, jnp.ones((HD, HD), BF)], 1)

    def store(j, total, level):
        stats = jnp.zeros((query_count, HD), F32)
        for h in range(per_kv):
            stats = jnp.where(lane == h, level[h * query_count : (h + 1) * query_count, :], stats)

        def put(out_ref):
            def run():
                for h in range(per_kv):
                    part = total[h * query_count : (h + 1) * query_count, :]
                    out_ref[:, h * HD : (h + 1) * HD] = part.astype(BF)
                write_level(out_ref, per_kv * HD, stats)

            return run

        choose(odd if j else jnp.logical_not(odd), put(keep_ref), put(send_ref))

    worst = jnp.ones((rows, HD), F32)
    found = []
    for j in range(columns // HD):
        near, selves, self_values = operands(j)
        near = jnp.exp2(near).astype(BF)
        selves = jnp.exp2(selves).astype(BF)
        total = dot(near, vaug[:, 2 * j * HD : (2 * j + 2) * HD]) + dot(selves, self_values)
        sums = total[:, HD:]
        inverse = 1.0 / sums
        worst = jnp.minimum(worst, jnp.minimum(sums, inverse))
        found.append((total[:, :HD] * inverse, jnp.log2(sums)))
    for j, result in enumerate(found):
        store(j, *result)

    @pl.when(jnp.logical_not(jnp.min(worst) > TINY))
    def _():
        key_ids = lax.broadcasted_iota(jnp.int32, (query_count, slab), 1)
        heads_ok = (host * q_rows + lane <= query_ids) & (lane < q_rows)
        for j in range(columns // HD):
            cols = slice(j * HD, (j + 1) * HD)
            self_keys = jnp.concatenate([selves_kv[0][:, cols], pad], 0).astype(BF)
            self_values = jnp.concatenate([selves_kv[1][:, cols], pad], 0).astype(BF)
            self_values = jnp.concatenate([self_values, jnp.ones((HD, HD), BF)], 1)
            mine = odd if j else jnp.logical_not(odd)

            def body(h, stats):
                at = pl.ds(pl.multiple_of((j * per_kv + h) * query_count, query_count), query_count)
                queries = q_all[at, :]
                near = dot(twice(queries), k_ref[2 * j * HD : 2 * (j + 1) * HD, :])
                near = jnp.where(key_ids < own_len, near, MASKED)
                selves = jnp.where(heads_ok, dot_t(queries, self_keys) * SCALE2, MASKED)
                peak = jnp.maximum(jnp.max(near, 1, keepdims=True), jnp.max(selves, 1, keepdims=True))
                near = jnp.exp2(near - peak).astype(BF)
                selves = jnp.exp2(selves - peak).astype(BF)
                total = dot(near, vaug[:, 2 * j * HD : (2 * j + 2) * HD]) + dot(selves, self_values)
                result = (total[:, :HD] / total[:, HD:]).astype(BF)

                def put(out_ref):
                    def run():
                        out_ref[:, lanes(h, HD)] = result

                    return run

                choose(mine, put(keep_ref), put(send_ref))
                return jnp.where(lane == h, peak + jnp.log2(total[:, HD:]), stats)

            stats = lax.fori_loop(0, per_kv, body, jnp.zeros((query_count, HD), F32))

            def put_level(out_ref):
                def run():
                    write_level(out_ref, per_kv * HD, stats)

                return run

            choose(mine, put_level(keep_ref), put_level(send_ref))


def source_part(lengths, own_k, own_v, query_kv, known, landed, q_rows, per_kv, after=()):
    slab, columns = own_v.shape
    width = per_kv * columns
    count = 8 * q_rows
    work = count * (width // HD) * slab
    return pl.pallas_call(
        functools.partial(source_kernel, per_kv, q_rows, H // KVH),
        out_shape=[jax.ShapeDtypeStruct((count, (per_kv + 1) * HD), BF)] * 2,
        in_specs=[VMEM] * 6 + [ANY] * len(after),
        out_specs=[VMEM] * 2,
        scratch_shapes=[pltpu.VMEM((count * width // HD, HD), BF), pltpu.VMEM((slab, 2 * columns), BF)],
        compiler_params=params(),
        cost_estimate=pl.CostEstimate(flops=work * HD * 8, bytes_accessed=2**21, transcendentals=work),
        name="query_source",
    )(lengths, own_k, own_v, query_kv, known, landed, *after)


def merge_part(groups, last, after=()):
    rows, wide = groups[0].shape
    width = wide - HD

    def kernel(*refs):
        in_refs, out_ref = refs[: len(groups)], refs[-1]
        levels = [read_level(ref, width) for ref in in_refs]
        peak = functools.reduce(jnp.maximum, levels)
        weights = [jnp.exp2(x - peak) for x in levels]
        whole = functools.reduce(jnp.add, weights)
        shares = [w / whole for w in weights]
        if not last:
            write_level(out_ref, width, peak + jnp.log2(whole))
        for h in range(width // HD):
            cols = slice(h * HD, (h + 1) * HD)
            total = sum(w[:, h : h + 1] * ref[:, cols].astype(F32) for w, ref in zip(shares, in_refs))
            out_ref[:, cols] = total.astype(BF)

    return small_call(kernel, "query_merge", [(rows, width if last else wide)], groups, after)[0]


def project_part(own, other, out_weight, after=()):
    rows, half = own.shape
    depth, columns = out_weight.shape

    def kernel(w_ref, own_ref, other_ref, *rest):
        out_ref, attended = rest[-2:]

        def put(first, second):
            def run():
                attended[:, :half] = first[...]
                attended[:, half:] = second[...]

            return run

        even = bit(lax.axis_index("hst"), 0) == 0
        choose(even, put(own_ref, other_ref), put(other_ref, own_ref))
        out_ref[...] = dot(attended[...], w_ref[...]).astype(BF)

    return pl.pallas_call(
        kernel,
        out_shape=jax.ShapeDtypeStruct((rows, columns), BF),
        in_specs=[VMEM] * 3 + [ANY] * len(after),
        out_specs=VMEM,
        scratch_shapes=[pltpu.VMEM((rows, depth), BF)],
        compiler_params=params(),
        cost_estimate=pl.CostEstimate(
            flops=2 * rows * depth * columns, bytes_accessed=2 * depth * columns, transcendentals=0
        ),
        name="query_project",
    )(out_weight, own, other, *after)


def general_queries(lengths, own_k, own_v, self_kv, query_q, out_weight, per_kv):
    own_kv = jnp.stack([own_k, own_v], 0)
    host_id = lax.axis_index("hst")
    local_heads = query_q.shape[1] // HD
    kv_local = own_kv.shape[2] // HD
    slab_rows = own_kv.shape[1]
    own_len = lengths[host_id]
    row_ids = jnp.arange(slab_rows)
    all_queries = lax.all_gather(query_q, "hst", axis=0, tiled=True)
    query_count = all_queries.shape[0]
    q_rows = query_q.shape[0]
    source = jnp.concatenate([own_kv, self_kv], 1)
    source = source.reshape(2, slab_rows + q_rows, kv_local, HD).transpose(0, 2, 1, 3)
    query_ids = jnp.arange(query_count)
    context_ok = jnp.broadcast_to(row_ids[None, :] < own_len, (query_count, slab_rows))
    self_ok = (host_id * q_rows + jnp.arange(q_rows))[None, :] <= query_ids[:, None]
    seen_ok = jnp.concatenate([context_ok, self_ok], 1)
    query_heads = all_queries.reshape(query_count, local_heads, HD).transpose(1, 0, 2)

    def score_head(operands):
        query_rows, head_index = operands
        kv_index = head_index // per_kv
        scores = dot_t(query_rows, source[0, kv_index]) * HD ** (-0.5)
        scores = jnp.where(seen_ok, scores, MASKED)
        peak = jnp.max(scores, axis=1)
        expo = jnp.exp(scores - peak[:, None])
        return peak, jnp.sum(expo, axis=1), dot(expo.astype(BF), source[1, kv_index])

    maxima, totals, outputs = lax.map(score_head, (query_heads, jnp.arange(local_heads)))
    factor = jnp.exp(maxima - lax.pmax(maxima, "hst"))
    denominator, summed = lax.psum((totals * factor, outputs * factor[..., None]), "hst")
    attended = (summed / denominator[..., None]).astype(BF)
    attended = attended.transpose(1, 0, 2).reshape(query_count, local_heads * HD)
    return lax.psum(dot(attended, out_weight), "tp").astype(BF)


def per_device(hosts, groups, ctx_q, ctx_kv, lengths, query_q, query_kv, out_weight):
    slab = ctx_q.shape[0]
    local_heads = ctx_q.shape[1] // HD
    group_size = H // KVH
    kv_local = max(1, local_heads // group_size)
    per_kv = min(local_heads, group_size)
    q_rows = query_q.shape[0]
    host = lax.axis_index("hst")
    fast = hosts == 8 and groups == 4
    fast = fast and q_rows == 8 and local_heads == 16 and per_kv == 8

    if not fast:
        kv_first = lax.axis_index("tp") * local_heads // group_size
        self_kv = lax.dynamic_slice_in_dim(query_kv, kv_first * HD, kv_local * HD, 2)
        own_k, own_v = pick(ctx_kv, kv_local, local_heads)
        query_out = general_queries(lengths, own_k, own_v, self_kv, query_q, out_weight, per_kv)
        k, v = spread(jnp.stack([own_k, own_v]), "hst", 0)
        lengths = lengths.reshape(1, hosts)
        own_k, own_v = prepare(own_k, own_v, False)
        anchor = prepare(k, v, False)
        state = own_part(ctx_q, own_k, own_v, 0, local_heads, per_kv)
        results = {}
        for first in range(0, local_heads, per_kv):
            cols = slice(2 * first // per_kv * HD, 2 * (first // per_kv + 1) * HD)
            last = first + per_kv == local_heads
            results[first] = anchor_part(
                lengths, ctx_q, {0: state}, own_k, own_v, (anchor[0][cols, :], anchor[1][:, cols]),
                first, per_kv, per_kv, dict(results) if last else None,
            )
        return results[first][0], query_out

    lengths = lengths.reshape(1, hosts)
    states = {}

    def own(first, count, after=()):
        states[first] = own_part(ctx_q, own_keys, own_values, first, count, per_kv, after)
        return states[first]

    along = ((2, 4), (4, 2))

    def is_even(h):
        return bit(h, 0) == 0

    def source_first(h):
        return h < 2

    def done_early(h):
        return (h <= 2) | (h == 5)

    bits = (6, 2, 4)
    landed = [swap(query_q, "hst", hosts, x, x) for x in bits]
    own_k, own_v = pick(ctx_kv, kv_local, local_heads)
    value_landed = swap(own_v, "hst", hosts, 1, 1)
    own_keys, own_values = prepare(own_k, own_v, False)
    done = own(0, 2)
    parts, parts_landed = {}, {}

    def send_off(kv, after):
        (parts[kv],) = relay(is_even, own_k, value_landed, after, kv)
        parts_landed[kv] = swap(parts[kv], "hst", hosts, *along[0])
        return parts[kv]

    done = send_off(0, (done,))
    done = own(2, 2, (done,))
    queries = by_chip(query_q, landed, bits, (done,))
    landed = swap(queries, "hst", hosts, 1, 1)
    anchor = {}

    def pass_on(kv, after):
        (parts[kv],) = relay(source_first, parts[kv], parts_landed[kv], after)
        parts_landed[kv] = swap(parts[kv], "hst", hosts, *along[1])
        return parts[kv]

    def complete(kv, after):
        (held,) = relay(done_early, parts[kv], parts_landed[kv], after)
        anchor[kv] = held, swap(held, "hst", hosts, 1, 1)
        return held

    keep, give = source_part(lengths, own_keys, own_v, query_kv, queries, landed, q_rows, per_kv, ())
    landed = swap(give, "hst", hosts, 1, 1)
    done = own(4, 4, (keep,))
    source = merge_part([keep, landed], False, (done,))
    landed = swap(source, "hst", hosts, *along[0])
    done = pass_on(0, (source,))
    done = own(8, 8, (done,))
    source = merge_part([source, landed], False, (done,))
    landed = swap(source, "hst", hosts, *along[1])
    done = complete(0, (source,))
    done = send_off(1, (done,))
    anchor[0] = prepare(*anchor[0], True, (done,))
    results = {}

    def anchors(first, count, after, last=False, weight=8):
        results[first] = anchor_part(
            lengths, ctx_q, states, own_keys, own_values, anchor[first // per_kv],
            first, count, per_kv, dict(results) if last else None, after, weight,
        )
        return results[first]

    done = anchors(0, 4, ())
    attended = merge_part([source, landed], True, (done,))
    landed = swap(attended, "hst", hosts, 1, 1)
    done = pass_on(1, (attended,))
    terms = project_part(attended, landed, out_weight, (done,))
    done = terms
    shares = [[(8, 8, True)], [(4, 2, False), (6, 2, False)]]
    step = 1
    while step < groups:
        landed = swap(terms, "tp", groups, step, step)
        last = False
        for first, count, last in shares.pop() if shares else ():
            if first == 6:
                done = complete(1, (done,))
            if first == per_kv:
                anchor[1] = prepare(*anchor[1], True, (done,))
            done = anchors(first, count, (terms, done), last, 8 if last else 1)
        terms = add_part(terms, landed, (done[1] if last else done,))
        step *= 2
    return done[0], terms


def solution(mesh):
    hosts, groups = mesh.shape["hst"], mesh.shape["tp"]
    return jax.shard_map(
        functools.partial(per_device, hosts, groups),
        mesh=mesh,
        in_specs=(
            P("hst", "tp"),
            P(None, "hst", None),
            P(),
            P("hst", "tp"),
            P(None, "hst", None),
            P("tp", "hst"),
        ),
        out_specs=(P("hst", "tp"), P(None, "hst")),
        check_vma=False,
    )
```

```python
import functools

import jax
import jax.numpy as jnp
from jax import lax
from jax.experimental import pallas as pl
from jax.experimental.pallas import tpu as pltpu
from jax.sharding import PartitionSpec as P

H = 64
KVH = 8
HD = 128
MASKED = -1e30
LOG2E = 1.4426950408889634
SCALE2 = HD ** (-0.5) * LOG2E
TINY = 2.0 ** -90
BF = jnp.bfloat16
F32 = jnp.float32
VMEM = pl.BlockSpec(memory_space=pltpu.VMEM)
ANY = pl.BlockSpec(memory_space=pl.ANY)
HBM = pl.BlockSpec(memory_space=pltpu.HBM)


def params(mib=20):
    return pltpu.CompilerParams(vmem_limit_bytes=mib * 2**20)


def dot_t(a, b):
    return lax.dot_general(a, b, (((1,), (1,)), ((), ())), preferred_element_type=F32)


def dot(a, b):
    return lax.dot_general(a, b, (((1,), (0,)), ((), ())), preferred_element_type=F32)


def spread(value, axis, source):
    kept = jnp.where(lax.axis_index(axis) == source, value, 0).astype(value.dtype)
    return lax.psum(kept, axis)


def swap(value, axis, size, even, odd):
    return lax.ppermute(value, axis, [(i, i ^ (odd if i & 1 else even)) for i in range(size)])


def pick_kernel(group_size, local_heads, kv_ref, k_ref, v_ref, sems):
    first = lax.axis_index("tp") * local_heads // group_size * HD
    cols = pl.ds(pl.multiple_of(first, HD), k_ref.shape[1])
    moves = [
        pltpu.make_async_copy(kv_ref.at[1, :, cols], v_ref, sems.at[1]),
        pltpu.make_async_copy(kv_ref.at[0, :, cols], k_ref, sems.at[0]),
    ]
    for move in moves:
        move.start()
    for move in moves:
        move.wait()


def pick(ctx_kv, kv_local, local_heads):
    return pl.pallas_call(
        functools.partial(pick_kernel, H // KVH, local_heads),
        out_shape=[jax.ShapeDtypeStruct((ctx_kv.shape[1], kv_local * HD), BF)] * 2,
        in_specs=[HBM],
        out_specs=[VMEM] * 2,
        scratch_shapes=[pltpu.SemaphoreType.DMA((2,))],
        compiler_params=params(52),
        cost_estimate=pl.CostEstimate(flops=0, bytes_accessed=2**22, transcendentals=0),
        name="pick_columns",
    )(ctx_kv)


def bit(value, at):
    return (value >> at) & 1


def small_call(kernel, name, shapes, inputs, after=()):
    return pl.pallas_call(
        kernel,
        out_shape=[jax.ShapeDtypeStruct(x, BF) for x in shapes],
        in_specs=[VMEM] * len(inputs) + [ANY] * len(after),
        out_specs=[VMEM] * len(shapes),
        compiler_params=params(),
        cost_estimate=pl.CostEstimate(flops=0, bytes_accessed=2**14, transcendentals=0),
        name=name,
    )(*inputs, *after)


def choose(condition, one, two):
    pl.when(condition)(one)
    pl.when(jnp.logical_not(condition))(two)


def take_rows(target, source, rows, cols=slice(None)):
    def run():
        target[:rows, :] = source[:rows, cols]

    return run


def by_chip(own, others, bits, after=()):
    rows, width = own.shape

    def kernel(*refs):
        out_ref, all_ref = refs[-2:]
        host = lax.axis_index("hst")
        for ref, flip in zip(refs, (0,) + tuple(bits)):
            start = pl.multiple_of((jnp.bitwise_xor(host, flip) >> 1) * rows, rows)
            all_ref[pl.ds(start, rows), :] = ref[...].astype(F32)
        out_ref[...] = all_ref[...].astype(BF)

    total = rows * (1 + len(bits))
    return pl.pallas_call(
        kernel,
        out_shape=jax.ShapeDtypeStruct((total, width), BF),
        in_specs=[VMEM] * (1 + len(bits)) + [ANY] * len(after),
        out_specs=VMEM,
        scratch_shapes=[pltpu.VMEM((total, width), F32)],
        compiler_params=params(),
        cost_estimate=pl.CostEstimate(flops=0, bytes_accessed=2**20, transcendentals=0),
        name="query_chips",
    )(own, *others, *after)


def relay(keep_of, one, two, after=(), split=1):
    slab, columns = one.shape
    width = columns // split

    def kernel(one_ref, two_ref, *rest):
        keep = keep_of(lax.axis_index("hst"))
        for j, out_ref in enumerate(rest[-split:]):
            cols = slice(j * width, (j + 1) * width)
            choose(keep, take_rows(out_ref, one_ref, slab, cols), take_rows(out_ref, two_ref, slab, cols))

    return small_call(kernel, "anchor_relay", [(slab, width)] * split, (one, two), after)


def add_part(one, two, after=()):
    def kernel(one_ref, two_ref, *rest):
        rest[-1][...] = (one_ref[...].astype(F32) + two_ref[...].astype(F32)).astype(BF)

    return small_call(kernel, "query_sum", [one.shape], (one, two), after)[0]


def prepare(first, second, swapped, after=()):
    slab, columns = first.shape

    def kernel(first_ref, second_ref, *rest):
        keys_ref, values_ref = rest[-2:]

        def fill(k_ref, v_ref):
            def run():
                for j in range(columns // HD):
                    cols = slice(j * HD, (j + 1) * HD)
                    at = 2 * j * HD
                    scaled = k_ref[:, cols].astype(F32) * SCALE2
                    high = scaled.astype(BF)
                    low = scaled - high.astype(F32)
                    keys_ref[at : at + HD, :] = high.astype(F32).T.astype(BF)
                    keys_ref[at + HD : at + 2 * HD, :] = low.T.astype(BF)
                    values_ref[:, at : at + HD] = v_ref[:, cols]
                    values_ref[:, at + HD : at + 2 * HD] = jnp.ones((slab, HD), BF)

            return run

        if swapped:
            even = bit(lax.axis_index("hst"), 0) == 0
            choose(even, fill(first_ref, second_ref), fill(second_ref, first_ref))
        else:
            fill(first_ref, second_ref)()

    shapes = [(2 * columns, slab), (slab, 2 * columns)]
    return small_call(kernel, "operands", shapes, (first, second), after)


def twice(query):
    return jnp.concatenate([query, query], 1)


def lanes(index, width):
    return pl.ds(pl.multiple_of(index * width, width), width)


def row_tile(slab):
    return 256 if slab % 256 == 0 else slab


def body_size(first, count, per_kv, most):
    def fits(size):
        bodies = range(first, first + count, size)
        return count % size == 0 and all(x // per_kv == (x + size - 1) // per_kv for x in bodies)

    return max(x for x in range(1, most + 1) if fits(x))


def own_kernel(first, count, per_kv, q_ref, k_ref, v_ref, *rest):
    state_ref = rest[-1]
    slab = q_ref.shape[0]
    tile = row_tile(slab)
    half = tile // 2
    heads = body_size(first, count, per_kv, 4)
    rows = lax.broadcasted_iota(jnp.int32, (half, half), 0)
    cols = lax.broadcasted_iota(jnp.int32, (half, half), 1)
    causal = cols <= rows
    chunks = slab // tile
    units = [(h, j) for h in range(heads) for j in range(chunks)]

    def body(i, carry):
        kv = lax.div(first + i * heads, per_kv)

        def scores(at):
            h, j = units[at]
            query = q_ref[j * tile :, lanes(first + i * heads + h, HD)]
            return dot(twice(query), k_ref[lanes(kv, 2 * HD), j * tile : (j + 1) * tile])

        def power(x):
            return jnp.exp2(x).astype(BF)

        def corner(x):
            return jnp.where(causal, jnp.exp2(x), 0.0).astype(BF)

        current = scores(0)
        totals = [None] * chunks
        for at, (h, j) in enumerate(units):
            following = scores(at + 1) if at + 1 < len(units) else None
            top = jnp.concatenate([corner(current[:half, :half]), jnp.zeros((half, half), BF)], 1)
            low = jnp.concatenate([power(current[half:tile, :half]), corner(current[half:tile, half:])], 1)
            expo = [top, low] if j == chunks - 1 else [top, low, power(current[tile:])]
            part = dot(jnp.concatenate(expo, 0), v_ref[j * tile : (j + 1) * tile, lanes(kv, 2 * HD)])
            for r in range(j, chunks):
                piece = part[(r - j) * tile : (r - j + 1) * tile]
                totals[r] = piece if j == 0 else totals[r] + piece
            state_ref[j * tile : (j + 1) * tile, lanes(i * heads + h, 2 * HD)] = totals[j]
            current = following
        return carry

    lax.fori_loop(0, count // heads, body, 0)


def own_part(ctx_q, own_k, own_v, first, count, per_kv, after=()):
    slab = ctx_q.shape[0]
    work = count * slab * (slab + row_tile(slab)) // 2
    return pl.pallas_call(
        functools.partial(own_kernel, first, count, per_kv),
        out_shape=jax.ShapeDtypeStruct((slab, count * 2 * HD), F32),
        in_specs=[VMEM] * 3 + [ANY] * len(after),
        out_specs=VMEM,
        compiler_params=params(),
        cost_estimate=pl.CostEstimate(
            flops=work * HD * 8, bytes_accessed=count * slab * HD * 6, transcendentals=work
        ),
        name="context_own",
    )(ctx_q, own_k, own_v, *after)


def length_of(lengths_ref, host):
    lengths = lengths_ref[...]
    index = lax.broadcasted_iota(jnp.int32, lengths.shape, 1)
    return jnp.sum(jnp.where(index == host, lengths, 0), axis=1, keepdims=True)


def anchor_kernel(first, count, bases, per_kv, last, befores, *refs):
    lengths_ref, q_ref, k_ref, v_ref, keys, vaug = refs[:6]
    hosts = lengths_ref.shape[1]
    state_refs = refs[6 : 6 + len(bases)]
    earlier = refs[6 + len(bases) : 6 + len(bases) + len(befores)]
    if last:
        full_ref, out_ref, sems = refs[-3:]
    else:
        out_ref = refs[-1]
    slab = q_ref.shape[0]
    heads = body_size(first, count, per_kv, 2 if last else 4)
    kv = first // per_kv
    host = lax.axis_index("hst")

    def hand_over(source, start, width, sem):
        target = full_ref.at[:, pl.ds(start * HD, width * HD)]
        return pltpu.make_async_copy(source, target, sems.at[sem])

    moves = [hand_over(earlier[n], *place, n) for n, place in enumerate(befores)]
    for move in moves:
        move.start()

    def part(start):
        def query_of(h):
            at = (first + start + h) * HD
            return q_ref[:, at : at + HD]

        def scores(h):
            return dot(twice(query_of(h)), keys[...])

        def state_of(h):
            head = first + start + h
            n = max(n for n, base in enumerate(bases) if base <= head)
            at = (head - bases[n]) * 2 * HD
            return state_refs[n][:, at : at + 2 * HD]

        def finish(h, total, sums, worst):
            inverse = pl.reciprocal(sums, approx=True)
            out_ref[:, (start + h) * HD : (start + h + 1) * HD] = (total * inverse).astype(BF)
            return jnp.minimum(worst, jnp.minimum(sums, inverse))

        def check(worst):
            @pl.when(jnp.logical_not(jnp.min(worst) > TINY))
            def _():
                exact_block(first + start, start, heads, host, kv, q_ref, k_ref, v_ref, keys, vaug, out_ref)

        @pl.when(host == 0)
        def _():
            worst = jnp.ones((slab, HD), F32)
            for h in range(heads):
                state = state_of(h)
                worst = finish(h, state[:, :HD], state[:, HD:], worst)
            check(worst)

        @pl.when(host > 0)
        def _():
            worst = jnp.ones((slab, HD), F32)
            current = scores(0)
            for h in range(heads):
                following = scores(h + 1) if h + 1 < heads else None
                expo = jnp.exp2(current)
                state = state_of(h)
                total = dot(expo.astype(BF), vaug[:, :HD]) + state[:, :HD]
                sums = jnp.sum(expo, axis=1, keepdims=True) + state[:, HD:]
                worst = finish(h, total, sums, worst)
                current = following
            check(worst)

        @pl.when(host * 4 >= hosts * 3)
        def _():
            own_len = length_of(lengths_ref, host)
            row_ids = lax.broadcasted_iota(jnp.int32, (slab, HD), 0)
            for h in range(start, start + heads):
                cols = slice(h * HD, (h + 1) * HD)
                kept = jnp.where(row_ids < own_len, out_ref[:, cols].astype(F32), 0.0)
                out_ref[:, cols] = kept.astype(BF)

        if last:
            source = out_ref.at[:, start * HD : (start + heads) * HD]
            move = hand_over(source, first + start, heads, len(befores) + start // heads)
            move.start()
            moves.append(move)

    for start in range(0, count, heads):
        part(start)
    for move in moves:
        move.wait()


def exact_block(q_head, out_head, heads, host, kv, q_ref, k_ref, v_ref, keys, vaug, out_ref):
    slab = q_ref.shape[0]
    tile = 64

    def body(i, carry):
        h = lax.div(i, slab // tile)
        r = lax.rem(i, slab // tile)
        at = pl.ds(pl.multiple_of(r * tile, tile), tile)
        query = q_ref[at, lanes(q_head + h, HD)]
        row_ids = lax.broadcasted_iota(jnp.int32, (tile, slab), 0) + r * tile
        key_ids = lax.broadcasted_iota(jnp.int32, (tile, slab), 1)
        own = dot(twice(query), k_ref[2 * kv * HD : 2 * (kv + 1) * HD, :])
        own = jnp.where(key_ids <= row_ids, own, MASKED)
        far = dot(twice(query), keys[...])
        far = jnp.where(host > 0, far, MASKED)
        peak = jnp.maximum(jnp.max(own, 1, keepdims=True), jnp.max(far, 1, keepdims=True))
        own = jnp.exp2(own - peak)
        far = jnp.where(host > 0, jnp.exp2(far - peak), 0.0)
        sums = jnp.sum(own, 1, keepdims=True) + jnp.sum(far, 1, keepdims=True)
        values = jnp.where(host > 0, vaug[:, :HD].astype(F32), 0.0).astype(BF)
        total = dot(own.astype(BF), v_ref[:, 2 * kv * HD : (2 * kv + 1) * HD]) + dot(far.astype(BF), values)
        out_ref[at, lanes(out_head + h, HD)] = (total / sums).astype(BF)
        return carry

    lax.fori_loop(0, heads * (slab // tile), body, 0)


def anchor_part(lengths, ctx_q, states, own_k, own_v, anchor, first, count, per_kv, befores=None, after=()):
    slab, width = ctx_q.shape
    work = count * slab * slab
    last = befores is not None
    ends = {x: x + y.shape[1] // (2 * HD) for x, y in states.items()}
    bases = tuple(x for x in sorted(states) if x < first + count and ends[x] > first)
    earlier = list(befores.values()) if last else []
    places = tuple((at, x.shape[1] // HD) for at, x in befores.items()) if last else ()
    results = jax.ShapeDtypeStruct((slab, count * HD), BF)
    scratch = []
    if last:
        scratch = [pltpu.VMEM(results.shape, BF), pltpu.SemaphoreType.DMA((len(earlier) + count,))]
        results = jax.ShapeDtypeStruct((slab, width), BF)
    return pl.pallas_call(
        functools.partial(anchor_kernel, first, count, bases, per_kv, last, places),
        out_shape=results,
        in_specs=[VMEM] * (6 + len(bases) + len(earlier)) + [ANY] * len(after),
        out_specs=ANY if last else VMEM,
        scratch_shapes=scratch,
        compiler_params=params(),
        cost_estimate=pl.CostEstimate(
            flops=work * HD * 8, bytes_accessed=count * slab * HD * 8, transcendentals=work
        ),
        name="context_anchor",
    )(lengths, ctx_q, own_k, own_v, *anchor, *[states[x] for x in bases], *earlier, *after)


PART = 16


def write_level(ref, width, level):
    lane = lax.broadcasted_iota(jnp.int32, level.shape, 1)
    parts = []
    for at in range(3):
        part = level.astype(BF).astype(F32)
        parts.append(part if at == 0 else pltpu.roll(part, at * PART, 1))
        level = level - part
    packed = jnp.where(lane < PART, parts[0], jnp.where(lane < 2 * PART, parts[1], parts[2]))
    ref[:, width : width + HD] = packed.astype(BF)


def read_level(ref, width):
    packed = ref[:, width : width + HD].astype(F32)
    return packed + pltpu.roll(packed, HD - PART, 1) + pltpu.roll(packed, HD - 2 * PART, 1)


def source_kernel(per_kv, q_rows, group_size, lengths_ref, k_ref, v_ref, self_ref, known_ref, landed_ref, *rest):
    keep_ref, send_ref, q_all, vaug = rest[-4:]
    slab, columns = v_ref.shape
    width = per_kv * columns
    query_count = 8 * q_rows
    host = lax.axis_index("hst")
    own_len = length_of(lengths_ref, host)
    rows = per_kv * query_count
    odd = bit(host, 0) == 1

    def place(even_ref, odd_ref):
        def run():
            parts = []
            for chip in range(4):
                at = slice(chip * q_rows, (chip + 1) * q_rows)
                parts += [even_ref[at, :].astype(F32), odd_ref[at, :].astype(F32)]
            queries = jnp.concatenate(parts, 0).astype(BF)
            for h in range(width // HD):
                q_all[h * query_count : (h + 1) * query_count, :] = queries[:, h * HD : (h + 1) * HD]

        return run

    choose(odd, place(landed_ref, known_ref), place(known_ref, landed_ref))

    first = lax.axis_index("tp") * (width // HD) // group_size * HD
    own_cols = pl.ds(pl.multiple_of(first, HD), columns)
    selves_kv = [self_ref[i, :, own_cols].astype(F32) for i in range(2)]
    lane = lax.broadcasted_iota(jnp.int32, (query_count, HD), 1)
    query_ids = lax.broadcasted_iota(jnp.int32, (query_count, HD), 0)
    self_ok = (host * q_rows + lane <= query_ids) & (lane < q_rows)
    self_ok = jnp.concatenate([self_ok] * per_kv, 0)
    pad = jnp.zeros((HD - q_rows, HD), F32)
    key_rows = lax.broadcasted_iota(jnp.int32, (slab, HD), 0)
    ones = jnp.where(key_rows < own_len, 1.0, 0.0).astype(BF)
    for j in range(columns // HD):
        values = v_ref[:, j * HD : (j + 1) * HD].astype(F32)
        vaug[:, 2 * j * HD : (2 * j + 1) * HD] = jnp.where(key_rows < own_len, values, 0.0).astype(BF)
        vaug[:, (2 * j + 1) * HD : (2 * j + 2) * HD] = ones

    def operands(j):
        cols = slice(j * HD, (j + 1) * HD)
        queries = q_all[j * rows : (j + 1) * rows, :]
        self_keys = jnp.concatenate([selves_kv[0][:, cols], pad], 0).astype(BF)
        self_values = jnp.concatenate([selves_kv[1][:, cols], pad], 0).astype(BF)
        near = dot(twice(queries), k_ref[2 * j * HD : 2 * (j + 1) * HD, :])
        selves = jnp.where(self_ok, dot_t(queries, self_keys) * SCALE2, MASKED)
        return near, selves, jnp.concatenate([self_values, jnp.ones((HD, HD), BF)], 1)

    def store(j, total, level):
        stats = jnp.zeros((query_count, HD), F32)
        for h in range(per_kv):
            stats = jnp.where(lane == h, level[h * query_count : (h + 1) * query_count, :], stats)

        def put(out_ref):
            def run():
                for h in range(per_kv):
                    part = total[h * query_count : (h + 1) * query_count, :]
                    out_ref[:, h * HD : (h + 1) * HD] = part.astype(BF)
                write_level(out_ref, per_kv * HD, stats)

            return run

        choose(odd if j else jnp.logical_not(odd), put(keep_ref), put(send_ref))

    worst = jnp.ones((rows, HD), F32)
    found = []
    for j in range(columns // HD):
        near, selves, self_values = operands(j)
        near = jnp.exp2(near).astype(BF)
        selves = jnp.exp2(selves).astype(BF)
        total = dot(near, vaug[:, 2 * j * HD : (2 * j + 2) * HD]) + dot(selves, self_values)
        sums = total[:, HD:]
        inverse = 1.0 / sums
        worst = jnp.minimum(worst, jnp.minimum(sums, inverse))
        found.append((total[:, :HD] * inverse, jnp.log2(sums)))
    for j, result in enumerate(found):
        store(j, *result)

    @pl.when(jnp.logical_not(jnp.min(worst) > TINY))
    def _():
        key_ids = lax.broadcasted_iota(jnp.int32, (query_count, slab), 1)
        heads_ok = (host * q_rows + lane <= query_ids) & (lane < q_rows)
        for j in range(columns // HD):
            cols = slice(j * HD, (j + 1) * HD)
            self_keys = jnp.concatenate([selves_kv[0][:, cols], pad], 0).astype(BF)
            self_values = jnp.concatenate([selves_kv[1][:, cols], pad], 0).astype(BF)
            self_values = jnp.concatenate([self_values, jnp.ones((HD, HD), BF)], 1)
            mine = odd if j else jnp.logical_not(odd)

            def body(h, stats):
                at = pl.ds(pl.multiple_of((j * per_kv + h) * query_count, query_count), query_count)
                queries = q_all[at, :]
                near = dot(twice(queries), k_ref[2 * j * HD : 2 * (j + 1) * HD, :])
                near = jnp.where(key_ids < own_len, near, MASKED)
                selves = jnp.where(heads_ok, dot_t(queries, self_keys) * SCALE2, MASKED)
                peak = jnp.maximum(jnp.max(near, 1, keepdims=True), jnp.max(selves, 1, keepdims=True))
                near = jnp.exp2(near - peak).astype(BF)
                selves = jnp.exp2(selves - peak).astype(BF)
                total = dot(near, vaug[:, 2 * j * HD : (2 * j + 2) * HD]) + dot(selves, self_values)
                result = (total[:, :HD] / total[:, HD:]).astype(BF)

                def put(out_ref):
                    def run():
                        out_ref[:, lanes(h, HD)] = result

                    return run

                choose(mine, put(keep_ref), put(send_ref))
                return jnp.where(lane == h, peak + jnp.log2(total[:, HD:]), stats)

            stats = lax.fori_loop(0, per_kv, body, jnp.zeros((query_count, HD), F32))

            def put_level(out_ref):
                def run():
                    write_level(out_ref, per_kv * HD, stats)

                return run

            choose(mine, put_level(keep_ref), put_level(send_ref))


def source_part(lengths, own_k, own_v, query_kv, known, landed, q_rows, per_kv, after=()):
    slab, columns = own_v.shape
    width = per_kv * columns
    count = 8 * q_rows
    work = count * (width // HD) * slab
    return pl.pallas_call(
        functools.partial(source_kernel, per_kv, q_rows, H // KVH),
        out_shape=[jax.ShapeDtypeStruct((count, (per_kv + 1) * HD), BF)] * 2,
        in_specs=[VMEM] * 6 + [ANY] * len(after),
        out_specs=[VMEM] * 2,
        scratch_shapes=[pltpu.VMEM((count * width // HD, HD), BF), pltpu.VMEM((slab, 2 * columns), BF)],
        compiler_params=params(),
        cost_estimate=pl.CostEstimate(flops=work * HD * 8, bytes_accessed=2**21, transcendentals=work),
        name="query_source",
    )(lengths, own_k, own_v, query_kv, known, landed, *after)


def merge_part(groups, last, after=()):
    rows, wide = groups[0].shape
    width = wide - HD

    def kernel(*refs):
        in_refs, out_ref = refs[: len(groups)], refs[-1]
        levels = [read_level(ref, width) for ref in in_refs]
        peak = functools.reduce(jnp.maximum, levels)
        weights = [jnp.exp2(x - peak) for x in levels]
        whole = functools.reduce(jnp.add, weights)
        shares = [w / whole for w in weights]
        if not last:
            write_level(out_ref, width, peak + jnp.log2(whole))
        for h in range(width // HD):
            cols = slice(h * HD, (h + 1) * HD)
            total = sum(w[:, h : h + 1] * ref[:, cols].astype(F32) for w, ref in zip(shares, in_refs))
            out_ref[:, cols] = total.astype(BF)

    return small_call(kernel, "query_merge", [(rows, width if last else wide)], groups, after)[0]


def project_part(own, other, out_weight, after=()):
    rows, half = own.shape
    depth, columns = out_weight.shape

    def kernel(w_ref, own_ref, other_ref, *rest):
        out_ref, attended = rest[-2:]

        def put(first, second):
            def run():
                attended[:, :half] = first[...]
                attended[:, half:] = second[...]

            return run

        even = bit(lax.axis_index("hst"), 0) == 0
        choose(even, put(own_ref, other_ref), put(other_ref, own_ref))
        out_ref[...] = dot(attended[...], w_ref[...]).astype(BF)

    return pl.pallas_call(
        kernel,
        out_shape=jax.ShapeDtypeStruct((rows, columns), BF),
        in_specs=[VMEM] * 3 + [ANY] * len(after),
        out_specs=VMEM,
        scratch_shapes=[pltpu.VMEM((rows, depth), BF)],
        compiler_params=params(),
        cost_estimate=pl.CostEstimate(
            flops=2 * rows * depth * columns, bytes_accessed=2 * depth * columns, transcendentals=0
        ),
        name="query_project",
    )(out_weight, own, other, *after)


def general_queries(lengths, own_k, own_v, self_kv, query_q, out_weight, per_kv):
    own_kv = jnp.stack([own_k, own_v], 0)
    host_id = lax.axis_index("hst")
    local_heads = query_q.shape[1] // HD
    kv_local = own_kv.shape[2] // HD
    slab_rows = own_kv.shape[1]
    own_len = lengths[host_id]
    row_ids = jnp.arange(slab_rows)
    all_queries = lax.all_gather(query_q, "hst", axis=0, tiled=True)
    query_count = all_queries.shape[0]
    q_rows = query_q.shape[0]
    source = jnp.concatenate([own_kv, self_kv], 1)
    source = source.reshape(2, slab_rows + q_rows, kv_local, HD).transpose(0, 2, 1, 3)
    query_ids = jnp.arange(query_count)
    context_ok = jnp.broadcast_to(row_ids[None, :] < own_len, (query_count, slab_rows))
    self_ok = (host_id * q_rows + jnp.arange(q_rows))[None, :] <= query_ids[:, None]
    seen_ok = jnp.concatenate([context_ok, self_ok], 1)
    query_heads = all_queries.reshape(query_count, local_heads, HD).transpose(1, 0, 2)

    def score_head(operands):
        query_rows, head_index = operands
        kv_index = head_index // per_kv
        scores = dot_t(query_rows, source[0, kv_index]) * HD ** (-0.5)
        scores = jnp.where(seen_ok, scores, MASKED)
        peak = jnp.max(scores, axis=1)
        expo = jnp.exp(scores - peak[:, None])
        return peak, jnp.sum(expo, axis=1), dot(expo.astype(BF), source[1, kv_index])

    maxima, totals, outputs = lax.map(score_head, (query_heads, jnp.arange(local_heads)))
    factor = jnp.exp(maxima - lax.pmax(maxima, "hst"))
    denominator, summed = lax.psum((totals * factor, outputs * factor[..., None]), "hst")
    attended = (summed / denominator[..., None]).astype(BF)
    attended = attended.transpose(1, 0, 2).reshape(query_count, local_heads * HD)
    return lax.psum(dot(attended, out_weight), "tp").astype(BF)


def per_device(hosts, groups, ctx_q, ctx_kv, lengths, query_q, query_kv, out_weight):
    slab = ctx_q.shape[0]
    local_heads = ctx_q.shape[1] // HD
    group_size = H // KVH
    kv_local = max(1, local_heads // group_size)
    per_kv = min(local_heads, group_size)
    q_rows = query_q.shape[0]
    host = lax.axis_index("hst")
    fast = hosts == 8 and groups & (groups - 1) == 0
    fast = fast and q_rows == 8 and local_heads == 16 and per_kv == 8

    if not fast:
        kv_first = lax.axis_index("tp") * local_heads // group_size
        self_kv = lax.dynamic_slice_in_dim(query_kv, kv_first * HD, kv_local * HD, 2)
        own_k, own_v = pick(ctx_kv, kv_local, local_heads)
        query_out = general_queries(lengths, own_k, own_v, self_kv, query_q, out_weight, per_kv)
        k, v = spread(jnp.stack([own_k, own_v]), "hst", 0)
        lengths = lengths.reshape(1, hosts)
        own_k, own_v = prepare(own_k, own_v, False)
        anchor = prepare(k, v, False)
        state = own_part(ctx_q, own_k, own_v, 0, local_heads, per_kv)
        results = {}
        for first in range(0, local_heads, per_kv):
            cols = slice(2 * first // per_kv * HD, 2 * (first // per_kv + 1) * HD)
            last = first + per_kv == local_heads
            results[first] = anchor_part(
                lengths, ctx_q, {0: state}, own_k, own_v, (anchor[0][cols, :], anchor[1][:, cols]),
                first, per_kv, per_kv, dict(results) if last else None,
            )
        return results[first], query_out

    lengths = lengths.reshape(1, hosts)
    states = {}

    def own(first, count, after=()):
        states[first] = own_part(ctx_q, own_keys, own_values, first, count, per_kv, after)
        return states[first]

    along = ((2, 4), (4, 2))

    def is_even(h):
        return bit(h, 0) == 0

    def source_first(h):
        return h < 2

    done_early = (
        lambda h: (h <= 2) | (h == 5),
        lambda h: (h <= 1) | (h == 3) | (h == 4),
    )

    bits = (6, 2, 4)
    landed = [swap(query_q, "hst", hosts, x, x) for x in bits]
    own_k, own_v = pick(ctx_kv, kv_local, local_heads)
    value_landed = swap(own_v, "hst", hosts, 1, 1)
    own_keys, own_values = prepare(own_k, own_v, False)
    done = own(0, 2)
    parts = list(relay(is_even, own_k, value_landed, (done,), kv_local))
    parts_landed = [swap(x, "hst", hosts, *along[kv]) for kv, x in enumerate(parts)]
    done = own(2, 2, (parts[0],))
    queries = by_chip(query_q, landed, bits, (done,))
    landed = swap(queries, "hst", hosts, 1, 1)
    anchor = {}

    def pass_on(kv, after):
        (parts[kv],) = relay(source_first, parts[kv], parts_landed[kv], after)
        parts_landed[kv] = swap(parts[kv], "hst", hosts, *along[1 - kv])
        return parts[kv]

    def complete(kv, after):
        (held,) = relay(done_early[kv], parts[kv], parts_landed[kv], after)
        anchor[kv] = held, swap(held, "hst", hosts, 1, 1)
        return held

    keep, give = source_part(lengths, own_keys, own_v, query_kv, queries, landed, q_rows, per_kv, ())
    landed = swap(give, "hst", hosts, 1, 1)
    done = own(4, 4, (keep,))
    source = merge_part([keep, landed], False, (done,))
    landed = swap(source, "hst", hosts, *along[0])
    done = pass_on(0, (source,))
    done = own(8, 8, (done,))
    source = merge_part([source, landed], False, (done,))
    landed = swap(source, "hst", hosts, *along[1])
    done = complete(0, (source,))
    done = pass_on(1, (done,))
    anchor[0] = prepare(*anchor[0], True, (done,))
    results = {}

    def anchors(first, count, after, last=False):
        results[first] = anchor_part(
            lengths, ctx_q, states, own_keys, own_values, anchor[first // per_kv],
            first, count, per_kv, dict(results) if last else None, after,
        )
        return results[first]

    done = anchors(0, 4, ())
    attended = merge_part([source, landed], True, (done,))
    landed = swap(attended, "hst", hosts, 1, 1)
    done = complete(1, (attended,))
    terms = project_part(attended, landed, out_weight, (done,))
    done = terms
    shares = [[(10, 6, True)], [(4, 4, False), (8, 2, False)]]
    step = 1
    while step < groups:
        landed = swap(terms, "tp", groups, step, step)
        last = False
        for first, count, last in shares.pop() if shares else ():
            if first == per_kv:
                anchor[1] = prepare(*anchor[1], True, (done,))
            done = anchors(first, count, (terms, done), last)
        terms = add_part(terms, landed, () if last else (done,))
        step *= 2
    for group in reversed(shares):
        for first, count, last in group:
            done = anchors(first, count, (), last)
    return done, terms


def solution(mesh):
    hosts, groups = mesh.shape["hst"], mesh.shape["tp"]
    return jax.shard_map(
        functools.partial(per_device, hosts, groups),
        mesh=mesh,
        in_specs=(
            P("hst", "tp"),
            P(None, "hst", None),
            P(),
            P("hst", "tp"),
            P(None, "hst", None),
            P("tp", "hst"),
        ),
        out_specs=(P("hst", "tp"), P(None, "hst")),
        check_vma=False,
    )
```

```python
import functools

import jax
import jax.numpy as jnp
from jax import lax
from jax.experimental import pallas as pl
from jax.experimental.pallas import tpu as pltpu
from jax.sharding import PartitionSpec as P

H = 64
KVH = 8
HD = 128
MASKED = -1e30
LOG2E = 1.4426950408889634
SCALE2 = HD ** (-0.5) * LOG2E
TINY = 2.0 ** -90
BF = jnp.bfloat16
F32 = jnp.float32
VMEM = pl.BlockSpec(memory_space=pltpu.VMEM)
ANY = pl.BlockSpec(memory_space=pl.ANY)
HBM = pl.BlockSpec(memory_space=pltpu.HBM)


def params(mib=20):
    return pltpu.CompilerParams(vmem_limit_bytes=mib * 2**20)


def dot_t(a, b):
    return lax.dot_general(a, b, (((1,), (1,)), ((), ())), preferred_element_type=F32)


def dot(a, b):
    return lax.dot_general(a, b, (((1,), (0,)), ((), ())), preferred_element_type=F32)


def spread(value, axis, source):
    kept = jnp.where(lax.axis_index(axis) == source, value, 0).astype(value.dtype)
    return lax.psum(kept, axis)


def swap(value, axis, size, even, odd):
    return lax.ppermute(value, axis, [(i, i ^ (odd if i & 1 else even)) for i in range(size)])


def pick_kernel(group_size, local_heads, kv_ref, k_ref, v_ref, sems):
    first = lax.axis_index("tp") * local_heads // group_size * HD
    cols = pl.ds(pl.multiple_of(first, HD), k_ref.shape[1])
    moves = [
        pltpu.make_async_copy(kv_ref.at[1, :, cols], v_ref, sems.at[1]),
        pltpu.make_async_copy(kv_ref.at[0, :, cols], k_ref, sems.at[0]),
    ]
    for move in moves:
        move.start()
    for move in moves:
        move.wait()


def pick(ctx_kv, kv_local, local_heads):
    return pl.pallas_call(
        functools.partial(pick_kernel, H // KVH, local_heads),
        out_shape=[jax.ShapeDtypeStruct((ctx_kv.shape[1], kv_local * HD), BF)] * 2,
        in_specs=[HBM],
        out_specs=[VMEM] * 2,
        scratch_shapes=[pltpu.SemaphoreType.DMA((2,))],
        compiler_params=params(52),
        cost_estimate=pl.CostEstimate(flops=0, bytes_accessed=2**22, transcendentals=0),
        name="pick_columns",
    )(ctx_kv)


def bit(value, at):
    return (value >> at) & 1


def small_call(kernel, name, shapes, inputs, after=()):
    return pl.pallas_call(
        kernel,
        out_shape=[jax.ShapeDtypeStruct(x, BF) for x in shapes],
        in_specs=[VMEM] * len(inputs) + [ANY] * len(after),
        out_specs=[VMEM] * len(shapes),
        compiler_params=params(),
        cost_estimate=pl.CostEstimate(flops=0, bytes_accessed=2**14, transcendentals=0),
        name=name,
    )(*inputs, *after)


def choose(condition, one, two):
    pl.when(condition)(one)
    pl.when(jnp.logical_not(condition))(two)


def take_rows(target, source, rows, cols=slice(None)):
    def run():
        target[:rows, :] = source[:rows, cols]

    return run


def by_chip(own, others, bits, after=()):
    rows, width = own.shape

    def kernel(*refs):
        out_ref, all_ref = refs[-2:]
        host = lax.axis_index("hst")
        for ref, flip in zip(refs, (0,) + tuple(bits)):
            start = pl.multiple_of((jnp.bitwise_xor(host, flip) >> 1) * rows, rows)
            all_ref[pl.ds(start, rows), :] = ref[...].astype(F32)
        out_ref[...] = all_ref[...].astype(BF)

    total = rows * (1 + len(bits))
    return pl.pallas_call(
        kernel,
        out_shape=jax.ShapeDtypeStruct((total, width), BF),
        in_specs=[VMEM] * (1 + len(bits)) + [ANY] * len(after),
        out_specs=VMEM,
        scratch_shapes=[pltpu.VMEM((total, width), F32)],
        compiler_params=params(),
        cost_estimate=pl.CostEstimate(flops=0, bytes_accessed=2**20, transcendentals=0),
        name="query_chips",
    )(own, *others, *after)


def relay(keep_of, one, two, after=(), split=1):
    slab, columns = one.shape
    width = columns // split

    def kernel(one_ref, two_ref, *rest):
        keep = keep_of(lax.axis_index("hst"))
        for j, out_ref in enumerate(rest[-split:]):
            cols = slice(j * width, (j + 1) * width)
            choose(keep, take_rows(out_ref, one_ref, slab, cols), take_rows(out_ref, two_ref, slab, cols))

    return small_call(kernel, "anchor_relay", [(slab, width)] * split, (one, two), after)


def add_part(one, two, after=()):
    def kernel(one_ref, two_ref, *rest):
        rest[-1][...] = (one_ref[...].astype(F32) + two_ref[...].astype(F32)).astype(BF)

    return small_call(kernel, "query_sum", [one.shape], (one, two), after)[0]


def prepare(first, second, swapped, after=()):
    slab, columns = first.shape

    def kernel(first_ref, second_ref, *rest):
        keys_ref, values_ref = rest[-2:]

        def fill(k_ref, v_ref):
            def run():
                for j in range(columns // HD):
                    cols = slice(j * HD, (j + 1) * HD)
                    at = 2 * j * HD
                    scaled = k_ref[:, cols].astype(F32) * SCALE2
                    high = scaled.astype(BF)
                    low = scaled - high.astype(F32)
                    keys_ref[at : at + HD, :] = high.astype(F32).T.astype(BF)
                    keys_ref[at + HD : at + 2 * HD, :] = low.T.astype(BF)
                    values_ref[:, at : at + HD] = v_ref[:, cols]
                    values_ref[:, at + HD : at + 2 * HD] = jnp.ones((slab, HD), BF)

            return run

        if swapped:
            even = bit(lax.axis_index("hst"), 0) == 0
            choose(even, fill(first_ref, second_ref), fill(second_ref, first_ref))
        else:
            fill(first_ref, second_ref)()

    shapes = [(2 * columns, slab), (slab, 2 * columns)]
    return small_call(kernel, "operands", shapes, (first, second), after)


def twice(query):
    return jnp.concatenate([query, query], 1)


def lanes(index, width):
    return pl.ds(pl.multiple_of(index * width, width), width)


def row_tile(slab):
    return 256 if slab % 256 == 0 else slab


def body_size(first, count, per_kv, most):
    def fits(size):
        bodies = range(first, first + count, size)
        return count % size == 0 and all(x // per_kv == (x + size - 1) // per_kv for x in bodies)

    return max(x for x in range(1, most + 1) if fits(x))


def own_kernel(first, count, per_kv, q_ref, k_ref, v_ref, *rest):
    state_ref = rest[-1]
    slab = q_ref.shape[0]
    tile = row_tile(slab)
    half = tile // 2
    heads = body_size(first, count, per_kv, 4)
    rows = lax.broadcasted_iota(jnp.int32, (half, half), 0)
    cols = lax.broadcasted_iota(jnp.int32, (half, half), 1)
    causal = cols <= rows
    chunks = slab // tile
    units = [(h, j) for h in range(heads) for j in range(chunks)]

    def body(i, carry):
        kv = lax.div(first + i * heads, per_kv)

        def scores(at):
            h, j = units[at]
            query = q_ref[j * tile :, lanes(first + i * heads + h, HD)]
            return dot(twice(query), k_ref[lanes(kv, 2 * HD), j * tile : (j + 1) * tile])

        def power(x):
            return jnp.exp2(x).astype(BF)

        def corner(x):
            return jnp.where(causal, jnp.exp2(x), 0.0).astype(BF)

        current = scores(0)
        totals = [None] * chunks
        for at, (h, j) in enumerate(units):
            following = scores(at + 1) if at + 1 < len(units) else None
            top = jnp.concatenate([corner(current[:half, :half]), jnp.zeros((half, half), BF)], 1)
            low = jnp.concatenate([power(current[half:tile, :half]), corner(current[half:tile, half:])], 1)
            expo = [top, low] if j == chunks - 1 else [top, low, power(current[tile:])]
            part = dot(jnp.concatenate(expo, 0), v_ref[j * tile : (j + 1) * tile, lanes(kv, 2 * HD)])
            for r in range(j, chunks):
                piece = part[(r - j) * tile : (r - j + 1) * tile]
                totals[r] = piece if j == 0 else totals[r] + piece
            state_ref[j * tile : (j + 1) * tile, lanes(i * heads + h, 2 * HD)] = totals[j]
            current = following
        return carry

    lax.fori_loop(0, count // heads, body, 0)


def own_part(ctx_q, own_k, own_v, first, count, per_kv, after=()):
    slab = ctx_q.shape[0]
    work = count * slab * (slab + row_tile(slab)) // 2
    return pl.pallas_call(
        functools.partial(own_kernel, first, count, per_kv),
        out_shape=jax.ShapeDtypeStruct((slab, count * 2 * HD), F32),
        in_specs=[VMEM] * 3 + [ANY] * len(after),
        out_specs=VMEM,
        compiler_params=params(),
        cost_estimate=pl.CostEstimate(
            flops=work * HD * 8, bytes_accessed=count * slab * HD * 6, transcendentals=work
        ),
        name="context_own",
    )(ctx_q, own_k, own_v, *after)


def length_of(lengths_ref, host):
    lengths = lengths_ref[...]
    index = lax.broadcasted_iota(jnp.int32, lengths.shape, 1)
    return jnp.sum(jnp.where(index == host, lengths, 0), axis=1, keepdims=True)


def anchor_kernel(first, count, bases, per_kv, last, befores, *refs):
    lengths_ref, q_ref, k_ref, v_ref, keys, vaug = refs[:6]
    hosts = lengths_ref.shape[1]
    state_refs = refs[6 : 6 + len(bases)]
    earlier = refs[6 + len(bases) : 6 + len(bases) + len(befores)]
    if last:
        full_ref, out_ref, sems = refs[-3:]
    else:
        out_ref = refs[-1]
    slab = q_ref.shape[0]
    heads = body_size(first, count, per_kv, 2 if last else 4)
    kv = first // per_kv
    host = lax.axis_index("hst")

    def hand_over(source, start, width, sem):
        target = full_ref.at[:, pl.ds(start * HD, width * HD)]
        return pltpu.make_async_copy(source, target, sems.at[sem])

    moves = [hand_over(earlier[n], *place, n) for n, place in enumerate(befores)]
    for move in moves:
        move.start()

    def part(start):
        def query_of(h):
            at = (first + start + h) * HD
            return q_ref[:, at : at + HD]

        def scores(h):
            return dot(twice(query_of(h)), keys[...])

        def state_of(h):
            head = first + start + h
            n = max(n for n, base in enumerate(bases) if base <= head)
            at = (head - bases[n]) * 2 * HD
            return state_refs[n][:, at : at + 2 * HD]

        def finish(h, total, sums, worst):
            inverse = pl.reciprocal(sums, approx=True)
            out_ref[:, (start + h) * HD : (start + h + 1) * HD] = (total * inverse).astype(BF)
            return jnp.minimum(worst, jnp.minimum(sums, inverse))

        def check(worst):
            @pl.when(jnp.logical_not(jnp.min(worst) > TINY))
            def _():
                exact_block(first + start, start, heads, host, kv, q_ref, k_ref, v_ref, keys, vaug, out_ref)

        @pl.when(host == 0)
        def _():
            worst = jnp.ones((slab, HD), F32)
            for h in range(heads):
                state = state_of(h)
                worst = finish(h, state[:, :HD], state[:, HD:], worst)
            check(worst)

        @pl.when(host > 0)
        def _():
            worst = jnp.ones((slab, HD), F32)
            current = scores(0)
            for h in range(heads):
                following = scores(h + 1) if h + 1 < heads else None
                expo = jnp.exp2(current)
                state = state_of(h)
                total = dot(expo.astype(BF), vaug[:, :HD]) + state[:, :HD]
                sums = jnp.sum(expo, axis=1, keepdims=True) + state[:, HD:]
                worst = finish(h, total, sums, worst)
                current = following
            check(worst)

        @pl.when(host * 4 >= hosts * 3)
        def _():
            own_len = length_of(lengths_ref, host)
            row_ids = lax.broadcasted_iota(jnp.int32, (slab, HD), 0)
            for h in range(start, start + heads):
                cols = slice(h * HD, (h + 1) * HD)
                kept = jnp.where(row_ids < own_len, out_ref[:, cols].astype(F32), 0.0)
                out_ref[:, cols] = kept.astype(BF)

        if last:
            source = out_ref.at[:, start * HD : (start + heads) * HD]
            move = hand_over(source, first + start, heads, len(befores) + start // heads)
            move.start()
            moves.append(move)

    for start in range(0, count, heads):
        part(start)
    for move in moves:
        move.wait()


def exact_block(q_head, out_head, heads, host, kv, q_ref, k_ref, v_ref, keys, vaug, out_ref):
    slab = q_ref.shape[0]
    tile = 64

    def body(i, carry):
        h = lax.div(i, slab // tile)
        r = lax.rem(i, slab // tile)
        at = pl.ds(pl.multiple_of(r * tile, tile), tile)
        query = q_ref[at, lanes(q_head + h, HD)]
        row_ids = lax.broadcasted_iota(jnp.int32, (tile, slab), 0) + r * tile
        key_ids = lax.broadcasted_iota(jnp.int32, (tile, slab), 1)
        own = dot(twice(query), k_ref[2 * kv * HD : 2 * (kv + 1) * HD, :])
        own = jnp.where(key_ids <= row_ids, own, MASKED)
        far = dot(twice(query), keys[...])
        far = jnp.where(host > 0, far, MASKED)
        peak = jnp.maximum(jnp.max(own, 1, keepdims=True), jnp.max(far, 1, keepdims=True))
        own = jnp.exp2(own - peak)
        far = jnp.where(host > 0, jnp.exp2(far - peak), 0.0)
        sums = jnp.sum(own, 1, keepdims=True) + jnp.sum(far, 1, keepdims=True)
        values = jnp.where(host > 0, vaug[:, :HD].astype(F32), 0.0).astype(BF)
        total = dot(own.astype(BF), v_ref[:, 2 * kv * HD : (2 * kv + 1) * HD]) + dot(far.astype(BF), values)
        out_ref[at, lanes(out_head + h, HD)] = (total / sums).astype(BF)
        return carry

    lax.fori_loop(0, heads * (slab // tile), body, 0)


def anchor_part(lengths, ctx_q, states, own_k, own_v, anchor, first, count, per_kv, befores=None, after=()):
    slab, width = ctx_q.shape
    work = count * slab * slab
    last = befores is not None
    ends = {x: x + y.shape[1] // (2 * HD) for x, y in states.items()}
    bases = tuple(x for x in sorted(states) if x < first + count and ends[x] > first)
    earlier = list(befores.values()) if last else []
    places = tuple((at, x.shape[1] // HD) for at, x in befores.items()) if last else ()
    results = jax.ShapeDtypeStruct((slab, count * HD), BF)
    scratch = []
    if last:
        scratch = [pltpu.VMEM(results.shape, BF), pltpu.SemaphoreType.DMA((len(earlier) + count,))]
        results = jax.ShapeDtypeStruct((slab, width), BF)
    return pl.pallas_call(
        functools.partial(anchor_kernel, first, count, bases, per_kv, last, places),
        out_shape=results,
        in_specs=[VMEM] * (6 + len(bases) + len(earlier)) + [ANY] * len(after),
        out_specs=ANY if last else VMEM,
        scratch_shapes=scratch,
        compiler_params=params(),
        cost_estimate=pl.CostEstimate(
            flops=work * HD * 8, bytes_accessed=count * slab * HD * 8, transcendentals=work
        ),
        name="context_anchor",
    )(lengths, ctx_q, own_k, own_v, *anchor, *[states[x] for x in bases], *earlier, *after)


PART = 16


def write_level(ref, width, level):
    lane = lax.broadcasted_iota(jnp.int32, level.shape, 1)
    parts = []
    for at in range(3):
        part = level.astype(BF).astype(F32)
        parts.append(part if at == 0 else pltpu.roll(part, at * PART, 1))
        level = level - part
    packed = jnp.where(lane < PART, parts[0], jnp.where(lane < 2 * PART, parts[1], parts[2]))
    ref[:, width : width + HD] = packed.astype(BF)


def read_level(ref, width):
    packed = ref[:, width : width + HD].astype(F32)
    return packed + pltpu.roll(packed, HD - PART, 1) + pltpu.roll(packed, HD - 2 * PART, 1)


def source_kernel(per_kv, q_rows, group_size, lengths_ref, k_ref, v_ref, self_ref, known_ref, landed_ref, *rest):
    keep_ref, send_ref, q_all, vaug = rest[-4:]
    slab, columns = v_ref.shape
    width = per_kv * columns
    query_count = 8 * q_rows
    host = lax.axis_index("hst")
    own_len = length_of(lengths_ref, host)
    rows = per_kv * query_count
    odd = bit(host, 0) == 1

    def place(even_ref, odd_ref):
        def run():
            parts = []
            for chip in range(4):
                at = slice(chip * q_rows, (chip + 1) * q_rows)
                parts += [even_ref[at, :].astype(F32), odd_ref[at, :].astype(F32)]
            queries = jnp.concatenate(parts, 0).astype(BF)
            for h in range(width // HD):
                q_all[h * query_count : (h + 1) * query_count, :] = queries[:, h * HD : (h + 1) * HD]

        return run

    choose(odd, place(landed_ref, known_ref), place(known_ref, landed_ref))

    first = lax.axis_index("tp") * (width // HD) // group_size * HD
    own_cols = pl.ds(pl.multiple_of(first, HD), columns)
    selves_kv = [self_ref[i, :, own_cols].astype(F32) for i in range(2)]
    lane = lax.broadcasted_iota(jnp.int32, (query_count, HD), 1)
    query_ids = lax.broadcasted_iota(jnp.int32, (query_count, HD), 0)
    self_ok = (host * q_rows + lane <= query_ids) & (lane < q_rows)
    self_ok = jnp.concatenate([self_ok] * per_kv, 0)
    pad = jnp.zeros((HD - q_rows, HD), F32)
    key_rows = lax.broadcasted_iota(jnp.int32, (slab, HD), 0)
    ones = jnp.where(key_rows < own_len, 1.0, 0.0).astype(BF)
    for j in range(columns // HD):
        values = v_ref[:, j * HD : (j + 1) * HD].astype(F32)
        vaug[:, 2 * j * HD : (2 * j + 1) * HD] = jnp.where(key_rows < own_len, values, 0.0).astype(BF)
        vaug[:, (2 * j + 1) * HD : (2 * j + 2) * HD] = ones

    def operands(j):
        cols = slice(j * HD, (j + 1) * HD)
        queries = q_all[j * rows : (j + 1) * rows, :]
        self_keys = jnp.concatenate([selves_kv[0][:, cols], pad], 0).astype(BF)
        self_values = jnp.concatenate([selves_kv[1][:, cols], pad], 0).astype(BF)
        near = dot(twice(queries), k_ref[2 * j * HD : 2 * (j + 1) * HD, :])
        selves = jnp.where(self_ok, dot_t(queries, self_keys) * SCALE2, MASKED)
        return near, selves, jnp.concatenate([self_values, jnp.ones((HD, HD), BF)], 1)

    def store(j, total, level):
        stats = jnp.zeros((query_count, HD), F32)
        for h in range(per_kv):
            stats = jnp.where(lane == h, level[h * query_count : (h + 1) * query_count, :], stats)

        def put(out_ref):
            def run():
                for h in range(per_kv):
                    part = total[h * query_count : (h + 1) * query_count, :]
                    out_ref[:, h * HD : (h + 1) * HD] = part.astype(BF)
                write_level(out_ref, per_kv * HD, stats)

            return run

        choose(odd if j else jnp.logical_not(odd), put(keep_ref), put(send_ref))

    worst = jnp.ones((rows, HD), F32)
    found = []
    for j in range(columns // HD):
        near, selves, self_values = operands(j)
        near = jnp.exp2(near).astype(BF)
        selves = jnp.exp2(selves).astype(BF)
        total = dot(near, vaug[:, 2 * j * HD : (2 * j + 2) * HD]) + dot(selves, self_values)
        sums = total[:, HD:]
        inverse = 1.0 / sums
        worst = jnp.minimum(worst, jnp.minimum(sums, inverse))
        found.append((total[:, :HD] * inverse, jnp.log2(sums)))
    for j, result in enumerate(found):
        store(j, *result)

    @pl.when(jnp.logical_not(jnp.min(worst) > TINY))
    def _():
        key_ids = lax.broadcasted_iota(jnp.int32, (query_count, slab), 1)
        heads_ok = (host * q_rows + lane <= query_ids) & (lane < q_rows)
        for j in range(columns // HD):
            cols = slice(j * HD, (j + 1) * HD)
            self_keys = jnp.concatenate([selves_kv[0][:, cols], pad], 0).astype(BF)
            self_values = jnp.concatenate([selves_kv[1][:, cols], pad], 0).astype(BF)
            self_values = jnp.concatenate([self_values, jnp.ones((HD, HD), BF)], 1)
            mine = odd if j else jnp.logical_not(odd)

            def body(h, stats):
                at = pl.ds(pl.multiple_of((j * per_kv + h) * query_count, query_count), query_count)
                queries = q_all[at, :]
                near = dot(twice(queries), k_ref[2 * j * HD : 2 * (j + 1) * HD, :])
                near = jnp.where(key_ids < own_len, near, MASKED)
                selves = jnp.where(heads_ok, dot_t(queries, self_keys) * SCALE2, MASKED)
                peak = jnp.maximum(jnp.max(near, 1, keepdims=True), jnp.max(selves, 1, keepdims=True))
                near = jnp.exp2(near - peak).astype(BF)
                selves = jnp.exp2(selves - peak).astype(BF)
                total = dot(near, vaug[:, 2 * j * HD : (2 * j + 2) * HD]) + dot(selves, self_values)
                result = (total[:, :HD] / total[:, HD:]).astype(BF)

                def put(out_ref):
                    def run():
                        out_ref[:, lanes(h, HD)] = result

                    return run

                choose(mine, put(keep_ref), put(send_ref))
                return jnp.where(lane == h, peak + jnp.log2(total[:, HD:]), stats)

            stats = lax.fori_loop(0, per_kv, body, jnp.zeros((query_count, HD), F32))

            def put_level(out_ref):
                def run():
                    write_level(out_ref, per_kv * HD, stats)

                return run

            choose(mine, put_level(keep_ref), put_level(send_ref))


def source_part(lengths, own_k, own_v, query_kv, known, landed, q_rows, per_kv, after=()):
    slab, columns = own_v.shape
    width = per_kv * columns
    count = 8 * q_rows
    work = count * (width // HD) * slab
    return pl.pallas_call(
        functools.partial(source_kernel, per_kv, q_rows, H // KVH),
        out_shape=[jax.ShapeDtypeStruct((count, (per_kv + 1) * HD), BF)] * 2,
        in_specs=[VMEM] * 6 + [ANY] * len(after),
        out_specs=[VMEM] * 2,
        scratch_shapes=[pltpu.VMEM((count * width // HD, HD), BF), pltpu.VMEM((slab, 2 * columns), BF)],
        compiler_params=params(),
        cost_estimate=pl.CostEstimate(flops=work * HD * 8, bytes_accessed=2**21, transcendentals=work),
        name="query_source",
    )(lengths, own_k, own_v, query_kv, known, landed, *after)


def merge_part(groups, last, after=()):
    rows, wide = groups[0].shape
    width = wide - HD

    def kernel(*refs):
        in_refs, out_ref = refs[: len(groups)], refs[-1]
        levels = [read_level(ref, width) for ref in in_refs]
        peak = functools.reduce(jnp.maximum, levels)
        weights = [jnp.exp2(x - peak) for x in levels]
        whole = functools.reduce(jnp.add, weights)
        shares = [w / whole for w in weights]
        if not last:
            write_level(out_ref, width, peak + jnp.log2(whole))
        for h in range(width // HD):
            cols = slice(h * HD, (h + 1) * HD)
            total = sum(w[:, h : h + 1] * ref[:, cols].astype(F32) for w, ref in zip(shares, in_refs))
            out_ref[:, cols] = total.astype(BF)

    return small_call(kernel, "query_merge", [(rows, width if last else wide)], groups, after)[0]


def project_part(own, other, out_weight, after=()):
    rows, half = own.shape
    depth, columns = out_weight.shape

    def kernel(w_ref, own_ref, other_ref, *rest):
        out_ref, attended = rest[-2:]

        def put(first, second):
            def run():
                attended[:, :half] = first[...]
                attended[:, half:] = second[...]

            return run

        even = bit(lax.axis_index("hst"), 0) == 0
        choose(even, put(own_ref, other_ref), put(other_ref, own_ref))
        out_ref[...] = dot(attended[...], w_ref[...]).astype(BF)

    return pl.pallas_call(
        kernel,
        out_shape=jax.ShapeDtypeStruct((rows, columns), BF),
        in_specs=[VMEM] * 3 + [ANY] * len(after),
        out_specs=VMEM,
        scratch_shapes=[pltpu.VMEM((rows, depth), BF)],
        compiler_params=params(),
        cost_estimate=pl.CostEstimate(
            flops=2 * rows * depth * columns, bytes_accessed=2 * depth * columns, transcendentals=0
        ),
        name="query_project",
    )(out_weight, own, other, *after)


def general_queries(lengths, own_k, own_v, self_kv, query_q, out_weight, per_kv):
    own_kv = jnp.stack([own_k, own_v], 0)
    host_id = lax.axis_index("hst")
    local_heads = query_q.shape[1] // HD
    kv_local = own_kv.shape[2] // HD
    slab_rows = own_kv.shape[1]
    own_len = lengths[host_id]
    row_ids = jnp.arange(slab_rows)
    all_queries = lax.all_gather(query_q, "hst", axis=0, tiled=True)
    query_count = all_queries.shape[0]
    q_rows = query_q.shape[0]
    source = jnp.concatenate([own_kv, self_kv], 1)
    source = source.reshape(2, slab_rows + q_rows, kv_local, HD).transpose(0, 2, 1, 3)
    query_ids = jnp.arange(query_count)
    context_ok = jnp.broadcast_to(row_ids[None, :] < own_len, (query_count, slab_rows))
    self_ok = (host_id * q_rows + jnp.arange(q_rows))[None, :] <= query_ids[:, None]
    seen_ok = jnp.concatenate([context_ok, self_ok], 1)
    query_heads = all_queries.reshape(query_count, local_heads, HD).transpose(1, 0, 2)

    def score_head(operands):
        query_rows, head_index = operands
        kv_index = head_index // per_kv
        scores = dot_t(query_rows, source[0, kv_index]) * HD ** (-0.5)
        scores = jnp.where(seen_ok, scores, MASKED)
        peak = jnp.max(scores, axis=1)
        expo = jnp.exp(scores - peak[:, None])
        return peak, jnp.sum(expo, axis=1), dot(expo.astype(BF), source[1, kv_index])

    maxima, totals, outputs = lax.map(score_head, (query_heads, jnp.arange(local_heads)))
    factor = jnp.exp(maxima - lax.pmax(maxima, "hst"))
    denominator, summed = lax.psum((totals * factor, outputs * factor[..., None]), "hst")
    attended = (summed / denominator[..., None]).astype(BF)
    attended = attended.transpose(1, 0, 2).reshape(query_count, local_heads * HD)
    return lax.psum(dot(attended, out_weight), "tp").astype(BF)


def per_device(hosts, groups, ctx_q, ctx_kv, lengths, query_q, query_kv, out_weight):
    slab = ctx_q.shape[0]
    local_heads = ctx_q.shape[1] // HD
    group_size = H // KVH
    kv_local = max(1, local_heads // group_size)
    per_kv = min(local_heads, group_size)
    q_rows = query_q.shape[0]
    host = lax.axis_index("hst")
    fast = hosts == 8 and groups & (groups - 1) == 0
    fast = fast and q_rows == 8 and local_heads == 16 and per_kv == 8

    if not fast:
        kv_first = lax.axis_index("tp") * local_heads // group_size
        self_kv = lax.dynamic_slice_in_dim(query_kv, kv_first * HD, kv_local * HD, 2)
        own_k, own_v = pick(ctx_kv, kv_local, local_heads)
        query_out = general_queries(lengths, own_k, own_v, self_kv, query_q, out_weight, per_kv)
        k, v = spread(jnp.stack([own_k, own_v]), "hst", 0)
        lengths = lengths.reshape(1, hosts)
        own_k, own_v = prepare(own_k, own_v, False)
        anchor = prepare(k, v, False)
        state = own_part(ctx_q, own_k, own_v, 0, local_heads, per_kv)
        results = {}
        for first in range(0, local_heads, per_kv):
            cols = slice(2 * first // per_kv * HD, 2 * (first // per_kv + 1) * HD)
            last = first + per_kv == local_heads
            results[first] = anchor_part(
                lengths, ctx_q, {0: state}, own_k, own_v, (anchor[0][cols, :], anchor[1][:, cols]),
                first, per_kv, per_kv, dict(results) if last else None,
            )
        return results[first], query_out

    lengths = lengths.reshape(1, hosts)
    states = {}

    def own(first, count, after=()):
        states[first] = own_part(ctx_q, own_keys, own_values, first, count, per_kv, after)
        return states[first]

    along = ((2, 4), (4, 2))

    def is_even(h):
        return bit(h, 0) == 0

    def source_first(h):
        return h < 2

    done_early = (
        lambda h: (h <= 2) | (h == 5),
        lambda h: (h <= 1) | (h == 3) | (h == 4),
    )

    bits = (6, 2, 4)
    landed = [swap(query_q, "hst", hosts, x, x) for x in bits]
    own_k, own_v = pick(ctx_kv, kv_local, local_heads)
    value_landed = swap(own_v, "hst", hosts, 1, 1)
    own_keys, own_values = prepare(own_k, own_v, False)
    done = own(0, 2)
    parts = list(relay(is_even, own_k, value_landed, (done,), kv_local))
    parts_landed = [swap(x, "hst", hosts, *along[kv]) for kv, x in enumerate(parts)]
    done = own(2, 2, (parts[0],))
    queries = by_chip(query_q, landed, bits, (done,))
    landed = swap(queries, "hst", hosts, 1, 1)
    anchor = {}

    def pass_on(kv, after):
        (parts[kv],) = relay(source_first, parts[kv], parts_landed[kv], after)
        parts_landed[kv] = swap(parts[kv], "hst", hosts, *along[1 - kv])
        return parts[kv]

    def complete(kv, after):
        (held,) = relay(done_early[kv], parts[kv], parts_landed[kv], after)
        anchor[kv] = held, swap(held, "hst", hosts, 1, 1)
        return held

    keep, give = source_part(lengths, own_keys, own_v, query_kv, queries, landed, q_rows, per_kv, ())
    landed = swap(give, "hst", hosts, 1, 1)
    done = own(4, 4, (keep,))
    source = merge_part([keep, landed], False, (done,))
    landed = swap(source, "hst", hosts, *along[0])
    done = pass_on(0, (source,))
    done = own(8, 8, (done,))
    source = merge_part([source, landed], False, (done,))
    landed = swap(source, "hst", hosts, *along[1])
    done = complete(0, (source,))
    done = pass_on(1, (done,))
    anchor[0] = prepare(*anchor[0], True, (done,))
    results = {}

    def anchors(first, count, after, last=False):
        results[first] = anchor_part(
            lengths, ctx_q, states, own_keys, own_values, anchor[first // per_kv],
            first, count, per_kv, dict(results) if last else None, after,
        )
        return results[first]

    done = anchors(0, 6, ())
    attended = merge_part([source, landed], True, (done,))
    landed = swap(attended, "hst", hosts, 1, 1)
    done = complete(1, (attended,))
    terms = project_part(attended, landed, out_weight, (done,))
    done = terms
    shares = [[(10, 6, True)], [(6, 2, False), (8, 2, False)]]
    step = 1
    while step < groups:
        landed = swap(terms, "tp", groups, step, step)
        last = False
        for first, count, last in shares.pop() if shares else ():
            if first == per_kv:
                anchor[1] = prepare(*anchor[1], True, (done,))
            done = anchors(first, count, (terms, done), last)
        terms = add_part(terms, landed, () if last else (done,))
        step *= 2
    for group in reversed(shares):
        for first, count, last in group:
            done = anchors(first, count, (), last)
    return done, terms


def solution(mesh):
    hosts, groups = mesh.shape["hst"], mesh.shape["tp"]
    return jax.shard_map(
        functools.partial(per_device, hosts, groups),
        mesh=mesh,
        in_specs=(
            P("hst", "tp"),
            P(None, "hst", None),
            P(),
            P("hst", "tp"),
            P(None, "hst", None),
            P("tp", "hst"),
        ),
        out_specs=(P("hst", "tp"), P(None, "hst")),
        check_vma=False,
    )
```
